32 devices in a mesh: dp: 8 (over y, x, core), head: 4 (over z).
Axes of the slice: x: 2, y: 2, z: 4, core: 2. Of those that a mesh axis runs over, the one named last changes fastest.
Arguments:
- frames_in: bfloat16 [8192, 768], P(('dp', 'head')), may hold values from -6 to 6
- step_embed: bfloat16 [24, 768], P('dp'), may hold values from -6 to 6
- text_feats: bfloat16 [6144, 768], P('dp'), may hold values from -6 to 6
- clip_frames: int32 [8, 3], P('dp'), may hold values from 250 to 512, as said below
- text_tokens: int32 [8, 3], P('dp'), may hold values from 5 to 256
- out_grad: bfloat16 [8192, 768], P(('dp', 'head')), may hold values from -6 to 6
- ada_weight: bfloat16 [768, 4608], P('dp'), may hold values from -0.21875 to 0.21875
- ada_bias: bfloat16 [4608], P('dp'), may hold values from -1.75 to 1.75
- qkv_weight: bfloat16 [768, 3, 768], P('dp', None, 'head'), may hold values from -0.21875 to 0.21875
- qv_bias: bfloat16 [2, 12, 64], P(None, 'head', 'dp'), may hold values from -1.75 to 1.75
- attn_out_weight: bfloat16 [768, 768], P('head', 'dp'), may hold values from -1.25 to 1.25
- attn_out_bias: bfloat16 [768], P('dp'), may hold values from -1.75 to 1.75
- cross_gain: bfloat16 [768], P('dp'), may hold values from 0.5 to 1.5
- cross_q_weight: bfloat16 [768, 768], P('dp', 'head'), may hold values from -0.21875 to 0.21875
- cross_q_bias: bfloat16 [12, 64], P('head', 'dp'), may hold values from -1.75 to 1.75
- cross_kv_weight: bfloat16 [768, 2, 768], P('dp', None, 'head'), may hold values from -0.21875 to 0.21875
- cross_v_bias: bfloat16 [12, 64], P('head', 'dp'), may hold values from -1.75 to 1.75
- cross_out_weight: bfloat16 [768, 768], P('head', 'dp'), may hold values from -0.875 to 0.875
- cross_out_bias: bfloat16 [768], P('dp'), may hold values from -1.75 to 1.75
- mlp_in_weight: bfloat16 [768, 3072], P('dp', 'head'), may hold values from -0.21875 to 0.21875
- mlp_in_bias: bfloat16 [12, 256], P('head', 'dp'), may hold values from -1.75 to 1.75
- mlp_out_weight: bfloat16 [3072, 768], P('head', 'dp'), may hold values from -0.109375 to 0.109375
- mlp_out_bias: bfloat16 [768], P('dp'), may hold values from -1.75 to 1.75
Outputs:
- layer_out: bfloat16 [8192, 768], P(('dp', 'head'))
- frames_grad: float32 [8192, 768], P(('dp', 'head'))
- step_grad: float32 [24, 768], P('dp')
- text_grad: float32 [6144, 768], P(('dp', 'head'))
- ada_weight_grad: float32 [768, 4608], P('dp')
- ada_bias_grad: float32 [4608], P('dp')
- qkv_weight_grad: float32 [768, 3, 768], P('dp', None, 'head')
- qv_bias_grad: float32 [2, 12, 64], P(None, 'head', 'dp')
- attn_out_weight_grad: float32 [768, 768], P('head', 'dp')
- attn_out_bias_grad: float32 [768], P('dp')
- cross_gain_grad: float32 [768], P('dp')
- cross_q_weight_grad: float32 [768, 768], P('dp', 'head')
- cross_q_bias_grad: float32 [12, 64], P('head', 'dp')
- cross_kv_weight_grad: float32 [768, 2, 768], P('dp', None, 'head')
- cross_v_bias_grad: float32 [12, 64], P('head', 'dp')
- cross_out_weight_grad: float32 [768, 768], P('head', 'dp')
- cross_out_bias_grad: float32 [768], P('dp')
- mlp_in_weight_grad: float32 [768, 3072], P('dp', 'head')
- mlp_in_bias_grad: float32 [12, 256], P('head', 'dp')
- mlp_out_weight_grad: float32 [3072, 768], P('head', 'dp')
- mlp_out_bias_grad: float32 [768], P('dp')
The draws below stay inside these ranges and needn't reach their ends.
Inputs may be any that keep to these rules, and one draw needn't show every extreme that they name: Each row of clip_frames sums to 1024; exactly one entry of each row is 512, every entry is 250 or more.
All inputs are finite; a program needn't handle non-finite values.
Results may differ from the reference program's by a relative error of at most 0.029.
Values may be sent and summed in bfloat16 or wider, within the bound.
No kernel may reach another device: no remote copies, remote signals or barrier semaphores. Data moves between devices by JAX's collectives and lax.ppermute only.
A program may use at most 192 MiB of HBM per device.

```python
import jax
import jax.numpy as jnp
from jax import lax

D = 768
HEADS = 12
HD = 64
FF = 3072
TXT = 256
CLIP_MIN = 250
GROUP = 1024
CLIPS = 3
CLIP_MAX = 512
FRAMES = 8192
ALL_CLIPS = 24
TEXT_ROWS = 6144
N_DP = 8


def draw_clip_frames(key, part):
    key = jax.random.fold_in(key, 7)
    others = CLIPS - 1
    spare = GROUP - CLIP_MAX - others * CLIP_MIN
    share_key, order_key = jax.random.split(key)
    shares = jax.random.randint(share_key, (N_DP, others), 1, 5).astype(jnp.int32)
    weight_total = jnp.sum(shares, axis=1, keepdims=True)
    extra = spare * shares // weight_total
    leftover = spare - jnp.sum(extra, axis=1)
    extra = extra.at[:, 0].add(leftover)
    longest = jnp.full((N_DP, 1), CLIP_MAX, jnp.int32)
    rows = jnp.concatenate([longest, (CLIP_MIN + extra).astype(jnp.int32)], axis=1)
    row_keys = jax.random.split(order_key, N_DP)

    def shuffle_order(row_key):
        return jax.random.permutation(row_key, CLIPS)
    order = jax.vmap(shuffle_order)(row_keys).astype(jnp.int32)
    return jnp.take_along_axis(rows, order, axis=1).astype(jnp.int32)


def plant(values, rng, least, high):
    longest = values.shape.index(max(values.shape))
    spots = []
    for shift in (0, 1):
        where = [jax.random.randint(jax.random.fold_in(rng, axis), (), 0, length) for axis, length in enumerate(values.shape)]
        where[longest] = (where[longest] + shift) % values.shape[longest]
        spots.append(tuple(where))
    return values.at[spots[0]].set(least).at[spots[1]].set(high)


def block_scale(stream_key, dims, cuts, least, top_value):
    level = 1.0
    for axis_at, blocks in cuts:
        draws = jax.random.uniform(jax.random.fold_in(jax.random.fold_in(stream_key, 6), axis_at), (blocks,), jnp.float32, least / len(cuts), top_value / len(cuts))
        level = level * jnp.repeat(jnp.exp(draws), dims[axis_at] // blocks).reshape((-1,) + (1,) * (len(dims) - 1 - axis_at))
    return level


def noise(rng, extent, scale, most, cuts=(), kind=jnp.bfloat16):
    values = jax.random.normal(rng, extent, jnp.float32) * scale
    if len(cuts) > 0:
        values = block_scale(rng, extent, cuts, -0.22, 0.18) * values
    return jnp.clip(values, min=-most, max=most).astype(kind)


def setup_inputs(seed: int = 0) -> dict:
    keys = jax.random.split(jax.random.key(seed), 24)
    return {
        "frames_in": noise(keys[0], (FRAMES, D), 1.0, 6.0, ((0, 32),)),
        "step_embed": noise(keys[1], (ALL_CLIPS, D), 1.0, 6.0, ((0, 8),)),
        "text_feats": noise(keys[2], (TEXT_ROWS, D), 1.0, 6.0, ((0, 8),)),
        "clip_frames": draw_clip_frames(jax.random.fold_in(keys[23], 71), 0),
        "text_tokens": plant(jax.random.randint(keys[4], (N_DP, CLIPS), 5, TXT + 1), jax.random.fold_in(keys[4], 1), 5, TXT).astype(jnp.int32),
        "out_grad": noise(keys[5], (FRAMES, D), 1.0, 6.0, ((0, 32),)),
        "ada_weight": noise(keys[6], (D, 6 * D), D ** -0.5, 0.21875, ((0, 8),)),
        "ada_bias": noise(keys[7], (6 * D,), 0.3, 1.75, ((0, 8),)),
        "qkv_weight": noise(keys[8], (D, 3, D), D ** -0.5, 0.21875, ((0, 8), (2, 4))),
        "qv_bias": noise(keys[9], (2, HEADS, HD), 0.3, 1.75, ((1, 4), (2, 8))),
        "attn_out_weight": noise(keys[10], (D, D), (D * 16 // CLIP_MAX) ** -0.5, 1.25, ((0, 4), (1, 8))),
        "attn_out_bias": noise(keys[11], (D,), 0.3, 1.75, ((0, 8),)),
        "cross_gain": jnp.clip(1.0 + 0.1 * jax.random.normal(keys[12], (D,), jnp.float32), 0.5, 1.5).astype(jnp.bfloat16),
        "cross_q_weight": noise(keys[13], (D, D), D ** -0.5, 0.21875, ((0, 8), (1, 4))),
        "cross_q_bias": noise(keys[14], (HEADS, HD), 0.3, 1.75, ((0, 4), (1, 8))),
        "cross_kv_weight": noise(keys[15], (D, 2, D), D ** -0.5, 0.21875, ((0, 8), (2, 4))),
        "cross_v_bias": noise(keys[16], (HEADS, HD), 0.3, 1.75, ((0, 4), (1, 8))),
        "cross_out_weight": noise(keys[17], (D, D), (D * 16 // TXT) ** -0.5, 0.875, ((0, 4), (1, 8))),
        "cross_out_bias": noise(keys[18], (D,), 0.3, 1.75, ((0, 8),)),
        "mlp_in_weight": noise(keys[19], (D, FF), D ** -0.5, 0.21875, ((0, 8), (1, 4))),
        "mlp_in_bias": noise(keys[20], (HEADS, FF // HEADS), 0.3, 1.75, ((0, 4), (1, 8))),
        "mlp_out_weight": noise(keys[21], (FF, D), FF ** -0.5, 0.109375, ((0, 4), (1, 8))),
        "mlp_out_bias": noise(keys[22], (D,), 0.3, 1.75, ((0, 8),)),
    }


@jax.custom_vjp
def low(v):
    return lax.optimization_barrier(v.astype(jnp.bfloat16)).astype(jnp.float32)

@jax.custom_vjp
def low_back(v):
    return v

def low_keep(v):
    return (low(v), None)

def low_pass(kept, grad):
    return (grad,)

def back_keep(v):
    return (v, None)

def back_low(kept, grad):
    return (low(grad),)
low.defvjp(low_keep, low_pass)
low_back.defvjp(back_keep, back_low)
epsilon = 1e-06
highest = lax.Precision.HIGHEST

def product(former, latter):
    return jnp.dot(former, latter, precision=highest)

def normalize(tensor):
    average = lax.optimization_barrier(jnp.mean(tensor, axis=-1, keepdims=True))
    centered = tensor - average
    spread = lax.optimization_barrier(jnp.mean(centered * centered, axis=-1, keepdims=True))
    return centered * lax.rsqrt(spread + epsilon)

def attend_block(queries, key_heads, value_heads, allowed):
    scores = jnp.einsum('rhd,khd->hrk', queries, key_heads, precision=highest) * 0.125
    scores = low_back(scores)
    scores = jnp.where(allowed[None], scores, -1e+30)
    weights = low(jax.nn.softmax(scores, axis=-1))
    return jnp.einsum('hrk,khd->rhd', weights, value_heads, precision=highest)

def attention(queries, key_heads, value_heads, query_clip, key_clip, key_live):
    row_count = queries.shape[0]
    block_rows = min(512, row_count)
    block_count = row_count // block_rows

    def one_block(pieces):
        query_block, clip_block = pieces
        allowed = (clip_block[:, None] == key_clip[None, :]) & key_live[None, :]
        return attend_block(query_block, key_heads, value_heads, allowed)
    outputs = lax.map(jax.checkpoint(one_block), (queries.reshape(block_count, block_rows, queries.shape[1], queries.shape[2]), query_clip.reshape(block_count, block_rows)))
    return outputs.reshape(queries.shape)

def layer_forward(params, frames, step_rows, text_rows, frame_clip, text_clip, text_live):
    ada_weight, ada_bias, qkv_weight, qv_bias, attn_out_weight, attn_out_bias, cross_gain, cross_q_weight, cross_q_bias, cross_kv_weight, cross_v_bias, cross_out_weight, cross_out_bias, mlp_in_weight, mlp_in_bias, mlp_out_weight, mlp_out_bias = params
    modulation = low_back(product(low(jax.nn.silu(step_rows)), ada_weight) + ada_bias)
    choose = (frame_clip[:, None] == jnp.arange(CLIPS, dtype=jnp.int32)[None, :]).astype(jnp.float32)
    per_frame = product(choose, modulation)
    shift_one, scale_one, gate_one, shift_two, scale_two, gate_two = jnp.split(per_frame, 6, axis=1)
    hidden_one = low(normalize(frames) * (1.0 + scale_one) + shift_one)
    zeros_row = jnp.zeros((D,), jnp.float32)
    qv_rows = qv_bias.reshape(2, D)
    qkv_bias = jnp.concatenate([qv_rows[0], zeros_row, qv_rows[1]])
    qkv_rows = low(low_back(product(hidden_one, qkv_weight.reshape(D, 3 * D)) + qkv_bias))
    head_rows = qkv_rows.reshape(GROUP, 3, HEADS, HD)
    all_live = frame_clip >= 0
    attended = attention(head_rows[:, 0], head_rows[:, 1], head_rows[:, 2], frame_clip, frame_clip, all_live)
    attended = low(low_back(attended.reshape(GROUP, D)))
    attn_branch = low_back(product(attended, attn_out_weight) + attn_out_bias)
    after_self = frames + gate_one * attn_branch
    hidden_two = low(normalize(after_self) * cross_gain)
    cross_query = low(low_back(product(hidden_two, cross_q_weight) + cross_q_bias.reshape(D)))
    cross_kv = low(low_back(product(text_rows, cross_kv_weight.reshape(D, 2 * D)) + jnp.concatenate([zeros_row, cross_v_bias.reshape(D)])))
    text_heads = cross_kv.reshape(CLIPS * TXT, 2, HEADS, HD)
    cross_attended = attention(cross_query.reshape(GROUP, HEADS, HD), text_heads[:, 0], text_heads[:, 1], frame_clip, text_clip, text_live)
    cross_attended = low(low_back(cross_attended.reshape(GROUP, D)))
    cross_branch = low_back(product(cross_attended, cross_out_weight) + cross_out_bias)
    after_cross = after_self + cross_branch
    hidden_three = low(normalize(after_cross) * (1.0 + scale_two) + shift_two)
    pre_activation = low_back(product(hidden_three, mlp_in_weight) + mlp_in_bias.reshape(FF))
    activated = low(jax.nn.gelu(pre_activation, approximate=True))
    mlp_branch = low_back(product(activated, mlp_out_weight) + mlp_out_bias)
    return after_cross + gate_two * mlp_branch

def reference(frames_in, step_embed, text_feats, clip_frames, text_tokens, out_grad, ada_weight, ada_bias, qkv_weight, qv_bias, attn_out_weight, attn_out_bias, cross_gain, cross_q_weight, cross_q_bias, cross_kv_weight, cross_v_bias, cross_out_weight, cross_out_bias, mlp_in_weight, mlp_in_bias, mlp_out_weight, mlp_out_bias):
    params = tuple((weight.astype(jnp.float32) for weight in (ada_weight, ada_bias, qkv_weight, qv_bias, attn_out_weight, attn_out_bias, cross_gain, cross_q_weight, cross_q_bias, cross_kv_weight, cross_v_bias, cross_out_weight, cross_out_bias, mlp_in_weight, mlp_in_bias, mlp_out_weight, mlp_out_bias)))
    frames = frames_in.astype(jnp.float32).reshape(N_DP, GROUP, D)
    step_all = step_embed.astype(jnp.float32).reshape(N_DP, CLIPS, D)
    text_all = text_feats.astype(jnp.float32).reshape(N_DP, CLIPS * TXT, D)
    cotangent = out_grad.astype(jnp.float32).reshape(N_DP, GROUP, D)

    def one_group(summed, pieces):
        frame_rows, step_rows, text_rows, lengths, tokens, grad_rows = pieces
        clip_ends = jnp.cumsum(lengths).astype(jnp.int32)
        position = jnp.arange(GROUP, dtype=jnp.int32)
        frame_clip = lax.optimization_barrier(jnp.sum((position[:, None] >= clip_ends[None, :]).astype(jnp.int32), axis=1)).astype(jnp.int32)
        text_index = jnp.arange(CLIPS * TXT, dtype=jnp.int32)
        text_clip = (text_index // TXT).astype(jnp.int32)
        text_live = text_index % TXT < tokens[text_clip]

        def forward(weights, frame_vals, step_vals, text_vals):
            return layer_forward(weights, frame_vals, step_vals, text_vals, frame_clip, text_clip, text_live)
        result, pullback = jax.vjp(forward, params, frame_rows, step_rows, text_rows)
        weight_grads, frame_grad, step_grad, text_grad = pullback(grad_rows)
        summed = jax.tree.map(jnp.add, summed, weight_grads)
        return (summed, (result.astype(jnp.bfloat16), frame_grad, step_grad, text_grad))
    initial = tuple((jnp.zeros_like(weight) for weight in params))
    summed, (results, frame_grads, step_grads, text_grads) = lax.scan(one_group, initial, (frames, step_all, text_all, clip_frames, text_tokens, cotangent))
    return (results.reshape(FRAMES, D), frame_grads.reshape(FRAMES, D), step_grads.reshape(ALL_CLIPS, D), text_grads.reshape(TEXT_ROWS, D), summed[0], summed[1], summed[2], summed[3], summed[4], summed[5], summed[6], summed[7], summed[8], summed[9], summed[10], summed[11], summed[12], summed[13], summed[14], summed[15], summed[16])
```

```python
from functools import partial

import jax
import jax.numpy as jnp
from jax import lax
from jax.experimental import pallas as pl
from jax.experimental.pallas import tpu as pltpu
from jax.sharding import PartitionSpec as P

D = 768
HD = 64
TXT = 256
WIN = 128
EPS = 1e-06
NEG = -1e30
F32 = jnp.float32
BF16 = jnp.bfloat16
HIGH = lax.Precision.HIGHEST
S_Z, S_END, S_TOK, S_OFF = 0, 1, 3, 8
S_LEN = 16


def nn(a, b):
    return lax.dot_general(a, b, (((1,), (0,)), ((), ())), preferred_element_type=F32)


def nt(a, b):
    return lax.dot_general(a, b, (((1,), (1,)), ((), ())), preferred_element_type=F32)


def tn(a, b):
    return lax.dot_general(a, b, (((0,), (0,)), ((), ())), preferred_element_type=F32)


def normalize(v):
    centered = v - jnp.mean(v, axis=-1, keepdims=True)
    inverse = lax.rsqrt(jnp.mean(centered * centered, axis=-1, keepdims=True) + EPS)
    return centered * inverse, inverse


def normalize_back(u, normed, inverse):
    return inverse * (
        u
        - jnp.mean(u, axis=-1, keepdims=True)
        - normed * jnp.mean(u * normed, axis=-1, keepdims=True)
    )


def clip_of(position, scal):
    return (position >= scal[S_END]).astype(jnp.int32) + (position >= scal[S_END + 1]).astype(
        jnp.int32
    )


def frame_position(index, block, rows, splits, scal):
    return lax.rem(scal[S_Z] - block + splits, splits) * rows + index


def per_row(mod_ref, part, clip):
    cols = slice(part * D, (part + 1) * D)
    first, second, third = (mod_ref[c : c + 1, cols] for c in range(3))
    return jnp.where(clip == 0, first, jnp.where(clip == 1, second, third))


def clip_sums(clip_row, value):
    which = lax.broadcasted_iota(jnp.int32, (8, clip_row.shape[1]), 0)
    choose = (which == clip_row).astype(F32)
    return lax.dot_general(
        choose, value, (((1,), (0,)), ((), ())), precision=HIGH, preferred_element_type=F32
    )


def lanes(rows, low):
    lane = lax.broadcasted_iota(jnp.int32, (rows, WIN), 1)
    return lane < HD if low else lane >= HD


def keep(value, low):
    return jnp.where(lanes(value.shape[0], low), value, jnp.zeros_like(value))


def swap(value):
    return pltpu.roll(value, HD, 1)


def load_start(pieces, buffer, sems, scal, first):
    copies = []
    for j, piece in enumerate(pieces):
        rows = piece.shape[1]
        start = pl.multiple_of(scal[S_OFF + j], 32)
        copy = pltpu.make_async_copy(piece, buffer.at[:, pl.ds(start, rows), :], sems.at[first + j])
        copy.start()
        copies.append(copy)
    return copies


def store_copies(buffer, z, outs, sems, scal, first):
    copies = []
    j = 0
    for out in outs:
        for i in range(out.shape[0]):
            rows = out.shape[2]
            start = pl.multiple_of(scal[S_OFF + j], 32)
            copies.append(
                pltpu.make_async_copy(
                    buffer.at[z, pl.ds(start, rows), :], out.at[i, z], sems.at[first + j, z]
                )
            )
            j += 1
    return copies


def attend(queries, kv, mask, scores, probs, count):
    rows = queries.shape[0]
    step = 256
    outs, totals = [], []
    for h in range(3):
        if h < 2:
            query = keep(queries[:, :WIN], h == 0)
            kcol, vcol = 0, 1
        else:
            query = queries[:, WIN:]
            kcol, vcol = 2, 3
        peak = None
        for lo in range(0, count, step):
            part = nt(kv(lo, lo + step, kcol), query) + mask[lo : lo + step, :]
            scores[lo : lo + step, :] = part
            top = jnp.max(part, axis=0, keepdims=True)
            peak = top if peak is None else jnp.maximum(peak, top)
        total = jnp.zeros((1, rows), F32)
        for lo in range(0, count, step):
            part = jnp.exp(scores[lo : lo + step, :] - peak)
            total = total + jnp.sum(part, axis=0, keepdims=True)
            probs[lo : lo + step, :] = part.astype(BF16)
        out = tn(kv(0, count, vcol), probs[0:count, :]) * (1.0 / total)
        outs.append(out)
        totals.append(peak + jnp.log(total))
    cat = jnp.concatenate(
        [jnp.zeros((HD, rows), F32), outs[2][:HD], outs[0][:HD], outs[1][HD:]], axis=0
    )
    return cat.T.astype(BF16), totals


def attend_back(queries, kv, out_grad, mask, totals, probs, grads, count, put):
    rows = queries.shape[0]
    step = 256
    wide = out_grad.astype(F32)
    second = keep(swap(wide[:, :WIN]), True).astype(BF16)
    query_parts = []
    heads = []
    for h in range(3):
        if h < 2:
            query = keep(queries[:, :WIN], h == 0)
            given = keep(out_grad[:, WIN:], h == 0)
            kcol, vcol = 0, 1
        else:
            query, given = queries[:, WIN:], second
            kcol, vcol = 2, 3
        heads.append((query, given))
        delta = jnp.zeros((1, rows), F32)
        for lo in range(0, count, step):
            part = nt(kv(lo, lo + step, kcol), query) + mask[lo : lo + step, :]
            weights = jnp.exp(part - totals[h])
            weight_grad = nt(kv(lo, lo + step, vcol), given)
            delta = delta + jnp.sum(weights * weight_grad, axis=0, keepdims=True)
            probs[h, lo : lo + step, :] = weights
            grads[h, lo : lo + step, :] = weight_grad
        query_part = jnp.zeros((rows, WIN), F32)
        for lo in range(0, count, step):
            part = probs[h, lo : lo + step, :]
            score_grad = (part * (grads[h, lo : lo + step, :] - delta)).astype(BF16)
            grads[h, lo : lo + step, :] = score_grad.astype(F32)
            query_part = query_part + tn(score_grad, kv(lo, lo + step, kcol))
        query_parts.append(query_part * 0.125)
    for lo in range(0, count, step):
        hi = lo + step
        prob = [probs[h, lo:hi, :].astype(BF16) for h in range(3)]
        grad = [grads[h, lo:hi, :].astype(BF16) for h in range(3)]
        put(
            lo,
            hi,
            nn(grad[0], heads[0][0]) + nn(grad[1], heads[1][0]),
            nn(prob[0], heads[0][1]) + nn(prob[1], heads[1][1]),
            nn(grad[2], heads[2][0]),
            nn(prob[2], heads[2][1]),
        )
    pair = jnp.where(lanes(rows, True), query_parts[0], query_parts[1])
    third = keep(swap(query_parts[2]), True)
    return pair, third


def self_mask(scal, mask, rows, splits):
    query = clip_of(
        frame_position(lax.broadcasted_iota(jnp.int32, (1, rows), 1), 0, rows, splits, scal), scal
    )
    for block in range(splits):
        key = clip_of(
            frame_position(
                lax.broadcasted_iota(jnp.int32, (rows, 1), 0), block, rows, splits, scal
            ),
            scal,
        )
        mask[block * rows : (block + 1) * rows, :] = jnp.where(key == query, 0.0, NEG)


def cross_mask(scal, mask, rows, splits, clips):
    query = clip_of(
        frame_position(lax.broadcasted_iota(jnp.int32, (1, rows), 1), 0, rows, splits, scal), scal
    )
    slot = lax.broadcasted_iota(jnp.int32, (TXT, 1), 0)
    for c in range(clips):
        allowed = (query == c) & (slot < scal[S_TOK + c])
        mask[c * TXT : (c + 1) * TXT, :] = jnp.where(allowed, 0.0, NEG)


def own_clip(scal, rows, splits, block=0):
    return clip_of(
        frame_position(lax.broadcasted_iota(jnp.int32, (rows, 1), 0), block, rows, splits, scal),
        scal,
    )


def own_clip_row(scal, rows, splits, block=0):
    return clip_of(
        frame_position(lax.broadcasted_iota(jnp.int32, (1, rows), 1), block, rows, splits, scal),
        scal,
    )


def shard_index(scal, z, splits):
    return lax.rem(scal[S_Z] - z + splits, splits)


def self_forward(n_p, splits, *refs):
    scal = refs[0]
    frames = refs[1 : 1 + splits]
    mod, bias, out_bias = refs[1 + splits : 4 + splits]
    pieces = refs[4 + splits : 4 + splits + n_p]
    hidden, kv_out, q_out, att_out, lse, branch_out, after = refs[
        4 + splits + n_p : 11 + splits + n_p
    ]
    weights, mask, scores, probs, sems = refs[11 + splits + n_p :]
    rows = frames[0].shape[0]
    count = rows * splits
    copies = load_start(pieces, weights, sems, scal, 0)
    self_mask(scal, mask, rows, splits)
    for block in range(splits):
        clip = own_clip(scal, rows, splits, block)
        normed, _ = normalize(frames[block][...].astype(F32))
        value = normed * (1.0 + per_row(mod, 1, clip)) + per_row(mod, 0, clip)
        hidden[block * rows : (block + 1) * rows, :] = value.astype(BF16)
    branch_out[...] = jnp.broadcast_to(out_bias[...], branch_out.shape)
    for copy in copies:
        copy.wait()

    def one(z, carry):
        bias_row = bias[shard_index(scal, z, splits)]
        for block in range(splits):
            span = slice(block * rows, (block + 1) * rows)
            part = nn(hidden[span, :], weights[z, :, WIN : 5 * WIN]) + bias_row[:, WIN : 5 * WIN]
            kv_out[z, span, :] = part.astype(BF16)
            if block == 0:
                third = keep(swap(part[:, 2 * WIN : 3 * WIN].astype(BF16).astype(F32)), False)
        pair = nn(hidden[0:rows, :], weights[z, :, 0:WIN]) + bias_row[:, 0:WIN]
        queries = (
            jnp.concatenate([pair.astype(BF16).astype(F32), third], axis=1) * 0.125
        ).astype(BF16)
        q_out[z] = queries

        def kv(lo, hi, col):
            return kv_out[z, lo:hi, col * WIN : (col + 1) * WIN]

        attended, totals = attend(queries, kv, mask, scores, probs, count)
        att_out[z] = attended
        for h in range(3):
            lse[z, h : h + 1, :] = totals[h]
        branch_out[...] += nt(attended, weights[z, :, 4 * WIN :])
        return carry

    lax.fori_loop(0, splits, one, 0)
    clip = own_clip(scal, rows, splits)
    after[...] = frames[0][...].astype(F32) + per_row(mod, 2, clip) * branch_out[...]


def cross_forward(n_p, splits, *refs):
    scal, after_self, text, gain, bias, out_bias = refs[:6]
    pieces = refs[6 : 6 + n_p]
    kv_out, q_out, att_out, lse, after = refs[6 + n_p : 11 + n_p]
    weights, mask, scores, probs, sems = refs[11 + n_p :]
    rows = after_self.shape[0]
    count = text.shape[0]
    copies = load_start(pieces, weights, sems, scal, 0)
    cross_mask(scal, mask, rows, splits, count // TXT)
    normed, _ = normalize(after_self[...])
    hidden = (normed * gain[...]).astype(BF16)
    after[...] = after_self[...] + out_bias[...]
    for copy in copies:
        copy.wait()

    def one(z, carry):
        bias_row = bias[shard_index(scal, z, splits)]
        for lo in range(0, count, 256):
            part = nn(text[lo : lo + 256, :], weights[z, :, WIN : 5 * WIN])
            kv_out[z, lo : lo + 256, :] = (part + bias_row[:, WIN : 5 * WIN]).astype(BF16)
        pair = nn(hidden, weights[z, :, 0:WIN]) + bias_row[:, 0:WIN]
        third = nn(hidden, weights[z, :, 3 * WIN : 4 * WIN]) + bias_row[:, 3 * WIN : 4 * WIN]
        third = keep(swap(third.astype(BF16).astype(F32)), False)
        queries = (
            jnp.concatenate([pair.astype(BF16).astype(F32), third], axis=1) * 0.125
        ).astype(BF16)
        q_out[z] = queries

        def kv(lo, hi, col):
            return kv_out[z, lo:hi, col * WIN : (col + 1) * WIN]

        attended, totals = attend(queries, kv, mask, scores, probs, count)
        att_out[z] = attended
        for h in range(3):
            lse[z, h : h + 1, :] = totals[h]
        after[...] += nt(attended, weights[z, :, 4 * WIN :])
        return carry

    lax.fori_loop(0, splits, one, 0)


def feed_forward(n_p, splits, *refs):
    scal, after_cross, upstream, mod, in_bias, out_bias = refs[:6]
    in_pieces = refs[6 : 6 + n_p]
    out_pieces = refs[6 + n_p : 6 + 2 * n_p]
    rest = refs[6 + 2 * n_p :]
    n_o = 2 if n_p > 1 else 1
    layer_out, d_after = rest[:2]
    in_grads = rest[2 : 2 + n_o]
    out_grads = rest[2 + n_o : 2 + 2 * n_o]
    in_bias_grad, out_bias_grad, sums = rest[2 + 2 * n_o : 5 + 2 * n_o]
    w_in, w_out, g_in, g_out, mlp, back, load_sems, store_sems = rest[5 + 2 * n_o :]
    rows = after_cross.shape[0]
    copies = load_start(in_pieces, w_in, load_sems, scal, 0)
    copies += load_start(out_pieces, w_out, load_sems, scal, n_p)
    clip = own_clip(scal, rows, splits)
    normed, inverse = normalize(after_cross[...])
    scale = 1.0 + per_row(mod, 4, clip)
    hidden = (normed * scale + per_row(mod, 3, clip)).astype(BF16)
    gate = per_row(mod, 5, clip)
    given = upstream[...].astype(F32)
    low = (given * gate).astype(BF16)
    low_wide = low.astype(F32)
    out_bias_grad[...] = jnp.sum(low_wide, axis=0, keepdims=True)
    hidden_t = hidden.astype(F32).T.astype(BF16)
    low_t = low_wide.T.astype(BF16)
    mlp[...] = jnp.broadcast_to(out_bias[...], mlp.shape)
    back[...] = jnp.zeros_like(back)
    for copy in copies:
        copy.wait()

    def one(z, carry):
        place = shard_index(scal, z, splits)
        pre = nn(hidden, w_in[z]) + in_bias[place]
        inner = 0.7978845608028654 * (pre + 0.044715 * (pre * pre * pre))
        curve = jnp.tanh(inner)
        half = 0.5 * (1.0 + curve)
        active = (pre * half).astype(BF16)
        slope = half + 0.5 * pre * (1.0 - curve * curve) * 0.7978845608028654 * (
            1.0 + 3.0 * 0.044715 * pre * pre
        )
        pre_grad = (slope * nn(low, w_out[z])).astype(BF16)
        in_bias_grad[place] = jnp.sum(pre_grad.astype(F32), axis=0, keepdims=True)
        mlp[...] += nt(active, w_out[z])
        back[...] += nt(pre_grad, w_in[z])
        g_in[z] = nn(hidden_t, pre_grad).astype(BF16)
        for copy in store_copies(g_in, z, in_grads, store_sems, scal, 0):
            copy.start()
        g_out[z] = nn(low_t, active).astype(BF16)
        for copy in store_copies(g_out, z, out_grads, store_sems, scal, n_p):
            copy.start()
        return carry

    lax.fori_loop(0, splits, one, 0)
    branch = mlp[...]
    layer_out[...] = (after_cross[...] + gate * branch).astype(BF16)
    hidden_grad = back[...]
    d_after[...] = given + normalize_back(hidden_grad * scale, normed, inverse)
    clip_row = own_clip_row(scal, rows, splits)
    sums[:, 0:D] = clip_sums(clip_row, hidden_grad)
    sums[:, D : 2 * D] = clip_sums(clip_row, hidden_grad * normed)
    sums[:, 2 * D :] = clip_sums(clip_row, given * branch)
    for z in range(splits):
        for copy in store_copies(g_in, z, in_grads, store_sems, scal, 0):
            copy.wait()
        for copy in store_copies(g_out, z, out_grads, store_sems, scal, n_p):
            copy.wait()


def cross_backward(n_p, splits, *refs):
    scal, d_cross, after_self, text, gain, mod, branch, kv_in, q_in, att_in, lse = refs[:11]
    pieces = refs[11 : 11 + n_p]
    rest = refs[11 + n_p :]
    n_o = 2 if n_p > 1 else 1
    grads = rest[:n_o]
    d_after, d_attn = rest[n_o : n_o + 2]
    text_own = rest[n_o + 2]
    text_parts = rest[n_o + 3 : n_o + 2 + splits]
    bias_grad, row_grads, sums = rest[n_o + 2 + splits : n_o + 5 + splits]
    weights, gbuf, mask, probs, dscore, key_grad, back, text_back, text_t, load_sems, store_sems = (
        rest[n_o + 5 + splits :]
    )
    rows = after_self.shape[0]
    count = text.shape[0]
    copies = load_start(pieces, weights, load_sems, scal, 0)
    cross_mask(scal, mask, rows, splits, count // TXT)
    normed, inverse = normalize(after_self[...])
    hidden = (normed * gain[...]).astype(BF16)
    hidden_t = hidden.astype(F32).T.astype(BF16)
    given = d_cross[...].astype(BF16)
    given_wide = given.astype(F32)
    given_t = given_wide.T.astype(BF16)
    for lo in range(0, count, 256):
        text_t[:, lo : lo + 256] = text[lo : lo + 256, :].astype(F32).T.astype(BF16)
    back[...] = jnp.zeros_like(back)
    text_back[...] = jnp.zeros_like(text_back)
    row_grads[...] = jnp.zeros_like(row_grads)
    row_grads[0:1, :] = jnp.sum(given_wide, axis=0, keepdims=True)
    for copy in copies:
        copy.wait()

    def one(z, carry):
        place = shard_index(scal, z, splits)

        def kv(lo, hi, col):
            return kv_in[z, lo:hi, col * WIN : (col + 1) * WIN]

        def put(lo, hi, k01, v01, k2, v2):
            key_grad[lo:hi, 0:WIN] = k01.astype(BF16)
            key_grad[lo:hi, WIN : 2 * WIN] = v01.astype(BF16)
            key_grad[lo:hi, 2 * WIN : 3 * WIN] = k2.astype(BF16)
            key_grad[lo:hi, 3 * WIN : 4 * WIN] = v2.astype(BF16)

        head_grad = nn(given, weights[z, :, 4 * WIN :]).astype(BF16)
        totals = [lse[z, h : h + 1, :] for h in range(3)]
        pair, third = attend_back(
            q_in[z], kv, head_grad, mask, totals, probs, dscore, count, put
        )
        pair, third = pair.astype(BF16), third.astype(BF16)
        part = nn(text_t[...], key_grad[...])
        out_part = nn(given_t, att_in[z])
        gbuf[z, :, 0:WIN] = nn(hidden_t, pair).astype(BF16)
        gbuf[z, :, WIN : 3 * WIN] = part[:, 0 : 2 * WIN].astype(BF16)
        gbuf[z, :, 3 * WIN : 4 * WIN] = (
            part[:, 2 * WIN : 3 * WIN] + nn(hidden_t, third)
        ).astype(BF16)
        gbuf[z, :, 4 * WIN : 5 * WIN] = (part[:, 3 * WIN :] + out_part[:, 0:WIN]).astype(BF16)
        gbuf[z, :, 5 * WIN :] = out_part[:, WIN:].astype(BF16)
        for copy in store_copies(gbuf, z, grads, store_sems, scal, 0):
            copy.start()
        back[...] += nt(pair, weights[z, :, 0:WIN]) + nt(third, weights[z, :, 3 * WIN : 4 * WIN])
        for lo in range(0, count, 256):
            text_back[lo : lo + 256, :] += nt(
                key_grad[lo : lo + 256, :], weights[z, :, WIN : 5 * WIN]
            )
        key_sums = jnp.sum(key_grad[...].astype(F32), axis=0, keepdims=True)
        bias_grad[place, :, 0:WIN] = jnp.sum(pair.astype(F32), axis=0, keepdims=True)
        bias_grad[place, :, WIN : 3 * WIN] = key_sums[:, 0 : 2 * WIN]
        bias_grad[place, :, 3 * WIN : 4 * WIN] = key_sums[:, 2 * WIN : 3 * WIN] + jnp.sum(
            third.astype(F32), axis=0, keepdims=True
        )
        bias_grad[place, :, 4 * WIN : 5 * WIN] = key_sums[:, 3 * WIN :]
        bias_grad[place, :, 5 * WIN :] = jnp.zeros((1, WIN), F32)
        return carry

    lax.fori_loop(0, splits, one, 0)
    hidden_grad = back[...]
    row_grads[1:2, :] = jnp.sum(hidden_grad * normed, axis=0, keepdims=True)
    total = d_cross[...] + normalize_back(hidden_grad * gain[...], normed, inverse)
    d_after[...] = total
    clip = own_clip(scal, rows, splits)
    d_attn[...] = (total * per_row(mod, 2, clip)).astype(BF16)
    sums[...] = clip_sums(own_clip_row(scal, rows, splits), total * branch[...])
    height = count // splits
    for k in range(splits):
        start = pl.multiple_of(shard_index(scal, k, splits) * height, 64)
        block = text_back[pl.ds(start, height), :]
        if k == 0:
            text_own[...] = block
        else:
            text_parts[k - 1][...] = block.astype(BF16)
    for z in range(splits):
        for copy in store_copies(gbuf, z, grads, store_sems, scal, 0):
            copy.wait()


def self_backward(n_p, splits, *refs):
    scal = refs[0]
    frames = refs[1 : 1 + splits]
    given_ref, hidden, kv_in, q_in, att_in, lse = refs[1 + splits : 7 + splits]
    pieces = refs[7 + splits : 7 + splits + n_p]
    rest = refs[7 + splits + n_p :]
    n_o = 2 if n_p > 1 else 1
    grads = rest[:n_o]
    own = rest[n_o]
    parts = rest[n_o + 1 : n_o + splits]
    bias_grad, row_grads, sums = rest[n_o + splits : n_o + 3 + splits]
    weights, gbuf, mask, probs, dscore, key_grad, back, hidden_t, load_sems, store_sems = rest[
        n_o + 3 + splits :
    ]
    rows = frames[0].shape[0]
    count = rows * splits
    copies = load_start(pieces, weights, load_sems, scal, 0)
    self_mask(scal, mask, rows, splits)
    given = given_ref[...]
    given_wide = given.astype(F32)
    given_t = given_wide.T.astype(BF16)
    for lo in range(0, count, 256):
        hidden_t[:, lo : lo + 256] = hidden[lo : lo + 256, :].astype(F32).T.astype(BF16)
    back[...] = jnp.zeros_like(back)
    row_grads[...] = jnp.zeros_like(row_grads)
    row_grads[0:1, :] = jnp.sum(given_wide, axis=0, keepdims=True)
    for copy in copies:
        copy.wait()

    def one(z, carry):
        place = shard_index(scal, z, splits)

        def kv(lo, hi, col):
            return kv_in[z, lo:hi, col * WIN : (col + 1) * WIN]

        def put(lo, hi, k01, v01, k2, v2):
            key_grad[lo:hi, 0:WIN] = k01.astype(BF16)
            key_grad[lo:hi, WIN : 2 * WIN] = v01.astype(BF16)
            key_grad[lo:hi, 2 * WIN : 3 * WIN] = k2.astype(BF16)
            key_grad[lo:hi, 3 * WIN : 4 * WIN] = v2.astype(BF16)

        head_grad = nn(given, weights[z, :, 4 * WIN :]).astype(BF16)
        totals = [lse[z, h : h + 1, :] for h in range(3)]
        pair, third = attend_back(
            q_in[z], kv, head_grad, mask, totals, probs, dscore, count, put
        )
        pair = pair.astype(BF16)
        key_grad[0:rows, 2 * WIN : 3 * WIN] = (
            key_grad[0:rows, 2 * WIN : 3 * WIN].astype(F32) + third
        ).astype(BF16)
        part = nn(hidden_t[...], key_grad[...])
        out_part = nn(given_t, att_in[z])
        gbuf[z, :, 0:WIN] = nn(hidden_t[:, 0:rows], pair).astype(BF16)
        gbuf[z, :, WIN : 4 * WIN] = part[:, 0 : 3 * WIN].astype(BF16)
        gbuf[z, :, 4 * WIN : 5 * WIN] = (part[:, 3 * WIN :] + out_part[:, 0:WIN]).astype(BF16)
        gbuf[z, :, 5 * WIN :] = out_part[:, WIN:].astype(BF16)
        for copy in store_copies(gbuf, z, grads, store_sems, scal, 0):
            copy.start()
        for lo in range(0, count, 256):
            back[lo : lo + 256, :] += nt(
                key_grad[lo : lo + 256, :], weights[z, :, WIN : 5 * WIN]
            )
        back[0:rows, :] += nt(pair, weights[z, :, 0:WIN])
        key_sums = jnp.sum(key_grad[...].astype(F32), axis=0, keepdims=True)
        bias_grad[place, :, 0:WIN] = jnp.sum(pair.astype(F32), axis=0, keepdims=True)
        bias_grad[place, :, WIN : 5 * WIN] = key_sums
        bias_grad[place, :, 5 * WIN :] = jnp.zeros((1, WIN), F32)
        return carry

    lax.fori_loop(0, splits, one, 0)
    shift = jnp.zeros((8, D), F32)
    scale = jnp.zeros((8, D), F32)
    for block in range(splits):
        value = back[block * rows : (block + 1) * rows, :]
        if block == 0:
            own[...] = value
        else:
            parts[block - 1][...] = value.astype(BF16)
        normed, _ = normalize(frames[block][...].astype(F32))
        clip_row = own_clip_row(scal, rows, splits, block)
        shift = shift + clip_sums(clip_row, value)
        scale = scale + clip_sums(clip_row, value * normed)
    sums[:, 0:D] = shift
    sums[:, D:] = scale
    for z in range(splits):
        for copy in store_copies(gbuf, z, grads, store_sems, scal, 0):
            copy.wait()


def finish(splits, *refs):
    scal, frames, mod, d_after, own = refs[:5]
    parts = refs[5 : 4 + splits]
    out = refs[4 + splits]
    rows = frames.shape[0]
    value = own[...]
    for part in parts:
        value = value + part[...].astype(F32)
    normed, inverse = normalize(frames[...].astype(F32))
    scale = 1.0 + per_row(mod, 1, own_clip(scal, rows, splits))
    out[...] = d_after[...] + normalize_back(value * scale, normed, inverse)


MEMORY = {"v": pltpu.VMEM, "s": pltpu.SMEM, "a": pl.ANY}


def call(body, inputs, outs, scratch, flops, name):
    moved = sum(a.size * a.dtype.itemsize for _, a in inputs)
    moved += sum(_size(s, t) for _, s, t in outs)
    return pl.pallas_call(
        body,
        out_shape=tuple(jax.ShapeDtypeStruct(s, t) for _, s, t in outs),
        in_specs=[pl.BlockSpec(memory_space=MEMORY[m]) for m, _ in inputs],
        out_specs=tuple(pl.BlockSpec(memory_space=MEMORY[m]) for m, _, _ in outs),
        scratch_shapes=scratch,
        compiler_params=pltpu.CompilerParams(vmem_limit_bytes=58 * 1024 * 1024),
        cost_estimate=pl.CostEstimate(flops=int(flops), bytes_accessed=int(moved), transcendentals=0),
        name=name,
    )(*[a for _, a in inputs])


def _size(shape, kind):
    total = jnp.dtype(kind).itemsize
    for s in shape:
        total *= s
    return total


class Ring:
    def __init__(self):
        self.n_dp = lax.axis_size("dp")
        self.splits = lax.axis_size("head")
        self.square = self.n_dp == 8
        if self.square:
            self.core = [(i, i ^ 1) for i in range(8)]
            self.first = [(i, i ^ (4 if i & 1 else 2)) for i in range(8)]
            self.second = [(i, i ^ (2 if i & 1 else 4)) for i in range(8)]

    def offsets(self):
        if not self.square:
            return [jnp.int32(0)]
        me = lax.axis_index("dp")
        rows = D // 8

        def kept(d):
            odd = d & 1
            return [d, d ^ (2 + 2 * odd), d ^ (4 - 2 * odd), d ^ 6]

        return [place * rows for place in kept(me) + kept(me ^ 1)]

    def z_pieces(self, value):
        n = self.splits
        return [value] + [
            lax.ppermute(value, "head", [(s, (s + k) % n) for s in range(n)]) for k in range(1, n)
        ]

    def z_back(self, parts):
        n = self.splits
        return [
            lax.ppermute(parts[k - 1], "head", [(s, (s - k) % n) for s in range(n)])
            for k in range(1, n)
        ]

    def gather(self, shard):
        mine = jnp.stack(self.z_pieces(shard))
        if not self.square:
            return [lax.all_gather(mine, "dp", axis=1, tiled=True)]
        one = lax.ppermute(mine, "dp", self.first)
        two = lax.ppermute(mine, "dp", self.second)
        three = lax.ppermute(one, "dp", self.second)
        kept = [mine, one, two, three]
        return kept + [lax.ppermute(k, "dp", self.core) for k in kept]

    def reduce(self, grads):
        if not self.square:
            mine = lax.psum_scatter(grads[0][0], "dp", scatter_dimension=1, tiled=True)
        else:
            other = lax.ppermute(grads[1], "dp", self.core)

            def added(i):
                return grads[0][i].astype(F32) + other[i].astype(F32)

            corner = lax.ppermute(added(3).astype(BF16), "dp", self.second)
            two = lax.ppermute(added(2).astype(BF16), "dp", self.second)
            one = lax.ppermute((added(1) + corner.astype(F32)).astype(BF16), "dp", self.first)
            mine = added(0) + one.astype(F32) + two.astype(F32)
        mine = mine.astype(F32)
        arrived = self.z_back([mine[k].astype(BF16) for k in range(1, self.splits)])
        total = mine[0]
        for part in arrived:
            total = total + part.astype(F32)
        return total


def to_layout(q, k, v, o):
    return jnp.concatenate(
        [
            q[:, :WIN],
            k[:, :WIN],
            v[:, :WIN],
            q[:, WIN:],
            k[:, WIN:],
            v[:, WIN:],
            o[:, WIN:],
            o[:, :WIN],
        ],
        axis=1,
    )


def from_layout(value):
    def pick(pair, third):
        return jnp.concatenate(
            [value[:, pair : pair + WIN], value[:, third : third + HD]], axis=1
        )

    return pick(0, 3 * WIN), pick(WIN, 3 * WIN + HD), pick(2 * WIN, 4 * WIN), pick(
        5 * WIN, 4 * WIN + HD
    )


def on_device(
    frames_in,
    step_embed,
    text_feats,
    clip_frames,
    text_tokens,
    out_grad,
    ada_weight,
    ada_bias,
    qkv_weight,
    qv_bias,
    attn_out_weight,
    attn_out_bias,
    cross_gain,
    cross_q_weight,
    cross_q_bias,
    cross_kv_weight,
    cross_v_bias,
    cross_out_weight,
    cross_out_bias,
    mlp_in_weight,
    mlp_in_bias,
    mlp_out_weight,
    mlp_out_bias,
):
    both = ("dp", "head")
    ring = Ring()
    n_dp, splits = ring.n_dp, ring.splits
    z_index = lax.axis_index("head")
    rows = frames_in.shape[0]
    count = rows * splits
    text_count = text_feats.shape[0]
    clips = clip_frames.shape[1]
    width = D // splits
    shard_rows = D // n_dp
    ends = jnp.cumsum(clip_frames[0])
    offs = ring.offsets()
    n_p = len(offs)
    scal = jnp.stack(
        [z_index, ends[0], ends[1], text_tokens[0, 0], text_tokens[0, 1], text_tokens[0, 2]]
        + [jnp.int32(0)] * 2
        + [o.astype(jnp.int32) for o in offs]
        + [jnp.int32(0)] * (S_LEN - S_OFF - n_p)
    ).astype(jnp.int32)

    shard_self = to_layout(
        qkv_weight[:, 0], qkv_weight[:, 1], qkv_weight[:, 2], attn_out_weight.T
    )
    shard_cross = to_layout(
        cross_q_weight, cross_kv_weight[:, 0], cross_kv_weight[:, 1], cross_out_weight.T
    )

    biases = [
        ada_bias,
        qv_bias.reshape(-1),
        attn_out_bias,
        cross_gain,
        cross_q_bias.reshape(-1),
        cross_v_bias.reshape(-1),
        cross_out_bias,
        mlp_in_bias.reshape(-1),
        mlp_out_bias,
    ]
    flat = jnp.concatenate(biases)
    cols = step_embed.reshape(clips, n_dp, shard_rows).transpose(1, 0, 2).reshape(n_dp, -1)
    sent = jnp.concatenate(
        [
            jnp.broadcast_to(flat[None, None], (n_dp, splits, flat.shape[0])),
            jnp.broadcast_to(cols[:, None], (n_dp, splits, cols.shape[1])),
        ],
        axis=2,
    ).reshape(n_dp * splits, -1)
    got = lax.all_to_all(sent, both, 0, 0, tiled=True).reshape(n_dp, splits, -1)
    step_cols = got[:, 0, flat.shape[0] :].reshape(n_dp * clips, shard_rows).astype(F32)
    silu_cols = jax.nn.silu(step_cols).astype(BF16)
    spots = []
    place = 0
    for b in biases:
        spots.append(got[:, :, place : place + b.shape[0]].astype(F32))
        place += b.shape[0]

    def over_dp(value):
        return value[:, 0].reshape(1, -1)

    def by_head(value, lead=1):
        n = value.shape[2] // (lead * 3)
        v = value.reshape(n_dp, splits, lead, 3, n).transpose(1, 2, 3, 0, 4)
        return v.reshape(splits, lead, 3 * n_dp * n)

    all_ada_bias = over_dp(spots[0])
    qv = by_head(spots[1], 2)
    nothing = jnp.zeros((splits, width), F32)
    bias_self = to_layout(qv[:, 0], nothing, qv[:, 1], nothing)[:, None]
    all_attn_bias = over_dp(spots[2])
    all_gain = over_dp(spots[3])
    bias_cross = to_layout(
        by_head(spots[4])[:, 0], nothing, by_head(spots[5])[:, 0], nothing
    )[:, None]
    all_cross_bias = over_dp(spots[6])
    all_in_bias = by_head(spots[7])
    all_out_bias = over_dp(spots[8])

    mod_part = jnp.dot(silu_cols, ada_weight, preferred_element_type=F32)
    mod_got = lax.all_to_all(mod_part.reshape(n_dp, clips, -1), "dp", 0, 0, tiled=True)
    mod = jnp.sum(mod_got, axis=0) + all_ada_bias

    frame_blocks = ring.z_pieces(frames_in)
    pieces_self = ring.gather(shard_self)
    pieces_cross = ring.gather(shard_cross)
    pieces_in = ring.gather(mlp_in_weight)
    pieces_out = ring.gather(mlp_out_weight.T)

    def dma(n):
        return pltpu.SemaphoreType.DMA(n)

    def any_of(arrays):
        return [("a", a) for a in arrays]

    def vmem_of(arrays):
        return [("v", a) for a in arrays]

    piece_rows = D // n_p
    kept_out = [("a", (max(n_p // 2, 1), splits, piece_rows, D), BF16)] * (2 if n_p > 1 else 1)
    n_o = len(kept_out)
    shard_type = pltpu.VMEM((splits, D, D), BF16)

    hidden_one, self_kv, self_q, self_att, self_lse, attn_branch, after_self = call(
        partial(self_forward, n_p, splits),
        [("s", scal)]
        + vmem_of(frame_blocks)
        + vmem_of([mod, bias_self, all_attn_bias])
        + any_of(pieces_self),
        [
            ("v", (count, D), BF16),
            ("v", (splits, count, 4 * WIN), BF16),
            ("v", (splits, rows, 2 * WIN), BF16),
            ("v", (splits, rows, 2 * WIN), BF16),
            ("v", (splits, 8, rows), F32),
            ("v", (rows, D), F32),
            ("v", (rows, D), F32),
        ],
        [
            shard_type,
            pltpu.VMEM((count, rows), F32),
            pltpu.VMEM((count, rows), F32),
            pltpu.VMEM((count, rows), BF16),
            dma((n_p,)),
        ],
        6e9,
        "self_forward",
    )
    cross_kv, cross_q, cross_att, cross_lse, after_cross = call(
        partial(cross_forward, n_p, splits),
        [("s", scal)]
        + vmem_of([after_self, text_feats, all_gain, bias_cross, all_cross_bias])
        + any_of(pieces_cross),
        [
            ("v", (splits, text_count, 4 * WIN), BF16),
            ("v", (splits, rows, 2 * WIN), BF16),
            ("v", (splits, rows, 2 * WIN), BF16),
            ("v", (splits, 8, rows), F32),
            ("v", (rows, D), F32),
        ],
        [
            shard_type,
            pltpu.VMEM((text_count, rows), F32),
            pltpu.VMEM((text_count, rows), F32),
            pltpu.VMEM((text_count, rows), BF16),
            dma((n_p,)),
        ],
        5e9,
        "cross_forward",
    )
    results = call(
        partial(feed_forward, n_p, splits),
        [("s", scal)]
        + vmem_of([after_cross, out_grad, mod, all_in_bias, all_out_bias])
        + any_of(pieces_in)
        + any_of(pieces_out),
        [("v", (rows, D), BF16), ("v", (rows, D), F32)]
        + kept_out
        + kept_out
        + [
            ("v", (splits, 1, D), F32),
            ("v", (1, D), F32),
            ("v", (8, 3 * D), F32),
        ],
        [
            shard_type,
            shard_type,
            shard_type,
            shard_type,
            pltpu.VMEM((rows, D), F32),
            pltpu.VMEM((rows, D), F32),
            dma((2 * n_p,)),
            dma((2 * n_p, splits)),
        ],
        8e9,
        "feed_forward",
    )
    layer_out, d_after_cross = results[:2]
    grads_in = results[2 : 2 + n_o]
    grads_out = results[2 + n_o : 2 + 2 * n_o]
    in_bias_grad, out_bias_grad, sums_two = results[2 + 2 * n_o :]
    height = text_count // splits
    results = call(
        partial(cross_backward, n_p, splits),
        [("s", scal)]
        + vmem_of(
            [
                d_after_cross,
                after_self,
                text_feats,
                all_gain,
                mod,
                attn_branch,
                cross_kv,
                cross_q,
                cross_att,
                cross_lse,
            ]
        )
        + any_of(pieces_cross),
        kept_out
        + [("v", (rows, D), F32), ("v", (rows, D), BF16), ("v", (height, D), F32)]
        + [("v", (height, D), BF16)] * (splits - 1)
        + [("v", (splits, 1, D), F32), ("v", (8, D), F32), ("v", (8, D), F32)],
        [
            shard_type,
            shard_type,
            pltpu.VMEM((text_count, rows), F32),
            pltpu.VMEM((3, text_count, rows), F32),
            pltpu.VMEM((3, text_count, rows), F32),
            pltpu.VMEM((text_count, 4 * WIN), BF16),
            pltpu.VMEM((rows, D), F32),
            pltpu.VMEM((text_count, D), F32),
            pltpu.VMEM((D, text_count), BF16),
            dma((n_p,)),
            dma((n_p, splits)),
        ],
        9e9,
        "cross_backward",
    )
    grads_cross = results[:n_o]
    d_after_self, d_attn, text_own = results[n_o : n_o + 3]
    text_parts = results[n_o + 3 : n_o + 2 + splits]
    cross_bias_grad, cross_rows, gate_sums = results[n_o + 2 + splits :]
    results = call(
        partial(self_backward, n_p, splits),
        [("s", scal)]
        + vmem_of(frame_blocks)
        + vmem_of([d_attn, hidden_one, self_kv, self_q, self_att, self_lse])
        + any_of(pieces_self),
        kept_out
        + [("v", (rows, D), F32)]
        + [("v", (rows, D), BF16)] * (splits - 1)
        + [("v", (splits, 1, D), F32), ("v", (8, D), F32), ("v", (8, 2 * D), F32)],
        [
            shard_type,
            shard_type,
            pltpu.VMEM((count, rows), F32),
            pltpu.VMEM((3, count, rows), F32),
            pltpu.VMEM((3, count, rows), F32),
            pltpu.VMEM((count, 4 * WIN), BF16),
            pltpu.VMEM((count, D), F32),
            pltpu.VMEM((D, count), BF16),
            dma((n_p,)),
            dma((n_p, splits)),
        ],
        12e9,
        "self_backward",
    )
    grads_self = results[:n_o]
    own_part = results[n_o]
    parts = results[n_o + 1 : n_o + splits]
    self_bias_grad, self_rows, sums_one = results[n_o + splits :]

    arrived = ring.z_back(parts)
    (frames_grad,) = call(
        partial(finish, splits),
        [("s", scal)] + vmem_of([frames_in, mod, d_after_self, own_part]) + vmem_of(arrived),
        [("v", (rows, D), F32)],
        [],
        1e8,
        "finish",
    )
    text_grad = text_own
    for part in ring.z_back(text_parts):
        text_grad = text_grad + part.astype(F32)

    mod_partial = jnp.concatenate([sums_one, gate_sums, sums_two], axis=1)[:clips]
    mod_sum = mod_partial
    for part in ring.z_back([mod_partial] * (splits - 1)):
        mod_sum = mod_sum + part
    mod_low = mod_sum.astype(BF16)
    mod_all = lax.all_to_all(
        jnp.broadcast_to(mod_low[None], (n_dp,) + mod_low.shape), "dp", 0, 0, tiled=True
    ).reshape(n_dp * clips, -1)
    grad_ada = lax.dot_general(
        silu_cols, mod_all, (((0,), (0,)), ((), ())), preferred_element_type=F32
    )
    dp_index = lax.axis_index("dp")
    bias_width = ada_bias.shape[0]
    grad_ada_bias = jnp.sum(
        lax.dynamic_slice_in_dim(mod_all, dp_index * bias_width, bias_width, 1).astype(F32), axis=0
    )
    step_part = lax.dot_general(
        mod_all, ada_weight, (((1,), (1,)), ((), ())), preferred_element_type=F32
    )
    step_got = lax.all_to_all(step_part.reshape(n_dp, clips, shard_rows), "dp", 0, 0, tiled=True)
    step_value = step_embed.astype(F32)
    _, silu_pull = jax.vjp(jax.nn.silu, step_value)
    step_grad = silu_pull(step_got.transpose(1, 0, 2).reshape(clips, D))[0]

    def spread(value):
        v = value.reshape(n_dp, 1, D // n_dp)
        return jnp.broadcast_to(v, (n_dp, splits, D // n_dp))

    def heads_out(value):
        n = value.shape[1] // (3 * n_dp)
        return value.reshape(splits, 3, n_dp, n).transpose(2, 0, 1, 3).reshape(n_dp, splits, 3 * n)

    sq, _, sv, _ = from_layout(self_bias_grad[:, 0])
    cq, _, cv, _ = from_layout(cross_bias_grad[:, 0])
    entries = [
        heads_out(sq),
        heads_out(sv),
        spread(self_rows[0]),
        spread(cross_rows[1]),
        heads_out(cq),
        heads_out(cv),
        spread(cross_rows[0]),
        heads_out(in_bias_grad[:, 0]),
        spread(out_bias_grad[0]),
    ]
    packed = jnp.concatenate(entries, axis=2).reshape(n_dp * splits, -1)
    bias_sum = jnp.sum(lax.all_to_all(packed, both, 0, 0, tiled=True), axis=0)
    bias_out = []
    place = 0
    for e in entries:
        bias_out.append(bias_sum[place : place + e.shape[2]])
        place += e.shape[2]

    total_in = ring.reduce(grads_in)
    total_out = ring.reduce(grads_out)
    total_cross = ring.reduce(grads_cross)
    total_self = ring.reduce(grads_self)
    gq, gk, gv, go = from_layout(total_self)
    hq, hk, hv, ho = from_layout(total_cross)
    return (
        layer_out,
        frames_grad,
        step_grad,
        text_grad,
        grad_ada,
        grad_ada_bias,
        jnp.stack([gq, gk, gv], axis=1),
        jnp.stack([bias_out[0], bias_out[1]]).reshape(qv_bias.shape),
        go.T,
        bias_out[2],
        bias_out[3],
        hq,
        bias_out[4].reshape(cross_q_bias.shape),
        jnp.stack([hk, hv], axis=1),
        bias_out[5].reshape(cross_v_bias.shape),
        ho.T,
        bias_out[6],
        total_in,
        bias_out[7].reshape(mlp_in_bias.shape),
        total_out.T,
        bias_out[8],
    )


def solution(mesh):
    rows_all, by_dp = P(("dp", "head"), None), P("dp", None)
    head_dp, dp_head = P("head", "dp"), P("dp", "head")
    dp_three, vector = P("dp", None, "head"), P("dp")
    params = (
        by_dp,
        vector,
        dp_three,
        P(None, "head", "dp"),
        head_dp,
        vector,
        vector,
        dp_head,
        head_dp,
        dp_three,
        head_dp,
        head_dp,
        vector,
        dp_head,
        head_dp,
        head_dp,
        vector,
    )
    return jax.shard_map(
        on_device,
        mesh=mesh,
        in_specs=(rows_all, by_dp, by_dp, by_dp, by_dp, rows_all) + params,
        out_specs=(rows_all, rows_all, by_dp, rows_all) + params,
        check_vma=False,
    )
```

```python
from functools import partial

import jax
import jax.numpy as jnp
from jax import lax
from jax.experimental import pallas as pl
from jax.experimental.pallas import tpu as pltpu
from jax.sharding import PartitionSpec as P

D = 768
HD = 64
TXT = 256
WIN = 128
EPS = 1e-06
NEG = -1e30
F32 = jnp.float32
BF16 = jnp.bfloat16
HIGH = lax.Precision.HIGHEST
S_Z, S_END, S_TOK, S_OFF = 0, 1, 3, 8
S_LEN = 16
US = 1.15e9


def nn(a, b):
    return lax.dot_general(a, b, (((1,), (0,)), ((), ())), preferred_element_type=F32)


def nt(a, b):
    return lax.dot_general(a, b, (((1,), (1,)), ((), ())), preferred_element_type=F32)


def tn(a, b):
    return lax.dot_general(a, b, (((0,), (0,)), ((), ())), preferred_element_type=F32)


def normalize(v):
    centered = v - jnp.mean(v, axis=-1, keepdims=True)
    inverse = lax.rsqrt(jnp.mean(centered * centered, axis=-1, keepdims=True) + EPS)
    return centered * inverse, inverse


def normalize_back(u, normed, inverse):
    return inverse * (
        u
        - jnp.mean(u, axis=-1, keepdims=True)
        - normed * jnp.mean(u * normed, axis=-1, keepdims=True)
    )


def clip_of(position, scal):
    return (position >= scal[S_END]).astype(jnp.int32) + (position >= scal[S_END + 1]).astype(
        jnp.int32
    )


def frame_position(index, block, rows, splits, scal):
    return lax.rem(scal[S_Z] - block + splits, splits) * rows + index


def per_row(mod_ref, part, clip):
    cols = slice(part * D, (part + 1) * D)
    first, second, third = (mod_ref[c : c + 1, cols] for c in range(3))
    return jnp.where(clip == 0, first, jnp.where(clip == 1, second, third))


def clip_sums(clip_row, value):
    which = lax.broadcasted_iota(jnp.int32, (8, clip_row.shape[1]), 0)
    choose = (which == clip_row).astype(F32)
    return lax.dot_general(
        choose, value, (((1,), (0,)), ((), ())), precision=HIGH, preferred_element_type=F32
    )


def lanes(rows, low):
    lane = lax.broadcasted_iota(jnp.int32, (rows, WIN), 1)
    return lane < HD if low else lane >= HD


def keep(value, low):
    return jnp.where(lanes(value.shape[0], low), value, jnp.zeros_like(value))


def swap(value):
    return pltpu.roll(value, HD, 1)


def load_start(pieces, buffer, sems, scal, col=0, low=0):
    count, _, width = buffer.shape
    copies = []
    for j, piece in enumerate(pieces):
        rows = piece.shape[1]
        start = pl.multiple_of(scal[S_OFF + j], 32)
        copy = pltpu.make_async_copy(
            piece.at[low : low + count, :, col : col + width],
            buffer.at[:, pl.ds(start, rows), :],
            sems.at[j],
        )
        copy.start()
        copies.append(copy)
    return copies


def store_copies(buffer, z, outs, sems, scal, col=0, first=0):
    copies = []
    j = 0
    for out in outs:
        for i in range(out.shape[0]):
            rows = out.shape[2]
            start = pl.multiple_of(scal[S_OFF + j], 32)
            copies.append(
                pltpu.make_async_copy(
                    buffer.at[z, pl.ds(start, rows), col : col + out.shape[3]],
                    out.at[i, z],
                    sems.at[first + j, z],
                )
            )
            j += 1
    return copies


def attend(queries, kv, mask, scores, probs, count):
    rows = queries.shape[0]
    step = 256
    outs, totals = [], []
    for h in range(3):
        if h < 2:
            query = keep(queries[:, :WIN], h == 0)
            kcol, vcol = 0, 1
        else:
            query = queries[:, WIN:]
            kcol, vcol = 2, 3
        peak = None
        for lo in range(0, count, step):
            part = nt(kv(lo, lo + step, kcol), query) + mask[lo : lo + step, :]
            scores[lo : lo + step, :] = part
            top = jnp.max(part, axis=0, keepdims=True)
            peak = top if peak is None else jnp.maximum(peak, top)
        total = jnp.zeros((1, rows), F32)
        for lo in range(0, count, step):
            part = jnp.exp(scores[lo : lo + step, :] - peak)
            total = total + jnp.sum(part, axis=0, keepdims=True)
            probs[lo : lo + step, :] = part.astype(BF16)
        out = tn(kv(0, count, vcol), probs[0:count, :]) * (1.0 / total)
        outs.append(out)
        totals.append(peak + jnp.log(total))
    cat = jnp.concatenate(
        [jnp.zeros((HD, rows), F32), outs[2][:HD], outs[0][:HD], outs[1][HD:]], axis=0
    )
    return cat.T.astype(BF16), totals


def attend_back(queries, kv, out_grad, mask, totals, probs, grads, count, put):
    rows = queries.shape[0]
    step = 256
    wide = out_grad.astype(F32)
    second = keep(swap(wide[:, :WIN]), True).astype(BF16)
    query_parts = []
    heads = []
    for h in range(3):
        if h < 2:
            query = keep(queries[:, :WIN], h == 0)
            given = keep(out_grad[:, WIN:], h == 0)
            kcol, vcol = 0, 1
        else:
            query, given = queries[:, WIN:], second
            kcol, vcol = 2, 3
        heads.append((query, given))
        delta = jnp.zeros((1, rows), F32)
        for lo in range(0, count, step):
            part = nt(kv(lo, lo + step, kcol), query) + mask[lo : lo + step, :]
            weights = jnp.exp(part - totals[h])
            weight_grad = nt(kv(lo, lo + step, vcol), given)
            delta = delta + jnp.sum(weights * weight_grad, axis=0, keepdims=True)
            probs[h, lo : lo + step, :] = weights
            grads[h, lo : lo + step, :] = weight_grad
        query_part = jnp.zeros((rows, WIN), F32)
        for lo in range(0, count, step):
            part = probs[h, lo : lo + step, :]
            score_grad = (part * (grads[h, lo : lo + step, :] - delta)).astype(BF16)
            grads[h, lo : lo + step, :] = score_grad.astype(F32)
            query_part = query_part + tn(score_grad, kv(lo, lo + step, kcol))
        query_parts.append(query_part * 0.125)
    for lo in range(0, count, step):
        hi = lo + step
        prob = [probs[h, lo:hi, :].astype(BF16) for h in range(3)]
        grad = [grads[h, lo:hi, :].astype(BF16) for h in range(3)]
        put(
            lo,
            hi,
            nn(grad[0], heads[0][0]) + nn(grad[1], heads[1][0]),
            nn(prob[0], heads[0][1]) + nn(prob[1], heads[1][1]),
            nn(grad[2], heads[2][0]),
            nn(prob[2], heads[2][1]),
        )
    pair = jnp.where(lanes(rows, True), query_parts[0], query_parts[1])
    third = keep(swap(query_parts[2]), True)
    return pair, third


def self_mask(scal, mask, rows, splits):
    query = clip_of(
        frame_position(lax.broadcasted_iota(jnp.int32, (1, rows), 1), 0, rows, splits, scal), scal
    )
    for block in range(splits):
        key = clip_of(
            frame_position(
                lax.broadcasted_iota(jnp.int32, (rows, 1), 0), block, rows, splits, scal
            ),
            scal,
        )
        mask[block * rows : (block + 1) * rows, :] = jnp.where(key == query, 0.0, NEG)


def cross_mask(scal, mask, rows, splits, clips):
    query = clip_of(
        frame_position(lax.broadcasted_iota(jnp.int32, (1, rows), 1), 0, rows, splits, scal), scal
    )
    slot = lax.broadcasted_iota(jnp.int32, (TXT, 1), 0)
    for c in range(clips):
        allowed = (query == c) & (slot < scal[S_TOK + c])
        mask[c * TXT : (c + 1) * TXT, :] = jnp.where(allowed, 0.0, NEG)


def own_clip(scal, rows, splits, block=0):
    return clip_of(
        frame_position(lax.broadcasted_iota(jnp.int32, (rows, 1), 0), block, rows, splits, scal),
        scal,
    )


def own_clip_row(scal, rows, splits, block=0):
    return clip_of(
        frame_position(lax.broadcasted_iota(jnp.int32, (1, rows), 1), block, rows, splits, scal),
        scal,
    )


def shard_index(scal, z, splits):
    return lax.rem(scal[S_Z] - z + splits, splits)


def self_forward(n_p, splits, *refs):
    scal = refs[0]
    frames = refs[1 : 1 + splits]
    mod, bias, out_bias = refs[1 + splits : 4 + splits]
    pieces = refs[4 + splits : 4 + splits + n_p]
    hidden, kv_out, q_out, att_out, lse, branch_out, after = refs[
        4 + splits + n_p : 11 + splits + n_p
    ]
    weights, mask, scores, probs, sems = refs[11 + splits + n_p :]
    rows = frames[0].shape[0]
    count = rows * splits
    copies = load_start(pieces, weights, sems, scal)
    self_mask(scal, mask, rows, splits)
    for block in range(splits):
        clip = own_clip(scal, rows, splits, block)
        normed, _ = normalize(frames[block][...].astype(F32))
        value = normed * (1.0 + per_row(mod, 1, clip)) + per_row(mod, 0, clip)
        hidden[block * rows : (block + 1) * rows, :] = value.astype(BF16)
    branch_out[...] = jnp.broadcast_to(out_bias[...], branch_out.shape)
    for copy in copies:
        copy.wait()

    def one(z, carry):
        bias_row = bias[shard_index(scal, z, splits)]
        for block in range(splits):
            span = slice(block * rows, (block + 1) * rows)
            part = nn(hidden[span, :], weights[z, :, WIN : 5 * WIN]) + bias_row[:, WIN : 5 * WIN]
            kv_out[z, span, :] = part.astype(BF16)
            if block == 0:
                third = keep(swap(part[:, 2 * WIN : 3 * WIN].astype(BF16).astype(F32)), False)
        pair = nn(hidden[0:rows, :], weights[z, :, 0:WIN]) + bias_row[:, 0:WIN]
        queries = (
            jnp.concatenate([pair.astype(BF16).astype(F32), third], axis=1) * 0.125
        ).astype(BF16)
        q_out[z] = queries

        def kv(lo, hi, col):
            return kv_out[z, lo:hi, col * WIN : (col + 1) * WIN]

        attended, totals = attend(queries, kv, mask, scores, probs, count)
        att_out[z] = attended
        for h in range(3):
            lse[z, h : h + 1, :] = totals[h]
        branch_out[...] += nt(attended, weights[z, :, 4 * WIN :])
        return carry

    lax.fori_loop(0, splits, one, 0)
    clip = own_clip(scal, rows, splits)
    after[...] = frames[0][...].astype(F32) + per_row(mod, 2, clip) * branch_out[...]


def cross_forward(n_p, splits, *refs):
    scal, after_self, text, gain, bias, out_bias = refs[:6]
    pieces = refs[6 : 6 + n_p]
    kv_out, q_out, att_out, lse, after = refs[6 + n_p : 11 + n_p]
    weights, mask, scores, probs, sems = refs[11 + n_p :]
    rows = after_self.shape[0]
    count = text.shape[0]
    copies = load_start(pieces, weights, sems, scal, D)
    cross_mask(scal, mask, rows, splits, count // TXT)
    normed, _ = normalize(after_self[...])
    hidden = (normed * gain[...]).astype(BF16)
    after[...] = after_self[...] + out_bias[...]
    for copy in copies:
        copy.wait()

    def one(z, carry):
        bias_row = bias[shard_index(scal, z, splits)]
        for lo in range(0, count, 256):
            part = nn(text[lo : lo + 256, :], weights[z, :, WIN : 5 * WIN])
            kv_out[z, lo : lo + 256, :] = (part + bias_row[:, WIN : 5 * WIN]).astype(BF16)
        pair = nn(hidden, weights[z, :, 0:WIN]) + bias_row[:, 0:WIN]
        third = nn(hidden, weights[z, :, 3 * WIN : 4 * WIN]) + bias_row[:, 3 * WIN : 4 * WIN]
        third = keep(swap(third.astype(BF16).astype(F32)), False)
        queries = (
            jnp.concatenate([pair.astype(BF16).astype(F32), third], axis=1) * 0.125
        ).astype(BF16)
        q_out[z] = queries

        def kv(lo, hi, col):
            return kv_out[z, lo:hi, col * WIN : (col + 1) * WIN]

        attended, totals = attend(queries, kv, mask, scores, probs, count)
        att_out[z] = attended
        for h in range(3):
            lse[z, h : h + 1, :] = totals[h]
        after[...] += nt(attended, weights[z, :, 4 * WIN :])
        return carry

    lax.fori_loop(0, splits, one, 0)


def feed_forward(n_p, splits, *refs):
    scal, after_cross, upstream, mod, in_bias, out_bias = refs[:6]
    pieces = refs[6 : 6 + n_p]
    rest = refs[6 + n_p :]
    n_o = 2 if n_p > 1 else 1
    layer_out, d_after = rest[:2]
    grads_in, grads_out = rest[2 : 2 + n_o], rest[2 + n_o : 2 + 2 * n_o]
    in_bias_grad, out_bias_grad, sums = rest[2 + 2 * n_o : 5 + 2 * n_o]
    weights, gbuf, mlp, back, load_sems, store_sems = rest[5 + 2 * n_o :]
    rows = after_cross.shape[0]
    copies = load_start(pieces, weights, load_sems, scal)
    clip = own_clip(scal, rows, splits)
    normed, inverse = normalize(after_cross[...])
    scale = 1.0 + per_row(mod, 4, clip)
    hidden = (normed * scale + per_row(mod, 3, clip)).astype(BF16)
    gate = per_row(mod, 5, clip)
    given = upstream[...].astype(F32)
    low = (given * gate).astype(BF16)
    low_wide = low.astype(F32)
    out_bias_grad[...] = jnp.sum(low_wide, axis=0, keepdims=True)
    hidden_t = hidden.astype(F32).T.astype(BF16)
    low_t = low_wide.T.astype(BF16)
    mlp[...] = jnp.broadcast_to(out_bias[...], mlp.shape)
    back[...] = jnp.zeros_like(back)
    for copy in copies:
        copy.wait()

    def stores(z):
        return store_copies(gbuf, z, grads_in, store_sems, scal) + store_copies(
            gbuf, z, grads_out, store_sems, scal, D, n_p
        )

    def one(z, carry):
        place = shard_index(scal, z, splits)
        pre = nn(hidden, weights[z, :, 0:D]) + in_bias[place]
        inner = 0.7978845608028654 * (pre + 0.044715 * (pre * pre * pre))
        curve = jnp.tanh(inner)
        half = 0.5 * (1.0 + curve)
        active = (pre * half).astype(BF16)
        slope = half + 0.5 * pre * (1.0 - curve * curve) * 0.7978845608028654 * (
            1.0 + 3.0 * 0.044715 * pre * pre
        )
        pre_grad = (slope * nn(low, weights[z, :, D:])).astype(BF16)
        in_bias_grad[place] = jnp.sum(pre_grad.astype(F32), axis=0, keepdims=True)
        mlp[...] += nt(active, weights[z, :, D:])
        back[...] += nt(pre_grad, weights[z, :, 0:D])
        gbuf[z, :, 0:D] = nn(hidden_t, pre_grad).astype(BF16)
        gbuf[z, :, D:] = nn(low_t, active).astype(BF16)
        for copy in stores(z):
            copy.start()
        return carry

    lax.fori_loop(0, splits, one, 0)
    branch = mlp[...]
    layer_out[...] = (after_cross[...] + gate * branch).astype(BF16)
    hidden_grad = back[...]
    d_after[...] = given + normalize_back(hidden_grad * scale, normed, inverse)
    clip_row = own_clip_row(scal, rows, splits)
    sums[:, 0:D] = clip_sums(clip_row, hidden_grad)
    sums[:, D : 2 * D] = clip_sums(clip_row, hidden_grad * normed)
    sums[:, 2 * D :] = clip_sums(clip_row, given * branch)
    for z in range(splits):
        for copy in stores(z):
            copy.wait()


def cross_backward(n_p, splits, low, high, *refs):
    scal, d_cross, after_self, text, gain, mod, branch, kv_in, q_in, att_in, lse = refs[:11]
    pieces = refs[11 : 11 + n_p]
    rest = refs[11 + n_p :]
    first, last = low == 0, high == splits
    if not first:
        back_in, text_in, bias_in = rest[:3]
        rest = rest[3:]
    n_o = 2 if n_p > 1 else 1
    grads = rest[:n_o]
    bias_grad = rest[n_o]
    rest = rest[n_o + 1 :]
    if last:
        d_after, d_attn, text_out, row_grads, sums, back, text_back = rest[:7]
        rest = rest[7:]
    else:
        back, text_back = rest[:2]
        rest = rest[2:]
    weights, gbuf, mask, probs, dscore, key_grad, text_t, load_sems, store_sems = rest
    rows = after_self.shape[0]
    count = text.shape[0]
    copies = load_start(pieces, weights, load_sems, scal, D, low)
    cross_mask(scal, mask, rows, splits, count // TXT)
    normed, inverse = normalize(after_self[...])
    hidden = (normed * gain[...]).astype(BF16)
    hidden_t = hidden.astype(F32).T.astype(BF16)
    given = d_cross[...].astype(BF16)
    given_wide = given.astype(F32)
    given_t = given_wide.T.astype(BF16)
    for lo in range(0, count, 256):
        text_t[:, lo : lo + 256] = text[lo : lo + 256, :].astype(F32).T.astype(BF16)
    if first:
        back[...] = jnp.zeros_like(back)
        text_back[...] = jnp.zeros_like(text_back)
        bias_grad[...] = jnp.zeros_like(bias_grad)
    else:
        back[...] = back_in[...]
        text_back[...] = text_in[...]
        bias_grad[...] = bias_in[...]
    for copy in copies:
        copy.wait()

    def one(i, carry):
        z = i + low
        place = shard_index(scal, z, splits)

        def kv(lo, hi, col):
            return kv_in[z, lo:hi, col * WIN : (col + 1) * WIN]

        def put(lo, hi, k01, v01, k2, v2):
            key_grad[lo:hi, 0:WIN] = k01.astype(BF16)
            key_grad[lo:hi, WIN : 2 * WIN] = v01.astype(BF16)
            key_grad[lo:hi, 2 * WIN : 3 * WIN] = k2.astype(BF16)
            key_grad[lo:hi, 3 * WIN : 4 * WIN] = v2.astype(BF16)

        head_grad = nn(given, weights[i, :, 4 * WIN :]).astype(BF16)
        totals = [lse[z, h : h + 1, :] for h in range(3)]
        pair, third = attend_back(
            q_in[z], kv, head_grad, mask, totals, probs, dscore, count, put
        )
        pair, third = pair.astype(BF16), third.astype(BF16)
        part = nn(text_t[...], key_grad[...])
        out_part = nn(given_t, att_in[z])
        gbuf[i, :, 0:WIN] = nn(hidden_t, pair).astype(BF16)
        gbuf[i, :, WIN : 3 * WIN] = part[:, 0 : 2 * WIN].astype(BF16)
        gbuf[i, :, 3 * WIN : 4 * WIN] = (
            part[:, 2 * WIN : 3 * WIN] + nn(hidden_t, third)
        ).astype(BF16)
        gbuf[i, :, 4 * WIN : 5 * WIN] = (part[:, 3 * WIN :] + out_part[:, 0:WIN]).astype(BF16)
        gbuf[i, :, 5 * WIN :] = out_part[:, WIN:].astype(BF16)
        for copy in store_copies(gbuf, i, grads, store_sems, scal):
            copy.start()
        back[...] += nt(pair, weights[i, :, 0:WIN]) + nt(third, weights[i, :, 3 * WIN : 4 * WIN])
        for lo in range(0, count, 256):
            text_back[lo : lo + 256, :] += nt(
                key_grad[lo : lo + 256, :], weights[i, :, WIN : 5 * WIN]
            )
        key_sums = jnp.sum(key_grad[...].astype(F32), axis=0, keepdims=True)
        bias_grad[place, :, 0:WIN] = jnp.sum(pair.astype(F32), axis=0, keepdims=True)
        bias_grad[place, :, WIN : 3 * WIN] = key_sums[:, 0 : 2 * WIN]
        bias_grad[place, :, 3 * WIN : 4 * WIN] = key_sums[:, 2 * WIN : 3 * WIN] + jnp.sum(
            third.astype(F32), axis=0, keepdims=True
        )
        bias_grad[place, :, 4 * WIN : 5 * WIN] = key_sums[:, 3 * WIN :]
        bias_grad[place, :, 5 * WIN :] = jnp.zeros((1, WIN), F32)
        return carry

    lax.fori_loop(0, high - low, one, 0)
    for i in range(high - low):
        for copy in store_copies(gbuf, i, grads, store_sems, scal):
            copy.wait()
    if not last:
        return
    row_grads[...] = jnp.zeros_like(row_grads)
    row_grads[0:1, :] = jnp.sum(given_wide, axis=0, keepdims=True)
    hidden_grad = back[...]
    row_grads[1:2, :] = jnp.sum(hidden_grad * normed, axis=0, keepdims=True)
    total = d_cross[...] + normalize_back(hidden_grad * gain[...], normed, inverse)
    d_after[...] = total
    clip = own_clip(scal, rows, splits)
    d_attn[...] = (total * per_row(mod, 2, clip)).astype(BF16)
    sums[...] = clip_sums(own_clip_row(scal, rows, splits), total * branch[...])
    text_out[...] = text_back[...].astype(BF16)


def self_backward(n_p, splits, low, high, *refs):
    scal = refs[0]
    frames = refs[1 : 1 + splits]
    given_ref, hidden, kv_in, q_in, att_in, lse = refs[1 + splits : 7 + splits]
    pieces = refs[7 + splits : 7 + splits + n_p]
    rest = refs[7 + splits + n_p :]
    first, last = low == 0, high == splits
    if not first:
        back_in, bias_in = rest[:2]
        rest = rest[2:]
    n_o = 2 if n_p > 1 else 1
    grads = rest[:n_o]
    bias_grad = rest[n_o]
    rest = rest[n_o + 1 :]
    if last:
        own = rest[0]
        parts = rest[1:splits]
        row_grads, sums, back = rest[splits : splits + 3]
        rest = rest[splits + 3 :]
    else:
        back = rest[0]
        rest = rest[1:]
    weights, gbuf, mask, probs, dscore, key_grad, hidden_t, load_sems, store_sems = rest
    rows = frames[0].shape[0]
    count = rows * splits
    copies = load_start(pieces, weights, load_sems, scal, 0, low)
    self_mask(scal, mask, rows, splits)
    given = given_ref[...]
    given_wide = given.astype(F32)
    given_t = given_wide.T.astype(BF16)
    for lo in range(0, count, 256):
        hidden_t[:, lo : lo + 256] = hidden[lo : lo + 256, :].astype(F32).T.astype(BF16)
    if first:
        back[...] = jnp.zeros_like(back)
        bias_grad[...] = jnp.zeros_like(bias_grad)
    else:
        back[...] = back_in[...]
        bias_grad[...] = bias_in[...]
    for copy in copies:
        copy.wait()

    def one(i, carry):
        z = i + low
        place = shard_index(scal, z, splits)

        def kv(lo, hi, col):
            return kv_in[z, lo:hi, col * WIN : (col + 1) * WIN]

        def put(lo, hi, k01, v01, k2, v2):
            key_grad[lo:hi, 0:WIN] = k01.astype(BF16)
            key_grad[lo:hi, WIN : 2 * WIN] = v01.astype(BF16)
            key_grad[lo:hi, 2 * WIN : 3 * WIN] = k2.astype(BF16)
            key_grad[lo:hi, 3 * WIN : 4 * WIN] = v2.astype(BF16)

        head_grad = nn(given, weights[i, :, 4 * WIN :]).astype(BF16)
        totals = [lse[z, h : h + 1, :] for h in range(3)]
        pair, third = attend_back(
            q_in[z], kv, head_grad, mask, totals, probs, dscore, count, put
        )
        pair = pair.astype(BF16)
        key_grad[0:rows, 2 * WIN : 3 * WIN] = (
            key_grad[0:rows, 2 * WIN : 3 * WIN].astype(F32) + third
        ).astype(BF16)
        part = nn(hidden_t[...], key_grad[...])
        out_part = nn(given_t, att_in[z])
        gbuf[i, :, 0:WIN] = nn(hidden_t[:, 0:rows], pair).astype(BF16)
        gbuf[i, :, WIN : 4 * WIN] = part[:, 0 : 3 * WIN].astype(BF16)
        gbuf[i, :, 4 * WIN : 5 * WIN] = (part[:, 3 * WIN :] + out_part[:, 0:WIN]).astype(BF16)
        gbuf[i, :, 5 * WIN :] = out_part[:, WIN:].astype(BF16)
        for copy in store_copies(gbuf, i, grads, store_sems, scal):
            copy.start()
        for lo in range(0, count, 256):
            back[lo : lo + 256, :] += nt(
                key_grad[lo : lo + 256, :], weights[i, :, WIN : 5 * WIN]
            )
        back[0:rows, :] += nt(pair, weights[i, :, 0:WIN])
        key_sums = jnp.sum(key_grad[...].astype(F32), axis=0, keepdims=True)
        bias_grad[place, :, 0:WIN] = jnp.sum(pair.astype(F32), axis=0, keepdims=True)
        bias_grad[place, :, WIN : 5 * WIN] = key_sums
        bias_grad[place, :, 5 * WIN :] = jnp.zeros((1, WIN), F32)
        return carry

    lax.fori_loop(0, high - low, one, 0)
    for i in range(high - low):
        for copy in store_copies(gbuf, i, grads, store_sems, scal):
            copy.wait()
    if not last:
        return
    row_grads[...] = jnp.zeros_like(row_grads)
    row_grads[0:1, :] = jnp.sum(given_wide, axis=0, keepdims=True)
    shift = jnp.zeros((8, D), F32)
    scale = jnp.zeros((8, D), F32)
    for block in range(splits):
        value = back[block * rows : (block + 1) * rows, :]
        if block == 0:
            own[...] = value
        else:
            parts[block - 1][...] = value.astype(BF16)
        normed, _ = normalize(frames[block][...].astype(F32))
        clip_row = own_clip_row(scal, rows, splits, block)
        shift = shift + clip_sums(clip_row, value)
        scale = scale + clip_sums(clip_row, value * normed)
    sums[:, 0:D] = shift
    sums[:, D:] = scale


def finish(splits, *refs):
    scal, frames, mod, d_after, own = refs[:5]
    parts = refs[5 : 4 + splits]
    out = refs[4 + splits]
    rows = frames.shape[0]
    value = own[...]
    for part in parts:
        value = value + part[...].astype(F32)
    normed, inverse = normalize(frames[...].astype(F32))
    scale = 1.0 + per_row(mod, 1, own_clip(scal, rows, splits))
    out[...] = d_after[...] + normalize_back(value * scale, normed, inverse)


MEMORY = {"v": pltpu.VMEM, "s": pltpu.SMEM, "a": pl.ANY}


def call(body, inputs, outs, scratch, flops, name):
    moved = sum(a.size * a.dtype.itemsize for _, a in inputs)
    moved += sum(_size(s, t) for _, s, t in outs)
    return pl.pallas_call(
        body,
        out_shape=tuple(jax.ShapeDtypeStruct(s, t) for _, s, t in outs),
        in_specs=[pl.BlockSpec(memory_space=MEMORY[m]) for m, _ in inputs],
        out_specs=tuple(pl.BlockSpec(memory_space=MEMORY[m]) for m, _, _ in outs),
        scratch_shapes=scratch,
        compiler_params=pltpu.CompilerParams(vmem_limit_bytes=58 * 1024 * 1024),
        cost_estimate=pl.CostEstimate(flops=int(flops), bytes_accessed=int(moved), transcendentals=0),
        name=name,
    )(*[a for _, a in inputs])


def _size(shape, kind):
    total = jnp.dtype(kind).itemsize
    for s in shape:
        total *= s
    return total


class Ring:
    def __init__(self):
        self.n_dp = lax.axis_size("dp")
        self.splits = lax.axis_size("head")
        self.square = self.n_dp == 8
        if self.square:
            self.core = [(i, i ^ 1) for i in range(8)]
            self.first = [(i, i ^ (4 if i & 1 else 2)) for i in range(8)]
            self.second = [(i, i ^ (2 if i & 1 else 4)) for i in range(8)]

    def offsets(self):
        if not self.square:
            return [jnp.int32(0)]
        me = lax.axis_index("dp")
        rows = D // 8

        def kept(d):
            odd = d & 1
            return [d, d ^ (2 + 2 * odd), d ^ (4 - 2 * odd), d ^ 6]

        return [place * rows for place in kept(me) + kept(me ^ 1)]

    def z_pieces(self, value):
        n = self.splits
        return [value] + [
            lax.ppermute(value, "head", [(s, (s + k) % n) for s in range(n)]) for k in range(1, n)
        ]

    def z_back(self, parts):
        n = self.splits
        return [
            lax.ppermute(parts[k - 1], "head", [(s, (s - k) % n) for s in range(n)])
            for k in range(1, n)
        ]

    def gather_z(self, shard):
        return jnp.stack(self.z_pieces(shard))

    def across(self, value, how):
        return lax.ppermute(value, "dp", how)

    def gather(self, mine):
        if not self.square:
            return [lax.all_gather(mine, "dp", axis=1, tiled=True)]
        one = self.across(mine, self.first)
        two = self.across(mine, self.second)
        three = self.across(one, self.second)
        kept = [mine, one, two, three]
        return kept + [self.across(k, self.core) for k in kept]

    def send_second(self, blocks):
        return self.across(blocks[2:4].astype(BF16), self.second)

    def send_first(self, blocks):
        return self.across(blocks[1].astype(BF16), self.first)

    def reduce_z(self, mine):
        arrived = self.z_back([mine[k].astype(BF16) for k in range(1, self.splits)])
        total = mine[0]
        for part in arrived:
            total = total + part.astype(F32)
        return total

    def reduce_other(self, grads):
        return lax.psum_scatter(grads[0][0], "dp", scatter_dimension=1, tiled=True).astype(F32)


def wide_sum(a, b):
    return a.astype(F32) + b.astype(F32)


def tie(value, *others):
    return lax.optimization_barrier((value,) + others)[0]


def to_layout(q, k, v, o):
    return jnp.concatenate(
        [
            q[:, :WIN],
            k[:, :WIN],
            v[:, :WIN],
            q[:, WIN:],
            k[:, WIN:],
            v[:, WIN:],
            o[:, WIN:],
            o[:, :WIN],
        ],
        axis=1,
    )


def from_layout(value):
    def pick(pair, third):
        return jnp.concatenate(
            [value[:, pair : pair + WIN], value[:, third : third + HD]], axis=1
        )

    return pick(0, 3 * WIN), pick(WIN, 3 * WIN + HD), pick(2 * WIN, 4 * WIN), pick(
        5 * WIN, 4 * WIN + HD
    )


def on_device(
    frames_in,
    step_embed,
    text_feats,
    clip_frames,
    text_tokens,
    out_grad,
    ada_weight,
    ada_bias,
    qkv_weight,
    qv_bias,
    attn_out_weight,
    attn_out_bias,
    cross_gain,
    cross_q_weight,
    cross_q_bias,
    cross_kv_weight,
    cross_v_bias,
    cross_out_weight,
    cross_out_bias,
    mlp_in_weight,
    mlp_in_bias,
    mlp_out_weight,
    mlp_out_bias,
):
    both = ("dp", "head")
    ring = Ring()
    n_dp, splits = ring.n_dp, ring.splits
    z_index = lax.axis_index("head")
    rows = frames_in.shape[0]
    count = rows * splits
    text_count = text_feats.shape[0]
    clips = clip_frames.shape[1]
    width = D // splits
    shard_rows = D // n_dp
    ends = jnp.cumsum(clip_frames[0])
    offs = ring.offsets()
    n_p = len(offs)
    scal = jnp.stack(
        [z_index, ends[0], ends[1], text_tokens[0, 0], text_tokens[0, 1], text_tokens[0, 2]]
        + [jnp.int32(0)] * 2
        + [o.astype(jnp.int32) for o in offs]
        + [jnp.int32(0)] * (S_LEN - S_OFF - n_p)
    ).astype(jnp.int32)

    shard_self = to_layout(
        qkv_weight[:, 0], qkv_weight[:, 1], qkv_weight[:, 2], attn_out_weight.T
    )
    shard_cross = to_layout(
        cross_q_weight, cross_kv_weight[:, 0], cross_kv_weight[:, 1], cross_out_weight.T
    )

    biases = [
        ada_bias,
        qv_bias.reshape(-1),
        attn_out_bias,
        cross_gain,
        cross_q_bias.reshape(-1),
        cross_v_bias.reshape(-1),
        cross_out_bias,
        mlp_in_bias.reshape(-1),
        mlp_out_bias,
    ]
    flat = jnp.concatenate(biases)
    cols = step_embed.reshape(clips, n_dp, shard_rows).transpose(1, 0, 2).reshape(n_dp, -1)
    sent = jnp.concatenate(
        [
            jnp.broadcast_to(flat[None, None], (n_dp, splits, flat.shape[0])),
            jnp.broadcast_to(cols[:, None], (n_dp, splits, cols.shape[1])),
        ],
        axis=2,
    ).reshape(n_dp * splits, -1)
    got = lax.all_to_all(sent, both, 0, 0, tiled=True).reshape(n_dp, splits, -1)
    step_cols = got[:, 0, flat.shape[0] :].reshape(n_dp * clips, shard_rows).astype(F32)
    silu_cols = jax.nn.silu(step_cols).astype(BF16)
    spots = []
    place = 0
    for b in biases:
        spots.append(got[:, :, place : place + b.shape[0]].astype(F32))
        place += b.shape[0]

    def over_dp(value):
        return value[:, 0].reshape(1, -1)

    def by_head(value, lead=1):
        n = value.shape[2] // (lead * 3)
        v = value.reshape(n_dp, splits, lead, 3, n).transpose(1, 2, 3, 0, 4)
        return v.reshape(splits, lead, 3 * n_dp * n)

    all_ada_bias = over_dp(spots[0])
    qv = by_head(spots[1], 2)
    nothing = jnp.zeros((splits, width), F32)
    bias_self = to_layout(qv[:, 0], nothing, qv[:, 1], nothing)[:, None]
    all_attn_bias = over_dp(spots[2])
    all_gain = over_dp(spots[3])
    bias_cross = to_layout(
        by_head(spots[4])[:, 0], nothing, by_head(spots[5])[:, 0], nothing
    )[:, None]
    all_cross_bias = over_dp(spots[6])
    all_in_bias = by_head(spots[7])
    all_out_bias = over_dp(spots[8])

    mod_part = jnp.dot(silu_cols, ada_weight, preferred_element_type=F32)
    mod_got = lax.all_to_all(mod_part.reshape(n_dp, clips, -1), "dp", 0, 0, tiled=True)
    mod = jnp.sum(mod_got, axis=0) + all_ada_bias

    frame_blocks = ring.z_pieces(frames_in)
    pieces_attn = ring.gather(
        ring.gather_z(jnp.concatenate([shard_self, shard_cross], axis=1))
    )
    mlp_mine = ring.gather_z(jnp.concatenate([mlp_in_weight, mlp_out_weight.T], axis=1))
    if ring.square:
        mlp_one = ring.across(mlp_mine, ring.first)
        mlp_two = ring.across(mlp_mine, ring.second)
    else:
        pieces_mlp = ring.gather(mlp_mine)

    def dma(n):
        return pltpu.SemaphoreType.DMA(n)

    def any_of(arrays):
        return [("a", a) for a in arrays]

    def vmem_of(arrays):
        return [("v", a) for a in arrays]

    piece_rows = D // n_p
    kept_out = [("a", (max(n_p // 2, 1), splits, piece_rows, D), BF16)] * (2 if n_p > 1 else 1)
    n_o = len(kept_out)
    shard_type = pltpu.VMEM((splits, D, D), BF16)

    hidden_one, self_kv, self_q, self_att, self_lse, attn_branch, after_self = call(
        partial(self_forward, n_p, splits),
        [("s", scal)]
        + vmem_of(frame_blocks)
        + vmem_of([mod, bias_self, all_attn_bias])
        + any_of(pieces_attn),
        [
            ("v", (count, D), BF16),
            ("v", (splits, count, 4 * WIN), BF16),
            ("v", (splits, rows, 2 * WIN), BF16),
            ("v", (splits, rows, 2 * WIN), BF16),
            ("v", (splits, 8, rows), F32),
            ("v", (rows, D), F32),
            ("v", (rows, D), F32),
        ],
        [
            shard_type,
            pltpu.VMEM((count, rows), F32),
            pltpu.VMEM((count, rows), F32),
            pltpu.VMEM((count, rows), BF16),
            dma((n_p,)),
        ],
        22 * US,
        "self_forward",
    )
    if ring.square:
        mlp_mine, mlp_one, mlp_two = (tie(v, after_self) for v in (mlp_mine, mlp_one, mlp_two))
        after_self = tie(after_self, mlp_one, mlp_two)
        mlp_three = ring.across(mlp_one, ring.second)
        mlp_other = [ring.across(v, ring.core) for v in (mlp_mine, mlp_one, mlp_two)]
    cross_kv, cross_q, cross_att, cross_lse, after_cross = call(
        partial(cross_forward, n_p, splits),
        [("s", scal)]
        + vmem_of([after_self, text_feats, all_gain, bias_cross, all_cross_bias])
        + any_of(pieces_attn),
        [
            ("v", (splits, text_count, 4 * WIN), BF16),
            ("v", (splits, rows, 2 * WIN), BF16),
            ("v", (splits, rows, 2 * WIN), BF16),
            ("v", (splits, 8, rows), F32),
            ("v", (rows, D), F32),
        ],
        [
            shard_type,
            pltpu.VMEM((text_count, rows), F32),
            pltpu.VMEM((text_count, rows), F32),
            pltpu.VMEM((text_count, rows), BF16),
            dma((n_p,)),
        ],
        17 * US,
        "cross_forward",
    )
    if ring.square:
        mlp_three = tie(mlp_three, after_cross)
        after_cross = tie(after_cross, mlp_three)
        pieces_mlp = [mlp_mine, mlp_one, mlp_two, mlp_three] + mlp_other
        pieces_mlp.append(ring.across(mlp_three, ring.core))
    results = call(
        partial(feed_forward, n_p, splits),
        [("s", scal)]
        + vmem_of([after_cross, out_grad, mod, all_in_bias, all_out_bias])
        + any_of(pieces_mlp),
        [("v", (rows, D), BF16), ("v", (rows, D), F32)]
        + kept_out
        + kept_out
        + [
            ("v", (splits, 1, D), F32),
            ("v", (1, D), F32),
            ("v", (8, 3 * D), F32),
        ],
        [
            pltpu.VMEM((splits, D, 2 * D), BF16),
            pltpu.VMEM((splits, D, 2 * D), BF16),
            pltpu.VMEM((rows, D), F32),
            pltpu.VMEM((rows, D), F32),
            dma((n_p,)),
            dma((2 * n_p, splits)),
        ],
        17 * US,
        "feed_forward",
    )
    layer_out, d_after_cross = results[:2]
    grads_in, grads_out = results[2 : 2 + n_o], results[2 + n_o : 2 + 2 * n_o]
    in_bias_grad, out_bias_grad, sums_two = results[2 + 2 * n_o :]
    half = splits // 2
    kept_half = [(m, (shape[0], half) + shape[2:], kind) for m, shape, kind in kept_out]
    half_type = pltpu.VMEM((half, D, D), BF16)

    def back_scratch(keys):
        return [
            half_type,
            half_type,
            pltpu.VMEM((keys, rows), F32),
            pltpu.VMEM((3, keys, rows), F32),
            pltpu.VMEM((3, keys, rows), F32),
            pltpu.VMEM((keys, 4 * WIN), BF16),
            pltpu.VMEM((D, keys), BF16),
            dma((n_p,)),
            dma((n_p, half)),
        ]

    if ring.square:
        core_in = ring.across(grads_in[1], ring.core)
        core_out = ring.across(grads_out[1], ring.core)
    cross_args = [
        d_after_cross,
        after_self,
        text_feats,
        all_gain,
        mod,
        attn_branch,
        cross_kv,
        cross_q,
        cross_att,
        cross_lse,
    ]
    cross_state = [("v", (rows, D), F32), ("v", (text_count, D), F32)]
    bias_type = [("v", (splits, 1, D), F32)]
    results = call(
        partial(cross_backward, n_p, splits, 0, half),
        [("s", scal)] + vmem_of(cross_args) + any_of(pieces_attn),
        kept_half + bias_type + cross_state,
        back_scratch(text_count),
        14 * US,
        "cross_backward_first",
    )
    grads_cross = [results[:n_o]]
    cross_bias_grad, cross_back, text_back = results[n_o:]
    if ring.square:
        core_in, core_out = tie(core_in, cross_back), tie(core_out, cross_back)
        cross_back = tie(cross_back, core_in, core_out)
        blocks_in = wide_sum(grads_in[0], core_in)
        blocks_out = wide_sum(grads_out[0], core_out)
        far_in = ring.send_second(blocks_in)
        core_cross = [ring.across(grads_cross[0][1], ring.core)]
    results = call(
        partial(cross_backward, n_p, splits, half, splits),
        [("s", scal)]
        + vmem_of(cross_args)
        + any_of(pieces_attn)
        + vmem_of([cross_back, text_back, cross_bias_grad]),
        kept_half
        + bias_type
        + [
            ("v", (rows, D), F32),
            ("v", (rows, D), BF16),
            ("v", (text_count, D), BF16),
            ("v", (8, D), F32),
            ("v", (8, D), F32),
        ],
        [pltpu.VMEM((rows, D), F32), pltpu.VMEM((text_count, D), F32)] + back_scratch(text_count),
        15 * US,
        "cross_backward_last",
    )
    grads_cross.append(results[:n_o])
    cross_bias_grad, d_after_self, d_attn, text_out, cross_rows, gate_sums = results[n_o:]
    self_args = [d_attn, hidden_one, self_kv, self_q, self_att, self_lse]
    if ring.square:
        far_in = tie(far_in, d_attn)
        core_cross[0] = tie(core_cross[0], d_attn)
        d_attn = tie(d_attn, far_in, core_cross[0])
        self_args[0] = d_attn
        blocks_in = wide_sum(blocks_in[0:2], far_in)
        near_in = ring.send_first(blocks_in)
        far_out = ring.send_second(tie(blocks_out, d_attn))
        core_cross.append(ring.across(grads_cross[1][1], ring.core))
    results = call(
        partial(self_backward, n_p, splits, 0, half),
        [("s", scal)] + vmem_of(frame_blocks) + vmem_of(self_args) + any_of(pieces_attn),
        kept_half + bias_type + [("v", (count, D), F32)],
        back_scratch(count),
        17 * US,
        "self_backward_first",
    )
    grads_self = [results[:n_o]]
    self_bias_grad, self_back = results[n_o:]
    if ring.square:
        near_in, far_out = tie(near_in, self_back), tie(far_out, self_back)
        core_cross[1] = tie(core_cross[1], self_back)
        self_back = tie(self_back, near_in, far_out, core_cross[1])
        shard_in = wide_sum(blocks_in[0], near_in)
        blocks_out = wide_sum(blocks_out[0:2], far_out)
        near_out = ring.send_first(blocks_out)
        blocks_cross = jnp.concatenate(
            [wide_sum(g[0], c) for g, c in zip(grads_cross, core_cross)], axis=1
        )
        far_cross = ring.send_second(blocks_cross)
        core_self = [ring.across(grads_self[0][1], ring.core)]
    results = call(
        partial(self_backward, n_p, splits, half, splits),
        [("s", scal)]
        + vmem_of(frame_blocks)
        + vmem_of(self_args)
        + any_of(pieces_attn)
        + vmem_of([self_back, self_bias_grad]),
        kept_half
        + bias_type
        + [("v", (rows, D), F32)]
        + [("v", (rows, D), BF16)] * (splits - 1)
        + [("v", (8, D), F32), ("v", (8, 2 * D), F32)],
        [pltpu.VMEM((count, D), F32)] + back_scratch(count),
        18 * US,
        "self_backward_last",
    )
    grads_self.append(results[:n_o])
    self_bias_grad, own_part = results[n_o : n_o + 2]
    parts = results[n_o + 2 : n_o + 1 + splits]
    self_rows, sums_one = results[n_o + 1 + splits :]

    arrived = ring.z_back(parts)
    (frames_grad,) = call(
        partial(finish, splits),
        [("s", scal)] + vmem_of([frames_in, mod, d_after_self, own_part]) + vmem_of(arrived),
        [("v", (rows, D), F32)],
        [],
        3 * US,
        "finish",
    )
    text_got = lax.all_to_all(
        text_out.reshape(splits, text_count // splits, D), "head", 0, 0, tiled=True
    )
    text_grad = jnp.sum(text_got.astype(F32), axis=0)

    mod_partial = jnp.concatenate([sums_one, gate_sums, sums_two], axis=1)[:clips]
    mod_sum = mod_partial
    for part in ring.z_back([mod_partial] * (splits - 1)):
        mod_sum = mod_sum + part
    mod_low = mod_sum.astype(BF16)
    mod_all = lax.all_to_all(
        jnp.broadcast_to(mod_low[None], (n_dp,) + mod_low.shape), "dp", 0, 0, tiled=True
    ).reshape(n_dp * clips, -1)
    grad_ada = lax.dot_general(
        silu_cols, mod_all, (((0,), (0,)), ((), ())), preferred_element_type=F32
    )
    dp_index = lax.axis_index("dp")
    bias_width = ada_bias.shape[0]
    grad_ada_bias = jnp.sum(
        lax.dynamic_slice_in_dim(mod_all, dp_index * bias_width, bias_width, 1).astype(F32), axis=0
    )
    step_part = lax.dot_general(
        mod_all, ada_weight, (((1,), (1,)), ((), ())), preferred_element_type=F32
    )
    step_got = lax.all_to_all(step_part.reshape(n_dp, clips, shard_rows), "dp", 0, 0, tiled=True)
    step_value = step_embed.astype(F32)
    _, silu_pull = jax.vjp(jax.nn.silu, step_value)
    step_grad = silu_pull(step_got.transpose(1, 0, 2).reshape(clips, D))[0]

    def spread(value):
        v = value.reshape(n_dp, 1, D // n_dp)
        return jnp.broadcast_to(v, (n_dp, splits, D // n_dp))

    def heads_out(value):
        n = value.shape[1] // (3 * n_dp)
        return value.reshape(splits, 3, n_dp, n).transpose(2, 0, 1, 3).reshape(n_dp, splits, 3 * n)

    sq, _, sv, _ = from_layout(self_bias_grad[:, 0])
    cq, _, cv, _ = from_layout(cross_bias_grad[:, 0])
    entries = [
        heads_out(sq),
        heads_out(sv),
        spread(self_rows[0]),
        spread(cross_rows[1]),
        heads_out(cq),
        heads_out(cv),
        spread(cross_rows[0]),
        heads_out(in_bias_grad[:, 0]),
        spread(out_bias_grad[0]),
    ]
    packed = jnp.concatenate(entries, axis=2).reshape(n_dp * splits, -1)
    bias_sum = jnp.sum(lax.all_to_all(packed, both, 0, 0, tiled=True), axis=0)
    bias_out = []
    place = 0
    for e in entries:
        bias_out.append(bias_sum[place : place + e.shape[2]])
        place += e.shape[2]

    if ring.square:
        total_in = ring.reduce_z(shard_in)
        total_out = ring.reduce_z(wide_sum(blocks_out[0], near_out))
        blocks_cross = wide_sum(blocks_cross[0:2], far_cross)
        total_cross = ring.reduce_z(wide_sum(blocks_cross[0], ring.send_first(blocks_cross)))
        core_self.append(ring.across(grads_self[1][1], ring.core))
        blocks_self = jnp.concatenate(
            [wide_sum(g[0], c) for g, c in zip(grads_self, core_self)], axis=1
        )
        blocks_self = wide_sum(blocks_self[0:2], ring.send_second(blocks_self))
        total_self = ring.reduce_z(wide_sum(blocks_self[0], ring.send_first(blocks_self)))
    else:

        def joined(halves):
            return ring.reduce_z(
                jnp.concatenate([ring.reduce_other(h) for h in halves], axis=0)
            )

        total_in = joined([grads_in])
        total_out = joined([grads_out])
        total_cross = joined(grads_cross)
        total_self = joined(grads_self)
    gq, gk, gv, go = from_layout(total_self)
    hq, hk, hv, ho = from_layout(total_cross)
    return (
        layer_out,
        frames_grad,
        step_grad,
        text_grad,
        grad_ada,
        grad_ada_bias,
        jnp.stack([gq, gk, gv], axis=1),
        jnp.stack([bias_out[0], bias_out[1]]).reshape(qv_bias.shape),
        go.T,
        bias_out[2],
        bias_out[3],
        hq,
        bias_out[4].reshape(cross_q_bias.shape),
        jnp.stack([hk, hv], axis=1),
        bias_out[5].reshape(cross_v_bias.shape),
        ho.T,
        bias_out[6],
        total_in,
        bias_out[7].reshape(mlp_in_bias.shape),
        total_out.T,
        bias_out[8],
    )


def solution(mesh):
    rows_all, by_dp = P(("dp", "head"), None), P("dp", None)
    head_dp, dp_head = P("head", "dp"), P("dp", "head")
    dp_three, vector = P("dp", None, "head"), P("dp")
    params = (
        by_dp,
        vector,
        dp_three,
        P(None, "head", "dp"),
        head_dp,
        vector,
        vector,
        dp_head,
        head_dp,
        dp_three,
        head_dp,
        head_dp,
        vector,
        dp_head,
        head_dp,
        head_dp,
        vector,
    )
    return jax.shard_map(
        on_device,
        mesh=mesh,
        in_specs=(rows_all, by_dp, by_dp, by_dp, by_dp, rows_all) + params,
        out_specs=(rows_all, rows_all, by_dp, rows_all) + params,
        check_vma=False,
    )
```

```python
from functools import partial

import jax
import jax.numpy as jnp
import numpy as np
from jax import lax
from jax.experimental import pallas as pl
from jax.experimental.pallas import tpu as pltpu
from jax.sharding import PartitionSpec as P

D = 768
HD = 64
TXT = 256
WIN = 128
EPS = 1e-06
NEG = -1e30
F32 = jnp.float32
BF16 = jnp.bfloat16
HIGH = lax.Precision.HIGHEST
S_Z, S_END, S_TOK, S_OFF = 0, 1, 3, 8
S_LEN = 16
US = 1.15e9


def nn(a, b):
    return lax.dot_general(a, b, (((1,), (0,)), ((), ())), preferred_element_type=F32)


def nt(a, b):
    return lax.dot_general(a, b, (((1,), (1,)), ((), ())), preferred_element_type=F32)


def tn(a, b):
    return lax.dot_general(a, b, (((0,), (0,)), ((), ())), preferred_element_type=F32)


def normalize(v):
    centered = v - jnp.mean(v, axis=-1, keepdims=True)
    inverse = lax.rsqrt(jnp.mean(centered * centered, axis=-1, keepdims=True) + EPS)
    return centered * inverse, inverse


def normalize_back(u, normed, inverse):
    return inverse * (
        u
        - jnp.mean(u, axis=-1, keepdims=True)
        - normed * jnp.mean(u * normed, axis=-1, keepdims=True)
    )


def clip_of(position, scal):
    return (position >= scal[S_END]).astype(jnp.int32) + (position >= scal[S_END + 1]).astype(
        jnp.int32
    )


def frame_position(index, block, rows, splits, scal):
    return lax.rem(scal[S_Z] - block + splits, splits) * rows + index


def per_row(mod_ref, part, clip):
    cols = slice(part * D, (part + 1) * D)
    first, second, third = (mod_ref[c : c + 1, cols] for c in range(3))
    return jnp.where(clip == 0, first, jnp.where(clip == 1, second, third))


def clip_sums(clip_row, value):
    which = lax.broadcasted_iota(jnp.int32, (8, clip_row.shape[1]), 0)
    choose = (which == clip_row).astype(F32)
    return lax.dot_general(
        choose, value, (((1,), (0,)), ((), ())), precision=HIGH, preferred_element_type=F32
    )


def lanes(rows, low):
    lane = lax.broadcasted_iota(jnp.int32, (rows, WIN), 1)
    return lane < HD if low else lane >= HD


def keep(value, low):
    return jnp.where(lanes(value.shape[0], low), value, jnp.zeros_like(value))


def swap(value):
    return pltpu.roll(value, HD, 1)


def load_start(pieces, buffer, sems, scal, col=0, low=0):
    count, _, width = buffer.shape
    copies = []
    for j, piece in enumerate(pieces):
        rows = piece.shape[1]
        start = pl.multiple_of(scal[S_OFF + j], 32)
        copy = pltpu.make_async_copy(
            piece.at[low : low + count, :, col : col + width],
            buffer.at[:, pl.ds(start, rows), :],
            sems.at[j],
        )
        copy.start()
        copies.append(copy)
    return copies


def store_copies(buffer, z, outs, sems, scal, col=0, first=0):
    copies = []
    j = 0
    for out in outs:
        for i in range(out.shape[0]):
            rows = out.shape[2]
            start = pl.multiple_of(scal[S_OFF + j], 32)
            copies.append(
                pltpu.make_async_copy(
                    buffer.at[z, pl.ds(start, rows), col : col + out.shape[3]],
                    out.at[i, z],
                    sems.at[first + j, z],
                )
            )
            j += 1
    return copies


def attend(queries, kv, mask, scores, probs, count):
    rows = queries.shape[0]
    step = 256
    outs, totals = [], []
    for h in range(3):
        if h < 2:
            query = keep(queries[:, :WIN], h == 0)
            kcol, vcol = 0, 1
        else:
            query = queries[:, WIN:]
            kcol, vcol = 2, 3
        peak = None
        for lo in range(0, count, step):
            part = nt(kv(lo, lo + step, kcol), query) + mask[lo : lo + step, :]
            scores[lo : lo + step, :] = part
            top = jnp.max(part, axis=0, keepdims=True)
            peak = top if peak is None else jnp.maximum(peak, top)
        total = jnp.zeros((1, rows), F32)
        for lo in range(0, count, step):
            part = jnp.exp(scores[lo : lo + step, :] - peak)
            total = total + jnp.sum(part, axis=0, keepdims=True)
            probs[lo : lo + step, :] = part.astype(BF16)
        out = tn(kv(0, count, vcol), probs[0:count, :]) * (1.0 / total)
        outs.append(out)
        totals.append(peak + jnp.log(total))
    cat = jnp.concatenate(
        [jnp.zeros((HD, rows), F32), outs[2][:HD], outs[0][:HD], outs[1][HD:]], axis=0
    )
    return cat.T.astype(BF16), totals


def attend_back(queries, kv, attended, out_grad, mask, totals, probs, dscore, count, put):
    rows = queries.shape[0]
    step = 256
    wide = out_grad.astype(F32)
    row = lax.broadcasted_iota(jnp.int32, (8, 2 * WIN), 0)
    part = lax.broadcasted_iota(jnp.int32, (8, 2 * WIN), 1) // HD
    choose = ((part == row + 2) & (row < 2)) | ((part == 1) & (row == 2))
    deltas = lax.dot_general(
        choose.astype(F32),
        wide * attended.astype(F32),
        (((1,), (1,)), ((), ())),
        precision=HIGH,
        preferred_element_type=F32,
    )
    second = keep(swap(wide[:, :WIN]), True).astype(BF16)
    query_parts = []
    heads = []
    for h in range(3):
        if h < 2:
            query = keep(queries[:, :WIN], h == 0)
            given = keep(out_grad[:, WIN:], h == 0)
            kcol, vcol = 0, 1
        else:
            query, given = queries[:, WIN:], second
            kcol, vcol = 2, 3
        heads.append((query, given))
        total, delta = totals[h], deltas[h : h + 1, :]
        for lo in range(0, count, step):
            hi = lo + step
            weights = jnp.exp(nt(kv(lo, hi, kcol), query) + mask[lo:hi, :] - total)
            probs[h, lo:hi, :] = weights.astype(BF16)
            weight_grad = nt(kv(lo, hi, vcol), given)
            dscore[h, lo:hi, :] = (weights * (weight_grad - delta)).astype(BF16)
        query_parts.append(tn(kv(0, count, kcol), dscore[h, 0:count, :]))
    for lo in range(0, count, step):
        hi = lo + step
        put(
            lo,
            hi,
            nn(dscore[0, lo:hi, :], heads[0][0]) + nn(dscore[1, lo:hi, :], heads[1][0]),
            nn(probs[0, lo:hi, :], heads[0][1]) + nn(probs[1, lo:hi, :], heads[1][1]),
            nn(dscore[2, lo:hi, :], heads[2][0]),
            nn(probs[2, lo:hi, :], heads[2][1]),
        )
    both = jnp.concatenate(
        [
            query_parts[0][:HD],
            query_parts[1][HD:],
            query_parts[2][HD:],
            jnp.zeros((HD, rows), F32),
        ],
        axis=0,
    )
    both = (both * 0.125).T
    return both[:, :WIN], both[:, WIN:]


def self_mask(scal, mask, rows, splits):
    query = clip_of(
        frame_position(lax.broadcasted_iota(jnp.int32, (1, rows), 1), 0, rows, splits, scal), scal
    )
    for block in range(splits):
        key = clip_of(
            frame_position(
                lax.broadcasted_iota(jnp.int32, (rows, 1), 0), block, rows, splits, scal
            ),
            scal,
        )
        mask[block * rows : (block + 1) * rows, :] = jnp.where(key == query, 0.0, NEG)


def cross_mask(scal, mask, rows, splits, clips):
    query = clip_of(
        frame_position(lax.broadcasted_iota(jnp.int32, (1, rows), 1), 0, rows, splits, scal), scal
    )
    slot = lax.broadcasted_iota(jnp.int32, (TXT, 1), 0)
    for c in range(clips):
        allowed = (query == c) & (slot < scal[S_TOK + c])
        mask[c * TXT : (c + 1) * TXT, :] = jnp.where(allowed, 0.0, NEG)


def own_clip(scal, rows, splits, block=0):
    return clip_of(
        frame_position(lax.broadcasted_iota(jnp.int32, (rows, 1), 0), block, rows, splits, scal),
        scal,
    )


def own_clip_row(scal, rows, splits, block=0):
    return clip_of(
        frame_position(lax.broadcasted_iota(jnp.int32, (1, rows), 1), block, rows, splits, scal),
        scal,
    )


def shard_index(scal, z, splits):
    return lax.rem(scal[S_Z] - z + splits, splits)


def self_forward(n_p, splits, *refs):
    scal = refs[0]
    frames = refs[1 : 1 + splits]
    mod, bias, out_bias = refs[1 + splits : 4 + splits]
    pieces = refs[4 + splits : 4 + splits + n_p]
    hidden_t, kv_out, q_out, att_out, lse, branch_out, after = refs[
        4 + splits + n_p : 11 + splits + n_p
    ]
    hidden, weights, mask, scores, probs, sems = refs[11 + splits + n_p :]
    rows = frames[0].shape[0]
    count = rows * splits
    copies = load_start(pieces, weights, sems, scal)
    self_mask(scal, mask, rows, splits)
    for block in range(splits):
        clip = own_clip(scal, rows, splits, block)
        normed, _ = normalize(frames[block][...].astype(F32))
        value = normed * (1.0 + per_row(mod, 1, clip)) + per_row(mod, 0, clip)
        hidden[block * rows : (block + 1) * rows, :] = value.astype(BF16)
        hidden_t[:, block * rows : (block + 1) * rows] = value.T.astype(BF16)
    branch_out[...] = jnp.broadcast_to(out_bias[...], branch_out.shape)
    for copy in copies:
        copy.wait()

    def one(z, carry):
        bias_row = bias[shard_index(scal, z, splits)]
        for block in range(splits):
            span = slice(block * rows, (block + 1) * rows)
            part = nn(hidden[span, :], weights[z, :, WIN : 5 * WIN]) + bias_row[:, WIN : 5 * WIN]
            kv_out[z, span, :] = part.astype(BF16)
            if block == 0:
                third = keep(swap(part[:, 2 * WIN : 3 * WIN].astype(BF16).astype(F32)), False)
        pair = nn(hidden[0:rows, :], weights[z, :, 0:WIN]) + bias_row[:, 0:WIN]
        queries = (
            jnp.concatenate([pair.astype(BF16).astype(F32), third], axis=1) * 0.125
        ).astype(BF16)
        q_out[z] = queries

        def kv(lo, hi, col):
            return kv_out[z, lo:hi, col * WIN : (col + 1) * WIN]

        attended, totals = attend(queries, kv, mask, scores, probs, count)
        att_out[z] = attended
        for h in range(3):
            lse[z, h : h + 1, :] = totals[h]
        branch_out[...] += nt(attended, weights[z, :, 4 * WIN :])
        return carry

    lax.fori_loop(0, splits, one, 0)
    clip = own_clip(scal, rows, splits)
    after[...] = frames[0][...].astype(F32) + per_row(mod, 2, clip) * branch_out[...]


def cross_forward(n_p, splits, *refs):
    scal, after_self, text, gain, bias, out_bias = refs[:6]
    pieces = refs[6 : 6 + n_p]
    hidden_t, text_t, kv_out, q_out, att_out, lse, after = refs[6 + n_p : 13 + n_p]
    weights, mask, scores, probs, sems = refs[13 + n_p :]
    rows = after_self.shape[0]
    count = text.shape[0]
    copies = load_start(pieces, weights, sems, scal, D)
    cross_mask(scal, mask, rows, splits, count // TXT)
    normed, _ = normalize(after_self[...])
    wide = normed * gain[...]
    hidden = wide.astype(BF16)
    hidden_t[...] = wide.T.astype(BF16)
    for lo in range(0, count, 256):
        text_t[:, lo : lo + 256] = text[lo : lo + 256, :].astype(F32).T.astype(BF16)
    after[...] = after_self[...] + out_bias[...]
    for copy in copies:
        copy.wait()

    def one(z, carry):
        bias_row = bias[shard_index(scal, z, splits)]
        for lo in range(0, count, 256):
            part = nn(text[lo : lo + 256, :], weights[z, :, WIN : 5 * WIN])
            kv_out[z, lo : lo + 256, :] = (part + bias_row[:, WIN : 5 * WIN]).astype(BF16)
        pair = nn(hidden, weights[z, :, 0:WIN]) + bias_row[:, 0:WIN]
        third = nn(hidden, weights[z, :, 3 * WIN : 4 * WIN]) + bias_row[:, 3 * WIN : 4 * WIN]
        third = keep(swap(third.astype(BF16).astype(F32)), False)
        queries = (
            jnp.concatenate([pair.astype(BF16).astype(F32), third], axis=1) * 0.125
        ).astype(BF16)
        q_out[z] = queries

        def kv(lo, hi, col):
            return kv_out[z, lo:hi, col * WIN : (col + 1) * WIN]

        attended, totals = attend(queries, kv, mask, scores, probs, count)
        att_out[z] = attended
        for h in range(3):
            lse[z, h : h + 1, :] = totals[h]
        after[...] += nt(attended, weights[z, :, 4 * WIN :])
        return carry

    lax.fori_loop(0, splits, one, 0)


def feed_forward(n_p, splits, low, high, *refs):
    scal, after_cross, upstream, mod, in_bias, out_bias = refs[:6]
    pieces = refs[6 : 6 + n_p]
    rest = refs[6 + n_p :]
    n_o = 2 if n_p > 1 else 1
    first, last = low == 0, high == splits
    if not first:
        mlp_in, back_in, bias_in = rest[:3]
        rest = rest[3:]
    grads = rest[:n_o]
    in_bias_grad = rest[n_o]
    rest = rest[n_o + 1 :]
    if last:
        layer_out, d_after, out_bias_grad, sums, mlp, back = rest[:6]
        rest = rest[6:]
    else:
        mlp, back = rest[:2]
        rest = rest[2:]
    weights, gbuf, load_sems, store_sems = rest
    rows = after_cross.shape[0]
    copies = load_start(pieces, weights, load_sems, scal)
    clip = own_clip(scal, rows, splits)
    normed, inverse = normalize(after_cross[...])
    scale = 1.0 + per_row(mod, 4, clip)
    wide = normed * scale + per_row(mod, 3, clip)
    hidden = wide.astype(BF16)
    hidden_t = wide.T.astype(BF16)
    gate = per_row(mod, 5, clip)
    given = upstream[...].astype(F32)
    low_wide = given * gate
    lowered = low_wide.astype(BF16)
    low_t = low_wide.T.astype(BF16)
    if first:
        mlp[...] = jnp.broadcast_to(out_bias[...], mlp.shape)
        back[...] = jnp.zeros_like(back)
        in_bias_grad[...] = jnp.zeros_like(in_bias_grad)
    else:
        mlp[...] = mlp_in[...]
        back[...] = back_in[...]
        in_bias_grad[...] = bias_in[...]
    for copy in copies:
        copy.wait()

    def one(i, carry):
        place = shard_index(scal, i + low, splits)
        pre = nn(hidden, weights[i, :, 0:D]) + in_bias[place]
        inner = 0.7978845608028654 * (pre + 0.044715 * (pre * pre * pre))
        curve = jnp.tanh(inner)
        half = 0.5 * (1.0 + curve)
        active = (pre * half).astype(BF16)
        slope = half + 0.5 * pre * (1.0 - curve * curve) * 0.7978845608028654 * (
            1.0 + 3.0 * 0.044715 * pre * pre
        )
        pre_grad = (slope * nn(lowered, weights[i, :, D:])).astype(BF16)
        in_bias_grad[place] = jnp.sum(pre_grad.astype(F32), axis=0, keepdims=True)
        mlp[...] += nt(active, weights[i, :, D:])
        back[...] += nt(pre_grad, weights[i, :, 0:D])
        gbuf[i, :, 0:D] = nn(hidden_t, pre_grad).astype(BF16)
        gbuf[i, :, D:] = nn(low_t, active).astype(BF16)
        for copy in store_copies(gbuf, i, grads, store_sems, scal):
            copy.start()
        return carry

    lax.fori_loop(0, high - low, one, 0)
    if last:
        out_bias_grad[...] = jnp.sum(lowered.astype(F32), axis=0, keepdims=True)
        branch = mlp[...]
        layer_out[...] = (after_cross[...] + gate * branch).astype(BF16)
        hidden_grad = back[...]
        d_after[...] = given + normalize_back(hidden_grad * scale, normed, inverse)
        clip_row = own_clip_row(scal, rows, splits)
        sums[:, 0:D] = clip_sums(clip_row, hidden_grad)
        sums[:, D : 2 * D] = clip_sums(clip_row, hidden_grad * normed)
        sums[:, 2 * D :] = clip_sums(clip_row, given * branch)
    for i in range(high - low):
        for copy in store_copies(gbuf, i, grads, store_sems, scal):
            copy.wait()


def cross_backward(n_p, splits, low, high, *refs):
    scal, d_cross, after_self, hidden_t, text_t, gain, mod, branch, kv_in, q_in, att_in, lse = refs[
        :12
    ]
    pieces = refs[12 : 12 + n_p]
    rest = refs[12 + n_p :]
    first, last = low == 0, high == splits
    if not first:
        back_in, text_in, bias_in = rest[:3]
        rest = rest[3:]
    n_o = 2 if n_p > 1 else 1
    grads = rest[:n_o]
    bias_grad = rest[n_o]
    rest = rest[n_o + 1 :]
    if last:
        d_after, d_attn, text_out, row_grads, sums, back, text_back = rest[:7]
        rest = rest[7:]
    else:
        back, text_back = rest[:2]
        rest = rest[2:]
    weights, gbuf, mask, probs, dscore, key_grad, load_sems, store_sems = rest
    rows = after_self.shape[0]
    count = text_t.shape[1]
    copies = load_start(pieces, weights, load_sems, scal, D, low)
    cross_mask(scal, mask, rows, splits, count // TXT)
    given = d_cross[...].astype(BF16)
    given_wide = given.astype(F32)
    given_t = given_wide.T.astype(BF16)
    if first:
        back[...] = jnp.zeros_like(back)
        text_back[...] = jnp.zeros_like(text_back)
        bias_grad[...] = jnp.zeros_like(bias_grad)
    else:
        back[...] = back_in[...]
        text_back[...] = text_in[...]
        bias_grad[...] = bias_in[...]
    for copy in copies:
        copy.wait()

    def one(i, carry):
        z = i + low
        place = shard_index(scal, z, splits)

        def kv(lo, hi, col):
            return kv_in[z, lo:hi, col * WIN : (col + 1) * WIN]

        def put(lo, hi, k01, v01, k2, v2):
            key_grad[lo:hi, 0:WIN] = k01.astype(BF16)
            key_grad[lo:hi, WIN : 2 * WIN] = v01.astype(BF16)
            key_grad[lo:hi, 2 * WIN : 3 * WIN] = k2.astype(BF16)
            key_grad[lo:hi, 3 * WIN : 4 * WIN] = v2.astype(BF16)

        head_grad = nn(given, weights[i, :, 4 * WIN :]).astype(BF16)
        totals = [lse[z, h : h + 1, :] for h in range(3)]
        pair, third = attend_back(
            q_in[z], kv, att_in[z], head_grad, mask, totals, probs, dscore, count, put
        )
        pair, third = pair.astype(BF16), third.astype(BF16)
        part = nn(text_t[...], key_grad[...])
        out_part = nn(given_t, att_in[z])
        gbuf[i, :, 0:WIN] = nn(hidden_t[...], pair).astype(BF16)
        gbuf[i, :, WIN : 3 * WIN] = part[:, 0 : 2 * WIN].astype(BF16)
        gbuf[i, :, 3 * WIN : 4 * WIN] = (
            part[:, 2 * WIN : 3 * WIN] + nn(hidden_t[...], third)
        ).astype(BF16)
        gbuf[i, :, 4 * WIN : 5 * WIN] = (part[:, 3 * WIN :] + out_part[:, 0:WIN]).astype(BF16)
        gbuf[i, :, 5 * WIN :] = out_part[:, WIN:].astype(BF16)
        for copy in store_copies(gbuf, i, grads, store_sems, scal):
            copy.start()
        back[...] += nt(pair, weights[i, :, 0:WIN]) + nt(third, weights[i, :, 3 * WIN : 4 * WIN])
        for lo in range(0, count, 256):
            text_back[lo : lo + 256, :] += nt(
                key_grad[lo : lo + 256, :], weights[i, :, WIN : 5 * WIN]
            )
        key_sums = jnp.sum(key_grad[...].astype(F32), axis=0, keepdims=True)
        bias_grad[place, :, 0:WIN] = jnp.sum(pair.astype(F32), axis=0, keepdims=True)
        bias_grad[place, :, WIN : 3 * WIN] = key_sums[:, 0 : 2 * WIN]
        bias_grad[place, :, 3 * WIN : 4 * WIN] = key_sums[:, 2 * WIN : 3 * WIN] + jnp.sum(
            third.astype(F32), axis=0, keepdims=True
        )
        bias_grad[place, :, 4 * WIN : 5 * WIN] = key_sums[:, 3 * WIN :]
        bias_grad[place, :, 5 * WIN :] = jnp.zeros((1, WIN), F32)
        return carry

    lax.fori_loop(0, high - low, one, 0)
    for i in range(high - low):
        for copy in store_copies(gbuf, i, grads, store_sems, scal):
            copy.wait()
    if not last:
        return
    row_grads[...] = jnp.zeros_like(row_grads)
    row_grads[0:1, :] = jnp.sum(given_wide, axis=0, keepdims=True)
    normed, inverse = normalize(after_self[...])
    hidden_grad = back[...]
    row_grads[1:2, :] = jnp.sum(hidden_grad * normed, axis=0, keepdims=True)
    total = d_cross[...] + normalize_back(hidden_grad * gain[...], normed, inverse)
    d_after[...] = total
    clip = own_clip(scal, rows, splits)
    d_attn[...] = (total * per_row(mod, 2, clip)).astype(BF16)
    sums[...] = clip_sums(own_clip_row(scal, rows, splits), total * branch[...])
    text_out[...] = text_back[...].astype(BF16)


def self_backward(n_p, splits, low, high, *refs):
    scal = refs[0]
    frames = refs[1 : 1 + splits]
    given_ref, hidden_t, kv_in, q_in, att_in, lse = refs[1 + splits : 7 + splits]
    pieces = refs[7 + splits : 7 + splits + n_p]
    rest = refs[7 + splits + n_p :]
    first, last = low == 0, high == splits
    if not first:
        back_in, bias_in = rest[:2]
        rest = rest[2:]
    n_o = 2 if n_p > 1 else 1
    grads = rest[:n_o]
    bias_grad = rest[n_o]
    rest = rest[n_o + 1 :]
    if last:
        own = rest[0]
        parts = rest[1:splits]
        row_grads, sums, back = rest[splits : splits + 3]
        rest = rest[splits + 3 :]
    else:
        back = rest[0]
        rest = rest[1:]
    weights, gbuf, mask, probs, dscore, key_grad, load_sems, store_sems = rest
    rows = frames[0].shape[0]
    count = rows * splits
    copies = load_start(pieces, weights, load_sems, scal, 0, low)
    self_mask(scal, mask, rows, splits)
    given = given_ref[...]
    given_wide = given.astype(F32)
    given_t = given_wide.T.astype(BF16)
    if first:
        back[...] = jnp.zeros_like(back)
        bias_grad[...] = jnp.zeros_like(bias_grad)
    else:
        back[...] = back_in[...]
        bias_grad[...] = bias_in[...]
    for copy in copies:
        copy.wait()

    def one(i, carry):
        z = i + low
        place = shard_index(scal, z, splits)

        def kv(lo, hi, col):
            return kv_in[z, lo:hi, col * WIN : (col + 1) * WIN]

        def put(lo, hi, k01, v01, k2, v2):
            key_grad[lo:hi, 0:WIN] = k01.astype(BF16)
            key_grad[lo:hi, WIN : 2 * WIN] = v01.astype(BF16)
            key_grad[lo:hi, 2 * WIN : 3 * WIN] = k2.astype(BF16)
            key_grad[lo:hi, 3 * WIN : 4 * WIN] = v2.astype(BF16)

        head_grad = nn(given, weights[i, :, 4 * WIN :]).astype(BF16)
        totals = [lse[z, h : h + 1, :] for h in range(3)]
        pair, third = attend_back(
            q_in[z], kv, att_in[z], head_grad, mask, totals, probs, dscore, count, put
        )
        pair = pair.astype(BF16)
        key_grad[0:rows, 2 * WIN : 3 * WIN] = (
            key_grad[0:rows, 2 * WIN : 3 * WIN].astype(F32) + third
        ).astype(BF16)
        part = nn(hidden_t[...], key_grad[...])
        out_part = nn(given_t, att_in[z])
        gbuf[i, :, 0:WIN] = nn(hidden_t[:, 0:rows], pair).astype(BF16)
        gbuf[i, :, WIN : 4 * WIN] = part[:, 0 : 3 * WIN].astype(BF16)
        gbuf[i, :, 4 * WIN : 5 * WIN] = (part[:, 3 * WIN :] + out_part[:, 0:WIN]).astype(BF16)
        gbuf[i, :, 5 * WIN :] = out_part[:, WIN:].astype(BF16)
        for copy in store_copies(gbuf, i, grads, store_sems, scal):
            copy.start()
        for lo in range(0, count, 256):
            back[lo : lo + 256, :] += nt(
                key_grad[lo : lo + 256, :], weights[i, :, WIN : 5 * WIN]
            )
        back[0:rows, :] += nt(pair, weights[i, :, 0:WIN])
        key_sums = jnp.sum(key_grad[...].astype(F32), axis=0, keepdims=True)
        bias_grad[place, :, 0:WIN] = jnp.sum(pair.astype(F32), axis=0, keepdims=True)
        bias_grad[place, :, WIN : 5 * WIN] = key_sums
        bias_grad[place, :, 5 * WIN :] = jnp.zeros((1, WIN), F32)
        return carry

    lax.fori_loop(0, high - low, one, 0)
    for i in range(high - low):
        for copy in store_copies(gbuf, i, grads, store_sems, scal):
            copy.wait()
    if not last:
        return
    row_grads[...] = jnp.zeros_like(row_grads)
    row_grads[0:1, :] = jnp.sum(given_wide, axis=0, keepdims=True)
    shift = jnp.zeros((8, D), F32)
    scale = jnp.zeros((8, D), F32)
    for block in range(splits):
        value = back[block * rows : (block + 1) * rows, :]
        if block == 0:
            own[...] = value
        else:
            parts[block - 1][...] = value.astype(BF16)
        normed, _ = normalize(frames[block][...].astype(F32))
        clip_row = own_clip_row(scal, rows, splits, block)
        shift = shift + clip_sums(clip_row, value)
        scale = scale + clip_sums(clip_row, value * normed)
    sums[:, 0:D] = shift
    sums[:, D:] = scale


def finish(splits, *refs):
    scal, frames, mod, d_after, own = refs[:5]
    parts = refs[5 : 4 + splits]
    out = refs[4 + splits]
    rows = frames.shape[0]
    value = own[...]
    for part in parts:
        value = value + part[...].astype(F32)
    normed, inverse = normalize(frames[...].astype(F32))
    scale = 1.0 + per_row(mod, 1, own_clip(scal, rows, splits))
    out[...] = d_after[...] + normalize_back(value * scale, normed, inverse)


def pack_small(
    table, own, cross, inner, own_rows, cross_rows, out_row, first, gate, second, packed
):
    n_dp = table.shape[1] // WIN
    splits, clips = packed.shape[0], packed.shape[1] - 2
    for z in range(splits):
        packed[z, 0:clips, 0 : 2 * D] = first[0:clips, :]
        packed[z, 0:clips, 2 * D : 3 * D] = gate[0:clips, :]
        packed[z, 0:clips, 3 * D :] = second[0:clips, :]
    packed[:, clips + 1, :] = jnp.zeros((splits, 6 * D), F32)
    lane = lax.broadcasted_iota(jnp.int32, (D, n_dp * WIN), 0)

    def moved(value, which):
        choose = (lane == table[which : which + 1, :]).astype(F32).astype(BF16)
        high = value.astype(BF16).astype(F32)
        middle = (value - high).astype(BF16).astype(F32)
        parts = jnp.concatenate([high, middle, value - high - middle], axis=0).astype(BF16)
        found = nn(parts, choose)
        count = value.shape[0]
        return found[:count] + found[count : 2 * count] + found[2 * count :]

    def by_shard(ref):
        return jnp.concatenate([ref[z] for z in range(splits)], axis=0)

    both = moved(jnp.concatenate([by_shard(own), by_shard(cross)], axis=0), 0)
    heads = both[:splits] + pltpu.roll(both[splits:], 48, 1)
    hidden = moved(by_shard(inner), 1)
    rows = moved(
        jnp.concatenate(
            [own_rows[0:1, :], cross_rows[0:2, :], out_row[...]] + [jnp.zeros((4, D), F32)], axis=0
        ),
        2,
    )
    for d in range(n_dp):
        span = slice(d * WIN, (d + 1) * WIN)
        parts = [heads[:, span], hidden[:, span]]
        parts += [jnp.broadcast_to(rows[r : r + 1, span], (splits, WIN)) for r in range(4)]
        packed[:, clips + d // 6, d % 6 * D : (d % 6 + 1) * D] = jnp.concatenate(parts, axis=1)


def bias_table(n_dp):
    table = np.full((8, n_dp * WIN), -1, np.int32)
    for d in range(n_dp):
        for i in range(48):
            part, h, r = i // 24, i % 24 // 8, i % 8
            spot = d * 8 + r
            start = (h * HD if h < 2 else 3 * WIN) if part == 0 else (2 + h / 2) * WIN
            table[0, d * WIN + i] = (start if part == 0 or h < 2 else 4 * WIN) + spot
        for i in range(96):
            table[1, d * WIN + i] = i // 32 * 256 + d * 32 + i % 32
            table[2, d * WIN + i] = d * 96 + i
    return table


MEMORY = {"v": pltpu.VMEM, "s": pltpu.SMEM, "a": pl.ANY}


def call(body, inputs, outs, scratch, flops, name):
    moved = sum(a.size * a.dtype.itemsize for _, a in inputs)
    moved += sum(_size(s, t) for _, s, t in outs)
    return pl.pallas_call(
        body,
        out_shape=tuple(jax.ShapeDtypeStruct(s, t) for _, s, t in outs),
        in_specs=[pl.BlockSpec(memory_space=MEMORY[m]) for m, _ in inputs],
        out_specs=tuple(pl.BlockSpec(memory_space=MEMORY[m]) for m, _, _ in outs),
        scratch_shapes=scratch,
        compiler_params=pltpu.CompilerParams(vmem_limit_bytes=58 * 1024 * 1024),
        cost_estimate=pl.CostEstimate(flops=int(flops), bytes_accessed=int(moved), transcendentals=0),
        name=name,
    )(*[a for _, a in inputs])


def _size(shape, kind):
    total = jnp.dtype(kind).itemsize
    for s in shape:
        total *= s
    return total


class Ring:
    def __init__(self):
        self.n_dp = lax.axis_size("dp")
        self.splits = lax.axis_size("head")
        self.square = self.n_dp == 8
        if self.square:
            self.core = [(i, i ^ 1) for i in range(8)]
            self.first = [(i, i ^ (4 if i & 1 else 2)) for i in range(8)]
            self.second = [(i, i ^ (2 if i & 1 else 4)) for i in range(8)]

    def offsets(self):
        if not self.square:
            return [jnp.int32(0)]
        me = lax.axis_index("dp")
        rows = D // 8

        def kept(d):
            odd = d & 1
            return [d, d ^ (2 + 2 * odd), d ^ (4 - 2 * odd), d ^ 6]

        return [place * rows for place in kept(me) + kept(me ^ 1)]

    def z_pieces(self, value, far=None):
        n = self.splits
        return [value] + [
            lax.ppermute(value, "head", [(s, (s + k) % n) for s in range(n)])
            for k in (range(1, n) if far is None else far)
        ]

    def z_back(self, parts):
        n = self.splits
        return [
            lax.ppermute(parts[k - 1], "head", [(s, (s - k) % n) for s in range(n)])
            for k in range(1, n)
        ]

    def across(self, value, how):
        return lax.ppermute(value, "dp", how)

    def z_move(self, value, k):
        n = self.splits
        return lax.ppermute(value, "head", [(s, (s - k) % n) for s in range(n)])


class GradSum:
    def __init__(self, ring, grads):
        self.ring, self.grads = ring, list(grads)
        self.moved = []
        self.arrived = []
        if not ring.square:
            self.whole = lax.psum_scatter(grads[0][0], "dp", scatter_dimension=1, tiled=True)

    def across(self, value, how):
        if self.ring.square:
            self.moved.append(self.ring.across(value.astype(BF16), how))

    def block(self, i):
        value = self.grads[0][i].astype(F32) + self.moved[0][i].astype(F32)
        if len(self.moved) > 1:
            value = value + self.moved[1][i].astype(F32)
        return value

    def core(self):
        if self.ring.square:
            self.across(self.grads[1], self.ring.core)

    def second(self):
        if self.ring.square:
            self.across(self.block(slice(2, 4)), self.ring.second)

    def first(self):
        if self.ring.square:
            self.across(self.block(1), self.ring.first)

    def own(self, i):
        if not self.ring.square:
            return self.whole[i].astype(F32)
        value = self.grads[0][0, i].astype(F32) + self.moved[2][i].astype(F32)
        return value + self.moved[0][0, i].astype(F32) + self.moved[1][0, i].astype(F32)

    def shard(self, start):
        count = self.grads[0].shape[1]
        for i in range(count):
            k = i if start == 1 else start + i
            if k > 0:
                self.arrived.append(self.ring.z_move(self.own(i).astype(BF16), k))


def join_second(low, high):
    if not low.ring.square:
        return []
    part = slice(2, 4)
    both = jnp.concatenate([low.block(part), high.block(part)], axis=1)
    return [low.ring.across(both.astype(BF16), low.ring.second)]


def join_first(low, high):
    if not low.ring.square:
        return []
    both = jnp.concatenate([low.block(1), high.block(1)], axis=0)
    return [low.ring.across(both.astype(BF16), low.ring.first)]


def join_take(low, high, moved):
    count = low.grads[0].shape[1]
    for value in moved:
        low.moved.append(value[..., :count, :, :])
        high.moved.append(value[..., count:, :, :])


def join_shards(pairs):
    ring = pairs[0][0].ring
    half = ring.splits // 2
    return [
        ring.z_move(
            jnp.concatenate([pair[k // half].own(k % half) for pair in pairs], axis=1).astype(BF16),
            k,
        )
        for k in range(1, ring.splits)
    ]


class Gather:
    def __init__(self, ring, mine):
        self.ring = ring
        if ring.square:
            self.kept, self.other = [mine], []
        else:
            self.kept, self.other = [lax.all_gather(mine, "dp", axis=1, tiled=True)], []

    def sides(self):
        if self.ring.square:
            self.kept.append(self.ring.across(self.kept[0], self.ring.first))
            self.kept.append(self.ring.across(self.kept[0], self.ring.second))

    def corner(self):
        if self.ring.square:
            self.kept.append(self.ring.across(self.kept[1], self.ring.second))

    def core(self, *which):
        if self.ring.square:
            for i in which:
                self.other.append(self.ring.across(self.kept[i], self.ring.core))

    def pieces(self):
        return self.kept + self.other


def meet(*groups):
    flat = [v for group in groups for v in group]
    flat = list(lax.optimization_barrier(tuple(flat)))
    for group in groups:
        for i in range(len(group)):
            group[i] = flat.pop(0)


def to_layout(q, k, v, o):
    return jnp.concatenate(
        [
            q[:, :WIN],
            k[:, :WIN],
            v[:, :WIN],
            q[:, WIN:],
            k[:, WIN:],
            v[:, WIN:],
            o[:, WIN:],
            o[:, :WIN],
        ],
        axis=1,
    )


def from_layout(value):
    def pick(pair, third):
        return jnp.concatenate(
            [value[:, pair : pair + WIN], value[:, third : third + HD]], axis=1
        )

    return pick(0, 3 * WIN), pick(WIN, 3 * WIN + HD), pick(2 * WIN, 4 * WIN), pick(
        5 * WIN, 4 * WIN + HD
    )


def mod_gradients(ring, sums, clips):
    part = jnp.concatenate(sums, axis=1)[:clips]
    got = lax.all_to_all(
        jnp.broadcast_to(part[None], (ring.splits,) + part.shape), "head", 0, 0, tiled=True
    )
    low = jnp.sum(got, axis=0).astype(BF16)
    return lax.all_to_all(
        jnp.broadcast_to(low[None], (ring.n_dp,) + low.shape), "dp", 0, 0, tiled=True
    ).reshape(ring.n_dp * clips, -1)


def on_device(
    frames_in,
    step_embed,
    text_feats,
    clip_frames,
    text_tokens,
    out_grad,
    ada_weight,
    ada_bias,
    qkv_weight,
    qv_bias,
    attn_out_weight,
    attn_out_bias,
    cross_gain,
    cross_q_weight,
    cross_q_bias,
    cross_kv_weight,
    cross_v_bias,
    cross_out_weight,
    cross_out_bias,
    mlp_in_weight,
    mlp_in_bias,
    mlp_out_weight,
    mlp_out_bias,
):
    both = ("dp", "head")
    ring = Ring()
    n_dp, splits = ring.n_dp, ring.splits
    z_index = lax.axis_index("head")
    rows = frames_in.shape[0]
    count = rows * splits
    text_count = text_feats.shape[0]
    clips = clip_frames.shape[1]
    width = D // splits
    shard_rows = D // n_dp
    ends = jnp.cumsum(clip_frames[0])
    offs = ring.offsets()
    n_p = len(offs)
    scal = jnp.stack(
        [z_index, ends[0], ends[1], text_tokens[0, 0], text_tokens[0, 1], text_tokens[0, 2]]
        + [jnp.int32(0)] * 2
        + [o.astype(jnp.int32) for o in offs]
        + [jnp.int32(0)] * (S_LEN - S_OFF - n_p)
    ).astype(jnp.int32)

    shard_self = to_layout(
        qkv_weight[:, 0], qkv_weight[:, 1], qkv_weight[:, 2], attn_out_weight.T
    )
    shard_cross = to_layout(
        cross_q_weight, cross_kv_weight[:, 0], cross_kv_weight[:, 1], cross_out_weight.T
    )

    biases = [
        ada_bias,
        qv_bias.reshape(-1),
        attn_out_bias,
        cross_gain,
        cross_q_bias.reshape(-1),
        cross_v_bias.reshape(-1),
        cross_out_bias,
        mlp_in_bias.reshape(-1),
        mlp_out_bias,
    ]
    flat = jnp.concatenate(biases)
    cols = step_embed.reshape(clips, n_dp, shard_rows).transpose(1, 0, 2).reshape(n_dp, -1)
    sent = jnp.concatenate(
        [
            jnp.broadcast_to(flat[None, None], (n_dp, splits, flat.shape[0])),
            jnp.broadcast_to(cols[:, None], (n_dp, splits, cols.shape[1])),
        ],
        axis=2,
    ).reshape(n_dp * splits, -1)
    got = lax.all_to_all(sent, both, 0, 0, tiled=True)
    attn_shards = ring.z_pieces(jnp.concatenate([shard_self, shard_cross], axis=1))
    mlp_shard = jnp.concatenate([mlp_in_weight, mlp_out_weight.T], axis=1)
    held = [got]
    meet(held, attn_shards)
    got = held[0].reshape(n_dp, splits, -1)
    step_cols = got[:, 0, flat.shape[0] :].reshape(n_dp * clips, shard_rows).astype(F32)
    silu_cols = jax.nn.silu(step_cols).astype(BF16)
    spots = []
    place = 0
    for b in biases:
        spots.append(got[:, :, place : place + b.shape[0]].astype(F32))
        place += b.shape[0]

    def over_dp(value):
        return value[:, 0].reshape(1, -1)

    def by_head(value, lead=1):
        n = value.shape[2] // (lead * 3)
        v = value.reshape(n_dp, splits, lead, 3, n).transpose(1, 2, 3, 0, 4)
        return v.reshape(splits, lead, 3 * n_dp * n)

    all_ada_bias = over_dp(spots[0])
    qv = by_head(spots[1], 2)
    nothing = jnp.zeros((splits, width), F32)
    bias_self = to_layout(qv[:, 0], nothing, qv[:, 1], nothing)[:, None]
    all_attn_bias = over_dp(spots[2])
    all_gain = over_dp(spots[3])
    bias_cross = to_layout(
        by_head(spots[4])[:, 0], nothing, by_head(spots[5])[:, 0], nothing
    )[:, None]
    all_cross_bias = over_dp(spots[6])
    all_in_bias = by_head(spots[7])
    all_out_bias = over_dp(spots[8])

    mod_part = jnp.dot(silu_cols, ada_weight, preferred_element_type=F32)
    mod_got = lax.all_to_all(mod_part.reshape(n_dp, clips, -1), "dp", 0, 0, tiled=True)

    half = splits // 2
    attn_gather = Gather(ring, jnp.stack(attn_shards))
    attn_gather.sides()
    frame_blocks = ring.z_pieces(frames_in)
    held = [mod_got, mlp_shard]
    meet(held, attn_gather.kept)
    mlp_shard = held[1]
    mod = jnp.sum(held[0], axis=0) + all_ada_bias
    attn_gather.corner()
    attn_gather.core(0, 1, 2, 3)
    mlp_shards = ring.z_pieces(mlp_shard, range(1, half))
    mlp_gathers = [Gather(ring, jnp.stack(mlp_shards))]
    mlp_gathers[0].sides()
    mlp_gathers[0].core(0)
    mlp_late = ring.z_pieces(mlp_shard, range(half, splits))[1:]

    def dma(n):
        return pltpu.SemaphoreType.DMA(n)

    def any_of(arrays):
        return [("a", a) for a in arrays]

    def vmem_of(arrays):
        return [("v", a) for a in arrays]

    piece_rows = D // n_p
    kept_out = [("a", (max(n_p // 2, 1), splits, piece_rows, D), BF16)] * (2 if n_p > 1 else 1)
    n_o = len(kept_out)
    shard_type = pltpu.VMEM((splits, D, D), BF16)

    results = list(call(
        partial(self_forward, n_p, splits),
        [("s", scal)]
        + vmem_of(frame_blocks)
        + vmem_of([mod, bias_self, all_attn_bias])
        + any_of(attn_gather.pieces()),
        [
            ("v", (D, count), BF16),
            ("v", (splits, count, 4 * WIN), BF16),
            ("v", (splits, rows, 2 * WIN), BF16),
            ("v", (splits, rows, 2 * WIN), BF16),
            ("v", (splits, 8, rows), F32),
            ("v", (rows, D), F32),
            ("v", (rows, D), F32),
        ],
        [
            pltpu.VMEM((count, D), BF16),
            shard_type,
            pltpu.VMEM((count, rows), F32),
            pltpu.VMEM((count, rows), F32),
            pltpu.VMEM((count, rows), BF16),
            dma((n_p,)),
        ],
        22 * US,
        "self_forward",
    ))
    meet(
        results, mlp_gathers[0].kept, mlp_gathers[0].other, mlp_late, attn_gather.kept, attn_gather.other
    )
    hidden_one, self_kv, self_q, self_att, self_lse, attn_branch, after_self = results
    mlp_gathers[0].corner()
    mlp_gathers[0].core(1, 2)
    mlp_gathers.append(Gather(ring, jnp.stack(mlp_late)))
    mlp_gathers[1].sides()

    results = list(call(
        partial(cross_forward, n_p, splits),
        [("s", scal)]
        + vmem_of([after_self, text_feats, all_gain, bias_cross, all_cross_bias])
        + any_of(attn_gather.pieces()),
        [
            ("v", (D, rows), BF16),
            ("v", (D, text_count), BF16),
            ("v", (splits, text_count, 4 * WIN), BF16),
            ("v", (splits, rows, 2 * WIN), BF16),
            ("v", (splits, rows, 2 * WIN), BF16),
            ("v", (splits, 8, rows), F32),
            ("v", (rows, D), F32),
        ],
        [
            shard_type,
            pltpu.VMEM((text_count, rows), F32),
            pltpu.VMEM((text_count, rows), F32),
            pltpu.VMEM((text_count, rows), BF16),
            dma((n_p,)),
        ],
        17 * US,
        "cross_forward",
    ))
    meet(results, mlp_gathers[0].kept, mlp_gathers[0].other, mlp_gathers[1].kept)
    hidden_two_t, text_t, cross_kv, cross_q, cross_att, cross_lse, after_cross = results
    mlp_gathers[0].core(3)
    mlp_gathers[1].corner()
    mlp_gathers[1].core(0, 1, 2)

    kept_half = [(m, (shape[0], half) + shape[2:], kind) for m, shape, kind in kept_out]
    kept_wide = [(m, shape[:3] + (2 * D,), kind) for m, shape, kind in kept_half]
    half_type = pltpu.VMEM((half, D, D), BF16)

    def back_scratch(keys):
        return [
            half_type,
            half_type,
            pltpu.VMEM((keys, rows), F32),
            pltpu.VMEM((3, keys, rows), BF16),
            pltpu.VMEM((3, keys, rows), BF16),
            pltpu.VMEM((keys, 4 * WIN), BF16),
            dma((n_p,)),
            dma((n_p, half)),
        ]

    bias_type = [("v", (splits, 1, D), F32)]
    mlp_args = [after_cross, out_grad, mod, all_in_bias, all_out_bias]
    mlp_scratch = [
        pltpu.VMEM((half, D, 2 * D), BF16),
        pltpu.VMEM((half, D, 2 * D), BF16),
        dma((n_p,)),
        dma((n_p, half)),
    ]
    results = call(
        partial(feed_forward, n_p, splits, 0, half),
        [("s", scal)] + vmem_of(mlp_args) + any_of(mlp_gathers[0].pieces()),
        kept_wide + bias_type + [("v", (rows, D), F32)] * 2,
        mlp_scratch,
        9 * US,
        "feed_forward_first",
    )
    results = list(results)
    meet(results, mlp_gathers[1].kept, mlp_gathers[1].other)
    mlp_gathers[1].core(3)
    sum_mlp = [GradSum(ring, results[:n_o])]
    in_bias_grad, mlp_state, mlp_back = results[n_o:]
    sum_mlp[0].core()
    results = call(
        partial(feed_forward, n_p, splits, half, splits),
        [("s", scal)]
        + vmem_of(mlp_args)
        + any_of(mlp_gathers[1].pieces())
        + vmem_of([mlp_state, mlp_back, in_bias_grad]),
        kept_wide
        + bias_type
        + [
            ("v", (rows, D), BF16),
            ("v", (rows, D), F32),
            ("v", (1, D), F32),
            ("v", (8, 3 * D), F32),
        ],
        [pltpu.VMEM((rows, D), F32), pltpu.VMEM((rows, D), F32)] + mlp_scratch,
        10 * US,
        "feed_forward_last",
    )
    results = list(results)
    meet(results, sum_mlp[0].moved)
    sum_mlp.append(GradSum(ring, results[:n_o]))
    in_bias_grad, layer_out, d_after_cross, out_bias_grad, sums_two = results[n_o:]
    sum_mlp[0].second()
    sum_mlp[1].core()
    cross_args = [
        d_after_cross,
        after_self,
        hidden_two_t,
        text_t,
        all_gain,
        mod,
        attn_branch,
        cross_kv,
        cross_q,
        cross_att,
        cross_lse,
    ]
    cross_state = [("v", (rows, D), F32), ("v", (text_count, D), F32)]
    results = call(
        partial(cross_backward, n_p, splits, 0, half),
        [("s", scal)] + vmem_of(cross_args) + any_of(attn_gather.pieces()),
        kept_half + bias_type + cross_state,
        back_scratch(text_count),
        14 * US,
        "cross_backward_first",
    )
    results = list(results)
    meet(results, sum_mlp[0].moved, sum_mlp[1].moved)
    sum_cross = [GradSum(ring, results[:n_o])]
    cross_bias_grad, cross_back, text_back = results[n_o:]
    sum_mlp[0].first()
    sum_mlp[1].second()
    sum_cross[0].core()
    results = call(
        partial(cross_backward, n_p, splits, half, splits),
        [("s", scal)]
        + vmem_of(cross_args)
        + any_of(attn_gather.pieces())
        + vmem_of([cross_back, text_back, cross_bias_grad]),
        kept_half
        + bias_type
        + [
            ("v", (rows, D), F32),
            ("v", (rows, D), BF16),
            ("v", (text_count, D), BF16),
            ("v", (8, D), F32),
            ("v", (8, D), F32),
        ],
        [pltpu.VMEM((rows, D), F32), pltpu.VMEM((text_count, D), F32)] + back_scratch(text_count),
        15 * US,
        "cross_backward_last",
    )
    results = list(results)
    meet(results, sum_mlp[0].moved, sum_mlp[1].moved, sum_cross[0].moved)
    sum_cross.append(GradSum(ring, results[:n_o]))
    cross_bias_grad, d_after_self, d_attn, text_out, cross_rows, gate_sums = results[n_o:]
    sum_mlp[0].shard(1)
    sum_mlp[1].first()
    sum_cross[0].second()
    sum_cross[1].core()
    text_got = lax.all_to_all(
        text_out.reshape(splits, text_count // splits, D), "head", 0, 0, tiled=True
    )
    self_args = [d_attn, hidden_one, self_kv, self_q, self_att, self_lse]
    results = call(
        partial(self_backward, n_p, splits, 0, half),
        [("s", scal)] + vmem_of(frame_blocks) + vmem_of(self_args) + any_of(attn_gather.pieces()),
        kept_half + bias_type + [("v", (count, D), F32)],
        back_scratch(count),
        17 * US,
        "self_backward_first",
    )
    results = list(results)
    held = [text_got]
    meet(
        results,
        held,
        sum_mlp[0].arrived,
        sum_mlp[1].moved,
        sum_cross[0].moved,
        sum_cross[1].moved,
    )
    text_got = held[0]
    sum_self = [GradSum(ring, results[:n_o])]
    self_bias_grad, self_back = results[n_o:]
    sum_mlp[1].shard(2)
    sum_cross[0].first()
    sum_cross[1].second()
    sum_self[0].core()
    results = call(
        partial(self_backward, n_p, splits, half, splits),
        [("s", scal)]
        + vmem_of(frame_blocks)
        + vmem_of(self_args)
        + any_of(attn_gather.pieces())
        + vmem_of([self_back, self_bias_grad]),
        kept_half
        + bias_type
        + [("v", (rows, D), F32)]
        + [("v", (rows, D), BF16)] * (splits - 1)
        + [("v", (8, D), F32), ("v", (8, 2 * D), F32)],
        [pltpu.VMEM((count, D), F32)] + back_scratch(count),
        18 * US,
        "self_backward_last",
    )
    results = list(results)
    held = [in_bias_grad, out_bias_grad, cross_bias_grad, cross_rows, gate_sums, sums_two]
    meet(
        results,
        held,
        sum_mlp[1].arrived,
        sum_cross[0].moved,
        sum_cross[1].moved,
        sum_self[0].moved,
    )
    sum_self.append(GradSum(ring, results[:n_o]))
    self_bias_grad, own_part = results[n_o : n_o + 2]
    parts = results[n_o + 2 : n_o + 1 + splits]
    self_rows, sums_one = results[n_o + 1 + splits :]

    sum_self[1].core()
    sum_cross[1].first()
    arrived = ring.z_back(parts)
    in_bias_grad, out_bias_grad, cross_bias_grad, cross_rows, gate_sums, sums_two = held
    small = [self_bias_grad, cross_bias_grad, in_bias_grad, self_rows, cross_rows, out_bias_grad]
    small += [sums_one, gate_sums, sums_two]
    far = join_second(*sum_self)
    early, late = arrived[0::2], arrived[1::2]
    meet(small, far, sum_cross[1].moved, early)
    join_take(*sum_self, far)
    near = join_first(*sum_self)
    if ring.square:
        (packed,) = call(
            pack_small,
            vmem_of([jnp.asarray(bias_table(n_dp))] + small),
            [("v", (splits, clips + 2, 6 * D), F32)],
            [],
            6 * US,
            "pack_small",
        )
        held = [lax.all_to_all(packed, "head", 0, 0, tiled=True)]
        got = jnp.sum(held[0], axis=0)
        mod_low = got[:clips].astype(BF16).astype(F32)
        bias_low = got[clips:].reshape(-1, 1, D)[:n_dp]
        sent = jnp.concatenate(
            [
                jnp.broadcast_to(mod_low[None], (n_dp,) + mod_low.shape),
                jnp.pad(bias_low, ((0, 0), (0, 0), (0, 5 * D))),
            ],
            axis=1,
        )
        held = [lax.all_to_all(sent, "dp", 0, 0, tiled=True)]
    meet(late, near)
    arrived = early + late
    join_take(*sum_self, near)
    last = join_shards([sum_cross, sum_self])
    self_bias_grad, cross_bias_grad, in_bias_grad, self_rows, cross_rows, out_bias_grad = small[:6]
    if ring.square:
        mod_all = held[0][:, :clips].reshape(n_dp * clips, -1).astype(BF16)
        bias_sum = jnp.sum(held[0][:, clips, :D], axis=0)
        places = [0, 24, 2 * WIN, 4 * WIN, 48, 72, 3 * WIN, WIN, 5 * WIN]
    else:
        mod_all = mod_gradients(ring, small[6:], clips)
    step_part = lax.dot_general(
        mod_all, ada_weight, (((1,), (1,)), ((), ())), preferred_element_type=F32
    )
    (frames_grad,) = call(
        partial(finish, splits),
        [("s", scal)] + vmem_of([frames_in, mod, d_after_self, own_part]) + vmem_of(arrived),
        [("v", (rows, D), F32)],
        [],
        3 * US,
        "finish",
    )
    text_grad = jnp.sum(text_got.astype(F32), axis=0)

    grad_ada = lax.dot_general(
        silu_cols, mod_all, (((0,), (0,)), ((), ())), preferred_element_type=F32
    )
    dp_index = lax.axis_index("dp")
    bias_width = ada_bias.shape[0]
    grad_ada_bias = jnp.sum(
        lax.dynamic_slice_in_dim(mod_all, dp_index * bias_width, bias_width, 1).astype(F32), axis=0
    )
    step_got = lax.all_to_all(step_part.reshape(n_dp, clips, shard_rows), "dp", 0, 0, tiled=True)
    step_got = [step_got]
    meet(last, step_got)
    (step_got,) = step_got
    total_cross, total_self = (
        pair[0].own(0) + sum(part[:, i * D : (i + 1) * D].astype(F32) for part in last)
        for i, pair in enumerate((sum_cross, sum_self))
    )
    step_value = step_embed.astype(F32)
    _, silu_pull = jax.vjp(jax.nn.silu, step_value)
    step_grad = silu_pull(step_got.transpose(1, 0, 2).reshape(clips, D))[0]

    def spread(value):
        v = value.reshape(n_dp, 1, D // n_dp)
        return jnp.broadcast_to(v, (n_dp, splits, D // n_dp))

    def heads_out(value):
        n = value.shape[1] // (3 * n_dp)
        return value.reshape(splits, 3, n_dp, n).transpose(2, 0, 1, 3).reshape(n_dp, splits, 3 * n)

    sq, _, sv, _ = from_layout(self_bias_grad[:, 0])
    cq, _, cv, _ = from_layout(cross_bias_grad[:, 0])
    entries = [
        heads_out(sq),
        heads_out(sv),
        spread(self_rows[0]),
        spread(cross_rows[1]),
        heads_out(cq),
        heads_out(cv),
        spread(cross_rows[0]),
        heads_out(in_bias_grad[:, 0]),
        spread(out_bias_grad[0]),
    ]
    if not ring.square:
        packed = jnp.concatenate(entries, axis=2)
        places = [sum(e.shape[2] for e in entries[:i]) for i in range(len(entries))]
        bias_sum = jnp.sum(
            lax.all_to_all(packed.reshape(n_dp * splits, -1), both, 0, 0, tiled=True), axis=0
        )
    bias_out = [bias_sum[p : p + e.shape[2]] for p, e in zip(places, entries)]

    total_mlp = sum_mlp[0].own(0) + sum(
        part.astype(F32) for part in sum_mlp[0].arrived + sum_mlp[1].arrived
    )
    gq, gk, gv, go = from_layout(total_self)
    hq, hk, hv, ho = from_layout(total_cross)
    return (
        layer_out,
        frames_grad,
        step_grad,
        text_grad,
        grad_ada,
        grad_ada_bias,
        jnp.stack([gq, gk, gv], axis=1),
        jnp.stack([bias_out[0], bias_out[1]]).reshape(qv_bias.shape),
        go.T,
        bias_out[2],
        bias_out[3],
        hq,
        bias_out[4].reshape(cross_q_bias.shape),
        jnp.stack([hk, hv], axis=1),
        bias_out[5].reshape(cross_v_bias.shape),
        ho.T,
        bias_out[6],
        total_mlp[:, :D],
        bias_out[7].reshape(mlp_in_bias.shape),
        total_mlp[:, D:].T,
        bias_out[8],
    )


def solution(mesh):
    rows_all, by_dp = P(("dp", "head"), None), P("dp", None)
    head_dp, dp_head = P("head", "dp"), P("dp", "head")
    dp_three, vector = P("dp", None, "head"), P("dp")
    params = (
        by_dp,
        vector,
        dp_three,
        P(None, "head", "dp"),
        head_dp,
        vector,
        vector,
        dp_head,
        head_dp,
        dp_three,
        head_dp,
        head_dp,
        vector,
        dp_head,
        head_dp,
        head_dp,
        vector,
    )
    return jax.shard_map(
        on_device,
        mesh=mesh,
        in_specs=(rows_all, by_dp, by_dp, by_dp, by_dp, rows_all) + params,
        out_specs=(rows_all, rows_all, by_dp, rows_all) + params,
        check_vma=False,
    )
```

```python
from functools import partial

import jax
import jax.numpy as jnp
import numpy as np
from jax import lax
from jax.experimental import pallas as pl
from jax.experimental.pallas import tpu as pltpu
from jax.sharding import PartitionSpec as P

D = 768
HD = 64
TXT = 256
WIN = 128
EPS = 1e-06
NEG = -1e30
F32 = jnp.float32
BF16 = jnp.bfloat16
HIGH = lax.Precision.HIGHEST
S_Z, S_END, S_TOK, S_OFF = 0, 1, 3, 8
S_LEN = 16
US = 1.15e9


def nn(a, b):
    return lax.dot_general(a, b, (((1,), (0,)), ((), ())), preferred_element_type=F32)


def nt(a, b):
    return lax.dot_general(a, b, (((1,), (1,)), ((), ())), preferred_element_type=F32)


def tn(a, b):
    return lax.dot_general(a, b, (((0,), (0,)), ((), ())), preferred_element_type=F32)


def normalize(v):
    centered = v - jnp.mean(v, axis=-1, keepdims=True)
    inverse = lax.rsqrt(jnp.mean(centered * centered, axis=-1, keepdims=True) + EPS)
    return centered * inverse, inverse


def normalize_back(u, normed, inverse):
    return inverse * (
        u
        - jnp.mean(u, axis=-1, keepdims=True)
        - normed * jnp.mean(u * normed, axis=-1, keepdims=True)
    )


def clip_of(position, scal):
    return (position >= scal[S_END]).astype(jnp.int32) + (position >= scal[S_END + 1]).astype(
        jnp.int32
    )


def frame_position(index, block, rows, splits, scal):
    return lax.rem(scal[S_Z] - block + splits, splits) * rows + index


def per_row(mod_ref, part, clip):
    cols = slice(part * D, (part + 1) * D)
    first, second, third = (mod_ref[c : c + 1, cols] for c in range(3))
    return jnp.where(clip == 0, first, jnp.where(clip == 1, second, third))


def clip_sums(clip_row, value):
    which = lax.broadcasted_iota(jnp.int32, (8, clip_row.shape[1]), 0)
    choose = (which == clip_row).astype(F32)
    return lax.dot_general(
        choose, value, (((1,), (0,)), ((), ())), precision=HIGH, preferred_element_type=F32
    )


def lanes(rows, low):
    lane = lax.broadcasted_iota(jnp.int32, (rows, WIN), 1)
    return lane < HD if low else lane >= HD


def keep(value, low):
    return jnp.where(lanes(value.shape[0], low), value, jnp.zeros_like(value))


def swap(value):
    return pltpu.roll(value, HD, 1)


def load_start(pieces, buffer, sems, scal, col=0, low=0):
    count, _, width = buffer.shape
    copies = []
    for j, piece in enumerate(pieces):
        rows = piece.shape[1]
        start = pl.multiple_of(scal[S_OFF + j], 32)
        copy = pltpu.make_async_copy(
            piece.at[low : low + count, :, col : col + width],
            buffer.at[:, pl.ds(start, rows), :],
            sems.at[j],
        )
        copy.start()
        copies.append(copy)
    return copies


def store_copies(buffer, z, outs, sems, scal, col=0, first=0):
    copies = []
    j = 0
    for out in outs:
        for i in range(out.shape[0]):
            rows = out.shape[2]
            start = pl.multiple_of(scal[S_OFF + j], 32)
            copies.append(
                pltpu.make_async_copy(
                    buffer.at[z, pl.ds(start, rows), col : col + out.shape[3]],
                    out.at[i, z],
                    sems.at[first + j, z],
                )
            )
            j += 1
    return copies


def attend(queries, kv, mask, scores, probs, count):
    rows = queries.shape[0]
    step = 256
    outs, totals = [], []
    for h in range(3):
        if h < 2:
            query = keep(queries[:, :WIN], h == 0)
            kcol, vcol = 0, 1
        else:
            query = queries[:, WIN:]
            kcol, vcol = 2, 3
        peak = None
        for lo in range(0, count, step):
            part = nt(kv(lo, lo + step, kcol), query) + mask[lo : lo + step, :]
            scores[lo : lo + step, :] = part
            top = jnp.max(part, axis=0, keepdims=True)
            peak = top if peak is None else jnp.maximum(peak, top)
        total = jnp.zeros((1, rows), F32)
        for lo in range(0, count, step):
            part = jnp.exp(scores[lo : lo + step, :] - peak)
            total = total + jnp.sum(part, axis=0, keepdims=True)
            probs[lo : lo + step, :] = part.astype(BF16)
        out = tn(kv(0, count, vcol), probs[0:count, :]) * (1.0 / total)
        outs.append(out)
        totals.append(peak + jnp.log(total))
    cat = jnp.concatenate(
        [jnp.zeros((HD, rows), F32), outs[2][:HD], outs[0][:HD], outs[1][HD:]], axis=0
    )
    return cat.T.astype(BF16), totals


def attend_back(queries, kv, attended, out_grad, mask, totals, probs, dscore, count, put):
    rows = queries.shape[0]
    step = 256
    wide = out_grad.astype(F32)
    row = lax.broadcasted_iota(jnp.int32, (8, 2 * WIN), 0)
    part = lax.broadcasted_iota(jnp.int32, (8, 2 * WIN), 1) // HD
    choose = ((part == row + 2) & (row < 2)) | ((part == 1) & (row == 2))
    deltas = lax.dot_general(
        choose.astype(F32),
        wide * attended.astype(F32),
        (((1,), (1,)), ((), ())),
        precision=HIGH,
        preferred_element_type=F32,
    )
    second = keep(swap(wide[:, :WIN]), True).astype(BF16)
    query_parts = []
    heads = []
    for h in range(3):
        if h < 2:
            query = keep(queries[:, :WIN], h == 0)
            given = keep(out_grad[:, WIN:], h == 0)
            kcol, vcol = 0, 1
        else:
            query, given = queries[:, WIN:], second
            kcol, vcol = 2, 3
        heads.append((query, given))
        total, delta = totals[h], deltas[h : h + 1, :]
        for lo in range(0, count, step):
            hi = lo + step
            weights = jnp.exp(nt(kv(lo, hi, kcol), query) + mask[lo:hi, :] - total)
            probs[h, lo:hi, :] = weights.astype(BF16)
            weight_grad = nt(kv(lo, hi, vcol), given)
            dscore[h, lo:hi, :] = (weights * (weight_grad - delta)).astype(BF16)
        query_parts.append(tn(kv(0, count, kcol), dscore[h, 0:count, :]))
    for lo in range(0, count, step):
        hi = lo + step
        put(
            lo,
            hi,
            nn(dscore[0, lo:hi, :], heads[0][0]) + nn(dscore[1, lo:hi, :], heads[1][0]),
            nn(probs[0, lo:hi, :], heads[0][1]) + nn(probs[1, lo:hi, :], heads[1][1]),
            nn(dscore[2, lo:hi, :], heads[2][0]),
            nn(probs[2, lo:hi, :], heads[2][1]),
        )
    both = jnp.concatenate(
        [
            query_parts[0][:HD],
            query_parts[1][HD:],
            query_parts[2][HD:],
            jnp.zeros((HD, rows), F32),
        ],
        axis=0,
    )
    both = (both * 0.125).T
    return both[:, :WIN], both[:, WIN:]


def self_mask(scal, mask, rows, splits):
    query = clip_of(
        frame_position(lax.broadcasted_iota(jnp.int32, (1, rows), 1), 0, rows, splits, scal), scal
    )
    for block in range(splits):
        key = clip_of(
            frame_position(
                lax.broadcasted_iota(jnp.int32, (rows, 1), 0), block, rows, splits, scal
            ),
            scal,
        )
        mask[block * rows : (block + 1) * rows, :] = jnp.where(key == query, 0.0, NEG)


def cross_mask(scal, mask, rows, splits, clips):
    query = clip_of(
        frame_position(lax.broadcasted_iota(jnp.int32, (1, rows), 1), 0, rows, splits, scal), scal
    )
    slot = lax.broadcasted_iota(jnp.int32, (TXT, 1), 0)
    for c in range(clips):
        allowed = (query == c) & (slot < scal[S_TOK + c])
        mask[c * TXT : (c + 1) * TXT, :] = jnp.where(allowed, 0.0, NEG)


def own_clip(scal, rows, splits, block=0):
    return clip_of(
        frame_position(lax.broadcasted_iota(jnp.int32, (rows, 1), 0), block, rows, splits, scal),
        scal,
    )


def own_clip_row(scal, rows, splits, block=0):
    return clip_of(
        frame_position(lax.broadcasted_iota(jnp.int32, (1, rows), 1), block, rows, splits, scal),
        scal,
    )


def shard_index(scal, z, splits):
    return lax.rem(scal[S_Z] - z + splits, splits)


def self_forward(n_p, splits, *refs):
    scal = refs[0]
    frames = refs[1 : 1 + splits]
    mod, bias, out_bias = refs[1 + splits : 4 + splits]
    pieces = refs[4 + splits : 4 + splits + n_p]
    hidden_t, kv_out, q_out, att_out, lse, branch_out, after = refs[
        4 + splits + n_p : 11 + splits + n_p
    ]
    hidden, weights, mask, scores, probs, sems = refs[11 + splits + n_p :]
    rows = frames[0].shape[0]
    count = rows * splits
    copies = load_start(pieces, weights, sems, scal)
    self_mask(scal, mask, rows, splits)
    for block in range(splits):
        clip = own_clip(scal, rows, splits, block)
        normed, _ = normalize(frames[block][...].astype(F32))
        value = normed * (1.0 + per_row(mod, 1, clip)) + per_row(mod, 0, clip)
        hidden[block * rows : (block + 1) * rows, :] = value.astype(BF16)
        hidden_t[:, block * rows : (block + 1) * rows] = value.T.astype(BF16)
    branch_out[...] = jnp.broadcast_to(out_bias[...], branch_out.shape)
    for copy in copies:
        copy.wait()

    def one(z, carry):
        bias_row = bias[shard_index(scal, z, splits)]
        for block in range(splits):
            span = slice(block * rows, (block + 1) * rows)
            part = nn(hidden[span, :], weights[z, :, WIN : 5 * WIN]) + bias_row[:, WIN : 5 * WIN]
            kv_out[z, span, :] = part.astype(BF16)
            if block == 0:
                third = keep(swap(part[:, 2 * WIN : 3 * WIN].astype(BF16).astype(F32)), False)
        pair = nn(hidden[0:rows, :], weights[z, :, 0:WIN]) + bias_row[:, 0:WIN]
        queries = (
            jnp.concatenate([pair.astype(BF16).astype(F32), third], axis=1) * 0.125
        ).astype(BF16)
        q_out[z] = queries

        def kv(lo, hi, col):
            return kv_out[z, lo:hi, col * WIN : (col + 1) * WIN]

        attended, totals = attend(queries, kv, mask, scores, probs, count)
        att_out[z] = attended
        for h in range(3):
            lse[z, h : h + 1, :] = totals[h]
        branch_out[...] += nt(attended, weights[z, :, 4 * WIN :])
        return carry

    lax.fori_loop(0, splits, one, 0)
    clip = own_clip(scal, rows, splits)
    after[...] = frames[0][...].astype(F32) + per_row(mod, 2, clip) * branch_out[...]


def cross_forward(n_p, splits, *refs):
    scal, after_self, text, gain, bias, out_bias = refs[:6]
    pieces = refs[6 : 6 + n_p]
    hidden_t, text_t, kv_out, q_out, att_out, lse, after = refs[6 + n_p : 13 + n_p]
    weights, mask, scores, probs, sems = refs[13 + n_p :]
    rows = after_self.shape[0]
    count = text.shape[0]
    copies = load_start(pieces, weights, sems, scal, D)
    cross_mask(scal, mask, rows, splits, count // TXT)
    normed, _ = normalize(after_self[...])
    wide = normed * gain[...]
    hidden = wide.astype(BF16)
    hidden_t[...] = wide.T.astype(BF16)
    for lo in range(0, count, 256):
        text_t[:, lo : lo + 256] = text[lo : lo + 256, :].astype(F32).T.astype(BF16)
    after[...] = after_self[...] + out_bias[...]
    for copy in copies:
        copy.wait()

    def one(z, carry):
        bias_row = bias[shard_index(scal, z, splits)]
        for lo in range(0, count, 256):
            part = nn(text[lo : lo + 256, :], weights[z, :, WIN : 5 * WIN])
            kv_out[z, lo : lo + 256, :] = (part + bias_row[:, WIN : 5 * WIN]).astype(BF16)
        pair = nn(hidden, weights[z, :, 0:WIN]) + bias_row[:, 0:WIN]
        third = nn(hidden, weights[z, :, 3 * WIN : 4 * WIN]) + bias_row[:, 3 * WIN : 4 * WIN]
        third = keep(swap(third.astype(BF16).astype(F32)), False)
        queries = (
            jnp.concatenate([pair.astype(BF16).astype(F32), third], axis=1) * 0.125
        ).astype(BF16)
        q_out[z] = queries

        def kv(lo, hi, col):
            return kv_out[z, lo:hi, col * WIN : (col + 1) * WIN]

        attended, totals = attend(queries, kv, mask, scores, probs, count)
        att_out[z] = attended
        for h in range(3):
            lse[z, h : h + 1, :] = totals[h]
        after[...] += nt(attended, weights[z, :, 4 * WIN :])
        return carry

    lax.fori_loop(0, splits, one, 0)


def feed_forward(n_p, splits, low, high, *refs):
    scal, after_cross, upstream, mod, in_bias, out_bias = refs[:6]
    pieces = refs[6 : 6 + n_p]
    rest = refs[6 + n_p :]
    n_o = 2 if n_p > 1 else 1
    first, last = low == 0, high == splits
    if not first:
        mlp_in, back_in, bias_in = rest[:3]
        rest = rest[3:]
    grads = rest[:n_o]
    in_bias_grad = rest[n_o]
    rest = rest[n_o + 1 :]
    if last:
        layer_out, d_after, out_bias_grad, sums, mlp, back = rest[:6]
        rest = rest[6:]
    else:
        mlp, back = rest[:2]
        rest = rest[2:]
    weights, gbuf, load_sems, store_sems = rest
    rows = after_cross.shape[0]
    copies = load_start(pieces, weights, load_sems, scal)
    clip = own_clip(scal, rows, splits)
    normed, inverse = normalize(after_cross[...])
    scale = 1.0 + per_row(mod, 4, clip)
    wide = normed * scale + per_row(mod, 3, clip)
    hidden = wide.astype(BF16)
    hidden_t = wide.T.astype(BF16)
    gate = per_row(mod, 5, clip)
    given = upstream[...].astype(F32)
    low_wide = given * gate
    lowered = low_wide.astype(BF16)
    low_t = low_wide.T.astype(BF16)
    if first:
        mlp[...] = jnp.broadcast_to(out_bias[...], mlp.shape)
        back[...] = jnp.zeros_like(back)
        in_bias_grad[...] = jnp.zeros_like(in_bias_grad)
    else:
        mlp[...] = mlp_in[...]
        back[...] = back_in[...]
        in_bias_grad[...] = bias_in[...]
    for copy in copies:
        copy.wait()

    def one(i, carry):
        place = shard_index(scal, i + low, splits)
        pre = nn(hidden, weights[i, :, 0:D]) + in_bias[place]
        inner = 0.7978845608028654 * (pre + 0.044715 * (pre * pre * pre))
        curve = jnp.tanh(inner)
        half = 0.5 * (1.0 + curve)
        active = (pre * half).astype(BF16)
        slope = half + 0.5 * pre * (1.0 - curve * curve) * 0.7978845608028654 * (
            1.0 + 3.0 * 0.044715 * pre * pre
        )
        pre_grad = (slope * nn(lowered, weights[i, :, D:])).astype(BF16)
        in_bias_grad[place] = jnp.sum(pre_grad.astype(F32), axis=0, keepdims=True)
        mlp[...] += nt(active, weights[i, :, D:])
        back[...] += nt(pre_grad, weights[i, :, 0:D])
        gbuf[i, :, 0:D] = nn(hidden_t, pre_grad).astype(BF16)
        gbuf[i, :, D:] = nn(low_t, active).astype(BF16)
        for copy in store_copies(gbuf, i, grads, store_sems, scal):
            copy.start()
        return carry

    lax.fori_loop(0, high - low, one, 0)
    if last:
        out_bias_grad[...] = jnp.sum(lowered.astype(F32), axis=0, keepdims=True)
        branch = mlp[...]
        layer_out[...] = (after_cross[...] + gate * branch).astype(BF16)
        hidden_grad = back[...]
        d_after[...] = given + normalize_back(hidden_grad * scale, normed, inverse)
        clip_row = own_clip_row(scal, rows, splits)
        sums[:, 0:D] = clip_sums(clip_row, hidden_grad)
        sums[:, D : 2 * D] = clip_sums(clip_row, hidden_grad * normed)
        sums[:, 2 * D :] = clip_sums(clip_row, given * branch)
    for i in range(high - low):
        for copy in store_copies(gbuf, i, grads, store_sems, scal):
            copy.wait()


def cross_backward(n_p, splits, low, high, *refs):
    scal, d_cross, after_self, hidden_t, text_t, gain, mod, branch, kv_in, q_in, att_in, lse = refs[
        :12
    ]
    pieces = refs[12 : 12 + n_p]
    rest = refs[12 + n_p :]
    first, last = low == 0, high == splits
    if not first:
        back_in, text_in, bias_in = rest[:3]
        rest = rest[3:]
    n_o = 2 if n_p > 1 else 1
    grads = rest[:n_o]
    bias_grad = rest[n_o]
    rest = rest[n_o + 1 :]
    if last:
        d_after, d_attn, text_out, row_grads, sums, back, text_back = rest[:7]
        rest = rest[7:]
    else:
        back, text_back = rest[:2]
        rest = rest[2:]
    weights, gbuf, mask, probs, dscore, key_grad, load_sems, store_sems = rest
    rows = after_self.shape[0]
    count = text_t.shape[1]
    copies = load_start(pieces, weights, load_sems, scal, D, low)
    cross_mask(scal, mask, rows, splits, count // TXT)
    given = d_cross[...].astype(BF16)
    given_wide = given.astype(F32)
    given_t = given_wide.T.astype(BF16)
    if first:
        back[...] = jnp.zeros_like(back)
        text_back[...] = jnp.zeros_like(text_back)
        bias_grad[...] = jnp.zeros_like(bias_grad)
    else:
        back[...] = back_in[...]
        text_back[...] = text_in[...]
        bias_grad[...] = bias_in[...]
    for copy in copies:
        copy.wait()

    def one(i, carry):
        z = i + low
        place = shard_index(scal, z, splits)

        def kv(lo, hi, col):
            return kv_in[z, lo:hi, col * WIN : (col + 1) * WIN]

        def put(lo, hi, k01, v01, k2, v2):
            key_grad[lo:hi, 0:WIN] = k01.astype(BF16)
            key_grad[lo:hi, WIN : 2 * WIN] = v01.astype(BF16)
            key_grad[lo:hi, 2 * WIN : 3 * WIN] = k2.astype(BF16)
            key_grad[lo:hi, 3 * WIN : 4 * WIN] = v2.astype(BF16)

        head_grad = nn(given, weights[i, :, 4 * WIN :]).astype(BF16)
        totals = [lse[z, h : h + 1, :] for h in range(3)]
        pair, third = attend_back(
            q_in[z], kv, att_in[z], head_grad, mask, totals, probs, dscore, count, put
        )
        pair, third = pair.astype(BF16), third.astype(BF16)
        part = nn(text_t[...], key_grad[...])
        out_part = nn(given_t, att_in[z])
        gbuf[i, :, 0:WIN] = nn(hidden_t[...], pair).astype(BF16)
        gbuf[i, :, WIN : 3 * WIN] = part[:, 0 : 2 * WIN].astype(BF16)
        gbuf[i, :, 3 * WIN : 4 * WIN] = (
            part[:, 2 * WIN : 3 * WIN] + nn(hidden_t[...], third)
        ).astype(BF16)
        gbuf[i, :, 4 * WIN : 5 * WIN] = (part[:, 3 * WIN :] + out_part[:, 0:WIN]).astype(BF16)
        gbuf[i, :, 5 * WIN :] = out_part[:, WIN:].astype(BF16)
        for copy in store_copies(gbuf, i, grads, store_sems, scal):
            copy.start()
        back[...] += nt(pair, weights[i, :, 0:WIN]) + nt(third, weights[i, :, 3 * WIN : 4 * WIN])
        for lo in range(0, count, 256):
            text_back[lo : lo + 256, :] += nt(
                key_grad[lo : lo + 256, :], weights[i, :, WIN : 5 * WIN]
            )
        key_sums = jnp.sum(key_grad[...].astype(F32), axis=0, keepdims=True)
        bias_grad[place, :, 0:WIN] = jnp.sum(pair.astype(F32), axis=0, keepdims=True)
        bias_grad[place, :, WIN : 3 * WIN] = key_sums[:, 0 : 2 * WIN]
        bias_grad[place, :, 3 * WIN : 4 * WIN] = key_sums[:, 2 * WIN : 3 * WIN] + jnp.sum(
            third.astype(F32), axis=0, keepdims=True
        )
        bias_grad[place, :, 4 * WIN : 5 * WIN] = key_sums[:, 3 * WIN :]
        bias_grad[place, :, 5 * WIN :] = jnp.zeros((1, WIN), F32)
        return carry

    lax.fori_loop(0, high - low, one, 0)

    def finish_stores():
        for i in range(high - low):
            for copy in store_copies(gbuf, i, grads, store_sems, scal):
                copy.wait()

    if not last:
        finish_stores()
        return
    row_grads[...] = jnp.zeros_like(row_grads)
    row_grads[0:1, :] = jnp.sum(given_wide, axis=0, keepdims=True)
    normed, inverse = normalize(after_self[...])
    hidden_grad = back[...]
    row_grads[1:2, :] = jnp.sum(hidden_grad * normed, axis=0, keepdims=True)
    total = d_cross[...] + normalize_back(hidden_grad * gain[...], normed, inverse)
    d_after[...] = total
    clip = own_clip(scal, rows, splits)
    d_attn[...] = (total * per_row(mod, 2, clip)).astype(BF16)
    sums[...] = clip_sums(own_clip_row(scal, rows, splits), total * branch[...])
    text_out[...] = text_back[...].astype(BF16)
    finish_stores()


def pack_small(table, own, cross, inner, given_sum, cross_rows, out_row, first, gate, second, out):
    n_dp = table.shape[1] // WIN
    splits, clips = out.shape[0], 3
    lane = lax.broadcasted_iota(jnp.int32, (D, n_dp * WIN), 0)

    def moved(value, which):
        choose = (lane == table[which : which + 1, :]).astype(F32).astype(BF16)
        high = value.astype(BF16).astype(F32)
        middle = (value - high).astype(BF16).astype(F32)
        parts = jnp.concatenate([high, middle, value - high - middle], axis=0).astype(BF16)
        found = nn(parts, choose)
        count = value.shape[0]
        return found[:count] + found[count : 2 * count] + found[2 * count :]

    def by_shard(ref):
        return jnp.concatenate([ref[z] for z in range(splits)], axis=0)

    both = moved(jnp.concatenate([by_shard(own), by_shard(cross)], axis=0), 0)
    heads = both[:splits] + pltpu.roll(both[splits:], 48, 1)
    hidden = moved(by_shard(inner), 1)
    rows = moved(
        jnp.concatenate(
            [given_sum, cross_rows[0:2, :], out_row[...]] + [jnp.zeros((4, D), F32)], axis=0
        ),
        2,
    )
    out[...] = jnp.zeros_like(out)
    for z in range(splits):
        for c in range(clips):
            for j in range(6):
                source, col = ((first, j), (gate, 0), (second, j - 3))[(j > 1) + (j > 2)]
                out[z, c * 6 + j : c * 6 + j + 1, :] = source[c : c + 1, col * D : (col + 1) * D]
        for d in range(n_dp):
            span = slice(d * WIN, (d + 1) * WIN)
            parts = [heads[z : z + 1, span], hidden[z : z + 1, span]]
            parts += [rows[r : r + 1, span] for r in range(4)]
            spot = clips * 6 + d
            out[z, spot : spot + 1, :] = jnp.concatenate(parts, axis=1)


def self_backward(n_p, splits, low, high, small, *refs):
    scal = refs[0]
    frames = refs[1 : 1 + splits]
    given_ref, hidden_t, kv_in, q_in, att_in, lse = refs[1 + splits : 7 + splits]
    pieces = refs[7 + splits : 7 + splits + n_p]
    rest = refs[7 + splits + n_p :]
    first, last = low == 0, high == splits
    if not first:
        back_in, bias_in = rest[:2]
        rest = rest[2:]
    if small:
        table, cross_bias, inner_bias, cross_rows, out_row, gate, second = rest[:7]
        rest = rest[7:]
    n_o = 2 if n_p > 1 else 1
    grads = rest[:n_o]
    bias_grad = rest[n_o]
    rest = rest[n_o + 1 :]
    if last:
        own = rest[0]
        parts = rest[1:splits]
        row_grads, sums = rest[splits : splits + 2]
        rest = rest[splits + 2 :]
        if small:
            own_small, small_rows, back = rest[0], rest[1], rest[2]
            rest = rest[3:]
        else:
            back = rest[0]
            rest = rest[1:]
    else:
        back = rest[0]
        rest = rest[1:]
    weights, gbuf, mask, probs, dscore, key_grad, load_sems, store_sems = rest
    rows = frames[0].shape[0]
    count = rows * splits
    copies = load_start(pieces, weights, load_sems, scal, 0, low)
    self_mask(scal, mask, rows, splits)
    given = given_ref[...]
    given_wide = given.astype(F32)
    given_t = given_wide.T.astype(BF16)
    if first:
        back[...] = jnp.zeros_like(back)
        bias_grad[...] = jnp.zeros_like(bias_grad)
    else:
        back[...] = back_in[...]
        bias_grad[...] = bias_in[...]
    for copy in copies:
        copy.wait()

    def one(i, carry):
        z = i + low
        place = shard_index(scal, z, splits)

        def kv(lo, hi, col):
            return kv_in[z, lo:hi, col * WIN : (col + 1) * WIN]

        def put(lo, hi, k01, v01, k2, v2):
            key_grad[lo:hi, 0:WIN] = k01.astype(BF16)
            key_grad[lo:hi, WIN : 2 * WIN] = v01.astype(BF16)
            key_grad[lo:hi, 2 * WIN : 3 * WIN] = k2.astype(BF16)
            key_grad[lo:hi, 3 * WIN : 4 * WIN] = v2.astype(BF16)

        head_grad = nn(given, weights[i, :, 4 * WIN :]).astype(BF16)
        totals = [lse[z, h : h + 1, :] for h in range(3)]
        pair, third = attend_back(
            q_in[z], kv, att_in[z], head_grad, mask, totals, probs, dscore, count, put
        )
        pair = pair.astype(BF16)
        key_grad[0:rows, 2 * WIN : 3 * WIN] = (
            key_grad[0:rows, 2 * WIN : 3 * WIN].astype(F32) + third
        ).astype(BF16)
        part = nn(hidden_t[...], key_grad[...])
        out_part = nn(given_t, att_in[z])
        gbuf[i, :, 0:WIN] = nn(hidden_t[:, 0:rows], pair).astype(BF16)
        gbuf[i, :, WIN : 4 * WIN] = part[:, 0 : 3 * WIN].astype(BF16)
        gbuf[i, :, 4 * WIN : 5 * WIN] = (part[:, 3 * WIN :] + out_part[:, 0:WIN]).astype(BF16)
        gbuf[i, :, 5 * WIN :] = out_part[:, WIN:].astype(BF16)
        for copy in store_copies(gbuf, i, grads, store_sems, scal):
            copy.start()
        for lo in range(0, count, 256):
            back[lo : lo + 256, :] += nt(
                key_grad[lo : lo + 256, :], weights[i, :, WIN : 5 * WIN]
            )
        back[0:rows, :] += nt(pair, weights[i, :, 0:WIN])
        key_sums = jnp.sum(key_grad[...].astype(F32), axis=0, keepdims=True)
        bias_grad[place, :, 0:WIN] = jnp.sum(pair.astype(F32), axis=0, keepdims=True)
        bias_grad[place, :, WIN : 5 * WIN] = key_sums
        bias_grad[place, :, 5 * WIN :] = jnp.zeros((1, WIN), F32)
        return carry

    lax.fori_loop(0, high - low, one, 0)

    def finish_stores():
        for i in range(high - low):
            for copy in store_copies(gbuf, i, grads, store_sems, scal):
                copy.wait()

    if not last:
        finish_stores()
        return
    given_sum = jnp.sum(given_wide, axis=0, keepdims=True)
    row_grads[...] = jnp.zeros_like(row_grads)
    row_grads[0:1, :] = given_sum
    shift = jnp.zeros((8, D), F32)
    scale = jnp.zeros((8, D), F32)
    for block in range(splits):
        value = back[block * rows : (block + 1) * rows, :]
        if block == 0:
            own[...] = value
        else:
            parts[block - 1][0:rows, :] = value.astype(BF16)
        normed, _ = normalize(frames[block][...].astype(F32))
        clip_row = own_clip_row(scal, rows, splits, block)
        shift = shift + clip_sums(clip_row, value)
        scale = scale + clip_sums(clip_row, value * normed)
    sums[:, 0:D] = shift
    sums[:, D:] = scale
    if small:
        pack_small(
            table,
            bias_grad,
            cross_bias,
            inner_bias,
            given_sum,
            cross_rows,
            out_row,
            sums,
            gate,
            second,
            small_rows,
        )
        for k in range(splits):
            value = small_rows[shard_index(scal, k, splits)]
            if k == 0:
                own_small[...] = value
            else:
                parts[k - 1][rows:, :] = value.astype(BF16)
    finish_stores()


def finish(splits, *refs):
    scal, frames, mod, d_after, own = refs[:5]
    parts = refs[5 : 4 + splits]
    out = refs[4 + splits]
    rows = frames.shape[0]
    value = own[...]
    for part in parts:
        value = value + part[0 : own.shape[0], :].astype(F32)
    normed, inverse = normalize(frames[...].astype(F32))
    scale = 1.0 + per_row(mod, 1, own_clip(scal, rows, splits))
    out[...] = d_after[...] + normalize_back(value * scale, normed, inverse)


def bias_table(n_dp):
    table = np.full((8, n_dp * WIN), -1, np.int32)
    for d in range(n_dp):
        for i in range(48):
            part, h, r = i // 24, i % 24 // 8, i % 8
            spot = d * 8 + r
            start = (h * HD if h < 2 else 3 * WIN) if part == 0 else (2 + h / 2) * WIN
            table[0, d * WIN + i] = (start if part == 0 or h < 2 else 4 * WIN) + spot
        for i in range(96):
            table[1, d * WIN + i] = i // 32 * 256 + d * 32 + i % 32
            table[2, d * WIN + i] = d * 96 + i
    return table


MEMORY = {"v": pltpu.VMEM, "s": pltpu.SMEM, "a": pl.ANY}


def call(body, inputs, outs, scratch, flops, name):
    moved = sum(a.size * a.dtype.itemsize for _, a in inputs)
    moved += sum(_size(s, t) for _, s, t in outs)
    return pl.pallas_call(
        body,
        out_shape=tuple(jax.ShapeDtypeStruct(s, t) for _, s, t in outs),
        in_specs=[pl.BlockSpec(memory_space=MEMORY[m]) for m, _ in inputs],
        out_specs=tuple(pl.BlockSpec(memory_space=MEMORY[m]) for m, _, _ in outs),
        scratch_shapes=scratch,
        compiler_params=pltpu.CompilerParams(vmem_limit_bytes=58 * 1024 * 1024),
        cost_estimate=pl.CostEstimate(flops=int(flops), bytes_accessed=int(moved), transcendentals=0),
        name=name,
    )(*[a for _, a in inputs])


def _size(shape, kind):
    total = jnp.dtype(kind).itemsize
    for s in shape:
        total *= s
    return total


class Ring:
    def __init__(self):
        self.n_dp = lax.axis_size("dp")
        self.splits = lax.axis_size("head")
        self.square = self.n_dp == 8
        if self.square:
            self.core = [(i, i ^ 1) for i in range(8)]
            self.first = [(i, i ^ (4 if i & 1 else 2)) for i in range(8)]
            self.second = [(i, i ^ (2 if i & 1 else 4)) for i in range(8)]

    def offsets(self):
        if not self.square:
            return [jnp.int32(0)]
        me = lax.axis_index("dp")
        rows = D // 8

        def kept(d):
            odd = d & 1
            return [d, d ^ (2 + 2 * odd), d ^ (4 - 2 * odd), d ^ 6]

        return [place * rows for place in kept(me) + kept(me ^ 1)]

    def z_pieces(self, value, far=None):
        n = self.splits
        return [value] + [
            lax.ppermute(value, "head", [(s, (s + k) % n) for s in range(n)])
            for k in (range(1, n) if far is None else far)
        ]

    def z_back(self, parts):
        n = self.splits
        return [
            lax.ppermute(parts[k - 1], "head", [(s, (s - k) % n) for s in range(n)])
            for k in range(1, n)
        ]

    def across(self, value, how):
        return lax.ppermute(value, "dp", how)

    def z_move(self, value, k):
        n = self.splits
        return lax.ppermute(value, "head", [(s, (s - k) % n) for s in range(n)])


class GradSum:
    def __init__(self, ring, grads):
        self.ring, self.grads = ring, list(grads)
        self.moved = []
        self.arrived = []
        if not ring.square:
            self.whole = lax.psum_scatter(grads[0][0], "dp", scatter_dimension=1, tiled=True)

    def across(self, value, how):
        if self.ring.square:
            self.moved.append(self.ring.across(value.astype(BF16), how))

    def block(self, i):
        value = self.grads[0][i].astype(F32) + self.moved[0][i].astype(F32)
        if len(self.moved) > 1:
            value = value + self.moved[1][i].astype(F32)
        return value

    def core(self):
        if self.ring.square:
            self.across(self.grads[1], self.ring.core)

    def second(self):
        if self.ring.square:
            self.across(self.block(slice(2, 4)), self.ring.second)

    def first(self):
        if self.ring.square:
            self.across(self.block(1), self.ring.first)

    def own(self, i):
        if not self.ring.square:
            return self.whole[i].astype(F32)
        value = self.grads[0][0, i].astype(F32) + self.moved[2][i].astype(F32)
        return value + self.moved[0][0, i].astype(F32) + self.moved[1][0, i].astype(F32)

    def shard(self, start):
        count = self.grads[0].shape[1]
        for i in range(count):
            k = i if start == 1 else start + i
            if k > 0:
                self.arrived.append(self.ring.z_move(self.own(i).astype(BF16), k))


def join_second(low, high):
    if not low.ring.square:
        return []
    part = slice(2, 4)
    both = jnp.concatenate([low.block(part), high.block(part)], axis=1)
    return [low.ring.across(both.astype(BF16), low.ring.second)]


def join_first(low, high):
    if not low.ring.square:
        return []
    both = jnp.concatenate([low.block(1), high.block(1)], axis=0)
    return [low.ring.across(both.astype(BF16), low.ring.first)]


def join_take(low, high, moved):
    count = low.grads[0].shape[1]
    for value in moved:
        low.moved.append(value[..., :count, :, :])
        high.moved.append(value[..., count:, :, :])


def join_shards(pairs):
    ring = pairs[0][0].ring
    half = ring.splits // 2
    return [
        ring.z_move(
            jnp.concatenate([pair[k // half].own(k % half) for pair in pairs], axis=1).astype(BF16),
            k,
        )
        for k in range(1, ring.splits)
    ]


class Gather:
    def __init__(self, ring, mine):
        self.ring = ring
        if ring.square:
            self.kept, self.other = [mine], []
        else:
            self.kept, self.other = [lax.all_gather(mine, "dp", axis=1, tiled=True)], []

    def sides(self):
        if self.ring.square:
            self.kept.append(self.ring.across(self.kept[0], self.ring.first))
            self.kept.append(self.ring.across(self.kept[0], self.ring.second))

    def corner(self):
        if self.ring.square:
            self.kept.append(self.ring.across(self.kept[1], self.ring.second))

    def core(self, *which):
        if self.ring.square:
            for i in which:
                self.other.append(self.ring.across(self.kept[i], self.ring.core))

    def pieces(self):
        return self.kept + self.other


def meet(*groups):
    flat = [v for group in groups for v in group]
    flat = list(lax.optimization_barrier(tuple(flat)))
    for group in groups:
        for i in range(len(group)):
            group[i] = flat.pop(0)


def to_layout(q, k, v, o):
    return jnp.concatenate(
        [
            q[:, :WIN],
            k[:, :WIN],
            v[:, :WIN],
            q[:, WIN:],
            k[:, WIN:],
            v[:, WIN:],
            o[:, WIN:],
            o[:, :WIN],
        ],
        axis=1,
    )


def from_layout(value):
    def pick(pair, third):
        return jnp.concatenate(
            [value[:, pair : pair + WIN], value[:, third : third + HD]], axis=1
        )

    return pick(0, 3 * WIN), pick(WIN, 3 * WIN + HD), pick(2 * WIN, 4 * WIN), pick(
        5 * WIN, 4 * WIN + HD
    )


def mod_gradients(ring, sums, clips):
    part = jnp.concatenate(sums, axis=1)[:clips]
    got = lax.all_to_all(
        jnp.broadcast_to(part[None], (ring.splits,) + part.shape), "head", 0, 0, tiled=True
    )
    low = jnp.sum(got, axis=0).astype(BF16)
    return lax.all_to_all(
        jnp.broadcast_to(low[None], (ring.n_dp,) + low.shape), "dp", 0, 0, tiled=True
    ).reshape(ring.n_dp * clips, -1)


def on_device(
    frames_in,
    step_embed,
    text_feats,
    clip_frames,
    text_tokens,
    out_grad,
    ada_weight,
    ada_bias,
    qkv_weight,
    qv_bias,
    attn_out_weight,
    attn_out_bias,
    cross_gain,
    cross_q_weight,
    cross_q_bias,
    cross_kv_weight,
    cross_v_bias,
    cross_out_weight,
    cross_out_bias,
    mlp_in_weight,
    mlp_in_bias,
    mlp_out_weight,
    mlp_out_bias,
):
    both = ("dp", "head")
    ring = Ring()
    n_dp, splits = ring.n_dp, ring.splits
    z_index = lax.axis_index("head")
    rows = frames_in.shape[0]
    count = rows * splits
    text_count = text_feats.shape[0]
    clips = clip_frames.shape[1]
    width = D // splits
    shard_rows = D // n_dp
    ends = jnp.cumsum(clip_frames[0])
    offs = ring.offsets()
    n_p = len(offs)
    scal = jnp.stack(
        [z_index, ends[0], ends[1], text_tokens[0, 0], text_tokens[0, 1], text_tokens[0, 2]]
        + [jnp.int32(0)] * 2
        + [o.astype(jnp.int32) for o in offs]
        + [jnp.int32(0)] * (S_LEN - S_OFF - n_p)
    ).astype(jnp.int32)

    shard_self = to_layout(
        qkv_weight[:, 0], qkv_weight[:, 1], qkv_weight[:, 2], attn_out_weight.T
    )
    shard_cross = to_layout(
        cross_q_weight, cross_kv_weight[:, 0], cross_kv_weight[:, 1], cross_out_weight.T
    )

    biases = [
        ada_bias,
        qv_bias.reshape(-1),
        attn_out_bias,
        cross_gain,
        cross_q_bias.reshape(-1),
        cross_v_bias.reshape(-1),
        cross_out_bias,
        mlp_in_bias.reshape(-1),
        mlp_out_bias,
    ]
    flat = jnp.concatenate(biases)
    cols = step_embed.reshape(clips, n_dp, shard_rows).transpose(1, 0, 2).reshape(n_dp, -1)
    sent = jnp.concatenate(
        [
            jnp.broadcast_to(flat[None, None], (n_dp, splits, flat.shape[0])),
            jnp.broadcast_to(cols[:, None], (n_dp, splits, cols.shape[1])),
        ],
        axis=2,
    ).reshape(n_dp * splits, -1)
    got = lax.all_to_all(sent, both, 0, 0, tiled=True)
    attn_shards = ring.z_pieces(jnp.concatenate([shard_self, shard_cross], axis=1))
    mlp_shard = jnp.concatenate([mlp_in_weight, mlp_out_weight.T], axis=1)
    held = [got]
    meet(held, attn_shards)
    got = held[0].reshape(n_dp, splits, -1)
    step_cols = got[:, 0, flat.shape[0] :].reshape(n_dp * clips, shard_rows).astype(F32)
    silu_cols = jax.nn.silu(step_cols).astype(BF16)
    spots = []
    place = 0
    for b in biases:
        spots.append(got[:, :, place : place + b.shape[0]].astype(F32))
        place += b.shape[0]

    def over_dp(value):
        return value[:, 0].reshape(1, -1)

    def by_head(value, lead=1):
        n = value.shape[2] // (lead * 3)
        v = value.reshape(n_dp, splits, lead, 3, n).transpose(1, 2, 3, 0, 4)
        return v.reshape(splits, lead, 3 * n_dp * n)

    all_ada_bias = over_dp(spots[0])
    qv = by_head(spots[1], 2)
    nothing = jnp.zeros((splits, width), F32)
    bias_self = to_layout(qv[:, 0], nothing, qv[:, 1], nothing)[:, None]
    all_attn_bias = over_dp(spots[2])
    all_gain = over_dp(spots[3])
    bias_cross = to_layout(
        by_head(spots[4])[:, 0], nothing, by_head(spots[5])[:, 0], nothing
    )[:, None]
    all_cross_bias = over_dp(spots[6])
    all_in_bias = by_head(spots[7])
    all_out_bias = over_dp(spots[8])

    mod_part = jnp.dot(silu_cols, ada_weight, preferred_element_type=F32)
    mod_got = lax.all_to_all(mod_part.reshape(n_dp, clips, -1), "dp", 0, 0, tiled=True)

    half = splits // 2
    attn_gather = Gather(ring, jnp.stack(attn_shards))
    attn_gather.sides()
    frame_blocks = ring.z_pieces(frames_in)
    held = [mod_got, mlp_shard]
    meet(held, attn_gather.kept)
    mlp_shard = held[1]
    mod = jnp.sum(held[0], axis=0) + all_ada_bias
    attn_gather.corner()
    attn_gather.core(0, 1, 2, 3)
    mlp_shards = ring.z_pieces(mlp_shard, range(1, half))
    mlp_gathers = [Gather(ring, jnp.stack(mlp_shards))]
    mlp_gathers[0].sides()
    mlp_gathers[0].core(0)
    mlp_late = ring.z_pieces(mlp_shard, range(half, splits))[1:]

    def dma(n):
        return pltpu.SemaphoreType.DMA(n)

    def any_of(arrays):
        return [("a", a) for a in arrays]

    def vmem_of(arrays):
        return [("v", a) for a in arrays]

    piece_rows = D // n_p
    kept_out = [("a", (max(n_p // 2, 1), splits, piece_rows, D), BF16)] * (2 if n_p > 1 else 1)
    n_o = len(kept_out)
    shard_type = pltpu.VMEM((splits, D, D), BF16)

    results = list(call(
        partial(self_forward, n_p, splits),
        [("s", scal)]
        + vmem_of(frame_blocks)
        + vmem_of([mod, bias_self, all_attn_bias])
        + any_of(attn_gather.pieces()),
        [
            ("v", (D, count), BF16),
            ("v", (splits, count, 4 * WIN), BF16),
            ("v", (splits, rows, 2 * WIN), BF16),
            ("v", (splits, rows, 2 * WIN), BF16),
            ("v", (splits, 8, rows), F32),
            ("v", (rows, D), F32),
            ("v", (rows, D), F32),
        ],
        [
            pltpu.VMEM((count, D), BF16),
            shard_type,
            pltpu.VMEM((count, rows), F32),
            pltpu.VMEM((count, rows), F32),
            pltpu.VMEM((count, rows), BF16),
            dma((n_p,)),
        ],
        22 * US,
        "self_forward",
    ))
    meet(
        results, mlp_gathers[0].kept, mlp_gathers[0].other, mlp_late, attn_gather.kept, attn_gather.other
    )
    hidden_one, self_kv, self_q, self_att, self_lse, attn_branch, after_self = results
    mlp_gathers[0].corner()
    mlp_gathers[0].core(1, 2)
    mlp_gathers.append(Gather(ring, jnp.stack(mlp_late)))
    mlp_gathers[1].sides()

    results = list(call(
        partial(cross_forward, n_p, splits),
        [("s", scal)]
        + vmem_of([after_self, text_feats, all_gain, bias_cross, all_cross_bias])
        + any_of(attn_gather.pieces()),
        [
            ("v", (D, rows), BF16),
            ("v", (D, text_count), BF16),
            ("v", (splits, text_count, 4 * WIN), BF16),
            ("v", (splits, rows, 2 * WIN), BF16),
            ("v", (splits, rows, 2 * WIN), BF16),
            ("v", (splits, 8, rows), F32),
            ("v", (rows, D), F32),
        ],
        [
            shard_type,
            pltpu.VMEM((text_count, rows), F32),
            pltpu.VMEM((text_count, rows), F32),
            pltpu.VMEM((text_count, rows), BF16),
            dma((n_p,)),
        ],
        17 * US,
        "cross_forward",
    ))
    meet(results, mlp_gathers[0].kept, mlp_gathers[0].other, mlp_gathers[1].kept)
    hidden_two_t, text_t, cross_kv, cross_q, cross_att, cross_lse, after_cross = results
    mlp_gathers[0].core(3)
    mlp_gathers[1].corner()
    mlp_gathers[1].core(0, 1, 2)

    kept_half = [(m, (shape[0], half) + shape[2:], kind) for m, shape, kind in kept_out]
    kept_wide = [(m, shape[:3] + (2 * D,), kind) for m, shape, kind in kept_half]
    half_type = pltpu.VMEM((half, D, D), BF16)

    def back_scratch(keys):
        return [
            half_type,
            half_type,
            pltpu.VMEM((keys, rows), F32),
            pltpu.VMEM((3, keys, rows), BF16),
            pltpu.VMEM((3, keys, rows), BF16),
            pltpu.VMEM((keys, 4 * WIN), BF16),
            dma((n_p,)),
            dma((n_p, half)),
        ]

    bias_type = [("v", (splits, 1, D), F32)]
    mlp_args = [after_cross, out_grad, mod, all_in_bias, all_out_bias]
    mlp_scratch = [
        pltpu.VMEM((half, D, 2 * D), BF16),
        pltpu.VMEM((half, D, 2 * D), BF16),
        dma((n_p,)),
        dma((n_p, half)),
    ]
    results = call(
        partial(feed_forward, n_p, splits, 0, half),
        [("s", scal)] + vmem_of(mlp_args) + any_of(mlp_gathers[0].pieces()),
        kept_wide + bias_type + [("v", (rows, D), F32)] * 2,
        mlp_scratch,
        9 * US,
        "feed_forward_first",
    )
    results = list(results)
    meet(results, mlp_gathers[1].kept, mlp_gathers[1].other)
    mlp_gathers[1].core(3)
    sum_mlp = [GradSum(ring, results[:n_o])]
    in_bias_grad, mlp_state, mlp_back = results[n_o:]
    sum_mlp[0].core()
    results = call(
        partial(feed_forward, n_p, splits, half, splits),
        [("s", scal)]
        + vmem_of(mlp_args)
        + any_of(mlp_gathers[1].pieces())
        + vmem_of([mlp_state, mlp_back, in_bias_grad]),
        kept_wide
        + bias_type
        + [
            ("v", (rows, D), BF16),
            ("v", (rows, D), F32),
            ("v", (1, D), F32),
            ("v", (8, 3 * D), F32),
        ],
        [pltpu.VMEM((rows, D), F32), pltpu.VMEM((rows, D), F32)] + mlp_scratch,
        10 * US,
        "feed_forward_last",
    )
    results = list(results)
    meet(results, sum_mlp[0].moved)
    sum_mlp.append(GradSum(ring, results[:n_o]))
    in_bias_grad, layer_out, d_after_cross, out_bias_grad, sums_two = results[n_o:]
    sum_mlp[0].second()
    sum_mlp[1].core()
    cross_args = [
        d_after_cross,
        after_self,
        hidden_two_t,
        text_t,
        all_gain,
        mod,
        attn_branch,
        cross_kv,
        cross_q,
        cross_att,
        cross_lse,
    ]
    cross_state = [("v", (rows, D), F32), ("v", (text_count, D), F32)]
    results = call(
        partial(cross_backward, n_p, splits, 0, half),
        [("s", scal)] + vmem_of(cross_args) + any_of(attn_gather.pieces()),
        kept_half + bias_type + cross_state,
        back_scratch(text_count),
        14 * US,
        "cross_backward_first",
    )
    results = list(results)
    meet(results, sum_mlp[0].moved, sum_mlp[1].moved)
    sum_cross = [GradSum(ring, results[:n_o])]
    cross_bias_grad, cross_back, text_back = results[n_o:]
    sum_mlp[0].first()
    sum_mlp[1].second()
    sum_cross[0].core()
    results = call(
        partial(cross_backward, n_p, splits, half, splits),
        [("s", scal)]
        + vmem_of(cross_args)
        + any_of(attn_gather.pieces())
        + vmem_of([cross_back, text_back, cross_bias_grad]),
        kept_half
        + bias_type
        + [
            ("v", (rows, D), F32),
            ("v", (rows, D), BF16),
            ("v", (text_count, D), BF16),
            ("v", (8, D), F32),
            ("v", (8, D), F32),
        ],
        [pltpu.VMEM((rows, D), F32), pltpu.VMEM((text_count, D), F32)] + back_scratch(text_count),
        15 * US,
        "cross_backward_last",
    )
    results = list(results)
    meet(results, sum_mlp[0].moved, sum_mlp[1].moved, sum_cross[0].moved)
    sum_cross.append(GradSum(ring, results[:n_o]))
    cross_bias_grad, d_after_self, d_attn, text_out, cross_rows, gate_sums = results[n_o:]
    sum_mlp[0].shard(1)
    sum_mlp[1].first()
    sum_cross[0].second()
    sum_cross[1].core()
    text_got = lax.all_to_all(
        text_out.reshape(splits, text_count // splits, D), "head", 0, 0, tiled=True
    )
    self_args = [d_attn, hidden_one, self_kv, self_q, self_att, self_lse]
    results = call(
        partial(self_backward, n_p, splits, 0, half, False),
        [("s", scal)] + vmem_of(frame_blocks) + vmem_of(self_args) + any_of(attn_gather.pieces()),
        kept_half + bias_type + [("v", (count, D), F32)],
        back_scratch(count),
        17 * US,
        "self_backward_first",
    )
    results = list(results)
    meet(
        results,
        sum_mlp[1].moved,
        sum_cross[0].moved,
        sum_cross[1].moved,
    )
    sum_self = [GradSum(ring, results[:n_o])]
    self_bias_grad, self_back = results[n_o:]
    sum_mlp[1].shard(2)
    sum_cross[1].second()
    sum_self[0].core()
    small_args, small_outs, small_scratch, small_count = [], [], [], 0
    if ring.square:
        small_count = 32
        small_args = [jnp.asarray(bias_table(n_dp)), cross_bias_grad, in_bias_grad]
        small_args += [cross_rows, out_bias_grad, gate_sums, sums_two]
        small_outs = [("v", (small_count, D), F32)]
        small_scratch = [pltpu.VMEM((splits, small_count, D), F32)]
    results = call(
        partial(self_backward, n_p, splits, half, splits, ring.square),
        [("s", scal)]
        + vmem_of(frame_blocks)
        + vmem_of(self_args)
        + any_of(attn_gather.pieces())
        + vmem_of([self_back, self_bias_grad] + small_args),
        kept_half
        + bias_type
        + [("v", (rows, D), F32)]
        + [("v", (rows + small_count, D), BF16)] * (splits - 1)
        + [("v", (8, D), F32), ("v", (8, 2 * D), F32)]
        + small_outs,
        small_scratch + [pltpu.VMEM((count, D), F32)] + back_scratch(count),
        18 * US,
        "self_backward_last",
    )
    results = list(results)
    held = [in_bias_grad, out_bias_grad, cross_bias_grad, cross_rows, gate_sums, sums_two]
    held.append(text_got)
    meet(
        results,
        held,
        sum_mlp[0].arrived,
        sum_mlp[1].arrived,
        sum_cross[0].moved,
        sum_cross[1].moved,
        sum_self[0].moved,
    )
    sum_self.append(GradSum(ring, results[:n_o]))
    self_bias_grad, own_part = results[n_o : n_o + 2]
    parts = results[n_o + 2 : n_o + 1 + splits]
    self_rows, sums_one = results[n_o + 1 + splits : n_o + 3 + splits]
    sum_self[1].core()
    near_cross = join_first(*sum_cross)
    arrived = ring.z_back(parts)
    in_bias_grad, out_bias_grad, cross_bias_grad, cross_rows, gate_sums, sums_two, text_got = held
    far = join_second(*sum_self)
    early, late = arrived[:1], arrived[1:]
    meet(far, near_cross, early)
    join_take(*sum_self, far)
    join_take(*sum_cross, near_cross)
    near = join_first(*sum_self)
    meet(late, near)
    arrived = early + late
    join_take(*sum_self, near)
    last = join_shards([sum_cross, sum_self])
    if ring.square:
        small = results[-1] + sum(part[rows:].astype(F32) for part in arrived)
        mod_low = small[: 6 * clips].astype(BF16).astype(F32)
        sent = jnp.concatenate(
            [
                jnp.broadcast_to(mod_low[None], (n_dp,) + mod_low.shape),
                small[6 * clips : 6 * clips + n_dp, None],
            ],
            axis=1,
        )
        held = [lax.all_to_all(sent, "dp", 0, 0, tiled=True)]
    if ring.square:
        mod_all = held[0][:, : 6 * clips].reshape(n_dp * clips, -1).astype(BF16)
        bias_sum = jnp.sum(held[0][:, 6 * clips], axis=0)
        places = [0, 24, 2 * WIN, 4 * WIN, 48, 72, 3 * WIN, WIN, 5 * WIN]
    else:
        mod_all = mod_gradients(ring, [sums_one, gate_sums, sums_two], clips)
    step_part = lax.dot_general(
        mod_all, ada_weight, (((1,), (1,)), ((), ())), preferred_element_type=F32
    )
    (frames_grad,) = call(
        partial(finish, splits),
        [("s", scal)] + vmem_of([frames_in, mod, d_after_self, own_part]) + vmem_of(arrived),
        [("v", (rows, D), F32)],
        [],
        3 * US,
        "finish",
    )
    text_grad = jnp.sum(text_got.astype(F32), axis=0)

    grad_ada = lax.dot_general(
        silu_cols, mod_all, (((0,), (0,)), ((), ())), preferred_element_type=F32
    )
    dp_index = lax.axis_index("dp")
    bias_width = ada_bias.shape[0]
    grad_ada_bias = jnp.sum(
        lax.dynamic_slice_in_dim(mod_all, dp_index * bias_width, bias_width, 1).astype(F32), axis=0
    )
    step_got = lax.all_to_all(step_part.reshape(n_dp, clips, shard_rows), "dp", 0, 0, tiled=True)
    step_got = [step_got]
    meet(last, step_got)
    (step_got,) = step_got
    total_cross, total_self = (
        pair[0].own(0) + sum(part[:, i * D : (i + 1) * D].astype(F32) for part in last)
        for i, pair in enumerate((sum_cross, sum_self))
    )
    step_value = step_embed.astype(F32)
    _, silu_pull = jax.vjp(jax.nn.silu, step_value)
    step_grad = silu_pull(step_got.transpose(1, 0, 2).reshape(clips, D))[0]

    def spread(value):
        v = value.reshape(n_dp, 1, D // n_dp)
        return jnp.broadcast_to(v, (n_dp, splits, D // n_dp))

    def heads_out(value):
        n = value.shape[1] // (3 * n_dp)
        return value.reshape(splits, 3, n_dp, n).transpose(2, 0, 1, 3).reshape(n_dp, splits, 3 * n)

    sq, _, sv, _ = from_layout(self_bias_grad[:, 0])
    cq, _, cv, _ = from_layout(cross_bias_grad[:, 0])
    entries = [
        heads_out(sq),
        heads_out(sv),
        spread(self_rows[0]),
        spread(cross_rows[1]),
        heads_out(cq),
        heads_out(cv),
        spread(cross_rows[0]),
        heads_out(in_bias_grad[:, 0]),
        spread(out_bias_grad[0]),
    ]
    if not ring.square:
        packed = jnp.concatenate(entries, axis=2)
        places = [sum(e.shape[2] for e in entries[:i]) for i in range(len(entries))]
        bias_sum = jnp.sum(
            lax.all_to_all(packed.reshape(n_dp * splits, -1), both, 0, 0, tiled=True), axis=0
        )
    bias_out = [bias_sum[p : p + e.shape[2]] for p, e in zip(places, entries)]

    total_mlp = sum_mlp[0].own(0) + sum(
        part.astype(F32) for part in sum_mlp[0].arrived + sum_mlp[1].arrived
    )
    gq, gk, gv, go = from_layout(total_self)
    hq, hk, hv, ho = from_layout(total_cross)
    return (
        layer_out,
        frames_grad,
        step_grad,
        text_grad,
        grad_ada,
        grad_ada_bias,
        jnp.stack([gq, gk, gv], axis=1),
        jnp.stack([bias_out[0], bias_out[1]]).reshape(qv_bias.shape),
        go.T,
        bias_out[2],
        bias_out[3],
        hq,
        bias_out[4].reshape(cross_q_bias.shape),
        jnp.stack([hk, hv], axis=1),
        bias_out[5].reshape(cross_v_bias.shape),
        ho.T,
        bias_out[6],
        total_mlp[:, :D],
        bias_out[7].reshape(mlp_in_bias.shape),
        total_mlp[:, D:].T,
        bias_out[8],
    )


def solution(mesh):
    rows_all, by_dp = P(("dp", "head"), None), P("dp", None)
    head_dp, dp_head = P("head", "dp"), P("dp", "head")
    dp_three, vector = P("dp", None, "head"), P("dp")
    params = (
        by_dp,
        vector,
        dp_three,
        P(None, "head", "dp"),
        head_dp,
        vector,
        vector,
        dp_head,
        head_dp,
        dp_three,
        head_dp,
        head_dp,
        vector,
        dp_head,
        head_dp,
        head_dp,
        vector,
    )
    return jax.shard_map(
        on_device,
        mesh=mesh,
        in_specs=(rows_all, by_dp, by_dp, by_dp, by_dp, rows_all) + params,
        out_specs=(rows_all, rows_all, by_dp, rows_all) + params,
        check_vma=False,
    )
```

```python
from functools import partial

import jax
import jax.numpy as jnp
import numpy as np
from jax import lax
from jax.experimental import pallas as pl
from jax.experimental.pallas import tpu as pltpu
from jax.sharding import PartitionSpec as P

D = 768
HD = 64
TXT = 256
WIN = 128
EPS = 1e-06
NEG = -1e30
F32 = jnp.float32
BF16 = jnp.bfloat16
HIGH = lax.Precision.HIGHEST
S_Z, S_END, S_TOK, S_OFF = 0, 1, 3, 8
S_LEN = 16
US = 1.15e9


def nn(a, b):
    return lax.dot_general(a, b, (((1,), (0,)), ((), ())), preferred_element_type=F32)


def nt(a, b):
    return lax.dot_general(a, b, (((1,), (1,)), ((), ())), preferred_element_type=F32)


def tn(a, b):
    return lax.dot_general(a, b, (((0,), (0,)), ((), ())), preferred_element_type=F32)


def normalize(v):
    centered = v - jnp.mean(v, axis=-1, keepdims=True)
    inverse = lax.rsqrt(jnp.mean(centered * centered, axis=-1, keepdims=True) + EPS)
    return centered * inverse, inverse


def normalize_back(u, normed, inverse):
    return inverse * (
        u
        - jnp.mean(u, axis=-1, keepdims=True)
        - normed * jnp.mean(u * normed, axis=-1, keepdims=True)
    )


def clip_of(position, scal):
    return (position >= scal[S_END]).astype(jnp.int32) + (position >= scal[S_END + 1]).astype(
        jnp.int32
    )


def frame_position(index, block, rows, splits, scal):
    return lax.rem(scal[S_Z] - block + splits, splits) * rows + index


def per_row(mod_ref, part, clip):
    cols = slice(part * D, (part + 1) * D)
    first, second, third = (mod_ref[c : c + 1, cols] for c in range(3))
    return jnp.where(clip == 0, first, jnp.where(clip == 1, second, third))


def clip_sums(clip_row, value):
    which = lax.broadcasted_iota(jnp.int32, (8, clip_row.shape[1]), 0)
    choose = (which == clip_row).astype(F32)
    return lax.dot_general(
        choose, value, (((1,), (0,)), ((), ())), precision=HIGH, preferred_element_type=F32
    )


def lanes(rows, low):
    lane = lax.broadcasted_iota(jnp.int32, (rows, WIN), 1)
    return lane < HD if low else lane >= HD


def keep(value, low):
    return jnp.where(lanes(value.shape[0], low), value, jnp.zeros_like(value))


def swap(value):
    return pltpu.roll(value, HD, 1)


def load_start(groups, buffer, sems, scal, low=0, col=0):
    width = buffer.shape[2]

    def place(j, rows):
        return pl.ds(pl.multiple_of(scal[S_OFF + j], 32), rows)

    for z in range(buffer.shape[0]):
        for pieces, start in groups:
            at = low + z - start
            if 0 <= at < pieces[0].shape[0]:
                for j, piece in enumerate(pieces):
                    pltpu.make_async_copy(
                        piece.at[at, :, col : col + width],
                        buffer.at[z, place(j, piece.shape[1]), :],
                        sems.at[j, z],
                    ).start()

    def wait(z):
        for j, piece in enumerate(groups[0][0]):
            here = buffer.at[z, place(j, piece.shape[1]), :]
            pltpu.make_async_copy(here, here, sems.at[j, z]).wait()

    return wait


def own_and_others(pieces):
    half = len(pieces) // 2
    return [(pieces[:half], 0), (pieces[half:], 1)]


def store_copies(buffer, z, outs, sems, scal, col=0, first=0):
    copies = []
    j = 0
    for out in outs:
        for i in range(out.shape[0]):
            rows = out.shape[2]
            start = pl.multiple_of(scal[S_OFF + j], 32)
            copies.append(
                pltpu.make_async_copy(
                    buffer.at[z, pl.ds(start, rows), col : col + out.shape[3]],
                    out.at[i, z],
                    sems.at[first + j, z],
                )
            )
            j += 1
    return copies


def attend(queries, kv, mask, scores, probs, count):
    rows = queries.shape[0]
    step = 256
    outs = []
    lane = lax.broadcasted_iota(jnp.int32, (rows, WIN), 1)
    totals = jnp.zeros((rows, WIN), F32)
    for h in range(3):
        if h < 2:
            query = keep(queries[:, :WIN], h == 0)
            kcol, vcol = 0, 1
        else:
            query = queries[:, WIN:]
            kcol, vcol = 2, 3
        top = None
        for lo in range(0, count, step):
            part = nt(query, kv(lo, lo + step, kcol)) + mask[:, lo : lo + step]
            scores[:, lo : lo + step] = part
            top = part if top is None else jnp.maximum(top, part)
        peak = jnp.max(top, axis=1, keepdims=True)
        wide = jnp.zeros((rows, step), F32)
        for lo in range(0, count, step):
            part = jnp.exp(scores[:, lo : lo + step] - peak)
            wide = wide + part
            probs[:, lo : lo + step] = part.astype(BF16)
        total = jnp.sum(wide, axis=1, keepdims=True)
        outs.append(nn(probs[:, 0:count], kv(0, count, vcol)) * (1.0 / total))
        totals = jnp.where(lane == h, peak + jnp.log(total), totals)
    pair = jnp.where(lane < HD, outs[0], outs[1])
    attended = jnp.concatenate([keep(swap(outs[2]), False), pair], axis=1)
    return attended.astype(BF16), totals.T[0:8, :]


def attend_back(queries, kv, attended, out_grad, mask, totals, probs, dscore, count, put):
    rows = queries.shape[0]
    step = 256
    wide = out_grad.astype(F32)
    row = lax.broadcasted_iota(jnp.int32, (8, 2 * WIN), 0)
    part = lax.broadcasted_iota(jnp.int32, (8, 2 * WIN), 1) // HD
    choose = ((part == row + 2) & (row < 2)) | ((part == 1) & (row == 2))
    deltas = lax.dot_general(
        choose.astype(F32),
        wide * attended.astype(F32),
        (((1,), (1,)), ((), ())),
        precision=HIGH,
        preferred_element_type=F32,
    )
    second = keep(swap(wide[:, :WIN]), True).astype(BF16)
    query_parts = []
    heads = []
    key_t = [kv(0, count, col).astype(F32).T.astype(BF16) for col in (0, 2)]
    for h in range(3):
        if h < 2:
            query = keep(queries[:, :WIN], h == 0)
            given = keep(out_grad[:, WIN:], h == 0)
            kcol, vcol = 0, 1
        else:
            query, given = queries[:, WIN:], second
            kcol, vcol = 2, 3
        heads.append((query, given))
        total, delta = totals[h], deltas[h : h + 1, :]
        for lo in range(0, count, step):
            hi = lo + step
            weights = jnp.exp(nt(kv(lo, hi, kcol), query) + mask[lo:hi, :] - total)
            probs[h, lo:hi, :] = weights.astype(BF16)
            weight_grad = nt(kv(lo, hi, vcol), given)
            dscore[h, lo:hi, :] = (weights * (weight_grad - delta)).astype(BF16)
        query_parts.append(nn(key_t[h // 2], dscore[h, 0:count, :]))
    for lo in range(0, count, step):
        hi = lo + step
        put(
            lo,
            hi,
            nn(dscore[0, lo:hi, :], heads[0][0]) + nn(dscore[1, lo:hi, :], heads[1][0]),
            nn(probs[0, lo:hi, :], heads[0][1]) + nn(probs[1, lo:hi, :], heads[1][1]),
            nn(dscore[2, lo:hi, :], heads[2][0]),
            nn(probs[2, lo:hi, :], heads[2][1]),
        )
    both = jnp.concatenate(
        [
            query_parts[0][:HD],
            query_parts[1][HD:],
            query_parts[2][HD:],
            jnp.zeros((HD, rows), F32),
        ],
        axis=0,
    )
    both = (both * 0.125).T
    return both[:, :WIN], both[:, WIN:]


def self_mask(scal, mask, rows, splits, forward=False):
    clip = own_clip if forward else own_clip_row
    query = clip(scal, rows, splits)
    for block in range(splits):
        span = slice(block * rows, (block + 1) * rows)
        key = (own_clip_row if forward else own_clip)(scal, rows, splits, block)
        value = jnp.where(key == query, 0.0, NEG)
        if forward:
            mask[:, span] = value
        else:
            mask[span, :] = value


def cross_mask(scal, mask, rows, splits, clips, forward=False):
    query = (own_clip if forward else own_clip_row)(scal, rows, splits)
    shape = (1, TXT) if forward else (TXT, 1)
    slot = lax.broadcasted_iota(jnp.int32, shape, 1 if forward else 0)
    for c in range(clips):
        span = slice(c * TXT, (c + 1) * TXT)
        value = jnp.where((query == c) & (slot < scal[S_TOK + c]), 0.0, NEG)
        if forward:
            mask[:, span] = value
        else:
            mask[span, :] = value


def own_clip(scal, rows, splits, block=0):
    return clip_of(
        frame_position(lax.broadcasted_iota(jnp.int32, (rows, 1), 0), block, rows, splits, scal),
        scal,
    )


def own_clip_row(scal, rows, splits, block=0):
    return clip_of(
        frame_position(lax.broadcasted_iota(jnp.int32, (1, rows), 1), block, rows, splits, scal),
        scal,
    )


def shard_index(scal, z, splits):
    return lax.rem(scal[S_Z] - z + splits, splits)


def self_forward(n_p, splits, *refs):
    n_w = 2 * n_p
    scal = refs[0]
    frames = refs[1 : 1 + splits]
    mod, bias, out_bias = refs[1 + splits : 4 + splits]
    pieces = refs[4 + splits : 4 + splits + n_w]
    hidden_t, kv_out, q_out, att_out, lse, branch_out, after = refs[
        4 + splits + n_w : 11 + splits + n_w
    ]
    hidden, kv_buf, weights, mask, scores, probs, sems, kv_sems = refs[11 + splits + n_w :]
    rows = frames[0].shape[0]
    count = rows * splits
    load_wait = load_start(own_and_others(pieces), weights, sems, scal)
    self_mask(scal, mask, rows, splits, True)
    for block in range(splits):
        clip = own_clip(scal, rows, splits, block)
        normed, _ = normalize(frames[block][...].astype(F32))
        value = normed * (1.0 + per_row(mod, 1, clip)) + per_row(mod, 0, clip)
        hidden[block * rows : (block + 1) * rows, :] = value.astype(BF16)
        hidden_t[:, block * rows : (block + 1) * rows] = value.T.astype(BF16)
    branch_out[...] = jnp.broadcast_to(out_bias[...], branch_out.shape)

    def one(z, carry):
        load_wait(z)
        bias_row = bias[shard_index(scal, z, splits)]
        for block in range(splits):
            span = slice(block * rows, (block + 1) * rows)
            part = nn(hidden[span, :], weights[z, :, WIN : 5 * WIN]) + bias_row[:, WIN : 5 * WIN]
            kv_buf[z, span, :] = part.astype(BF16)
            if block == 0:
                third = keep(swap(part[:, 2 * WIN : 3 * WIN].astype(BF16).astype(F32)), False)
        pair = nn(hidden[0:rows, :], weights[z, :, 0:WIN]) + bias_row[:, 0:WIN]
        queries = (
            jnp.concatenate([pair.astype(BF16).astype(F32), third], axis=1) * 0.125
        ).astype(BF16)
        q_out[z] = queries
        pltpu.make_async_copy(kv_buf.at[z], kv_out.at[z], kv_sems.at[z]).start()

        def kv(lo, hi, col):
            return kv_buf[z, lo:hi, col * WIN : (col + 1) * WIN]

        attended, totals = attend(queries, kv, mask, scores, probs, count)
        att_out[z] = attended
        lse[z] = totals
        branch_out[...] += nt(attended, weights[z, :, 4 * WIN :])
        return carry

    lax.fori_loop(0, splits, one, 0)
    clip = own_clip(scal, rows, splits)
    after[...] = frames[0][...].astype(F32) + per_row(mod, 2, clip) * branch_out[...]
    for z in range(splits):
        pltpu.make_async_copy(kv_buf.at[z], kv_out.at[z], kv_sems.at[z]).wait()


def cross_forward(n_p, splits, *refs):
    n_w = 2 * n_p
    scal, after_self, text, gain, bias, out_bias = refs[:6]
    pieces = refs[6 : 6 + n_w]
    hidden_t, text_t, kv_out, q_out, att_out, lse, after = refs[6 + n_w : 13 + n_w]
    kv_buf, weights, mask, scores, probs, sems, kv_sems = refs[13 + n_w :]
    rows = after_self.shape[0]
    count = text.shape[0]
    load_wait = load_start(own_and_others(pieces), weights, sems, scal, 0, D)
    cross_mask(scal, mask, rows, splits, count // TXT, True)
    normed, _ = normalize(after_self[...])
    wide = normed * gain[...]
    hidden = wide.astype(BF16)
    hidden_t[...] = wide.T.astype(BF16)
    for lo in range(0, count, 256):
        text_t[:, lo : lo + 256] = text[lo : lo + 256, :].astype(F32).T.astype(BF16)
    after[...] = after_self[...] + out_bias[...]

    def one(z, carry):
        load_wait(z)
        bias_row = bias[shard_index(scal, z, splits)]
        for lo in range(0, count, 256):
            part = nn(text[lo : lo + 256, :], weights[z, :, WIN : 5 * WIN])
            kv_buf[z, lo : lo + 256, :] = (part + bias_row[:, WIN : 5 * WIN]).astype(BF16)
        pair = nn(hidden, weights[z, :, 0:WIN]) + bias_row[:, 0:WIN]
        third = nn(hidden, weights[z, :, 3 * WIN : 4 * WIN]) + bias_row[:, 3 * WIN : 4 * WIN]
        third = keep(swap(third.astype(BF16).astype(F32)), False)
        queries = (
            jnp.concatenate([pair.astype(BF16).astype(F32), third], axis=1) * 0.125
        ).astype(BF16)
        q_out[z] = queries
        pltpu.make_async_copy(kv_buf.at[z], kv_out.at[z], kv_sems.at[z]).start()

        def kv(lo, hi, col):
            return kv_buf[z, lo:hi, col * WIN : (col + 1) * WIN]

        attended, totals = attend(queries, kv, mask, scores, probs, count)
        att_out[z] = attended
        lse[z] = totals
        after[...] += nt(attended, weights[z, :, 4 * WIN :])
        return carry

    lax.fori_loop(0, splits, one, 0)
    for z in range(splits):
        pltpu.make_async_copy(kv_buf.at[z], kv_out.at[z], kv_sems.at[z]).wait()


def feed_forward(n_p, splits, low, high, *refs):
    scal, after_cross, upstream, mod, in_bias, out_bias = refs[:6]
    pieces = refs[6 : 6 + n_p]
    rest = refs[6 + n_p :]
    n_o = 2 if n_p > 1 else 1
    first, last = low == 0, high == splits
    if not first:
        mlp_in, back_in, bias_in = rest[:3]
        rest = rest[3:]
    grads = rest[:n_o]
    in_bias_grad = rest[n_o]
    rest = rest[n_o + 1 :]
    if last:
        layer_out, d_after, out_bias_grad, sums, mlp, back = rest[:6]
        rest = rest[6:]
    else:
        mlp, back = rest[:2]
        rest = rest[2:]
    weights, gbuf, load_sems, store_sems = rest
    rows = after_cross.shape[0]
    load_wait = load_start([(pieces, 0)], weights, load_sems, scal)
    clip = own_clip(scal, rows, splits)
    normed, inverse = normalize(after_cross[...])
    scale = 1.0 + per_row(mod, 4, clip)
    wide = normed * scale + per_row(mod, 3, clip)
    hidden = wide.astype(BF16)
    hidden_t = wide.T.astype(BF16)
    gate = per_row(mod, 5, clip)
    given = upstream[...].astype(F32)
    low_wide = given * gate
    lowered = low_wide.astype(BF16)
    low_t = low_wide.T.astype(BF16)
    if first:
        mlp[...] = jnp.broadcast_to(out_bias[...], mlp.shape)
        back[...] = jnp.zeros_like(back)
        in_bias_grad[...] = jnp.zeros_like(in_bias_grad)
    else:
        mlp[...] = mlp_in[...]
        back[...] = back_in[...]
        in_bias_grad[...] = bias_in[...]

    def one(i, carry):
        load_wait(i)
        place = shard_index(scal, i + low, splits)
        pre = nn(hidden, weights[i, :, 0:D]) + in_bias[place]
        inner = 0.7978845608028654 * (pre + 0.044715 * (pre * pre * pre))
        curve = jnp.tanh(inner)
        half = 0.5 * (1.0 + curve)
        active = (pre * half).astype(BF16)
        slope = half + 0.5 * pre * (1.0 - curve * curve) * 0.7978845608028654 * (
            1.0 + 3.0 * 0.044715 * pre * pre
        )
        pre_grad = (slope * nn(lowered, weights[i, :, D:])).astype(BF16)
        in_bias_grad[place] = jnp.sum(pre_grad.astype(F32), axis=0, keepdims=True)
        mlp[...] += nt(active, weights[i, :, D:])
        back[...] += nt(pre_grad, weights[i, :, 0:D])
        gbuf[i, :, 0:D] = nn(hidden_t, pre_grad).astype(BF16)
        gbuf[i, :, D:] = nn(low_t, active).astype(BF16)
        for copy in store_copies(gbuf, i, grads, store_sems, scal):
            copy.start()
        return carry

    lax.fori_loop(0, high - low, one, 0)
    if last:
        out_bias_grad[...] = jnp.sum(lowered.astype(F32), axis=0, keepdims=True)
        branch = mlp[...]
        layer_out[...] = (after_cross[...] + gate * branch).astype(BF16)
        hidden_grad = back[...]
        d_after[...] = given + normalize_back(hidden_grad * scale, normed, inverse)
        clip_row = own_clip_row(scal, rows, splits)
        sums[:, 0:D] = clip_sums(clip_row, hidden_grad)
        sums[:, D : 2 * D] = clip_sums(clip_row, hidden_grad * normed)
        sums[:, 2 * D :] = clip_sums(clip_row, given * branch)
    for i in range(high - low):
        for copy in store_copies(gbuf, i, grads, store_sems, scal):
            copy.wait()


def cross_backward(n_p, splits, low, high, *refs):
    n_w = 2 * n_p
    scal, d_cross, after_self, hidden_t, text_t, gain, mod, branch, kv_in, q_in, att_in, lse = refs[
        :12
    ]
    pieces = refs[12 : 12 + n_w]
    rest = refs[12 + n_w :]
    first, last = low == 0, high == splits
    if not first:
        back_in, text_in, bias_in = rest[:3]
        rest = rest[3:]
    n_o = 2 if n_p > 1 else 1
    grads = rest[:n_o]
    bias_grad = rest[n_o]
    rest = rest[n_o + 1 :]
    if last:
        d_after, d_attn, text_out, row_grads, sums, back, text_back = rest[:7]
        rest = rest[7:]
    else:
        back, text_back = rest[:2]
        rest = rest[2:]
    weights, gbuf, mask, probs, dscore, key_grad, load_sems, store_sems = rest
    rows = after_self.shape[0]
    count = text_t.shape[1]
    load_wait = load_start(own_and_others(pieces), weights, load_sems, scal, low, D)
    cross_mask(scal, mask, rows, splits, count // TXT)
    given = d_cross[...].astype(BF16)
    given_wide = given.astype(F32)
    given_t = given_wide.T.astype(BF16)
    if first:
        back[...] = jnp.zeros_like(back)
        text_back[...] = jnp.zeros_like(text_back)
        bias_grad[...] = jnp.zeros_like(bias_grad)
    else:
        back[...] = back_in[...]
        text_back[...] = text_in[...]
        bias_grad[...] = bias_in[...]

    def one(i, carry):
        load_wait(i)
        z = i + low
        place = shard_index(scal, z, splits)

        def kv(lo, hi, col):
            return kv_in[z, lo:hi, col * WIN : (col + 1) * WIN]

        def put(lo, hi, k01, v01, k2, v2):
            key_grad[lo:hi, 0:WIN] = k01.astype(BF16)
            key_grad[lo:hi, WIN : 2 * WIN] = v01.astype(BF16)
            key_grad[lo:hi, 2 * WIN : 3 * WIN] = k2.astype(BF16)
            key_grad[lo:hi, 3 * WIN : 4 * WIN] = v2.astype(BF16)

        head_grad = nn(given, weights[i, :, 4 * WIN :]).astype(BF16)
        totals = [lse[z, h : h + 1, :] for h in range(3)]
        pair, third = attend_back(
            q_in[z], kv, att_in[z], head_grad, mask, totals, probs, dscore, count, put
        )
        pair, third = pair.astype(BF16), third.astype(BF16)
        part = nn(text_t[...], key_grad[...])
        out_part = nn(given_t, att_in[z])
        gbuf[i, :, 0:WIN] = nn(hidden_t[...], pair).astype(BF16)
        gbuf[i, :, WIN : 3 * WIN] = part[:, 0 : 2 * WIN].astype(BF16)
        gbuf[i, :, 3 * WIN : 4 * WIN] = (
            part[:, 2 * WIN : 3 * WIN] + nn(hidden_t[...], third)
        ).astype(BF16)
        gbuf[i, :, 4 * WIN : 5 * WIN] = (part[:, 3 * WIN :] + out_part[:, 0:WIN]).astype(BF16)
        gbuf[i, :, 5 * WIN :] = out_part[:, WIN:].astype(BF16)
        for copy in store_copies(gbuf, i, grads, store_sems, scal):
            copy.start()
        back[...] += nt(pair, weights[i, :, 0:WIN]) + nt(third, weights[i, :, 3 * WIN : 4 * WIN])
        for lo in range(0, count, 256):
            text_back[lo : lo + 256, :] += nt(
                key_grad[lo : lo + 256, :], weights[i, :, WIN : 5 * WIN]
            )
        key_sums = jnp.sum(key_grad[...].astype(F32), axis=0, keepdims=True)
        bias_grad[place, :, 0:WIN] = jnp.sum(pair.astype(F32), axis=0, keepdims=True)
        bias_grad[place, :, WIN : 3 * WIN] = key_sums[:, 0 : 2 * WIN]
        bias_grad[place, :, 3 * WIN : 4 * WIN] = key_sums[:, 2 * WIN : 3 * WIN] + jnp.sum(
            third.astype(F32), axis=0, keepdims=True
        )
        bias_grad[place, :, 4 * WIN : 5 * WIN] = key_sums[:, 3 * WIN :]
        bias_grad[place, :, 5 * WIN :] = jnp.zeros((1, WIN), F32)
        return carry

    lax.fori_loop(0, high - low, one, 0)

    def finish_stores():
        for i in range(high - low):
            for copy in store_copies(gbuf, i, grads, store_sems, scal):
                copy.wait()

    if not last:
        finish_stores()
        return
    row_grads[...] = jnp.zeros_like(row_grads)
    row_grads[0:1, :] = jnp.sum(given_wide, axis=0, keepdims=True)
    normed, inverse = normalize(after_self[...])
    hidden_grad = back[...]
    row_grads[1:2, :] = jnp.sum(hidden_grad * normed, axis=0, keepdims=True)
    total = d_cross[...] + normalize_back(hidden_grad * gain[...], normed, inverse)
    d_after[...] = total
    clip = own_clip(scal, rows, splits)
    d_attn[...] = (total * per_row(mod, 2, clip)).astype(BF16)
    sums[...] = clip_sums(own_clip_row(scal, rows, splits), total * branch[...])
    text_out[...] = text_back[...].astype(BF16)
    finish_stores()


def pack_small(table, own, cross, inner, given_sum, cross_rows, out_row, first, gate, second, out):
    n_dp = table.shape[1] // WIN
    splits, clips = out.shape[0], 3
    lane = lax.broadcasted_iota(jnp.int32, (D, n_dp * WIN), 0)

    def moved(value, which):
        choose = (lane == table[which : which + 1, :]).astype(F32).astype(BF16)
        high = value.astype(BF16).astype(F32)
        middle = (value - high).astype(BF16).astype(F32)
        parts = jnp.concatenate([high, middle, value - high - middle], axis=0).astype(BF16)
        found = nn(parts, choose)
        count = value.shape[0]
        return found[:count] + found[count : 2 * count] + found[2 * count :]

    def by_shard(ref):
        return jnp.concatenate([ref[z] for z in range(splits)], axis=0)

    both = moved(jnp.concatenate([by_shard(own), by_shard(cross)], axis=0), 0)
    heads = both[:splits] + pltpu.roll(both[splits:], 48, 1)
    hidden = moved(by_shard(inner), 1)
    rows = moved(
        jnp.concatenate(
            [given_sum, cross_rows[0:2, :], out_row[...]] + [jnp.zeros((4, D), F32)], axis=0
        ),
        2,
    )
    out[...] = jnp.zeros_like(out)
    for z in range(splits):
        for c in range(clips):
            for j in range(6):
                source, col = ((first, j), (gate, 0), (second, j - 3))[(j > 1) + (j > 2)]
                out[z, c * 6 + j : c * 6 + j + 1, :] = source[c : c + 1, col * D : (col + 1) * D]
        for d in range(n_dp):
            span = slice(d * WIN, (d + 1) * WIN)
            parts = [heads[z : z + 1, span], hidden[z : z + 1, span]]
            parts += [rows[r : r + 1, span] for r in range(4)]
            spot = clips * 6 + d
            out[z, spot : spot + 1, :] = jnp.concatenate(parts, axis=1)


def self_backward(n_p, splits, low, high, small, *refs):
    n_w = 2 * n_p
    scal = refs[0]
    frames = refs[1 : 1 + splits]
    given_ref, hidden_t, kv_in, q_in, att_in, lse = refs[1 + splits : 7 + splits]
    pieces = refs[7 + splits : 7 + splits + n_w]
    rest = refs[7 + splits + n_w :]
    first, last = low == 0, high == splits
    if not first:
        back_in, bias_in = rest[:2]
        rest = rest[2:]
    if small:
        table, cross_bias, inner_bias, cross_rows, out_row, gate, second = rest[:7]
        rest = rest[7:]
    n_o = 2 if n_p > 1 else 1
    grads = rest[:n_o]
    bias_grad = rest[n_o]
    rest = rest[n_o + 1 :]
    if last:
        own = rest[0]
        parts = rest[1:splits]
        row_grads, sums = rest[splits : splits + 2]
        rest = rest[splits + 2 :]
        if small:
            own_small, small_rows, back = rest[0], rest[1], rest[2]
            rest = rest[3:]
        else:
            back = rest[0]
            rest = rest[1:]
    else:
        back = rest[0]
        rest = rest[1:]
    weights, gbuf, mask, probs, dscore, key_grad, load_sems, store_sems = rest
    rows = frames[0].shape[0]
    count = rows * splits
    load_wait = load_start(own_and_others(pieces), weights, load_sems, scal, low)
    self_mask(scal, mask, rows, splits)
    given = given_ref[...]
    given_wide = given.astype(F32)
    given_t = given_wide.T.astype(BF16)
    if first:
        back[...] = jnp.zeros_like(back)
        bias_grad[...] = jnp.zeros_like(bias_grad)
    else:
        back[...] = back_in[...]
        bias_grad[...] = bias_in[...]

    def one(i, carry):
        load_wait(i)
        z = i + low
        place = shard_index(scal, z, splits)

        def kv(lo, hi, col):
            return kv_in[z, lo:hi, col * WIN : (col + 1) * WIN]

        def put(lo, hi, k01, v01, k2, v2):
            key_grad[lo:hi, 0:WIN] = k01.astype(BF16)
            key_grad[lo:hi, WIN : 2 * WIN] = v01.astype(BF16)
            key_grad[lo:hi, 2 * WIN : 3 * WIN] = k2.astype(BF16)
            key_grad[lo:hi, 3 * WIN : 4 * WIN] = v2.astype(BF16)

        head_grad = nn(given, weights[i, :, 4 * WIN :]).astype(BF16)
        totals = [lse[z, h : h + 1, :] for h in range(3)]
        pair, third = attend_back(
            q_in[z], kv, att_in[z], head_grad, mask, totals, probs, dscore, count, put
        )
        pair = pair.astype(BF16)
        key_grad[0:rows, 2 * WIN : 3 * WIN] = (
            key_grad[0:rows, 2 * WIN : 3 * WIN].astype(F32) + third
        ).astype(BF16)
        part = nn(hidden_t[...], key_grad[...])
        out_part = nn(given_t, att_in[z])
        gbuf[i, :, 0:WIN] = nn(hidden_t[:, 0:rows], pair).astype(BF16)
        gbuf[i, :, WIN : 4 * WIN] = part[:, 0 : 3 * WIN].astype(BF16)
        gbuf[i, :, 4 * WIN : 5 * WIN] = (part[:, 3 * WIN :] + out_part[:, 0:WIN]).astype(BF16)
        gbuf[i, :, 5 * WIN :] = out_part[:, WIN:].astype(BF16)
        for copy in store_copies(gbuf, i, grads, store_sems, scal):
            copy.start()
        for lo in range(0, count, 256):
            back[lo : lo + 256, :] += nt(
                key_grad[lo : lo + 256, :], weights[i, :, WIN : 5 * WIN]
            )
        back[0:rows, :] += nt(pair, weights[i, :, 0:WIN])
        key_sums = jnp.sum(key_grad[...].astype(F32), axis=0, keepdims=True)
        bias_grad[place, :, 0:WIN] = jnp.sum(pair.astype(F32), axis=0, keepdims=True)
        bias_grad[place, :, WIN : 5 * WIN] = key_sums
        bias_grad[place, :, 5 * WIN :] = jnp.zeros((1, WIN), F32)
        return carry

    lax.fori_loop(0, high - low, one, 0)

    def finish_stores():
        for i in range(high - low):
            for copy in store_copies(gbuf, i, grads, store_sems, scal):
                copy.wait()

    if not last:
        finish_stores()
        return
    given_sum = jnp.sum(given_wide, axis=0, keepdims=True)
    row_grads[...] = jnp.zeros_like(row_grads)
    row_grads[0:1, :] = given_sum
    shift = jnp.zeros((8, D), F32)
    scale = jnp.zeros((8, D), F32)
    for block in range(splits):
        value = back[block * rows : (block + 1) * rows, :]
        if block == 0:
            own[...] = value
        else:
            parts[block - 1][0:rows, :] = value.astype(BF16)
        normed, _ = normalize(frames[block][...].astype(F32))
        clip_row = own_clip_row(scal, rows, splits, block)
        shift = shift + clip_sums(clip_row, value)
        scale = scale + clip_sums(clip_row, value * normed)
    sums[:, 0:D] = shift
    sums[:, D:] = scale
    if small:
        pack_small(
            table,
            bias_grad,
            cross_bias,
            inner_bias,
            given_sum,
            cross_rows,
            out_row,
            sums,
            gate,
            second,
            small_rows,
        )
        for k in range(splits):
            value = small_rows[shard_index(scal, k, splits)]
            if k == 0:
                own_small[...] = value
            else:
                parts[k - 1][rows:, :] = value.astype(BF16)
    finish_stores()


def finish(splits, *refs):
    scal, frames, mod, d_after, own = refs[:5]
    parts = refs[5 : 4 + splits]
    out = refs[4 + splits]
    rows = frames.shape[0]
    value = own[...]
    for part in parts:
        value = value + part[0 : own.shape[0], :].astype(F32)
    normed, inverse = normalize(frames[...].astype(F32))
    scale = 1.0 + per_row(mod, 1, own_clip(scal, rows, splits))
    out[...] = d_after[...] + normalize_back(value * scale, normed, inverse)


def bias_table(n_dp):
    table = np.full((8, n_dp * WIN), -1, np.int32)
    for d in range(n_dp):
        for i in range(48):
            part, h, r = i // 24, i % 24 // 8, i % 8
            spot = d * 8 + r
            start = (h * HD if h < 2 else 3 * WIN) if part == 0 else (2 + h / 2) * WIN
            table[0, d * WIN + i] = (start if part == 0 or h < 2 else 4 * WIN) + spot
        for i in range(96):
            table[1, d * WIN + i] = i // 32 * 256 + d * 32 + i % 32
            table[2, d * WIN + i] = d * 96 + i
    return table


MEMORY = {"v": pltpu.VMEM, "s": pltpu.SMEM, "a": pl.ANY}


def call(body, inputs, outs, scratch, flops, name):
    moved = sum(a.size * a.dtype.itemsize for _, a in inputs)
    moved += sum(_size(s, t) for _, s, t in outs)
    return pl.pallas_call(
        body,
        out_shape=tuple(jax.ShapeDtypeStruct(s, t) for _, s, t in outs),
        in_specs=[pl.BlockSpec(memory_space=MEMORY[m]) for m, _ in inputs],
        out_specs=tuple(pl.BlockSpec(memory_space=MEMORY[m]) for m, _, _ in outs),
        scratch_shapes=scratch,
        compiler_params=pltpu.CompilerParams(vmem_limit_bytes=58 * 1024 * 1024),
        cost_estimate=pl.CostEstimate(flops=int(flops), bytes_accessed=int(moved), transcendentals=0),
        name=name,
    )(*[a for _, a in inputs])


def _size(shape, kind):
    total = jnp.dtype(kind).itemsize
    for s in shape:
        total *= s
    return total


class Ring:
    def __init__(self):
        self.n_dp = lax.axis_size("dp")
        self.splits = lax.axis_size("head")
        self.square = self.n_dp == 8
        if self.square:
            self.core = [(i, i ^ 1) for i in range(8)]
            self.first = [(i, i ^ (4 if i & 1 else 2)) for i in range(8)]
            self.second = [(i, i ^ (2 if i & 1 else 4)) for i in range(8)]

    def offsets(self):
        if not self.square:
            return [jnp.int32(0)]
        me = lax.axis_index("dp")
        rows = D // 8

        def kept(d):
            odd = d & 1
            return [d, d ^ (2 + 2 * odd), d ^ (4 - 2 * odd), d ^ 6]

        return [place * rows for place in kept(me) + kept(me ^ 1)]

    def z_pieces(self, value, far=None):
        n = self.splits
        return [value] + [
            lax.ppermute(value, "head", [(s, (s + k) % n) for s in range(n)])
            for k in (range(1, n) if far is None else far)
        ]

    def z_back(self, parts):
        n = self.splits
        return [
            lax.ppermute(parts[k - 1], "head", [(s, (s - k) % n) for s in range(n)])
            for k in range(1, n)
        ]

    def across(self, value, how):
        return lax.ppermute(value, "dp", how)

    def z_move(self, value, k):
        n = self.splits
        return lax.ppermute(value, "head", [(s, (s - k) % n) for s in range(n)])


class GradSum:
    def __init__(self, ring, grads):
        self.ring, self.grads = ring, list(grads)
        self.moved = []
        self.arrived = []
        if not ring.square:
            self.whole = lax.psum_scatter(grads[0][0], "dp", scatter_dimension=1, tiled=True)

    def across(self, value, how):
        if self.ring.square:
            self.moved.append(self.ring.across(value.astype(BF16), how))

    def block(self, i):
        value = self.grads[0][i].astype(F32) + self.moved[0][i].astype(F32)
        if len(self.moved) > 1:
            value = value + self.moved[1][i].astype(F32)
        return value

    def core(self):
        if self.ring.square:
            self.across(self.grads[1], self.ring.core)

    def second(self):
        if self.ring.square:
            self.across(self.block(slice(2, 4)), self.ring.second)

    def first(self):
        if self.ring.square:
            self.across(self.block(1), self.ring.first)

    def own(self, i):
        if not self.ring.square:
            return self.whole[i].astype(F32)
        value = self.grads[0][0, i].astype(F32) + self.moved[2][i].astype(F32)
        return value + self.moved[0][0, i].astype(F32) + self.moved[1][0, i].astype(F32)

    def shard(self, start):
        count = self.grads[0].shape[1]
        for i in range(count):
            k = i if start == 1 else start + i
            if k > 0:
                self.arrived.append(self.ring.z_move(self.own(i).astype(BF16), k))


def join_second(low, high):
    if not low.ring.square:
        return []
    part = slice(2, 4)
    both = jnp.concatenate([low.block(part), high.block(part)], axis=1)
    return [low.ring.across(both.astype(BF16), low.ring.second)]


def join_first(low, high):
    if not low.ring.square:
        return []
    both = jnp.concatenate([low.block(1), high.block(1)], axis=0)
    return [low.ring.across(both.astype(BF16), low.ring.first)]


def join_take(low, high, moved):
    count = low.grads[0].shape[1]
    for value in moved:
        low.moved.append(value[..., :count, :, :])
        high.moved.append(value[..., count:, :, :])


def join_shards(pairs):
    ring = pairs[0][0].ring
    half = ring.splits // 2
    return [
        ring.z_move(
            jnp.concatenate([pair[k // half].own(k % half) for pair in pairs], axis=1).astype(BF16),
            k,
        )
        for k in range(1, ring.splits)
    ]


class Gather:
    def __init__(self, ring, mine):
        self.ring = ring
        if ring.square:
            self.kept, self.other = [mine], []
        else:
            self.kept, self.other = [lax.all_gather(mine, "dp", axis=1, tiled=True)], []

    def sides(self):
        if self.ring.square:
            self.kept.append(self.ring.across(self.kept[0], self.ring.first))
            self.kept.append(self.ring.across(self.kept[0], self.ring.second))

    def corner(self):
        if self.ring.square:
            self.kept.append(self.ring.across(self.kept[1], self.ring.second))

    def core(self, *which):
        if self.ring.square:
            for i in which:
                self.other.append(self.ring.across(self.kept[i], self.ring.core))

    def pieces(self):
        return self.kept + self.other


def meet(*groups):
    flat = [v for group in groups for v in group]
    flat = list(lax.optimization_barrier(tuple(flat)))
    for group in groups:
        for i in range(len(group)):
            group[i] = flat.pop(0)


def to_layout(q, k, v, o):
    return jnp.concatenate(
        [
            q[:, :WIN],
            k[:, :WIN],
            v[:, :WIN],
            q[:, WIN:],
            k[:, WIN:],
            v[:, WIN:],
            o[:, WIN:],
            o[:, :WIN],
        ],
        axis=1,
    )


def from_layout(value):
    def pick(pair, third):
        return jnp.concatenate(
            [value[:, pair : pair + WIN], value[:, third : third + HD]], axis=1
        )

    return pick(0, 3 * WIN), pick(WIN, 3 * WIN + HD), pick(2 * WIN, 4 * WIN), pick(
        5 * WIN, 4 * WIN + HD
    )


def mod_gradients(ring, sums, clips):
    part = jnp.concatenate(sums, axis=1)[:clips]
    got = lax.all_to_all(
        jnp.broadcast_to(part[None], (ring.splits,) + part.shape), "head", 0, 0, tiled=True
    )
    low = jnp.sum(got, axis=0).astype(BF16)
    return lax.all_to_all(
        jnp.broadcast_to(low[None], (ring.n_dp,) + low.shape), "dp", 0, 0, tiled=True
    ).reshape(ring.n_dp * clips, -1)


def on_device(
    frames_in,
    step_embed,
    text_feats,
    clip_frames,
    text_tokens,
    out_grad,
    ada_weight,
    ada_bias,
    qkv_weight,
    qv_bias,
    attn_out_weight,
    attn_out_bias,
    cross_gain,
    cross_q_weight,
    cross_q_bias,
    cross_kv_weight,
    cross_v_bias,
    cross_out_weight,
    cross_out_bias,
    mlp_in_weight,
    mlp_in_bias,
    mlp_out_weight,
    mlp_out_bias,
):
    both = ("dp", "head")
    ring = Ring()
    n_dp, splits = ring.n_dp, ring.splits
    z_index = lax.axis_index("head")
    rows = frames_in.shape[0]
    count = rows * splits
    text_count = text_feats.shape[0]
    clips = clip_frames.shape[1]
    width = D // splits
    shard_rows = D // n_dp
    ends = jnp.cumsum(clip_frames[0])
    offs = ring.offsets()
    n_p = len(offs)
    scal = jnp.stack(
        [z_index, ends[0], ends[1], text_tokens[0, 0], text_tokens[0, 1], text_tokens[0, 2]]
        + [jnp.int32(0)] * 2
        + [o.astype(jnp.int32) for o in offs]
        + [jnp.int32(0)] * (S_LEN - S_OFF - n_p)
    ).astype(jnp.int32)

    shard_self = to_layout(
        qkv_weight[:, 0], qkv_weight[:, 1], qkv_weight[:, 2], attn_out_weight.T
    )
    shard_cross = to_layout(
        cross_q_weight, cross_kv_weight[:, 0], cross_kv_weight[:, 1], cross_out_weight.T
    )

    biases = [
        ada_bias,
        qv_bias.reshape(-1),
        attn_out_bias,
        cross_gain,
        cross_q_bias.reshape(-1),
        cross_v_bias.reshape(-1),
        cross_out_bias,
        mlp_in_bias.reshape(-1),
        mlp_out_bias,
    ]
    flat = jnp.concatenate(biases)
    cols = step_embed.reshape(clips, n_dp, shard_rows).transpose(1, 0, 2).reshape(n_dp, -1)
    sent = jnp.concatenate(
        [
            jnp.broadcast_to(flat[None, None], (n_dp, splits, flat.shape[0])),
            jnp.broadcast_to(cols[:, None], (n_dp, splits, cols.shape[1])),
        ],
        axis=2,
    ).reshape(n_dp * splits, -1)
    got = lax.all_to_all(sent, both, 0, 0, tiled=True)
    attn_shard = jnp.concatenate([shard_self, shard_cross], axis=1)
    attn_shards = ring.z_pieces(attn_shard)[1:]
    own_gather = Gather(ring, attn_shard[None])
    own_gather.sides()
    own_gather.corner()
    own_gather.core(0, 1, 2, 3)
    mlp_shard = jnp.concatenate([mlp_in_weight, mlp_out_weight.T], axis=1)
    held = [got]
    meet(held, attn_shards, own_gather.kept, own_gather.other)
    got = held[0].reshape(n_dp, splits, -1)
    step_cols = got[:, 0, flat.shape[0] :].reshape(n_dp * clips, shard_rows).astype(F32)
    silu_cols = jax.nn.silu(step_cols).astype(BF16)
    spots = []
    place = 0
    for b in biases:
        spots.append(got[:, :, place : place + b.shape[0]].astype(F32))
        place += b.shape[0]

    def over_dp(value):
        return value[:, 0].reshape(1, -1)

    def by_head(value, lead=1):
        n = value.shape[2] // (lead * 3)
        v = value.reshape(n_dp, splits, lead, 3, n).transpose(1, 2, 3, 0, 4)
        return v.reshape(splits, lead, 3 * n_dp * n)

    all_ada_bias = over_dp(spots[0])
    qv = by_head(spots[1], 2)
    nothing = jnp.zeros((splits, width), F32)
    bias_self = to_layout(qv[:, 0], nothing, qv[:, 1], nothing)[:, None]
    all_attn_bias = over_dp(spots[2])
    all_gain = over_dp(spots[3])
    bias_cross = to_layout(
        by_head(spots[4])[:, 0], nothing, by_head(spots[5])[:, 0], nothing
    )[:, None]
    all_cross_bias = over_dp(spots[6])
    all_in_bias = by_head(spots[7])
    all_out_bias = over_dp(spots[8])

    mod_part = jnp.dot(silu_cols, ada_weight, preferred_element_type=F32)
    mod_got = lax.all_to_all(mod_part.reshape(n_dp, clips, -1), "dp", 0, 0, tiled=True)

    half = splits // 2
    attn_gather = Gather(ring, jnp.stack(attn_shards))
    attn_gather.sides()
    frame_blocks = ring.z_pieces(frames_in)
    held = [mod_got, mlp_shard]
    meet(held, attn_gather.kept)
    mlp_shard = held[1]
    mod = jnp.sum(held[0], axis=0) + all_ada_bias
    attn_gather.corner()
    attn_gather.core(0, 1, 2, 3)
    mlp_shards = ring.z_pieces(mlp_shard, range(1, half))
    mlp_gathers = [Gather(ring, jnp.stack(mlp_shards))]
    mlp_gathers[0].sides()
    mlp_gathers[0].core(0)
    mlp_late = ring.z_pieces(mlp_shard, range(half, splits))[1:]

    def dma(n):
        return pltpu.SemaphoreType.DMA(n)

    def any_of(arrays):
        return [("a", a) for a in arrays]

    def vmem_of(arrays):
        return [("v", a) for a in arrays]

    piece_rows = D // n_p
    kept_out = [("a", (max(n_p // 2, 1), splits, piece_rows, D), BF16)] * (2 if n_p > 1 else 1)
    n_o = len(kept_out)
    shard_type = pltpu.VMEM((splits, D, D), BF16)

    results = list(call(
        partial(self_forward, n_p, splits),
        [("s", scal)]
        + vmem_of(frame_blocks)
        + vmem_of([mod, bias_self, all_attn_bias])
        + any_of(own_gather.pieces() + attn_gather.pieces()),
        [
            ("v", (D, count), BF16),
            ("a", (splits, count, 4 * WIN), BF16),
            ("v", (splits, rows, 2 * WIN), BF16),
            ("v", (splits, rows, 2 * WIN), BF16),
            ("v", (splits, 8, rows), F32),
            ("v", (rows, D), F32),
            ("v", (rows, D), F32),
        ],
        [
            pltpu.VMEM((count, D), BF16),
            pltpu.VMEM((splits, count, 4 * WIN), BF16),
            shard_type,
            pltpu.VMEM((rows, count), F32),
            pltpu.VMEM((rows, count), F32),
            pltpu.VMEM((rows, count), BF16),
            dma((n_p, splits)),
            dma((splits,)),
        ],
        22 * US,
        "self_forward",
    ))
    meet(
        results, mlp_gathers[0].kept, mlp_gathers[0].other, mlp_late, attn_gather.kept, attn_gather.other
    )
    hidden_one, self_kv, self_q, self_att, self_lse, attn_branch, after_self = results
    mlp_gathers[0].corner()
    mlp_gathers[0].core(1, 2)
    mlp_gathers.append(Gather(ring, jnp.stack(mlp_late)))
    mlp_gathers[1].sides()

    results = list(call(
        partial(cross_forward, n_p, splits),
        [("s", scal)]
        + vmem_of([after_self, text_feats, all_gain, bias_cross, all_cross_bias])
        + any_of(own_gather.pieces() + attn_gather.pieces()),
        [
            ("v", (D, rows), BF16),
            ("v", (D, text_count), BF16),
            ("a", (splits, text_count, 4 * WIN), BF16),
            ("v", (splits, rows, 2 * WIN), BF16),
            ("v", (splits, rows, 2 * WIN), BF16),
            ("v", (splits, 8, rows), F32),
            ("v", (rows, D), F32),
        ],
        [
            pltpu.VMEM((splits, text_count, 4 * WIN), BF16),
            shard_type,
            pltpu.VMEM((rows, text_count), F32),
            pltpu.VMEM((rows, text_count), F32),
            pltpu.VMEM((rows, text_count), BF16),
            dma((n_p, splits)),
            dma((splits,)),
        ],
        17 * US,
        "cross_forward",
    ))
    meet(results, mlp_gathers[0].kept, mlp_gathers[0].other, mlp_gathers[1].kept)
    hidden_two_t, text_t, cross_kv, cross_q, cross_att, cross_lse, after_cross = results
    mlp_gathers[0].core(3)
    mlp_gathers[1].corner()
    mlp_gathers[1].core(0, 1, 2)

    kept_half = [(m, (shape[0], half) + shape[2:], kind) for m, shape, kind in kept_out]
    kept_wide = [(m, shape[:3] + (2 * D,), kind) for m, shape, kind in kept_half]
    half_type = pltpu.VMEM((half, D, D), BF16)

    def back_scratch(keys):
        return [
            half_type,
            half_type,
            pltpu.VMEM((keys, rows), F32),
            pltpu.VMEM((3, keys, rows), BF16),
            pltpu.VMEM((3, keys, rows), BF16),
            pltpu.VMEM((keys, 4 * WIN), BF16),
            dma((n_p, half)),
            dma((n_p, half)),
        ]

    bias_type = [("v", (splits, 1, D), F32)]
    mlp_args = [after_cross, out_grad, mod, all_in_bias, all_out_bias]
    mlp_scratch = [
        pltpu.VMEM((half, D, 2 * D), BF16),
        pltpu.VMEM((half, D, 2 * D), BF16),
        dma((n_p, half)),
        dma((n_p, half)),
    ]
    results = call(
        partial(feed_forward, n_p, splits, 0, half),
        [("s", scal)] + vmem_of(mlp_args) + any_of(mlp_gathers[0].pieces()),
        kept_wide + bias_type + [("v", (rows, D), F32)] * 2,
        mlp_scratch,
        9 * US,
        "feed_forward_first",
    )
    results = list(results)
    meet(results, mlp_gathers[1].kept, mlp_gathers[1].other)
    mlp_gathers[1].core(3)
    sum_mlp = [GradSum(ring, results[:n_o])]
    in_bias_grad, mlp_state, mlp_back = results[n_o:]
    sum_mlp[0].core()
    results = call(
        partial(feed_forward, n_p, splits, half, splits),
        [("s", scal)]
        + vmem_of(mlp_args)
        + any_of(mlp_gathers[1].pieces())
        + vmem_of([mlp_state, mlp_back, in_bias_grad]),
        kept_wide
        + bias_type
        + [
            ("v", (rows, D), BF16),
            ("v", (rows, D), F32),
            ("v", (1, D), F32),
            ("v", (8, 3 * D), F32),
        ],
        [pltpu.VMEM((rows, D), F32), pltpu.VMEM((rows, D), F32)] + mlp_scratch,
        10 * US,
        "feed_forward_last",
    )
    results = list(results)
    meet(results, sum_mlp[0].moved)
    sum_mlp.append(GradSum(ring, results[:n_o]))
    in_bias_grad, layer_out, d_after_cross, out_bias_grad, sums_two = results[n_o:]
    sum_mlp[0].second()
    sum_mlp[1].core()
    cross_args = [
        d_after_cross,
        after_self,
        hidden_two_t,
        text_t,
        all_gain,
        mod,
        attn_branch,
        cross_kv,
        cross_q,
        cross_att,
        cross_lse,
    ]
    cross_state = [("v", (rows, D), F32), ("v", (text_count, D), F32)]
    results = call(
        partial(cross_backward, n_p, splits, 0, half),
        [("s", scal)] + vmem_of(cross_args) + any_of(own_gather.pieces() + attn_gather.pieces()),
        kept_half + bias_type + cross_state,
        back_scratch(text_count),
        14 * US,
        "cross_backward_first",
    )
    results = list(results)
    meet(results, sum_mlp[0].moved, sum_mlp[1].moved)
    sum_cross = [GradSum(ring, results[:n_o])]
    cross_bias_grad, cross_back, text_back = results[n_o:]
    sum_mlp[0].first()
    sum_mlp[1].second()
    sum_cross[0].core()
    results = call(
        partial(cross_backward, n_p, splits, half, splits),
        [("s", scal)]
        + vmem_of(cross_args)
        + any_of(own_gather.pieces() + attn_gather.pieces())
        + vmem_of([cross_back, text_back, cross_bias_grad]),
        kept_half
        + bias_type
        + [
            ("v", (rows, D), F32),
            ("v", (rows, D), BF16),
            ("v", (text_count, D), BF16),
            ("v", (8, D), F32),
            ("v", (8, D), F32),
        ],
        [pltpu.VMEM((rows, D), F32), pltpu.VMEM((text_count, D), F32)] + back_scratch(text_count),
        15 * US,
        "cross_backward_last",
    )
    results = list(results)
    meet(results, sum_mlp[0].moved, sum_mlp[1].moved, sum_cross[0].moved)
    sum_cross.append(GradSum(ring, results[:n_o]))
    cross_bias_grad, d_after_self, d_attn, text_out, cross_rows, gate_sums = results[n_o:]
    sum_mlp[0].shard(1)
    sum_mlp[1].first()
    sum_cross[0].second()
    sum_cross[1].core()
    text_got = lax.all_to_all(
        text_out.reshape(splits, text_count // splits, D), "head", 0, 0, tiled=True
    )
    self_args = [d_attn, hidden_one, self_kv, self_q, self_att, self_lse]
    results = call(
        partial(self_backward, n_p, splits, 0, half, False),
        [("s", scal)] + vmem_of(frame_blocks) + vmem_of(self_args) + any_of(own_gather.pieces() + attn_gather.pieces()),
        kept_half + bias_type + [("v", (count, D), F32)],
        back_scratch(count),
        17 * US,
        "self_backward_first",
    )
    results = list(results)
    meet(
        results,
        sum_mlp[1].moved,
        sum_cross[0].moved,
        sum_cross[1].moved,
    )
    sum_self = [GradSum(ring, results[:n_o])]
    self_bias_grad, self_back = results[n_o:]
    sum_mlp[1].shard(2)
    sum_cross[1].second()
    sum_self[0].core()
    small_args, small_outs, small_scratch, small_count = [], [], [], 0
    if ring.square:
        small_count = 32
        small_args = [jnp.asarray(bias_table(n_dp)), cross_bias_grad, in_bias_grad]
        small_args += [cross_rows, out_bias_grad, gate_sums, sums_two]
        small_outs = [("v", (small_count, D), F32)]
        small_scratch = [pltpu.VMEM((splits, small_count, D), F32)]
    results = call(
        partial(self_backward, n_p, splits, half, splits, ring.square),
        [("s", scal)]
        + vmem_of(frame_blocks)
        + vmem_of(self_args)
        + any_of(own_gather.pieces() + attn_gather.pieces())
        + vmem_of([self_back, self_bias_grad] + small_args),
        kept_half
        + bias_type
        + [("v", (rows, D), F32)]
        + [("v", (rows + small_count, D), BF16)] * (splits - 1)
        + [("v", (8, D), F32), ("v", (8, 2 * D), F32)]
        + small_outs,
        small_scratch + [pltpu.VMEM((count, D), F32)] + back_scratch(count),
        18 * US,
        "self_backward_last",
    )
    results = list(results)
    held = [in_bias_grad, out_bias_grad, cross_bias_grad, cross_rows, gate_sums, sums_two]
    held.append(text_got)
    meet(
        results,
        held,
        sum_mlp[0].arrived,
        sum_mlp[1].arrived,
        sum_cross[0].moved,
        sum_cross[1].moved,
        sum_self[0].moved,
    )
    sum_self.append(GradSum(ring, results[:n_o]))
    self_bias_grad, own_part = results[n_o : n_o + 2]
    parts = results[n_o + 2 : n_o + 1 + splits]
    self_rows, sums_one = results[n_o + 1 + splits : n_o + 3 + splits]
    sum_self[1].core()
    near_cross = join_first(*sum_cross)
    arrived = ring.z_back(parts)
    in_bias_grad, out_bias_grad, cross_bias_grad, cross_rows, gate_sums, sums_two, text_got = held
    far = join_second(*sum_self)
    early, late = arrived[:1], arrived[1:]
    meet(far, near_cross, early)
    join_take(*sum_self, far)
    join_take(*sum_cross, near_cross)
    near = join_first(*sum_self)
    meet(late, near)
    arrived = early + late
    join_take(*sum_self, near)
    last = join_shards([sum_cross, sum_self])
    if ring.square:
        small = results[-1] + sum(part[rows:].astype(F32) for part in arrived)
        mod_low = small[: 6 * clips].astype(BF16).astype(F32)
        sent = jnp.concatenate(
            [
                jnp.broadcast_to(mod_low[None], (n_dp,) + mod_low.shape),
                small[6 * clips : 6 * clips + n_dp, None],
            ],
            axis=1,
        )
        held = [lax.all_to_all(sent, "dp", 0, 0, tiled=True)]
    if ring.square:
        mod_all = held[0][:, : 6 * clips].reshape(n_dp * clips, -1).astype(BF16)
        bias_sum = jnp.sum(held[0][:, 6 * clips], axis=0)
        places = [0, 24, 2 * WIN, 4 * WIN, 48, 72, 3 * WIN, WIN, 5 * WIN]
    else:
        mod_all = mod_gradients(ring, [sums_one, gate_sums, sums_two], clips)
    step_part = lax.dot_general(
        mod_all, ada_weight, (((1,), (1,)), ((), ())), preferred_element_type=F32
    )
    (frames_grad,) = call(
        partial(finish, splits),
        [("s", scal)] + vmem_of([frames_in, mod, d_after_self, own_part]) + vmem_of(arrived),
        [("v", (rows, D), F32)],
        [],
        3 * US,
        "finish",
    )
    text_grad = jnp.sum(text_got.astype(F32), axis=0)

    grad_ada = lax.dot_general(
        silu_cols, mod_all, (((0,), (0,)), ((), ())), preferred_element_type=F32
    )
    dp_index = lax.axis_index("dp")
    bias_width = ada_bias.shape[0]
    grad_ada_bias = jnp.sum(
        lax.dynamic_slice_in_dim(mod_all, dp_index * bias_width, bias_width, 1).astype(F32), axis=0
    )
    step_got = lax.all_to_all(step_part.reshape(n_dp, clips, shard_rows), "dp", 0, 0, tiled=True)
    step_got = [step_got]
    meet(last, step_got)
    (step_got,) = step_got
    total_cross, total_self = (
        pair[0].own(0) + sum(part[:, i * D : (i + 1) * D].astype(F32) for part in last)
        for i, pair in enumerate((sum_cross, sum_self))
    )
    step_value = step_embed.astype(F32)
    _, silu_pull = jax.vjp(jax.nn.silu, step_value)
    step_grad = silu_pull(step_got.transpose(1, 0, 2).reshape(clips, D))[0]

    def spread(value):
        v = value.reshape(n_dp, 1, D // n_dp)
        return jnp.broadcast_to(v, (n_dp, splits, D // n_dp))

    def heads_out(value):
        n = value.shape[1] // (3 * n_dp)
        return value.reshape(splits, 3, n_dp, n).transpose(2, 0, 1, 3).reshape(n_dp, splits, 3 * n)

    sq, _, sv, _ = from_layout(self_bias_grad[:, 0])
    cq, _, cv, _ = from_layout(cross_bias_grad[:, 0])
    entries = [
        heads_out(sq),
        heads_out(sv),
        spread(self_rows[0]),
        spread(cross_rows[1]),
        heads_out(cq),
        heads_out(cv),
        spread(cross_rows[0]),
        heads_out(in_bias_grad[:, 0]),
        spread(out_bias_grad[0]),
    ]
    if not ring.square:
        packed = jnp.concatenate(entries, axis=2)
        places = [sum(e.shape[2] for e in entries[:i]) for i in range(len(entries))]
        bias_sum = jnp.sum(
            lax.all_to_all(packed.reshape(n_dp * splits, -1), both, 0, 0, tiled=True), axis=0
        )
    bias_out = [bias_sum[p : p + e.shape[2]] for p, e in zip(places, entries)]

    total_mlp = sum_mlp[0].own(0) + sum(
        part.astype(F32) for part in sum_mlp[0].arrived + sum_mlp[1].arrived
    )
    gq, gk, gv, go = from_layout(total_self)
    hq, hk, hv, ho = from_layout(total_cross)
    return (
        layer_out,
        frames_grad,
        step_grad,
        text_grad,
        grad_ada,
        grad_ada_bias,
        jnp.stack([gq, gk, gv], axis=1),
        jnp.stack([bias_out[0], bias_out[1]]).reshape(qv_bias.shape),
        go.T,
        bias_out[2],
        bias_out[3],
        hq,
        bias_out[4].reshape(cross_q_bias.shape),
        jnp.stack([hk, hv], axis=1),
        bias_out[5].reshape(cross_v_bias.shape),
        ho.T,
        bias_out[6],
        total_mlp[:, :D],
        bias_out[7].reshape(mlp_in_bias.shape),
        total_mlp[:, D:].T,
        bias_out[8],
    )


def solution(mesh):
    rows_all, by_dp = P(("dp", "head"), None), P("dp", None)
    head_dp, dp_head = P("head", "dp"), P("dp", "head")
    dp_three, vector = P("dp", None, "head"), P("dp")
    params = (
        by_dp,
        vector,
        dp_three,
        P(None, "head", "dp"),
        head_dp,
        vector,
        vector,
        dp_head,
        head_dp,
        dp_three,
        head_dp,
        head_dp,
        vector,
        dp_head,
        head_dp,
        head_dp,
        vector,
    )
    return jax.shard_map(
        on_device,
        mesh=mesh,
        in_specs=(rows_all, by_dp, by_dp, by_dp, by_dp, rows_all) + params,
        out_specs=(rows_all, rows_all, by_dp, rows_all) + params,
        check_vma=False,
    )
```

```python
from functools import partial

import jax
import jax.numpy as jnp
import numpy as np
from jax import lax
from jax.experimental import pallas as pl
from jax.experimental.pallas import tpu as pltpu
from jax.sharding import PartitionSpec as P

D = 768
HD = 64
TXT = 256
WIN = 128
EPS = 1e-06
NEG = -1e30
F32 = jnp.float32
BF16 = jnp.bfloat16
HIGH = lax.Precision.HIGHEST
S_Z, S_END, S_TOK, S_OFF = 0, 1, 3, 8
S_LEN = 16
US = 1.15e9


def nn(a, b):
    return lax.dot_general(a, b, (((1,), (0,)), ((), ())), preferred_element_type=F32)


def nt(a, b):
    return lax.dot_general(a, b, (((1,), (1,)), ((), ())), preferred_element_type=F32)


def tn(a, b):
    return lax.dot_general(a, b, (((0,), (0,)), ((), ())), preferred_element_type=F32)


def normalize(v):
    centered = v - jnp.mean(v, axis=-1, keepdims=True)
    inverse = lax.rsqrt(jnp.mean(centered * centered, axis=-1, keepdims=True) + EPS)
    return centered * inverse, inverse


def normalize_back(u, normed, inverse):
    return inverse * (
        u
        - jnp.mean(u, axis=-1, keepdims=True)
        - normed * jnp.mean(u * normed, axis=-1, keepdims=True)
    )


def clip_of(position, scal):
    return (position >= scal[S_END]).astype(jnp.int32) + (position >= scal[S_END + 1]).astype(
        jnp.int32
    )


def frame_position(index, block, rows, splits, scal):
    return lax.rem(scal[S_Z] - block + splits, splits) * rows + index


def per_row(mod_ref, part, clip):
    cols = slice(part * D, (part + 1) * D)
    first, second, third = (mod_ref[c : c + 1, cols] for c in range(3))
    return jnp.where(clip == 0, first, jnp.where(clip == 1, second, third))


def clip_sums(clip_row, value):
    which = lax.broadcasted_iota(jnp.int32, (8, clip_row.shape[1]), 0)
    choose = (which == clip_row).astype(F32)
    return lax.dot_general(
        choose, value, (((1,), (0,)), ((), ())), precision=HIGH, preferred_element_type=F32
    )


def lanes(rows, low):
    lane = lax.broadcasted_iota(jnp.int32, (rows, WIN), 1)
    return lane < HD if low else lane >= HD


def keep(value, low):
    return jnp.where(lanes(value.shape[0], low), value, jnp.zeros_like(value))


def swap(value):
    return pltpu.roll(value, HD, 1)


def load_start(groups, buffer, sems, scal, low=0, col=0):
    width = buffer.shape[2]

    def place(j, rows):
        return pl.ds(pl.multiple_of(scal[S_OFF + j], 32), rows)

    for z in range(buffer.shape[0]):
        for pieces, start in groups:
            at = low + z - start
            if 0 <= at < pieces[0].shape[0]:
                for j, piece in enumerate(pieces):
                    pltpu.make_async_copy(
                        piece.at[at, :, col : col + width],
                        buffer.at[z, place(j, piece.shape[1]), :],
                        sems.at[j, z],
                    ).start()

    def wait(z):
        for j, piece in enumerate(groups[0][0]):
            here = buffer.at[z, place(j, piece.shape[1]), :]
            pltpu.make_async_copy(here, here, sems.at[j, z]).wait()

    return wait


def own_and_others(pieces):
    half = len(pieces) // 2
    return [(pieces[:half], 0), (pieces[half:], 1)]


def store_copies(buffer, z, outs, sems, scal, col=0, first=0):
    copies = []
    j = 0
    for out in outs:
        for i in range(out.shape[0]):
            rows = out.shape[2]
            start = pl.multiple_of(scal[S_OFF + j], 32)
            copies.append(
                pltpu.make_async_copy(
                    buffer.at[z, pl.ds(start, rows), col : col + out.shape[3]],
                    out.at[i, z],
                    sems.at[first + j, z],
                )
            )
            j += 1
    return copies


def attend(queries, kv, mask, scores, probs, count):
    rows = queries.shape[0]
    step = 256
    outs = []
    lane = lax.broadcasted_iota(jnp.int32, (rows, WIN), 1)
    totals = jnp.zeros((rows, WIN), F32)
    for h in range(3):
        if h < 2:
            query = keep(queries[:, :WIN], h == 0)
            kcol, vcol = 0, 1
        else:
            query = queries[:, WIN:]
            kcol, vcol = 2, 3
        top = None
        for lo in range(0, count, step):
            part = nt(query, kv(lo, lo + step, kcol)) + mask[:, lo : lo + step]
            scores[:, lo : lo + step] = part
            top = part if top is None else jnp.maximum(top, part)
        peak = jnp.max(top, axis=1, keepdims=True)
        wide = jnp.zeros((rows, step), F32)
        for lo in range(0, count, step):
            part = jnp.exp(scores[:, lo : lo + step] - peak)
            wide = wide + part
            probs[:, lo : lo + step] = part.astype(BF16)
        total = jnp.sum(wide, axis=1, keepdims=True)
        outs.append(nn(probs[:, 0:count], kv(0, count, vcol)) * (1.0 / total))
        totals = jnp.where(lane == h, peak + jnp.log(total), totals)
    pair = jnp.where(lane < HD, outs[0], outs[1])
    attended = jnp.concatenate([keep(swap(outs[2]), False), pair], axis=1)
    return attended.astype(BF16), totals.T[0:8, :]


def attend_back(queries, kv, attended, out_grad, mask, totals, probs, dscore, count, put):
    rows = queries.shape[0]
    step = 256
    wide = out_grad.astype(F32)
    row = lax.broadcasted_iota(jnp.int32, (8, 2 * WIN), 0)
    part = lax.broadcasted_iota(jnp.int32, (8, 2 * WIN), 1) // HD
    choose = ((part == row + 2) & (row < 2)) | ((part == 1) & (row == 2))
    deltas = lax.dot_general(
        choose.astype(F32),
        wide * attended.astype(F32),
        (((1,), (1,)), ((), ())),
        precision=HIGH,
        preferred_element_type=F32,
    )
    second = keep(swap(wide[:, :WIN]), True).astype(BF16)
    query_parts = []
    heads = []
    key_t = [kv(0, count, col).astype(F32).T.astype(BF16) for col in (0, 2)]
    for h in range(3):
        if h < 2:
            query = keep(queries[:, :WIN], h == 0)
            given = keep(out_grad[:, WIN:], h == 0)
            kcol, vcol = 0, 1
        else:
            query, given = queries[:, WIN:], second
            kcol, vcol = 2, 3
        heads.append((query, given))
        total, delta = totals[h], deltas[h : h + 1, :]
        for lo in range(0, count, step):
            hi = lo + step
            weights = jnp.exp(nt(kv(lo, hi, kcol), query) + mask[lo:hi, :] - total)
            probs[h, lo:hi, :] = weights.astype(BF16)
            weight_grad = nt(kv(lo, hi, vcol), given)
            dscore[h, lo:hi, :] = (weights * (weight_grad - delta)).astype(BF16)
        query_parts.append(nn(key_t[h // 2], dscore[h, 0:count, :]))
    for lo in range(0, count, step):
        hi = lo + step
        put(
            lo,
            hi,
            nn(dscore[0, lo:hi, :], heads[0][0]) + nn(dscore[1, lo:hi, :], heads[1][0]),
            nn(probs[0, lo:hi, :], heads[0][1]) + nn(probs[1, lo:hi, :], heads[1][1]),
            nn(dscore[2, lo:hi, :], heads[2][0]),
            nn(probs[2, lo:hi, :], heads[2][1]),
        )
    both = jnp.concatenate(
        [
            query_parts[0][:HD],
            query_parts[1][HD:],
            query_parts[2][HD:],
            jnp.zeros((HD, rows), F32),
        ],
        axis=0,
    )
    both = (both * 0.125).T
    return both[:, :WIN], both[:, WIN:]


def self_mask(scal, mask, rows, splits, forward=False):
    clip = own_clip if forward else own_clip_row
    query = clip(scal, rows, splits)
    for block in range(splits):
        span = slice(block * rows, (block + 1) * rows)
        key = (own_clip_row if forward else own_clip)(scal, rows, splits, block)
        value = jnp.where(key == query, 0.0, NEG)
        if forward:
            mask[:, span] = value
        else:
            mask[span, :] = value


def cross_mask(scal, mask, rows, splits, clips, forward=False):
    query = (own_clip if forward else own_clip_row)(scal, rows, splits)
    shape = (1, TXT) if forward else (TXT, 1)
    slot = lax.broadcasted_iota(jnp.int32, shape, 1 if forward else 0)
    for c in range(clips):
        span = slice(c * TXT, (c + 1) * TXT)
        value = jnp.where((query == c) & (slot < scal[S_TOK + c]), 0.0, NEG)
        if forward:
            mask[:, span] = value
        else:
            mask[span, :] = value


def own_clip(scal, rows, splits, block=0):
    return clip_of(
        frame_position(lax.broadcasted_iota(jnp.int32, (rows, 1), 0), block, rows, splits, scal),
        scal,
    )


def own_clip_row(scal, rows, splits, block=0):
    return clip_of(
        frame_position(lax.broadcasted_iota(jnp.int32, (1, rows), 1), block, rows, splits, scal),
        scal,
    )


def shard_index(scal, z, splits):
    return lax.rem(scal[S_Z] - z + splits, splits)


def self_forward(n_p, splits, *refs):
    n_w = 2 * n_p
    scal = refs[0]
    frames = refs[1 : 1 + splits]
    mod, bias, out_bias = refs[1 + splits : 4 + splits]
    pieces = refs[4 + splits : 4 + splits + n_w]
    hidden_t, kv_out, q_out, att_out, lse, branch_out, after = refs[
        4 + splits + n_w : 11 + splits + n_w
    ]
    hidden, kv_buf, weights, mask, scores, probs, sems, kv_sems = refs[11 + splits + n_w :]
    rows = frames[0].shape[0]
    count = rows * splits
    load_wait = load_start(own_and_others(pieces), weights, sems, scal)
    self_mask(scal, mask, rows, splits, True)
    for block in range(splits):
        clip = own_clip(scal, rows, splits, block)
        normed, _ = normalize(frames[block][...].astype(F32))
        value = normed * (1.0 + per_row(mod, 1, clip)) + per_row(mod, 0, clip)
        hidden[block * rows : (block + 1) * rows, :] = value.astype(BF16)
        hidden_t[:, block * rows : (block + 1) * rows] = value.T.astype(BF16)
    branch_out[...] = jnp.broadcast_to(out_bias[...], branch_out.shape)

    def one(z, carry):
        load_wait(z)
        bias_row = bias[shard_index(scal, z, splits)]
        for block in range(splits):
            span = slice(block * rows, (block + 1) * rows)
            part = nn(hidden[span, :], weights[z, :, WIN : 5 * WIN]) + bias_row[:, WIN : 5 * WIN]
            kv_buf[z, span, :] = part.astype(BF16)
            if block == 0:
                third = keep(swap(part[:, 2 * WIN : 3 * WIN].astype(BF16).astype(F32)), False)
        pair = nn(hidden[0:rows, :], weights[z, :, 0:WIN]) + bias_row[:, 0:WIN]
        queries = (
            jnp.concatenate([pair.astype(BF16).astype(F32), third], axis=1) * 0.125
        ).astype(BF16)
        q_out[z] = queries
        pltpu.make_async_copy(kv_buf.at[z], kv_out.at[z], kv_sems.at[z]).start()

        def kv(lo, hi, col):
            return kv_buf[z, lo:hi, col * WIN : (col + 1) * WIN]

        attended, totals = attend(queries, kv, mask, scores, probs, count)
        att_out[z] = attended
        lse[z] = totals
        branch_out[...] += nt(attended, weights[z, :, 4 * WIN :])
        return carry

    lax.fori_loop(0, splits, one, 0)
    clip = own_clip(scal, rows, splits)
    after[...] = frames[0][...].astype(F32) + per_row(mod, 2, clip) * branch_out[...]
    for z in range(splits):
        pltpu.make_async_copy(kv_buf.at[z], kv_out.at[z], kv_sems.at[z]).wait()


def cross_forward(n_p, splits, *refs):
    n_w = 2 * n_p
    scal, after_self, text, gain, bias, out_bias = refs[:6]
    pieces = refs[6 : 6 + n_w]
    hidden_t, text_t, kv_out, q_out, att_out, lse, after = refs[6 + n_w : 13 + n_w]
    kv_buf, weights, mask, scores, probs, sems, kv_sems = refs[13 + n_w :]
    rows = after_self.shape[0]
    count = text.shape[0]
    load_wait = load_start(own_and_others(pieces), weights, sems, scal, 0, D)
    cross_mask(scal, mask, rows, splits, count // TXT, True)
    normed, _ = normalize(after_self[...])
    wide = normed * gain[...]
    hidden = wide.astype(BF16)
    hidden_t[...] = wide.T.astype(BF16)
    for lo in range(0, count, 256):
        text_t[:, lo : lo + 256] = text[lo : lo + 256, :].astype(F32).T.astype(BF16)
    after[...] = after_self[...] + out_bias[...]

    def one(z, carry):
        load_wait(z)
        bias_row = bias[shard_index(scal, z, splits)]
        for lo in range(0, count, 256):
            part = nn(text[lo : lo + 256, :], weights[z, :, WIN : 5 * WIN])
            kv_buf[z, lo : lo + 256, :] = (part + bias_row[:, WIN : 5 * WIN]).astype(BF16)
        pair = nn(hidden, weights[z, :, 0:WIN]) + bias_row[:, 0:WIN]
        third = nn(hidden, weights[z, :, 3 * WIN : 4 * WIN]) + bias_row[:, 3 * WIN : 4 * WIN]
        third = keep(swap(third.astype(BF16).astype(F32)), False)
        queries = (
            jnp.concatenate([pair.astype(BF16).astype(F32), third], axis=1) * 0.125
        ).astype(BF16)
        q_out[z] = queries
        pltpu.make_async_copy(kv_buf.at[z], kv_out.at[z], kv_sems.at[z]).start()

        def kv(lo, hi, col):
            return kv_buf[z, lo:hi, col * WIN : (col + 1) * WIN]

        attended, totals = attend(queries, kv, mask, scores, probs, count)
        att_out[z] = attended
        lse[z] = totals
        after[...] += nt(attended, weights[z, :, 4 * WIN :])
        return carry

    lax.fori_loop(0, splits, one, 0)
    for z in range(splits):
        pltpu.make_async_copy(kv_buf.at[z], kv_out.at[z], kv_sems.at[z]).wait()


def feed_forward(n_p, splits, low, high, *refs):
    scal, after_cross, upstream, mod, in_bias, out_bias = refs[:6]
    pieces = refs[6 : 6 + n_p]
    rest = refs[6 + n_p :]
    n_o = 2 if n_p > 1 else 1
    first, last = low == 0, high == splits
    if not first:
        mlp_in, back_in, bias_in = rest[:3]
        rest = rest[3:]
    grads = rest[:n_o]
    in_bias_grad = rest[n_o]
    rest = rest[n_o + 1 :]
    if last:
        layer_out, d_after, out_bias_grad, sums, mlp, back = rest[:6]
        rest = rest[6:]
    else:
        mlp, back = rest[:2]
        rest = rest[2:]
    weights, gbuf, load_sems, store_sems = rest
    rows = after_cross.shape[0]
    load_wait = load_start([(pieces, 0)], weights, load_sems, scal)
    clip = own_clip(scal, rows, splits)
    normed, inverse = normalize(after_cross[...])
    scale = 1.0 + per_row(mod, 4, clip)
    wide = normed * scale + per_row(mod, 3, clip)
    hidden = wide.astype(BF16)
    hidden_t = wide.T.astype(BF16)
    gate = per_row(mod, 5, clip)
    given = upstream[...].astype(F32)
    low_wide = given * gate
    lowered = low_wide.astype(BF16)
    low_t = low_wide.T.astype(BF16)
    if first:
        mlp[...] = jnp.broadcast_to(out_bias[...], mlp.shape)
        back[...] = jnp.zeros_like(back)
        in_bias_grad[...] = jnp.zeros_like(in_bias_grad)
    else:
        mlp[...] = mlp_in[...]
        back[...] = back_in[...]
        in_bias_grad[...] = bias_in[...]

    def one(i, carry):
        load_wait(i)
        place = shard_index(scal, i + low, splits)
        pre = nn(hidden, weights[i, :, 0:D]) + in_bias[place]
        inner = 0.7978845608028654 * (pre + 0.044715 * (pre * pre * pre))
        curve = jnp.tanh(inner)
        half = 0.5 * (1.0 + curve)
        active = (pre * half).astype(BF16)
        slope = half + 0.5 * pre * (1.0 - curve * curve) * 0.7978845608028654 * (
            1.0 + 3.0 * 0.044715 * pre * pre
        )
        pre_grad = (slope * nn(lowered, weights[i, :, D:])).astype(BF16)
        in_bias_grad[place] = jnp.sum(pre_grad.astype(F32), axis=0, keepdims=True)
        mlp[...] += nt(active, weights[i, :, D:])
        back[...] += nt(pre_grad, weights[i, :, 0:D])
        gbuf[i, :, 0:D] = nn(hidden_t, pre_grad).astype(BF16)
        gbuf[i, :, D:] = nn(low_t, active).astype(BF16)
        for copy in store_copies(gbuf, i, grads, store_sems, scal):
            copy.start()
        return carry

    lax.fori_loop(0, high - low, one, 0)
    if last:
        out_bias_grad[...] = jnp.sum(lowered.astype(F32), axis=0, keepdims=True)
        branch = mlp[...]
        layer_out[...] = (after_cross[...] + gate * branch).astype(BF16)
        hidden_grad = back[...]
        d_after[...] = given + normalize_back(hidden_grad * scale, normed, inverse)
        clip_row = own_clip_row(scal, rows, splits)
        sums[:, 0:D] = clip_sums(clip_row, hidden_grad)
        sums[:, D : 2 * D] = clip_sums(clip_row, hidden_grad * normed)
        sums[:, 2 * D :] = clip_sums(clip_row, given * branch)
    for i in range(high - low):
        for copy in store_copies(gbuf, i, grads, store_sems, scal):
            copy.wait()


def cross_backward(n_p, splits, low, high, *refs):
    n_w = 2 * n_p
    scal, d_cross, after_self, hidden_t, text_t, gain, mod, branch, kv_in, q_in, att_in, lse = refs[
        :12
    ]
    pieces = refs[12 : 12 + n_w]
    rest = refs[12 + n_w :]
    first, last = low == 0, high == splits
    if not first:
        back_in, text_in, bias_in = rest[:3]
        rest = rest[3:]
    n_o = 2 if n_p > 1 else 1
    grads = rest[:n_o]
    bias_grad = rest[n_o]
    rest = rest[n_o + 1 :]
    if last:
        d_after, d_attn, text_out, row_grads, sums, back, text_back = rest[:7]
        rest = rest[7:]
    else:
        back, text_back = rest[:2]
        rest = rest[2:]
    weights, gbuf, mask, probs, dscore, key_grad, load_sems, store_sems = rest
    rows = after_self.shape[0]
    count = text_t.shape[1]
    load_wait = load_start(own_and_others(pieces), weights, load_sems, scal, low, D)
    cross_mask(scal, mask, rows, splits, count // TXT)
    given = d_cross[...].astype(BF16)
    given_wide = given.astype(F32)
    given_t = given_wide.T.astype(BF16)
    if first:
        back[...] = jnp.zeros_like(back)
        text_back[...] = jnp.zeros_like(text_back)
        bias_grad[...] = jnp.zeros_like(bias_grad)
    else:
        back[...] = back_in[...]
        text_back[...] = text_in[...]
        bias_grad[...] = bias_in[...]

    def one(i, carry):
        load_wait(i)
        z = i + low
        place = shard_index(scal, z, splits)

        def kv(lo, hi, col):
            return kv_in[z, lo:hi, col * WIN : (col + 1) * WIN]

        def put(lo, hi, k01, v01, k2, v2):
            key_grad[lo:hi, 0:WIN] = k01.astype(BF16)
            key_grad[lo:hi, WIN : 2 * WIN] = v01.astype(BF16)
            key_grad[lo:hi, 2 * WIN : 3 * WIN] = k2.astype(BF16)
            key_grad[lo:hi, 3 * WIN : 4 * WIN] = v2.astype(BF16)

        head_grad = nn(given, weights[i, :, 4 * WIN :]).astype(BF16)
        totals = [lse[z, h : h + 1, :] for h in range(3)]
        pair, third = attend_back(
            q_in[z], kv, att_in[z], head_grad, mask, totals, probs, dscore, count, put
        )
        pair, third = pair.astype(BF16), third.astype(BF16)
        part = nn(text_t[...], key_grad[...])
        out_part = nn(given_t, att_in[z])
        gbuf[i, :, 0:WIN] = nn(hidden_t[...], pair).astype(BF16)
        gbuf[i, :, WIN : 3 * WIN] = part[:, 0 : 2 * WIN].astype(BF16)
        gbuf[i, :, 3 * WIN : 4 * WIN] = (
            part[:, 2 * WIN : 3 * WIN] + nn(hidden_t[...], third)
        ).astype(BF16)
        gbuf[i, :, 4 * WIN : 5 * WIN] = (part[:, 3 * WIN :] + out_part[:, 0:WIN]).astype(BF16)
        gbuf[i, :, 5 * WIN :] = out_part[:, WIN:].astype(BF16)
        for copy in store_copies(gbuf, i, grads, store_sems, scal):
            copy.start()
        back[...] += nt(pair, weights[i, :, 0:WIN]) + nt(third, weights[i, :, 3 * WIN : 4 * WIN])
        for lo in range(0, count, 256):
            text_back[lo : lo + 256, :] += nt(
                key_grad[lo : lo + 256, :], weights[i, :, WIN : 5 * WIN]
            )
        key_sums = jnp.sum(key_grad[...].astype(F32), axis=0, keepdims=True)
        bias_grad[place, :, 0:WIN] = jnp.sum(pair.astype(F32), axis=0, keepdims=True)
        bias_grad[place, :, WIN : 3 * WIN] = key_sums[:, 0 : 2 * WIN]
        bias_grad[place, :, 3 * WIN : 4 * WIN] = key_sums[:, 2 * WIN : 3 * WIN] + jnp.sum(
            third.astype(F32), axis=0, keepdims=True
        )
        bias_grad[place, :, 4 * WIN : 5 * WIN] = key_sums[:, 3 * WIN :]
        bias_grad[place, :, 5 * WIN :] = jnp.zeros((1, WIN), F32)
        return carry

    lax.fori_loop(0, high - low, one, 0)

    def finish_stores():
        for i in range(high - low):
            for copy in store_copies(gbuf, i, grads, store_sems, scal):
                copy.wait()

    if not last:
        finish_stores()
        return
    row_grads[...] = jnp.zeros_like(row_grads)
    row_grads[0:1, :] = jnp.sum(given_wide, axis=0, keepdims=True)
    normed, inverse = normalize(after_self[...])
    hidden_grad = back[...]
    row_grads[1:2, :] = jnp.sum(hidden_grad * normed, axis=0, keepdims=True)
    total = d_cross[...] + normalize_back(hidden_grad * gain[...], normed, inverse)
    d_after[...] = total
    clip = own_clip(scal, rows, splits)
    d_attn[...] = (total * per_row(mod, 2, clip)).astype(BF16)
    sums[...] = clip_sums(own_clip_row(scal, rows, splits), total * branch[...])
    text_out[...] = text_back[...].astype(BF16)
    finish_stores()


def pack_small(table, own, cross, inner, given_sum, cross_rows, out_row, first, gate, second, out):
    n_dp = table.shape[1] // WIN
    splits, clips = out.shape[0], 3
    lane = lax.broadcasted_iota(jnp.int32, (D, n_dp * WIN), 0)

    def moved(value, which):
        choose = (lane == table[which : which + 1, :]).astype(F32).astype(BF16)
        high = value.astype(BF16).astype(F32)
        middle = (value - high).astype(BF16).astype(F32)
        parts = jnp.concatenate([high, middle, value - high - middle], axis=0).astype(BF16)
        found = nn(parts, choose)
        count = value.shape[0]
        return found[:count] + found[count : 2 * count] + found[2 * count :]

    def by_shard(ref):
        return jnp.concatenate([ref[z] for z in range(splits)], axis=0)

    both = moved(jnp.concatenate([by_shard(own), by_shard(cross)], axis=0), 0)
    heads = both[:splits] + pltpu.roll(both[splits:], 48, 1)
    hidden = moved(by_shard(inner), 1)
    rows = moved(
        jnp.concatenate(
            [given_sum, cross_rows[0:2, :], out_row[...]] + [jnp.zeros((4, D), F32)], axis=0
        ),
        2,
    )
    out[...] = jnp.zeros_like(out)
    for z in range(splits):
        for c in range(clips):
            for j in range(6):
                source, col = ((first, j), (gate, 0), (second, j - 3))[(j > 1) + (j > 2)]
                out[z, c * 6 + j : c * 6 + j + 1, :] = source[c : c + 1, col * D : (col + 1) * D]
        for d in range(n_dp):
            span = slice(d * WIN, (d + 1) * WIN)
            parts = [heads[z : z + 1, span], hidden[z : z + 1, span]]
            parts += [rows[r : r + 1, span] for r in range(4)]
            spot = clips * 6 + d
            out[z, spot : spot + 1, :] = jnp.concatenate(parts, axis=1)


def self_backward(n_p, splits, low, high, small, *refs):
    n_w = 2 * n_p
    scal = refs[0]
    frames = refs[1 : 1 + splits]
    given_ref, hidden_t, kv_in, q_in, att_in, lse = refs[1 + splits : 7 + splits]
    pieces = refs[7 + splits : 7 + splits + n_w]
    rest = refs[7 + splits + n_w :]
    first, last = low == 0, high == splits
    if not first:
        back_in, bias_in = rest[:2]
        rest = rest[2:]
    if small:
        table, cross_bias, inner_bias, cross_rows, out_row, gate, second = rest[:7]
        rest = rest[7:]
    n_o = 2 if n_p > 1 else 1
    grads = rest[:n_o]
    bias_grad = rest[n_o]
    rest = rest[n_o + 1 :]
    if last:
        own = rest[0]
        parts = rest[1:splits]
        row_grads, sums = rest[splits : splits + 2]
        rest = rest[splits + 2 :]
        if small:
            own_small, small_rows, back = rest[0], rest[1], rest[2]
            rest = rest[3:]
        else:
            back = rest[0]
            rest = rest[1:]
    else:
        back = rest[0]
        rest = rest[1:]
    weights, gbuf, mask, probs, dscore, key_grad, load_sems, store_sems = rest
    rows = frames[0].shape[0]
    count = rows * splits
    load_wait = load_start(own_and_others(pieces), weights, load_sems, scal, low)
    self_mask(scal, mask, rows, splits)
    given = given_ref[...]
    given_wide = given.astype(F32)
    given_t = given_wide.T.astype(BF16)
    if first:
        back[...] = jnp.zeros_like(back)
        bias_grad[...] = jnp.zeros_like(bias_grad)
    else:
        back[...] = back_in[...]
        bias_grad[...] = bias_in[...]

    def one(i, carry):
        load_wait(i)
        z = i + low
        place = shard_index(scal, z, splits)

        def kv(lo, hi, col):
            return kv_in[z, lo:hi, col * WIN : (col + 1) * WIN]

        def put(lo, hi, k01, v01, k2, v2):
            key_grad[lo:hi, 0:WIN] = k01.astype(BF16)
            key_grad[lo:hi, WIN : 2 * WIN] = v01.astype(BF16)
            key_grad[lo:hi, 2 * WIN : 3 * WIN] = k2.astype(BF16)
            key_grad[lo:hi, 3 * WIN : 4 * WIN] = v2.astype(BF16)

        head_grad = nn(given, weights[i, :, 4 * WIN :]).astype(BF16)
        totals = [lse[z, h : h + 1, :] for h in range(3)]
        pair, third = attend_back(
            q_in[z], kv, att_in[z], head_grad, mask, totals, probs, dscore, count, put
        )
        pair = pair.astype(BF16)
        key_grad[0:rows, 2 * WIN : 3 * WIN] = (
            key_grad[0:rows, 2 * WIN : 3 * WIN].astype(F32) + third
        ).astype(BF16)
        part = nn(hidden_t[...], key_grad[...])
        out_part = nn(given_t, att_in[z])
        gbuf[i, :, 0:WIN] = nn(hidden_t[:, 0:rows], pair).astype(BF16)
        gbuf[i, :, WIN : 4 * WIN] = part[:, 0 : 3 * WIN].astype(BF16)
        gbuf[i, :, 4 * WIN : 5 * WIN] = (part[:, 3 * WIN :] + out_part[:, 0:WIN]).astype(BF16)
        gbuf[i, :, 5 * WIN :] = out_part[:, WIN:].astype(BF16)
        for copy in store_copies(gbuf, i, grads, store_sems, scal):
            copy.start()
        for lo in range(0, count, 256):
            back[lo : lo + 256, :] += nt(
                key_grad[lo : lo + 256, :], weights[i, :, WIN : 5 * WIN]
            )
        back[0:rows, :] += nt(pair, weights[i, :, 0:WIN])
        key_sums = jnp.sum(key_grad[...].astype(F32), axis=0, keepdims=True)
        bias_grad[place, :, 0:WIN] = jnp.sum(pair.astype(F32), axis=0, keepdims=True)
        bias_grad[place, :, WIN : 5 * WIN] = key_sums
        bias_grad[place, :, 5 * WIN :] = jnp.zeros((1, WIN), F32)
        return carry

    lax.fori_loop(0, high - low, one, 0)

    def finish_stores():
        for i in range(high - low):
            for copy in store_copies(gbuf, i, grads, store_sems, scal):
                copy.wait()

    if not last:
        finish_stores()
        return
    given_sum = jnp.sum(given_wide, axis=0, keepdims=True)
    row_grads[...] = jnp.zeros_like(row_grads)
    row_grads[0:1, :] = given_sum
    shift = jnp.zeros((8, D), F32)
    scale = jnp.zeros((8, D), F32)
    for block in range(splits):
        value = back[block * rows : (block + 1) * rows, :]
        if block == 0:
            own[...] = value
        else:
            parts[block - 1][0:rows, :] = value.astype(BF16)
        normed, _ = normalize(frames[block][...].astype(F32))
        clip_row = own_clip_row(scal, rows, splits, block)
        shift = shift + clip_sums(clip_row, value)
        scale = scale + clip_sums(clip_row, value * normed)
    sums[:, 0:D] = shift
    sums[:, D:] = scale
    if small:
        pack_small(
            table,
            bias_grad,
            cross_bias,
            inner_bias,
            given_sum,
            cross_rows,
            out_row,
            sums,
            gate,
            second,
            small_rows,
        )
        for k in range(splits):
            value = small_rows[shard_index(scal, k, splits)]
            if k == 0:
                own_small[...] = value
            else:
                parts[k - 1][rows:, :] = value.astype(BF16)
    finish_stores()


def finish(splits, *refs):
    scal, frames, mod, d_after, own = refs[:5]
    parts = refs[5 : 4 + splits]
    out = refs[4 + splits]
    rows = frames.shape[0]
    value = own[...]
    for part in parts:
        value = value + part[0 : own.shape[0], :].astype(F32)
    normed, inverse = normalize(frames[...].astype(F32))
    scale = 1.0 + per_row(mod, 1, own_clip(scal, rows, splits))
    out[...] = d_after[...] + normalize_back(value * scale, normed, inverse)


def bias_table(n_dp):
    table = np.full((8, n_dp * WIN), -1, np.int32)
    for d in range(n_dp):
        for i in range(48):
            part, h, r = i // 24, i % 24 // 8, i % 8
            spot = d * 8 + r
            start = (h * HD if h < 2 else 3 * WIN) if part == 0 else (2 + h / 2) * WIN
            table[0, d * WIN + i] = (start if part == 0 or h < 2 else 4 * WIN) + spot
        for i in range(96):
            table[1, d * WIN + i] = i // 32 * 256 + d * 32 + i % 32
            table[2, d * WIN + i] = d * 96 + i
    return table


MEMORY = {"v": pltpu.VMEM, "s": pltpu.SMEM, "a": pl.ANY}


def call(body, inputs, outs, scratch, flops, name):
    moved = sum(a.size * a.dtype.itemsize for _, a in inputs)
    moved += sum(_size(s, t) for _, s, t in outs)
    return pl.pallas_call(
        body,
        out_shape=tuple(jax.ShapeDtypeStruct(s, t) for _, s, t in outs),
        in_specs=[pl.BlockSpec(memory_space=MEMORY[m]) for m, _ in inputs],
        out_specs=tuple(pl.BlockSpec(memory_space=MEMORY[m]) for m, _, _ in outs),
        scratch_shapes=scratch,
        compiler_params=pltpu.CompilerParams(vmem_limit_bytes=58 * 1024 * 1024),
        cost_estimate=pl.CostEstimate(flops=int(flops), bytes_accessed=int(moved), transcendentals=0),
        name=name,
    )(*[a for _, a in inputs])


def _size(shape, kind):
    total = jnp.dtype(kind).itemsize
    for s in shape:
        total *= s
    return total


class Ring:
    def __init__(self):
        self.n_dp = lax.axis_size("dp")
        self.splits = lax.axis_size("head")
        self.square = self.n_dp == 8
        if self.square:
            self.core = [(i, i ^ 1) for i in range(8)]
            self.first = [(i, i ^ (4 if i & 1 else 2)) for i in range(8)]
            self.second = [(i, i ^ (2 if i & 1 else 4)) for i in range(8)]

    def offsets(self):
        if not self.square:
            return [jnp.int32(0)]
        me = lax.axis_index("dp")
        rows = D // 8

        def kept(d):
            odd = d & 1
            return [d, d ^ (2 + 2 * odd), d ^ (4 - 2 * odd), d ^ 6]

        return [place * rows for place in kept(me) + kept(me ^ 1)]

    def z_pieces(self, value, far=None):
        n = self.splits
        return [value] + [
            lax.ppermute(value, "head", [(s, (s + k) % n) for s in range(n)])
            for k in (range(1, n) if far is None else far)
        ]

    def z_back(self, parts):
        n = self.splits
        return [
            lax.ppermute(parts[k - 1], "head", [(s, (s - k) % n) for s in range(n)])
            for k in range(1, n)
        ]

    def across(self, value, how):
        return lax.ppermute(value, "dp", how)

    def z_move(self, value, k):
        n = self.splits
        return lax.ppermute(value, "head", [(s, (s - k) % n) for s in range(n)])


class GradSum:
    def __init__(self, ring, grads):
        self.ring, self.grads = ring, list(grads)
        self.moved = []
        self.arrived = []
        if not ring.square:
            self.whole = lax.psum_scatter(grads[0][0], "dp", scatter_dimension=1, tiled=True)

    def across(self, value, how):
        if self.ring.square:
            self.moved.append(self.ring.across(value.astype(BF16), how))

    def block(self, i):
        value = self.grads[0][i].astype(F32) + self.moved[0][i].astype(F32)
        if len(self.moved) > 1:
            value = value + self.moved[1][i].astype(F32)
        return value

    def core(self):
        if self.ring.square:
            self.across(self.grads[1], self.ring.core)

    def second(self):
        if self.ring.square:
            self.across(self.block(slice(2, 4)), self.ring.second)

    def first(self):
        if self.ring.square:
            self.across(self.block(1), self.ring.first)

    def own(self, i):
        if not self.ring.square:
            return self.whole[i].astype(F32)
        value = self.grads[0][0, i].astype(F32) + self.moved[2][i].astype(F32)
        return value + self.moved[0][0, i].astype(F32) + self.moved[1][0, i].astype(F32)

    def shard(self, start):
        count = self.grads[0].shape[1]
        for i in range(count):
            k = i if start == 1 else start + i
            if k > 0:
                self.arrived.append(self.ring.z_move(self.own(i).astype(BF16), k))


def join_second(low, high):
    if not low.ring.square:
        return []
    part = slice(2, 4)
    both = jnp.concatenate([low.block(part), high.block(part)], axis=1)
    return [low.ring.across(both.astype(BF16), low.ring.second)]


def join_first(low, high):
    if not low.ring.square:
        return []
    both = jnp.concatenate([low.block(1), high.block(1)], axis=0)
    return [low.ring.across(both.astype(BF16), low.ring.first)]


def join_take(low, high, moved):
    count = low.grads[0].shape[1]
    for value in moved:
        low.moved.append(value[..., :count, :, :])
        high.moved.append(value[..., count:, :, :])


def join_shards(pairs):
    ring = pairs[0][0].ring
    half = ring.splits // 2
    return [
        ring.z_move(
            jnp.concatenate([pair[k // half].own(k % half) for pair in pairs], axis=1).astype(BF16),
            k,
        )
        for k in range(1, ring.splits)
    ]


class Gather:
    def __init__(self, ring, mine):
        self.ring = ring
        if ring.square:
            self.kept, self.other = [mine], []
        else:
            self.kept, self.other = [lax.all_gather(mine, "dp", axis=1, tiled=True)], []

    def sides(self):
        if self.ring.square:
            self.kept.append(self.ring.across(self.kept[0], self.ring.first))
            self.kept.append(self.ring.across(self.kept[0], self.ring.second))

    def corner(self):
        if self.ring.square:
            self.kept.append(self.ring.across(self.kept[1], self.ring.second))

    def core(self, *which):
        if self.ring.square:
            for i in which:
                self.other.append(self.ring.across(self.kept[i], self.ring.core))

    def pieces(self):
        return self.kept + self.other


def meet(*groups):
    flat = [v for group in groups for v in group]
    flat = list(lax.optimization_barrier(tuple(flat)))
    for group in groups:
        for i in range(len(group)):
            group[i] = flat.pop(0)


def to_layout(q, k, v, o):
    return jnp.concatenate(
        [
            q[:, :WIN],
            k[:, :WIN],
            v[:, :WIN],
            q[:, WIN:],
            k[:, WIN:],
            v[:, WIN:],
            o[:, WIN:],
            o[:, :WIN],
        ],
        axis=1,
    )


def from_layout(value):
    def pick(pair, third):
        return jnp.concatenate(
            [value[:, pair : pair + WIN], value[:, third : third + HD]], axis=1
        )

    return pick(0, 3 * WIN), pick(WIN, 3 * WIN + HD), pick(2 * WIN, 4 * WIN), pick(
        5 * WIN, 4 * WIN + HD
    )


def mod_gradients(ring, sums, clips):
    part = jnp.concatenate(sums, axis=1)[:clips]
    got = lax.all_to_all(
        jnp.broadcast_to(part[None], (ring.splits,) + part.shape), "head", 0, 0, tiled=True
    )
    low = jnp.sum(got, axis=0).astype(BF16)
    return lax.all_to_all(
        jnp.broadcast_to(low[None], (ring.n_dp,) + low.shape), "dp", 0, 0, tiled=True
    ).reshape(ring.n_dp * clips, -1)


def on_device(
    frames_in,
    step_embed,
    text_feats,
    clip_frames,
    text_tokens,
    out_grad,
    ada_weight,
    ada_bias,
    qkv_weight,
    qv_bias,
    attn_out_weight,
    attn_out_bias,
    cross_gain,
    cross_q_weight,
    cross_q_bias,
    cross_kv_weight,
    cross_v_bias,
    cross_out_weight,
    cross_out_bias,
    mlp_in_weight,
    mlp_in_bias,
    mlp_out_weight,
    mlp_out_bias,
):
    both = ("dp", "head")
    ring = Ring()
    n_dp, splits = ring.n_dp, ring.splits
    z_index = lax.axis_index("head")
    rows = frames_in.shape[0]
    count = rows * splits
    text_count = text_feats.shape[0]
    clips = clip_frames.shape[1]
    width = D // splits
    shard_rows = D // n_dp
    ends = jnp.cumsum(clip_frames[0])
    offs = ring.offsets()
    n_p = len(offs)
    scal = jnp.stack(
        [z_index, ends[0], ends[1], text_tokens[0, 0], text_tokens[0, 1], text_tokens[0, 2]]
        + [jnp.int32(0)] * 2
        + [o.astype(jnp.int32) for o in offs]
        + [jnp.int32(0)] * (S_LEN - S_OFF - n_p)
    ).astype(jnp.int32)

    shard_self = to_layout(
        qkv_weight[:, 0], qkv_weight[:, 1], qkv_weight[:, 2], attn_out_weight.T
    )
    shard_cross = to_layout(
        cross_q_weight, cross_kv_weight[:, 0], cross_kv_weight[:, 1], cross_out_weight.T
    )

    biases = [
        ada_bias,
        qv_bias.reshape(-1),
        attn_out_bias,
        cross_gain,
        cross_q_bias.reshape(-1),
        cross_v_bias.reshape(-1),
        cross_out_bias,
        mlp_in_bias.reshape(-1),
        mlp_out_bias,
    ]
    flat = jnp.concatenate(biases)
    cols = step_embed.reshape(clips, n_dp, shard_rows).transpose(1, 0, 2).reshape(n_dp, -1)
    sent = jnp.concatenate(
        [
            jnp.broadcast_to(flat[None, None], (n_dp, splits, flat.shape[0])),
            jnp.broadcast_to(cols[:, None], (n_dp, splits, cols.shape[1])),
        ],
        axis=2,
    ).reshape(n_dp * splits, -1)
    got = lax.all_to_all(sent, both, 0, 0, tiled=True)
    attn_shard = jnp.concatenate([shard_self, shard_cross], axis=1)
    attn_shards = ring.z_pieces(attn_shard)[1:]
    own_gather = Gather(ring, attn_shard[None])
    own_gather.sides()
    own_gather.corner()
    own_gather.core(0, 1, 2, 3)
    mlp_shard = jnp.concatenate([mlp_in_weight, mlp_out_weight.T], axis=1)
    held = [got]
    meet(held, attn_shards, own_gather.kept, own_gather.other)
    got = held[0].reshape(n_dp, splits, -1)
    step_cols = got[:, 0, flat.shape[0] :].reshape(n_dp * clips, shard_rows).astype(F32)
    silu_cols = jax.nn.silu(step_cols).astype(BF16)
    spots = []
    place = 0
    for b in biases:
        spots.append(got[:, :, place : place + b.shape[0]].astype(F32))
        place += b.shape[0]

    def over_dp(value):
        return value[:, 0].reshape(1, -1)

    def by_head(value, lead=1):
        n = value.shape[2] // (lead * 3)
        v = value.reshape(n_dp, splits, lead, 3, n).transpose(1, 2, 3, 0, 4)
        return v.reshape(splits, lead, 3 * n_dp * n)

    all_ada_bias = over_dp(spots[0])
    qv = by_head(spots[1], 2)
    nothing = jnp.zeros((splits, width), F32)
    bias_self = to_layout(qv[:, 0], nothing, qv[:, 1], nothing)[:, None]
    all_attn_bias = over_dp(spots[2])
    all_gain = over_dp(spots[3])
    bias_cross = to_layout(
        by_head(spots[4])[:, 0], nothing, by_head(spots[5])[:, 0], nothing
    )[:, None]
    all_cross_bias = over_dp(spots[6])
    all_in_bias = by_head(spots[7])
    all_out_bias = over_dp(spots[8])

    mod_part = jnp.dot(silu_cols, ada_weight, preferred_element_type=F32)
    mod_got = lax.all_to_all(mod_part.reshape(n_dp, clips, -1), "dp", 0, 0, tiled=True)

    half = splits // 2
    attn_gather = Gather(ring, jnp.stack(attn_shards))
    attn_gather.sides()
    frame_blocks = ring.z_pieces(frames_in)
    held = [mod_got, mlp_shard]
    meet(held, attn_gather.kept)
    mlp_shard = held[1]
    mod = jnp.sum(held[0], axis=0) + all_ada_bias
    attn_gather.corner()
    attn_gather.core(0, 1, 2, 3)
    mlp_shards = ring.z_pieces(mlp_shard, range(1, half))
    mlp_gathers = [Gather(ring, jnp.stack(mlp_shards))]
    mlp_gathers[0].sides()
    mlp_gathers[0].core(0)
    mlp_late = ring.z_pieces(mlp_shard, range(half, splits))[1:]

    def dma(n):
        return pltpu.SemaphoreType.DMA(n)

    def any_of(arrays):
        return [("a", a) for a in arrays]

    def vmem_of(arrays):
        return [("v", a) for a in arrays]

    piece_rows = D // n_p
    kept_out = [("a", (max(n_p // 2, 1), splits, piece_rows, D), BF16)] * (2 if n_p > 1 else 1)
    n_o = len(kept_out)
    shard_type = pltpu.VMEM((splits, D, D), BF16)

    results = list(call(
        partial(self_forward, n_p, splits),
        [("s", scal)]
        + vmem_of(frame_blocks)
        + vmem_of([mod, bias_self, all_attn_bias])
        + any_of(own_gather.pieces() + attn_gather.pieces()),
        [
            ("v", (D, count), BF16),
            ("a", (splits, count, 4 * WIN), BF16),
            ("v", (splits, rows, 2 * WIN), BF16),
            ("v", (splits, rows, 2 * WIN), BF16),
            ("v", (splits, 8, rows), F32),
            ("v", (rows, D), F32),
            ("v", (rows, D), F32),
        ],
        [
            pltpu.VMEM((count, D), BF16),
            pltpu.VMEM((splits, count, 4 * WIN), BF16),
            shard_type,
            pltpu.VMEM((rows, count), F32),
            pltpu.VMEM((rows, count), F32),
            pltpu.VMEM((rows, count), BF16),
            dma((n_p, splits)),
            dma((splits,)),
        ],
        22 * US,
        "self_forward",
    ))
    meet(
        results, mlp_gathers[0].kept, mlp_gathers[0].other, mlp_late, attn_gather.kept, attn_gather.other
    )
    hidden_one, self_kv, self_q, self_att, self_lse, attn_branch, after_self = results
    mlp_gathers[0].corner()
    mlp_gathers[0].core(1, 2)
    mlp_gathers.append(Gather(ring, jnp.stack(mlp_late)))
    mlp_gathers[1].sides()

    results = list(call(
        partial(cross_forward, n_p, splits),
        [("s", scal)]
        + vmem_of([after_self, text_feats, all_gain, bias_cross, all_cross_bias])
        + any_of(own_gather.pieces() + attn_gather.pieces()),
        [
            ("v", (D, rows), BF16),
            ("v", (D, text_count), BF16),
            ("a", (splits, text_count, 4 * WIN), BF16),
            ("v", (splits, rows, 2 * WIN), BF16),
            ("v", (splits, rows, 2 * WIN), BF16),
            ("v", (splits, 8, rows), F32),
            ("v", (rows, D), F32),
        ],
        [
            pltpu.VMEM((splits, text_count, 4 * WIN), BF16),
            shard_type,
            pltpu.VMEM((rows, text_count), F32),
            pltpu.VMEM((rows, text_count), F32),
            pltpu.VMEM((rows, text_count), BF16),
            dma((n_p, splits)),
            dma((splits,)),
        ],
        17 * US,
        "cross_forward",
    ))
    meet(results, mlp_gathers[0].kept, mlp_gathers[0].other, mlp_gathers[1].kept)
    hidden_two_t, text_t, cross_kv, cross_q, cross_att, cross_lse, after_cross = results
    mlp_gathers[0].core(3)
    mlp_gathers[1].corner()
    mlp_gathers[1].core(0, 1, 2)

    kept_half = [(m, (shape[0], half) + shape[2:], kind) for m, shape, kind in kept_out]
    kept_wide = [(m, shape[:3] + (2 * D,), kind) for m, shape, kind in kept_half]
    half_type = pltpu.VMEM((half, D, D), BF16)

    def back_scratch(keys):
        return [
            half_type,
            half_type,
            pltpu.VMEM((keys, rows), F32),
            pltpu.VMEM((3, keys, rows), BF16),
            pltpu.VMEM((3, keys, rows), BF16),
            pltpu.VMEM((keys, 4 * WIN), BF16),
            dma((n_p, half)),
            dma((n_p, half)),
        ]

    bias_type = [("v", (splits, 1, D), F32)]
    mlp_args = [after_cross, out_grad, mod, all_in_bias, all_out_bias]
    mlp_scratch = [
        pltpu.VMEM((half, D, 2 * D), BF16),
        pltpu.VMEM((half, D, 2 * D), BF16),
        dma((n_p, half)),
        dma((n_p, half)),
    ]
    results = call(
        partial(feed_forward, n_p, splits, 0, half),
        [("s", scal)] + vmem_of(mlp_args) + any_of(mlp_gathers[0].pieces()),
        kept_wide + bias_type + [("v", (rows, D), F32)] * 2,
        mlp_scratch,
        9 * US,
        "feed_forward_first",
    )
    results = list(results)
    meet(results, mlp_gathers[1].kept, mlp_gathers[1].other)
    mlp_gathers[1].core(3)
    sum_mlp = [GradSum(ring, results[:n_o])]
    in_bias_grad, mlp_state, mlp_back = results[n_o:]
    sum_mlp[0].core()
    results = call(
        partial(feed_forward, n_p, splits, half, splits),
        [("s", scal)]
        + vmem_of(mlp_args)
        + any_of(mlp_gathers[1].pieces())
        + vmem_of([mlp_state, mlp_back, in_bias_grad]),
        kept_wide
        + bias_type
        + [
            ("v", (rows, D), BF16),
            ("v", (rows, D), F32),
            ("v", (1, D), F32),
            ("v", (8, 3 * D), F32),
        ],
        [pltpu.VMEM((rows, D), F32), pltpu.VMEM((rows, D), F32)] + mlp_scratch,
        10 * US,
        "feed_forward_last",
    )
    results = list(results)
    meet(results, sum_mlp[0].moved)
    sum_mlp.append(GradSum(ring, results[:n_o]))
    in_bias_grad, layer_out, d_after_cross, out_bias_grad, sums_two = results[n_o:]
    sum_mlp[0].second()
    sum_mlp[1].core()
    cross_args = [
        d_after_cross,
        after_self,
        hidden_two_t,
        text_t,
        all_gain,
        mod,
        attn_branch,
        cross_kv,
        cross_q,
        cross_att,
        cross_lse,
    ]
    cross_state = [("v", (rows, D), F32), ("v", (text_count, D), F32)]
    results = call(
        partial(cross_backward, n_p, splits, 0, half),
        [("s", scal)] + vmem_of(cross_args) + any_of(own_gather.pieces() + attn_gather.pieces()),
        kept_half + bias_type + cross_state,
        back_scratch(text_count),
        14 * US,
        "cross_backward_first",
    )
    results = list(results)
    meet(results, sum_mlp[0].moved, sum_mlp[1].moved)
    sum_cross = [GradSum(ring, results[:n_o])]
    cross_bias_grad, cross_back, text_back = results[n_o:]
    sum_mlp[0].first()
    sum_mlp[1].second()
    sum_cross[0].core()
    results = call(
        partial(cross_backward, n_p, splits, half, splits),
        [("s", scal)]
        + vmem_of(cross_args)
        + any_of(own_gather.pieces() + attn_gather.pieces())
        + vmem_of([cross_back, text_back, cross_bias_grad]),
        kept_half
        + bias_type
        + [
            ("v", (rows, D), F32),
            ("v", (rows, D), BF16),
            ("v", (text_count, D), BF16),
            ("v", (8, D), F32),
            ("v", (8, D), F32),
        ],
        [pltpu.VMEM((rows, D), F32), pltpu.VMEM((text_count, D), F32)] + back_scratch(text_count),
        15 * US,
        "cross_backward_last",
    )
    results = list(results)
    meet(results, sum_mlp[0].moved, sum_mlp[1].moved, sum_cross[0].moved)
    sum_cross.append(GradSum(ring, results[:n_o]))
    cross_bias_grad, d_after_self, d_attn, text_out, cross_rows, gate_sums = results[n_o:]
    sum_mlp[0].shard(1)
    sum_mlp[1].first()
    sum_cross[0].second()
    sum_cross[1].core()
    text_got = lax.all_to_all(
        text_out.reshape(splits, text_count // splits, D), "head", 0, 0, tiled=True
    )
    self_args = [d_attn, hidden_one, self_kv, self_q, self_att, self_lse]
    results = call(
        partial(self_backward, n_p, splits, 0, half, False),
        [("s", scal)] + vmem_of(frame_blocks) + vmem_of(self_args) + any_of(own_gather.pieces() + attn_gather.pieces()),
        kept_half + bias_type + [("v", (count, D), F32)],
        back_scratch(count),
        17 * US,
        "self_backward_first",
    )
    results = list(results)
    meet(
        results,
        sum_mlp[1].moved,
        sum_cross[0].moved,
        sum_cross[1].moved,
    )
    sum_self = [GradSum(ring, results[:n_o])]
    self_bias_grad, self_back = results[n_o:]
    sum_mlp[1].shard(2)
    sum_cross[1].second()
    sum_self[0].core()
    small_args, small_outs, small_scratch, small_count = [], [], [], 0
    if ring.square:
        small_count = 32
        small_args = [jnp.asarray(bias_table(n_dp)), cross_bias_grad, in_bias_grad]
        small_args += [cross_rows, out_bias_grad, gate_sums, sums_two]
        small_outs = [("v", (small_count, D), F32)]
        small_scratch = [pltpu.VMEM((splits, small_count, D), F32)]
    results = call(
        partial(self_backward, n_p, splits, half, splits, ring.square),
        [("s", scal)]
        + vmem_of(frame_blocks)
        + vmem_of(self_args)
        + any_of(own_gather.pieces() + attn_gather.pieces())
        + vmem_of([self_back, self_bias_grad] + small_args),
        kept_half
        + bias_type
        + [("v", (rows, D), F32)]
        + [("v", (rows + small_count, D), BF16)] * (splits - 1)
        + [("v", (8, D), F32), ("v", (8, 2 * D), F32)]
        + small_outs,
        small_scratch + [pltpu.VMEM((count, D), F32)] + back_scratch(count),
        18 * US,
        "self_backward_last",
    )
    results = list(results)
    held = [in_bias_grad, out_bias_grad, cross_bias_grad, cross_rows, gate_sums, sums_two]
    held.append(text_got)
    meet(
        results,
        held,
        sum_mlp[0].arrived,
        sum_mlp[1].arrived,
        sum_cross[0].moved,
        sum_cross[1].moved,
        sum_self[0].moved,
    )
    sum_self.append(GradSum(ring, results[:n_o]))
    self_bias_grad, own_part = results[n_o : n_o + 2]
    parts = results[n_o + 2 : n_o + 1 + splits]
    self_rows, sums_one = results[n_o + 1 + splits : n_o + 3 + splits]
    sum_self[1].core()
    arrived = ring.z_back(parts)
    in_bias_grad, out_bias_grad, cross_bias_grad, cross_rows, gate_sums, sums_two, text_got = held
    early, late = arrived[:1], arrived[1:]
    meet(sum_self[1].moved, sum_cross[1].moved, early)
    far = join_second(*sum_self)
    near_cross = join_first(*sum_cross)
    meet(far, near_cross)
    join_take(*sum_self, far)
    join_take(*sum_cross, near_cross)
    near = join_first(*sum_self)
    meet(late, near)
    arrived = early + late
    join_take(*sum_self, near)
    last = join_shards([sum_cross, sum_self])
    if ring.square:
        small = results[-1] + sum(part[rows:].astype(F32) for part in arrived)
        mod_low = small[: 6 * clips].astype(BF16).astype(F32)
        sent = jnp.concatenate(
            [
                jnp.broadcast_to(mod_low[None], (n_dp,) + mod_low.shape),
                small[6 * clips : 6 * clips + n_dp, None],
            ],
            axis=1,
        )
        held = [lax.all_to_all(sent, "dp", 0, 0, tiled=True)]
    if ring.square:
        mod_all = held[0][:, : 6 * clips].reshape(n_dp * clips, -1).astype(BF16)
        bias_sum = jnp.sum(held[0][:, 6 * clips], axis=0)
        places = [0, 24, 2 * WIN, 4 * WIN, 48, 72, 3 * WIN, WIN, 5 * WIN]
    else:
        mod_all = mod_gradients(ring, [sums_one, gate_sums, sums_two], clips)
    step_part = lax.dot_general(
        mod_all, ada_weight, (((1,), (1,)), ((), ())), preferred_element_type=F32
    )
    (frames_grad,) = call(
        partial(finish, splits),
        [("s", scal)] + vmem_of([frames_in, mod, d_after_self, own_part]) + vmem_of(arrived),
        [("v", (rows, D), F32)],
        [],
        3 * US,
        "finish",
    )
    text_grad = jnp.sum(text_got.astype(F32), axis=0)

    grad_ada = lax.dot_general(
        silu_cols, mod_all, (((0,), (0,)), ((), ())), preferred_element_type=F32
    )
    dp_index = lax.axis_index("dp")
    bias_width = ada_bias.shape[0]
    grad_ada_bias = jnp.sum(
        lax.dynamic_slice_in_dim(mod_all, dp_index * bias_width, bias_width, 1).astype(F32), axis=0
    )
    step_got = lax.all_to_all(step_part.reshape(n_dp, clips, shard_rows), "dp", 0, 0, tiled=True)
    step_got = [step_got]
    meet(last, step_got)
    (step_got,) = step_got
    total_cross, total_self = (
        pair[0].own(0) + sum(part[:, i * D : (i + 1) * D].astype(F32) for part in last)
        for i, pair in enumerate((sum_cross, sum_self))
    )
    step_value = step_embed.astype(F32)
    _, silu_pull = jax.vjp(jax.nn.silu, step_value)
    step_grad = silu_pull(step_got.transpose(1, 0, 2).reshape(clips, D))[0]

    def spread(value):
        v = value.reshape(n_dp, 1, D // n_dp)
        return jnp.broadcast_to(v, (n_dp, splits, D // n_dp))

    def heads_out(value):
        n = value.shape[1] // (3 * n_dp)
        return value.reshape(splits, 3, n_dp, n).transpose(2, 0, 1, 3).reshape(n_dp, splits, 3 * n)

    sq, _, sv, _ = from_layout(self_bias_grad[:, 0])
    cq, _, cv, _ = from_layout(cross_bias_grad[:, 0])
    entries = [
        heads_out(sq),
        heads_out(sv),
        spread(self_rows[0]),
        spread(cross_rows[1]),
        heads_out(cq),
        heads_out(cv),
        spread(cross_rows[0]),
        heads_out(in_bias_grad[:, 0]),
        spread(out_bias_grad[0]),
    ]
    if not ring.square:
        packed = jnp.concatenate(entries, axis=2)
        places = [sum(e.shape[2] for e in entries[:i]) for i in range(len(entries))]
        bias_sum = jnp.sum(
            lax.all_to_all(packed.reshape(n_dp * splits, -1), both, 0, 0, tiled=True), axis=0
        )
    bias_out = [bias_sum[p : p + e.shape[2]] for p, e in zip(places, entries)]

    total_mlp = sum_mlp[0].own(0) + sum(
        part.astype(F32) for part in sum_mlp[0].arrived + sum_mlp[1].arrived
    )
    gq, gk, gv, go = from_layout(total_self)
    hq, hk, hv, ho = from_layout(total_cross)
    return (
        layer_out,
        frames_grad,
        step_grad,
        text_grad,
        grad_ada,
        grad_ada_bias,
        jnp.stack([gq, gk, gv], axis=1),
        jnp.stack([bias_out[0], bias_out[1]]).reshape(qv_bias.shape),
        go.T,
        bias_out[2],
        bias_out[3],
        hq,
        bias_out[4].reshape(cross_q_bias.shape),
        jnp.stack([hk, hv], axis=1),
        bias_out[5].reshape(cross_v_bias.shape),
        ho.T,
        bias_out[6],
        total_mlp[:, :D],
        bias_out[7].reshape(mlp_in_bias.shape),
        total_mlp[:, D:].T,
        bias_out[8],
    )


def solution(mesh):
    rows_all, by_dp = P(("dp", "head"), None), P("dp", None)
    head_dp, dp_head = P("head", "dp"), P("dp", "head")
    dp_three, vector = P("dp", None, "head"), P("dp")
    params = (
        by_dp,
        vector,
        dp_three,
        P(None, "head", "dp"),
        head_dp,
        vector,
        vector,
        dp_head,
        head_dp,
        dp_three,
        head_dp,
        head_dp,
        vector,
        dp_head,
        head_dp,
        head_dp,
        vector,
    )
    return jax.shard_map(
        on_device,
        mesh=mesh,
        in_specs=(rows_all, by_dp, by_dp, by_dp, by_dp, rows_all) + params,
        out_specs=(rows_all, rows_all, by_dp, rows_all) + params,
        check_vma=False,
    )
```

```python
from functools import partial

import jax
import jax.numpy as jnp
import numpy as np
from jax import lax
from jax.experimental import pallas as pl
from jax.experimental.pallas import tpu as pltpu
from jax.sharding import PartitionSpec as P

D = 768
HD = 64
TXT = 256
WIN = 128
EPS = 1e-06
NEG = -1e30
F32 = jnp.float32
BF16 = jnp.bfloat16
HIGH = lax.Precision.HIGHEST
S_Z, S_END, S_TOK, S_OFF = 0, 1, 3, 8
S_LEN = 16
US = 1.15e9


def nn(a, b):
    return lax.dot_general(a, b, (((1,), (0,)), ((), ())), preferred_element_type=F32)


def nt(a, b):
    return lax.dot_general(a, b, (((1,), (1,)), ((), ())), preferred_element_type=F32)


def tn(a, b):
    return lax.dot_general(a, b, (((0,), (0,)), ((), ())), preferred_element_type=F32)


def normalize(v):
    centered = v - jnp.mean(v, axis=-1, keepdims=True)
    inverse = lax.rsqrt(jnp.mean(centered * centered, axis=-1, keepdims=True) + EPS)
    return centered * inverse, inverse


def normalize_back(u, normed, inverse):
    return inverse * (
        u
        - jnp.mean(u, axis=-1, keepdims=True)
        - normed * jnp.mean(u * normed, axis=-1, keepdims=True)
    )


def clip_of(position, scal):
    return (position >= scal[S_END]).astype(jnp.int32) + (position >= scal[S_END + 1]).astype(
        jnp.int32
    )


def frame_position(index, block, rows, splits, scal):
    return lax.rem(scal[S_Z] - block + splits, splits) * rows + index


def per_row(mod_ref, part, clip):
    cols = slice(part * D, (part + 1) * D)
    first, second, third = (mod_ref[c : c + 1, cols] for c in range(3))
    return jnp.where(clip == 0, first, jnp.where(clip == 1, second, third))


def clip_sums(clip_row, value):
    which = lax.broadcasted_iota(jnp.int32, (8, clip_row.shape[1]), 0)
    choose = (which == clip_row).astype(F32)
    return lax.dot_general(
        choose, value, (((1,), (0,)), ((), ())), precision=HIGH, preferred_element_type=F32
    )


def lanes(rows, low):
    lane = lax.broadcasted_iota(jnp.int32, (rows, WIN), 1)
    return lane < HD if low else lane >= HD


def keep(value, low):
    return jnp.where(lanes(value.shape[0], low), value, jnp.zeros_like(value))


def swap(value):
    return pltpu.roll(value, HD, 1)


def load_start(groups, buffer, sems, scal, low=0, col=0):
    width = buffer.shape[2]

    def place(j, rows):
        return pl.ds(pl.multiple_of(scal[S_OFF + j], 32), rows)

    for z in range(buffer.shape[0]):
        for pieces, start in groups:
            at = low + z - start
            if 0 <= at < pieces[0].shape[0]:
                for j, piece in enumerate(pieces):
                    pltpu.make_async_copy(
                        piece.at[at, :, col : col + width],
                        buffer.at[z, place(j, piece.shape[1]), :],
                        sems.at[j, z],
                    ).start()

    def wait(z):
        for j, piece in enumerate(groups[0][0]):
            here = buffer.at[z, place(j, piece.shape[1]), :]
            pltpu.make_async_copy(here, here, sems.at[j, z]).wait()

    return wait


def own_and_others(pieces):
    half = len(pieces) // 2
    return [(pieces[:half], 0), (pieces[half:], 1)]


def store_copies(buffer, z, outs, sems, scal, col=0, first=0):
    copies = []
    j = 0
    for out in outs:
        for i in range(out.shape[0]):
            rows = out.shape[2]
            start = pl.multiple_of(scal[S_OFF + j], 32)
            copies.append(
                pltpu.make_async_copy(
                    buffer.at[z, pl.ds(start, rows), col : col + out.shape[3]],
                    out.at[i, z],
                    sems.at[first + j, z],
                )
            )
            j += 1
    return copies


def attend(queries, kv, mask, scores, probs, count):
    rows = queries.shape[0]
    step = 256
    outs = []
    lane = lax.broadcasted_iota(jnp.int32, (rows, WIN), 1)
    totals = jnp.zeros((rows, WIN), F32)
    for h in range(3):
        if h < 2:
            query = keep(queries[:, :WIN], h == 0)
            kcol, vcol = 0, 1
        else:
            query = queries[:, WIN:]
            kcol, vcol = 2, 3
        top = None
        for lo in range(0, count, step):
            part = nt(query, kv(lo, lo + step, kcol)) + mask[:, lo : lo + step]
            scores[:, lo : lo + step] = part
            top = part if top is None else jnp.maximum(top, part)
        peak = jnp.max(top, axis=1, keepdims=True)
        wide = jnp.zeros((rows, step), F32)
        for lo in range(0, count, step):
            part = jnp.exp(scores[:, lo : lo + step] - peak)
            wide = wide + part
            probs[:, lo : lo + step] = part.astype(BF16)
        total = jnp.sum(wide, axis=1, keepdims=True)
        outs.append(nn(probs[:, 0:count], kv(0, count, vcol)) * (1.0 / total))
        totals = jnp.where(lane == h, peak + jnp.log(total), totals)
    pair = jnp.where(lane < HD, outs[0], outs[1])
    attended = jnp.concatenate([keep(swap(outs[2]), False), pair], axis=1)
    return attended.astype(BF16), totals.T[0:8, :]


def attend_back(queries, kv, attended, out_grad, mask, totals, probs, dscore, count, put):
    rows = queries.shape[0]
    step = 256
    wide = out_grad.astype(F32)
    row = lax.broadcasted_iota(jnp.int32, (8, 2 * WIN), 0)
    part = lax.broadcasted_iota(jnp.int32, (8, 2 * WIN), 1) // HD
    choose = ((part == row + 2) & (row < 2)) | ((part == 1) & (row == 2))
    deltas = lax.dot_general(
        choose.astype(F32),
        wide * attended.astype(F32),
        (((1,), (1,)), ((), ())),
        precision=HIGH,
        preferred_element_type=F32,
    )
    second = keep(swap(wide[:, :WIN]), True).astype(BF16)
    query_parts = []
    heads = []
    key_t = [kv(0, count, col).astype(F32).T.astype(BF16) for col in (0, 2)]
    for h in range(3):
        if h < 2:
            query = keep(queries[:, :WIN], h == 0)
            given = keep(out_grad[:, WIN:], h == 0)
            kcol, vcol = 0, 1
        else:
            query, given = queries[:, WIN:], second
            kcol, vcol = 2, 3
        heads.append((query, given))
        total, delta = totals[h], deltas[h : h + 1, :]
        for lo in range(0, count, step):
            hi = lo + step
            weights = jnp.exp(nt(kv(lo, hi, kcol), query) + mask[lo:hi, :] - total)
            probs[h, lo:hi, :] = weights.astype(BF16)
            weight_grad = nt(kv(lo, hi, vcol), given)
            dscore[h, lo:hi, :] = (weights * (weight_grad - delta)).astype(BF16)
        query_parts.append(nn(key_t[h // 2], dscore[h, 0:count, :]))
    for lo in range(0, count, step):
        hi = lo + step
        put(
            lo,
            hi,
            nn(dscore[0, lo:hi, :], heads[0][0]) + nn(dscore[1, lo:hi, :], heads[1][0]),
            nn(probs[0, lo:hi, :], heads[0][1]) + nn(probs[1, lo:hi, :], heads[1][1]),
            nn(dscore[2, lo:hi, :], heads[2][0]),
            nn(probs[2, lo:hi, :], heads[2][1]),
        )
    both = jnp.concatenate(
        [
            query_parts[0][:HD],
            query_parts[1][HD:],
            query_parts[2][HD:],
            jnp.zeros((HD, rows), F32),
        ],
        axis=0,
    )
    both = (both * 0.125).T
    return both[:, :WIN], both[:, WIN:]


def self_mask(scal, mask, rows, splits, forward=False):
    clip = own_clip if forward else own_clip_row
    query = clip(scal, rows, splits)
    for block in range(splits):
        span = slice(block * rows, (block + 1) * rows)
        key = (own_clip_row if forward else own_clip)(scal, rows, splits, block)
        value = jnp.where(key == query, 0.0, NEG)
        if forward:
            mask[:, span] = value
        else:
            mask[span, :] = value


def cross_mask(scal, mask, rows, splits, clips, forward=False):
    query = (own_clip if forward else own_clip_row)(scal, rows, splits)
    shape = (1, TXT) if forward else (TXT, 1)
    slot = lax.broadcasted_iota(jnp.int32, shape, 1 if forward else 0)
    for c in range(clips):
        span = slice(c * TXT, (c + 1) * TXT)
        value = jnp.where((query == c) & (slot < scal[S_TOK + c]), 0.0, NEG)
        if forward:
            mask[:, span] = value
        else:
            mask[span, :] = value


def own_clip(scal, rows, splits, block=0):
    return clip_of(
        frame_position(lax.broadcasted_iota(jnp.int32, (rows, 1), 0), block, rows, splits, scal),
        scal,
    )


def own_clip_row(scal, rows, splits, block=0):
    return clip_of(
        frame_position(lax.broadcasted_iota(jnp.int32, (1, rows), 1), block, rows, splits, scal),
        scal,
    )


def shard_index(scal, z, splits):
    return lax.rem(scal[S_Z] - z + splits, splits)


def self_forward(n_p, splits, *refs):
    n_w = 2 * n_p
    scal = refs[0]
    frames = refs[1 : 1 + splits]
    mod, bias, out_bias = refs[1 + splits : 4 + splits]
    pieces = refs[4 + splits : 4 + splits + n_w]
    hidden_t, kv_out, q_out, att_out, lse, branch_out, after = refs[
        4 + splits + n_w : 11 + splits + n_w
    ]
    hidden, kv_buf, weights, mask, scores, probs, sems, kv_sems = refs[11 + splits + n_w :]
    rows = frames[0].shape[0]
    count = rows * splits
    load_wait = load_start(own_and_others(pieces), weights, sems, scal)
    self_mask(scal, mask, rows, splits, True)
    for block in range(splits):
        clip = own_clip(scal, rows, splits, block)
        normed, _ = normalize(frames[block][...].astype(F32))
        value = normed * (1.0 + per_row(mod, 1, clip)) + per_row(mod, 0, clip)
        hidden[block * rows : (block + 1) * rows, :] = value.astype(BF16)
        hidden_t[:, block * rows : (block + 1) * rows] = value.T.astype(BF16)
    branch_out[...] = jnp.broadcast_to(out_bias[...], branch_out.shape)

    def one(z, carry):
        load_wait(z)
        bias_row = bias[shard_index(scal, z, splits)]
        for block in range(splits):
            span = slice(block * rows, (block + 1) * rows)
            part = nn(hidden[span, :], weights[z, :, WIN : 5 * WIN]) + bias_row[:, WIN : 5 * WIN]
            kv_buf[z, span, :] = part.astype(BF16)
            if block == 0:
                third = keep(swap(part[:, 2 * WIN : 3 * WIN].astype(BF16).astype(F32)), False)
        pair = nn(hidden[0:rows, :], weights[z, :, 0:WIN]) + bias_row[:, 0:WIN]
        queries = (
            jnp.concatenate([pair.astype(BF16).astype(F32), third], axis=1) * 0.125
        ).astype(BF16)
        q_out[z] = queries
        pltpu.make_async_copy(kv_buf.at[z], kv_out.at[z], kv_sems.at[z]).start()

        def kv(lo, hi, col):
            return kv_buf[z, lo:hi, col * WIN : (col + 1) * WIN]

        attended, totals = attend(queries, kv, mask, scores, probs, count)
        att_out[z] = attended
        lse[z] = totals
        branch_out[...] += nt(attended, weights[z, :, 4 * WIN :])
        return carry

    lax.fori_loop(0, splits, one, 0)
    clip = own_clip(scal, rows, splits)
    after[...] = frames[0][...].astype(F32) + per_row(mod, 2, clip) * branch_out[...]
    for z in range(splits):
        pltpu.make_async_copy(kv_buf.at[z], kv_out.at[z], kv_sems.at[z]).wait()


def cross_forward(n_p, splits, *refs):
    n_w = 2 * n_p
    scal, after_self, text, gain, bias, out_bias = refs[:6]
    pieces = refs[6 : 6 + n_w]
    hidden_t, text_t, kv_out, q_out, att_out, lse, after = refs[6 + n_w : 13 + n_w]
    kv_buf, weights, mask, scores, probs, sems, kv_sems = refs[13 + n_w :]
    rows = after_self.shape[0]
    count = text.shape[0]
    load_wait = load_start(own_and_others(pieces), weights, sems, scal, 0, D)
    cross_mask(scal, mask, rows, splits, count // TXT, True)
    normed, _ = normalize(after_self[...])
    wide = normed * gain[...]
    hidden = wide.astype(BF16)
    hidden_t[...] = wide.T.astype(BF16)
    for lo in range(0, count, 256):
        text_t[:, lo : lo + 256] = text[lo : lo + 256, :].astype(F32).T.astype(BF16)
    after[...] = after_self[...] + out_bias[...]

    def one(z, carry):
        load_wait(z)
        bias_row = bias[shard_index(scal, z, splits)]
        for lo in range(0, count, 256):
            part = nn(text[lo : lo + 256, :], weights[z, :, WIN : 5 * WIN])
            kv_buf[z, lo : lo + 256, :] = (part + bias_row[:, WIN : 5 * WIN]).astype(BF16)
        pair = nn(hidden, weights[z, :, 0:WIN]) + bias_row[:, 0:WIN]
        third = nn(hidden, weights[z, :, 3 * WIN : 4 * WIN]) + bias_row[:, 3 * WIN : 4 * WIN]
        third = keep(swap(third.astype(BF16).astype(F32)), False)
        queries = (
            jnp.concatenate([pair.astype(BF16).astype(F32), third], axis=1) * 0.125
        ).astype(BF16)
        q_out[z] = queries
        pltpu.make_async_copy(kv_buf.at[z], kv_out.at[z], kv_sems.at[z]).start()

        def kv(lo, hi, col):
            return kv_buf[z, lo:hi, col * WIN : (col + 1) * WIN]

        attended, totals = attend(queries, kv, mask, scores, probs, count)
        att_out[z] = attended
        lse[z] = totals
        after[...] += nt(attended, weights[z, :, 4 * WIN :])
        return carry

    lax.fori_loop(0, splits, one, 0)
    for z in range(splits):
        pltpu.make_async_copy(kv_buf.at[z], kv_out.at[z], kv_sems.at[z]).wait()


def feed_forward(n_p, splits, low, high, *refs):
    scal, after_cross, upstream, mod, in_bias, out_bias = refs[:6]
    pieces = refs[6 : 6 + n_p]
    rest = refs[6 + n_p :]
    n_o = 2 if n_p > 1 else 1
    first, last = low == 0, high == splits
    if not first:
        mlp_in, back_in, bias_in = rest[:3]
        rest = rest[3:]
    grads = rest[:n_o]
    in_bias_grad = rest[n_o]
    rest = rest[n_o + 1 :]
    if last:
        layer_out, d_after, out_bias_grad, sums, mlp, back = rest[:6]
        rest = rest[6:]
    else:
        mlp, back = rest[:2]
        rest = rest[2:]
    weights, gbuf, load_sems, store_sems = rest
    rows = after_cross.shape[0]
    load_wait = load_start([(pieces, 0)], weights, load_sems, scal)
    clip = own_clip(scal, rows, splits)
    normed, inverse = normalize(after_cross[...])
    scale = 1.0 + per_row(mod, 4, clip)
    wide = normed * scale + per_row(mod, 3, clip)
    hidden = wide.astype(BF16)
    hidden_t = wide.T.astype(BF16)
    gate = per_row(mod, 5, clip)
    given = upstream[...].astype(F32)
    low_wide = given * gate
    lowered = low_wide.astype(BF16)
    low_t = low_wide.T.astype(BF16)
    if first:
        mlp[...] = jnp.broadcast_to(out_bias[...], mlp.shape)
        back[...] = jnp.zeros_like(back)
        in_bias_grad[...] = jnp.zeros_like(in_bias_grad)
    else:
        mlp[...] = mlp_in[...]
        back[...] = back_in[...]
        in_bias_grad[...] = bias_in[...]

    def one(i, carry):
        load_wait(i)
        place = shard_index(scal, i + low, splits)
        pre = nn(hidden, weights[i, :, 0:D]) + in_bias[place]
        inner = 0.7978845608028654 * (pre + 0.044715 * (pre * pre * pre))
        curve = jnp.tanh(inner)
        half = 0.5 * (1.0 + curve)
        active = (pre * half).astype(BF16)
        slope = half + 0.5 * pre * (1.0 - curve * curve) * 0.7978845608028654 * (
            1.0 + 3.0 * 0.044715 * pre * pre
        )
        pre_grad = (slope * nn(lowered, weights[i, :, D:])).astype(BF16)
        in_bias_grad[place] = jnp.sum(pre_grad.astype(F32), axis=0, keepdims=True)
        mlp[...] += nt(active, weights[i, :, D:])
        back[...] += nt(pre_grad, weights[i, :, 0:D])
        gbuf[i, :, 0:D] = nn(hidden_t, pre_grad).astype(BF16)
        gbuf[i, :, D:] = nn(low_t, active).astype(BF16)
        for copy in store_copies(gbuf, i, grads, store_sems, scal):
            copy.start()
        return carry

    lax.fori_loop(0, high - low, one, 0)
    if last:
        out_bias_grad[...] = jnp.sum(lowered.astype(F32), axis=0, keepdims=True)
        branch = mlp[...]
        layer_out[...] = (after_cross[...] + gate * branch).astype(BF16)
        hidden_grad = back[...]
        d_after[...] = given + normalize_back(hidden_grad * scale, normed, inverse)
        clip_row = own_clip_row(scal, rows, splits)
        sums[:, 0:D] = clip_sums(clip_row, hidden_grad)
        sums[:, D : 2 * D] = clip_sums(clip_row, hidden_grad * normed)
        sums[:, 2 * D :] = clip_sums(clip_row, given * branch)
    for i in range(high - low):
        for copy in store_copies(gbuf, i, grads, store_sems, scal):
            copy.wait()


def cross_backward(n_p, splits, low, high, *refs):
    n_w = 2 * n_p
    scal, d_cross, after_self, hidden_t, text_t, gain, mod, branch, kv_in, q_in, att_in, lse = refs[
        :12
    ]
    pieces = refs[12 : 12 + n_w]
    rest = refs[12 + n_w :]
    first, last = low == 0, high == splits
    if not first:
        back_in, text_in, bias_in = rest[:3]
        rest = rest[3:]
    n_o = 2 if n_p > 1 else 1
    grads = rest[:n_o]
    bias_grad = rest[n_o]
    rest = rest[n_o + 1 :]
    if last:
        d_after, d_attn, text_out, row_grads, sums, back, text_back = rest[:7]
        rest = rest[7:]
    else:
        back, text_back = rest[:2]
        rest = rest[2:]
    weights, gbuf, mask, probs, dscore, key_grad, load_sems, store_sems = rest
    rows = after_self.shape[0]
    count = text_t.shape[1]
    load_wait = load_start(own_and_others(pieces), weights, load_sems, scal, low, D)
    cross_mask(scal, mask, rows, splits, count // TXT)
    given = d_cross[...].astype(BF16)
    given_wide = given.astype(F32)
    given_t = given_wide.T.astype(BF16)
    if first:
        back[...] = jnp.zeros_like(back)
        text_back[...] = jnp.zeros_like(text_back)
        bias_grad[...] = jnp.zeros_like(bias_grad)
    else:
        back[...] = back_in[...]
        text_back[...] = text_in[...]
        bias_grad[...] = bias_in[...]

    def one(i, carry):
        load_wait(i)
        z = i + low
        place = shard_index(scal, z, splits)

        def kv(lo, hi, col):
            return kv_in[z, lo:hi, col * WIN : (col + 1) * WIN]

        def put(lo, hi, k01, v01, k2, v2):
            key_grad[lo:hi, 0:WIN] = k01.astype(BF16)
            key_grad[lo:hi, WIN : 2 * WIN] = v01.astype(BF16)
            key_grad[lo:hi, 2 * WIN : 3 * WIN] = k2.astype(BF16)
            key_grad[lo:hi, 3 * WIN : 4 * WIN] = v2.astype(BF16)

        head_grad = nn(given, weights[i, :, 4 * WIN :]).astype(BF16)
        totals = [lse[z, h : h + 1, :] for h in range(3)]
        pair, third = attend_back(
            q_in[z], kv, att_in[z], head_grad, mask, totals, probs, dscore, count, put
        )
        pair, third = pair.astype(BF16), third.astype(BF16)
        part = nn(text_t[...], key_grad[...])
        out_part = nn(given_t, att_in[z])
        gbuf[i, :, 0:WIN] = nn(hidden_t[...], pair).astype(BF16)
        gbuf[i, :, WIN : 3 * WIN] = part[:, 0 : 2 * WIN].astype(BF16)
        gbuf[i, :, 3 * WIN : 4 * WIN] = (
            part[:, 2 * WIN : 3 * WIN] + nn(hidden_t[...], third)
        ).astype(BF16)
        gbuf[i, :, 4 * WIN : 5 * WIN] = (part[:, 3 * WIN :] + out_part[:, 0:WIN]).astype(BF16)
        gbuf[i, :, 5 * WIN :] = out_part[:, WIN:].astype(BF16)
        for copy in store_copies(gbuf, i, grads, store_sems, scal):
            copy.start()
        back[...] += nt(pair, weights[i, :, 0:WIN]) + nt(third, weights[i, :, 3 * WIN : 4 * WIN])
        for lo in range(0, count, 256):
            text_back[lo : lo + 256, :] += nt(
                key_grad[lo : lo + 256, :], weights[i, :, WIN : 5 * WIN]
            )
        key_sums = jnp.sum(key_grad[...].astype(F32), axis=0, keepdims=True)
        bias_grad[place, :, 0:WIN] = jnp.sum(pair.astype(F32), axis=0, keepdims=True)
        bias_grad[place, :, WIN : 3 * WIN] = key_sums[:, 0 : 2 * WIN]
        bias_grad[place, :, 3 * WIN : 4 * WIN] = key_sums[:, 2 * WIN : 3 * WIN] + jnp.sum(
            third.astype(F32), axis=0, keepdims=True
        )
        bias_grad[place, :, 4 * WIN : 5 * WIN] = key_sums[:, 3 * WIN :]
        bias_grad[place, :, 5 * WIN :] = jnp.zeros((1, WIN), F32)
        return carry

    lax.fori_loop(0, high - low, one, 0)

    def finish_stores():
        for i in range(high - low):
            for copy in store_copies(gbuf, i, grads, store_sems, scal):
                copy.wait()

    if not last:
        finish_stores()
        return
    row_grads[...] = jnp.zeros_like(row_grads)
    row_grads[0:1, :] = jnp.sum(given_wide, axis=0, keepdims=True)
    normed, inverse = normalize(after_self[...])
    hidden_grad = back[...]
    row_grads[1:2, :] = jnp.sum(hidden_grad * normed, axis=0, keepdims=True)
    total = d_cross[...] + normalize_back(hidden_grad * gain[...], normed, inverse)
    d_after[...] = total
    clip = own_clip(scal, rows, splits)
    d_attn[...] = (total * per_row(mod, 2, clip)).astype(BF16)
    sums[...] = clip_sums(own_clip_row(scal, rows, splits), total * branch[...])
    text_out[...] = text_back[...].astype(BF16)
    finish_stores()


def pack_small(table, own, cross, inner, given_sum, cross_rows, out_row, first, gate, second, out):
    n_dp = table.shape[1] // WIN
    splits, clips = out.shape[0], 3
    lane = lax.broadcasted_iota(jnp.int32, (D, n_dp * WIN), 0)

    def moved(value, which):
        choose = (lane == table[which : which + 1, :]).astype(F32).astype(BF16)
        high = value.astype(BF16).astype(F32)
        middle = (value - high).astype(BF16).astype(F32)
        parts = jnp.concatenate([high, middle, value - high - middle], axis=0).astype(BF16)
        found = nn(parts, choose)
        count = value.shape[0]
        return found[:count] + found[count : 2 * count] + found[2 * count :]

    def by_shard(ref):
        return jnp.concatenate([ref[z] for z in range(splits)], axis=0)

    both = moved(jnp.concatenate([by_shard(own), by_shard(cross)], axis=0), 0)
    heads = both[:splits] + pltpu.roll(both[splits:], 48, 1)
    hidden = moved(by_shard(inner), 1)
    rows = moved(
        jnp.concatenate(
            [given_sum, cross_rows[0:2, :], out_row[...]] + [jnp.zeros((4, D), F32)], axis=0
        ),
        2,
    )
    out[...] = jnp.zeros_like(out)
    for z in range(splits):
        for c in range(clips):
            for j in range(6):
                source, col = ((first, j), (gate, 0), (second, j - 3))[(j > 1) + (j > 2)]
                out[z, c * 6 + j : c * 6 + j + 1, :] = source[c : c + 1, col * D : (col + 1) * D]
        for d in range(n_dp):
            span = slice(d * WIN, (d + 1) * WIN)
            parts = [heads[z : z + 1, span], hidden[z : z + 1, span]]
            parts += [rows[r : r + 1, span] for r in range(4)]
            spot = clips * 6 + d
            out[z, spot : spot + 1, :] = jnp.concatenate(parts, axis=1)


def self_backward(n_p, splits, low, high, small, *refs):
    n_w = 2 * n_p
    scal = refs[0]
    frames = refs[1 : 1 + splits]
    given_ref, hidden_t, kv_in, q_in, att_in, lse = refs[1 + splits : 7 + splits]
    pieces = refs[7 + splits : 7 + splits + n_w]
    rest = refs[7 + splits + n_w :]
    first, last = low == 0, high == splits
    if not first:
        back_in, bias_in = rest[:2]
        rest = rest[2:]
    if small:
        table, cross_bias, inner_bias, cross_rows, out_row, gate, second = rest[:7]
        rest = rest[7:]
    n_o = 2 if n_p > 1 else 1
    grads = rest[:n_o]
    bias_grad = rest[n_o]
    rest = rest[n_o + 1 :]
    if last:
        own = rest[0]
        parts = rest[1:splits]
        row_grads, sums = rest[splits : splits + 2]
        rest = rest[splits + 2 :]
        if small:
            own_small, small_rows, back = rest[0], rest[1], rest[2]
            rest = rest[3:]
        else:
            back = rest[0]
            rest = rest[1:]
    else:
        back = rest[0]
        rest = rest[1:]
    weights, gbuf, mask, probs, dscore, key_grad, load_sems, store_sems = rest
    rows = frames[0].shape[0]
    count = rows * splits
    load_wait = load_start(own_and_others(pieces), weights, load_sems, scal, low)
    self_mask(scal, mask, rows, splits)
    given = given_ref[...]
    given_wide = given.astype(F32)
    given_t = given_wide.T.astype(BF16)
    if first:
        back[...] = jnp.zeros_like(back)
        bias_grad[...] = jnp.zeros_like(bias_grad)
    else:
        back[...] = back_in[...]
        bias_grad[...] = bias_in[...]

    def one(i, carry):
        load_wait(i)
        z = i + low
        place = shard_index(scal, z, splits)

        def kv(lo, hi, col):
            return kv_in[z, lo:hi, col * WIN : (col + 1) * WIN]

        def put(lo, hi, k01, v01, k2, v2):
            key_grad[lo:hi, 0:WIN] = k01.astype(BF16)
            key_grad[lo:hi, WIN : 2 * WIN] = v01.astype(BF16)
            key_grad[lo:hi, 2 * WIN : 3 * WIN] = k2.astype(BF16)
            key_grad[lo:hi, 3 * WIN : 4 * WIN] = v2.astype(BF16)

        head_grad = nn(given, weights[i, :, 4 * WIN :]).astype(BF16)
        totals = [lse[z, h : h + 1, :] for h in range(3)]
        pair, third = attend_back(
            q_in[z], kv, att_in[z], head_grad, mask, totals, probs, dscore, count, put
        )
        pair = pair.astype(BF16)
        key_grad[0:rows, 2 * WIN : 3 * WIN] = (
            key_grad[0:rows, 2 * WIN : 3 * WIN].astype(F32) + third
        ).astype(BF16)
        part = nn(hidden_t[...], key_grad[...])
        out_part = nn(given_t, att_in[z])
        gbuf[i, :, 0:WIN] = nn(hidden_t[:, 0:rows], pair).astype(BF16)
        gbuf[i, :, WIN : 4 * WIN] = part[:, 0 : 3 * WIN].astype(BF16)
        gbuf[i, :, 4 * WIN : 5 * WIN] = (part[:, 3 * WIN :] + out_part[:, 0:WIN]).astype(BF16)
        gbuf[i, :, 5 * WIN :] = out_part[:, WIN:].astype(BF16)
        for copy in store_copies(gbuf, i, grads, store_sems, scal):
            copy.start()
        for lo in range(0, count, 256):
            back[lo : lo + 256, :] += nt(
                key_grad[lo : lo + 256, :], weights[i, :, WIN : 5 * WIN]
            )
        back[0:rows, :] += nt(pair, weights[i, :, 0:WIN])
        key_sums = jnp.sum(key_grad[...].astype(F32), axis=0, keepdims=True)
        bias_grad[place, :, 0:WIN] = jnp.sum(pair.astype(F32), axis=0, keepdims=True)
        bias_grad[place, :, WIN : 5 * WIN] = key_sums
        bias_grad[place, :, 5 * WIN :] = jnp.zeros((1, WIN), F32)
        return carry

    lax.fori_loop(0, high - low, one, 0)

    def finish_stores():
        for i in range(high - low):
            for copy in store_copies(gbuf, i, grads, store_sems, scal):
                copy.wait()

    if not last:
        finish_stores()
        return
    given_sum = jnp.sum(given_wide, axis=0, keepdims=True)
    row_grads[...] = jnp.zeros_like(row_grads)
    row_grads[0:1, :] = given_sum
    shift = jnp.zeros((8, D), F32)
    scale = jnp.zeros((8, D), F32)
    for block in range(splits):
        value = back[block * rows : (block + 1) * rows, :]
        if block == 0:
            own[...] = value
        else:
            parts[block - 1][0:rows, :] = value.astype(BF16)
        normed, _ = normalize(frames[block][...].astype(F32))
        clip_row = own_clip_row(scal, rows, splits, block)
        shift = shift + clip_sums(clip_row, value)
        scale = scale + clip_sums(clip_row, value * normed)
    sums[:, 0:D] = shift
    sums[:, D:] = scale
    if small:
        pack_small(
            table,
            bias_grad,
            cross_bias,
            inner_bias,
            given_sum,
            cross_rows,
            out_row,
            sums,
            gate,
            second,
            small_rows,
        )
        for k in range(splits):
            value = small_rows[shard_index(scal, k, splits)]
            if k == 0:
                own_small[...] = value
            else:
                parts[k - 1][rows:, :] = value.astype(BF16)
    finish_stores()


def finish(splits, *refs):
    scal, frames, mod, d_after, own = refs[:5]
    parts = refs[5 : 4 + splits]
    out = refs[4 + splits]
    rows = frames.shape[0]
    value = own[...]
    for part in parts:
        value = value + part[0 : own.shape[0], :].astype(F32)
    normed, inverse = normalize(frames[...].astype(F32))
    scale = 1.0 + per_row(mod, 1, own_clip(scal, rows, splits))
    out[...] = d_after[...] + normalize_back(value * scale, normed, inverse)


def bias_table(n_dp):
    table = np.full((8, n_dp * WIN), -1, np.int32)
    for d in range(n_dp):
        for i in range(48):
            part, h, r = i // 24, i % 24 // 8, i % 8
            spot = d * 8 + r
            start = (h * HD if h < 2 else 3 * WIN) if part == 0 else (2 + h / 2) * WIN
            table[0, d * WIN + i] = (start if part == 0 or h < 2 else 4 * WIN) + spot
        for i in range(96):
            table[1, d * WIN + i] = i // 32 * 256 + d * 32 + i % 32
            table[2, d * WIN + i] = d * 96 + i
    return table


MEMORY = {"v": pltpu.VMEM, "s": pltpu.SMEM, "a": pl.ANY}


def call(body, inputs, outs, scratch, flops, name):
    moved = sum(a.size * a.dtype.itemsize for _, a in inputs)
    moved += sum(_size(s, t) for _, s, t in outs)
    return pl.pallas_call(
        body,
        out_shape=tuple(jax.ShapeDtypeStruct(s, t) for _, s, t in outs),
        in_specs=[pl.BlockSpec(memory_space=MEMORY[m]) for m, _ in inputs],
        out_specs=tuple(pl.BlockSpec(memory_space=MEMORY[m]) for m, _, _ in outs),
        scratch_shapes=scratch,
        compiler_params=pltpu.CompilerParams(vmem_limit_bytes=58 * 1024 * 1024),
        cost_estimate=pl.CostEstimate(flops=int(flops), bytes_accessed=int(moved), transcendentals=0),
        name=name,
    )(*[a for _, a in inputs])


def _size(shape, kind):
    total = jnp.dtype(kind).itemsize
    for s in shape:
        total *= s
    return total


class Ring:
    def __init__(self):
        self.n_dp = lax.axis_size("dp")
        self.splits = lax.axis_size("head")
        self.square = self.n_dp == 8
        if self.square:
            self.core = [(i, i ^ 1) for i in range(8)]
            self.first = [(i, i ^ (4 if i & 1 else 2)) for i in range(8)]
            self.second = [(i, i ^ (2 if i & 1 else 4)) for i in range(8)]

    def offsets(self):
        if not self.square:
            return [jnp.int32(0)]
        me = lax.axis_index("dp")
        rows = D // 8

        def kept(d):
            odd = d & 1
            return [d, d ^ (2 + 2 * odd), d ^ (4 - 2 * odd), d ^ 6]

        return [place * rows for place in kept(me) + kept(me ^ 1)]

    def z_pieces(self, value, far=None):
        n = self.splits
        return [value] + [
            lax.ppermute(value, "head", [(s, (s + k) % n) for s in range(n)])
            for k in (range(1, n) if far is None else far)
        ]

    def z_back(self, parts):
        n = self.splits
        return [
            lax.ppermute(parts[k - 1], "head", [(s, (s - k) % n) for s in range(n)])
            for k in range(1, n)
        ]

    def across(self, value, how):
        return lax.ppermute(value, "dp", how)

    def z_move(self, value, k):
        n = self.splits
        return lax.ppermute(value, "head", [(s, (s - k) % n) for s in range(n)])


class GradSum:
    def __init__(self, ring, grads):
        self.ring, self.grads = ring, list(grads)
        self.moved = []
        self.arrived = []
        if not ring.square:
            self.whole = lax.psum_scatter(grads[0][0], "dp", scatter_dimension=1, tiled=True)

    def across(self, value, how):
        if self.ring.square:
            self.moved.append(self.ring.across(value.astype(BF16), how))

    def block(self, i):
        value = self.grads[0][i].astype(F32) + self.moved[0][i].astype(F32)
        if len(self.moved) > 1:
            value = value + self.moved[1][i].astype(F32)
        return value

    def core(self):
        if self.ring.square:
            self.across(self.grads[1], self.ring.core)

    def second(self):
        if self.ring.square:
            self.across(self.block(slice(2, 4)), self.ring.second)

    def first(self):
        if self.ring.square:
            self.across(self.block(1), self.ring.first)

    def own(self, i):
        if not self.ring.square:
            return self.whole[i].astype(F32)
        value = self.grads[0][0, i].astype(F32) + self.moved[2][i].astype(F32)
        return value + self.moved[0][0, i].astype(F32) + self.moved[1][0, i].astype(F32)

    def shard(self, start):
        count = self.grads[0].shape[1]
        for i in range(count):
            k = i if start == 1 else start + i
            if k > 0:
                self.arrived.append(self.ring.z_move(self.own(i).astype(BF16), k))


def join_second(low, high):
    if not low.ring.square:
        return []
    part = slice(2, 4)
    both = jnp.concatenate([low.block(part), high.block(part)], axis=1)
    return [low.ring.across(both.astype(BF16), low.ring.second)]


def join_first(low, high):
    if not low.ring.square:
        return []
    both = jnp.concatenate([low.block(1), high.block(1)], axis=0)
    return [low.ring.across(both.astype(BF16), low.ring.first)]


def join_take(low, high, moved):
    count = low.grads[0].shape[1]
    for value in moved:
        low.moved.append(value[..., :count, :, :])
        high.moved.append(value[..., count:, :, :])


def join_shards(pairs):
    ring = pairs[0][0].ring
    half = ring.splits // 2
    return [
        ring.z_move(
            jnp.concatenate([pair[k // half].own(k % half) for pair in pairs], axis=1).astype(BF16),
            k,
        )
        for k in range(1, ring.splits)
    ]


class Gather:
    def __init__(self, ring, mine):
        self.ring = ring
        if ring.square:
            self.kept, self.other = [mine], []
        else:
            self.kept, self.other = [lax.all_gather(mine, "dp", axis=1, tiled=True)], []

    def sides(self):
        if self.ring.square:
            self.kept.append(self.ring.across(self.kept[0], self.ring.first))
            self.kept.append(self.ring.across(self.kept[0], self.ring.second))

    def corner(self):
        if self.ring.square:
            self.kept.append(self.ring.across(self.kept[1], self.ring.second))

    def core(self, *which):
        if self.ring.square:
            for i in which:
                self.other.append(self.ring.across(self.kept[i], self.ring.core))

    def pieces(self):
        return self.kept + self.other


def meet(*groups):
    flat = [v for group in groups for v in group]
    flat = list(lax.optimization_barrier(tuple(flat)))
    for group in groups:
        for i in range(len(group)):
            group[i] = flat.pop(0)


def to_layout(q, k, v, o):
    return jnp.concatenate(
        [
            q[:, :WIN],
            k[:, :WIN],
            v[:, :WIN],
            q[:, WIN:],
            k[:, WIN:],
            v[:, WIN:],
            o[:, WIN:],
            o[:, :WIN],
        ],
        axis=1,
    )


def from_layout(value):
    def pick(pair, third):
        return jnp.concatenate(
            [value[:, pair : pair + WIN], value[:, third : third + HD]], axis=1
        )

    return pick(0, 3 * WIN), pick(WIN, 3 * WIN + HD), pick(2 * WIN, 4 * WIN), pick(
        5 * WIN, 4 * WIN + HD
    )


def mod_gradients(ring, sums, clips):
    part = jnp.concatenate(sums, axis=1)[:clips]
    got = lax.all_to_all(
        jnp.broadcast_to(part[None], (ring.splits,) + part.shape), "head", 0, 0, tiled=True
    )
    low = jnp.sum(got, axis=0).astype(BF16)
    return lax.all_to_all(
        jnp.broadcast_to(low[None], (ring.n_dp,) + low.shape), "dp", 0, 0, tiled=True
    ).reshape(ring.n_dp * clips, -1)


def on_device(
    frames_in,
    step_embed,
    text_feats,
    clip_frames,
    text_tokens,
    out_grad,
    ada_weight,
    ada_bias,
    qkv_weight,
    qv_bias,
    attn_out_weight,
    attn_out_bias,
    cross_gain,
    cross_q_weight,
    cross_q_bias,
    cross_kv_weight,
    cross_v_bias,
    cross_out_weight,
    cross_out_bias,
    mlp_in_weight,
    mlp_in_bias,
    mlp_out_weight,
    mlp_out_bias,
):
    both = ("dp", "head")
    ring = Ring()
    n_dp, splits = ring.n_dp, ring.splits
    z_index = lax.axis_index("head")
    rows = frames_in.shape[0]
    count = rows * splits
    text_count = text_feats.shape[0]
    clips = clip_frames.shape[1]
    width = D // splits
    shard_rows = D // n_dp
    ends = jnp.cumsum(clip_frames[0])
    offs = ring.offsets()
    n_p = len(offs)
    scal = jnp.stack(
        [z_index, ends[0], ends[1], text_tokens[0, 0], text_tokens[0, 1], text_tokens[0, 2]]
        + [jnp.int32(0)] * 2
        + [o.astype(jnp.int32) for o in offs]
        + [jnp.int32(0)] * (S_LEN - S_OFF - n_p)
    ).astype(jnp.int32)

    shard_self = to_layout(
        qkv_weight[:, 0], qkv_weight[:, 1], qkv_weight[:, 2], attn_out_weight.T
    )
    shard_cross = to_layout(
        cross_q_weight, cross_kv_weight[:, 0], cross_kv_weight[:, 1], cross_out_weight.T
    )

    biases = [
        ada_bias,
        qv_bias.reshape(-1),
        attn_out_bias,
        cross_gain,
        cross_q_bias.reshape(-1),
        cross_v_bias.reshape(-1),
        cross_out_bias,
        mlp_in_bias.reshape(-1),
        mlp_out_bias,
    ]
    flat = jnp.concatenate(biases)
    cols = step_embed.reshape(clips, n_dp, shard_rows).transpose(1, 0, 2).reshape(n_dp, -1)
    sent = jnp.concatenate(
        [
            jnp.broadcast_to(flat[None, None], (n_dp, splits, flat.shape[0])),
            jnp.broadcast_to(cols[:, None], (n_dp, splits, cols.shape[1])),
        ],
        axis=2,
    ).reshape(n_dp * splits, -1)
    got = lax.all_to_all(sent, both, 0, 0, tiled=True)
    attn_shard = jnp.concatenate([shard_self, shard_cross], axis=1)
    attn_shards = ring.z_pieces(attn_shard)[1:]
    own_gather = Gather(ring, attn_shard[None])
    own_gather.sides()
    own_gather.corner()
    own_gather.core(0, 1, 2, 3)
    mlp_shard = jnp.concatenate([mlp_in_weight, mlp_out_weight.T], axis=1)
    held = [got]
    meet(held, attn_shards, own_gather.kept, own_gather.other)
    got = held[0].reshape(n_dp, splits, -1)
    step_cols = got[:, 0, flat.shape[0] :].reshape(n_dp * clips, shard_rows).astype(F32)
    silu_cols = jax.nn.silu(step_cols).astype(BF16)
    spots = []
    place = 0
    for b in biases:
        spots.append(got[:, :, place : place + b.shape[0]].astype(F32))
        place += b.shape[0]

    def over_dp(value):
        return value[:, 0].reshape(1, -1)

    def by_head(value, lead=1):
        n = value.shape[2] // (lead * 3)
        v = value.reshape(n_dp, splits, lead, 3, n).transpose(1, 2, 3, 0, 4)
        return v.reshape(splits, lead, 3 * n_dp * n)

    all_ada_bias = over_dp(spots[0])
    qv = by_head(spots[1], 2)
    nothing = jnp.zeros((splits, width), F32)
    bias_self = to_layout(qv[:, 0], nothing, qv[:, 1], nothing)[:, None]
    all_attn_bias = over_dp(spots[2])
    all_gain = over_dp(spots[3])
    bias_cross = to_layout(
        by_head(spots[4])[:, 0], nothing, by_head(spots[5])[:, 0], nothing
    )[:, None]
    all_cross_bias = over_dp(spots[6])
    all_in_bias = by_head(spots[7])
    all_out_bias = over_dp(spots[8])

    mod_part = jnp.dot(silu_cols, ada_weight, preferred_element_type=F32)
    mod_got = lax.all_to_all(mod_part.reshape(n_dp, clips, -1), "dp", 0, 0, tiled=True)

    half = splits // 2
    attn_gather = Gather(ring, jnp.stack(attn_shards))
    attn_gather.sides()
    frame_blocks = ring.z_pieces(frames_in)
    held = [mlp_shard]
    meet(held, attn_gather.kept)
    mlp_shard = held[0]
    mod = jnp.sum(mod_got, axis=0) + all_ada_bias
    attn_gather.corner()
    attn_gather.core(0, 1, 2, 3)
    mlp_shards = ring.z_pieces(mlp_shard, range(1, half))
    mlp_gathers = [Gather(ring, jnp.stack(mlp_shards))]
    mlp_gathers[0].sides()
    mlp_gathers[0].core(0)
    mlp_late = ring.z_pieces(mlp_shard, range(half, splits))[1:]

    def dma(n):
        return pltpu.SemaphoreType.DMA(n)

    def any_of(arrays):
        return [("a", a) for a in arrays]

    def vmem_of(arrays):
        return [("v", a) for a in arrays]

    piece_rows = D // n_p
    kept_out = [("a", (max(n_p // 2, 1), splits, piece_rows, D), BF16)] * (2 if n_p > 1 else 1)
    n_o = len(kept_out)
    shard_type = pltpu.VMEM((splits, D, D), BF16)

    results = list(call(
        partial(self_forward, n_p, splits),
        [("s", scal)]
        + vmem_of(frame_blocks)
        + vmem_of([mod, bias_self, all_attn_bias])
        + any_of(own_gather.pieces() + attn_gather.pieces()),
        [
            ("v", (D, count), BF16),
            ("a", (splits, count, 4 * WIN), BF16),
            ("v", (splits, rows, 2 * WIN), BF16),
            ("v", (splits, rows, 2 * WIN), BF16),
            ("v", (splits, 8, rows), F32),
            ("v", (rows, D), F32),
            ("v", (rows, D), F32),
        ],
        [
            pltpu.VMEM((count, D), BF16),
            pltpu.VMEM((splits, count, 4 * WIN), BF16),
            shard_type,
            pltpu.VMEM((rows, count), F32),
            pltpu.VMEM((rows, count), F32),
            pltpu.VMEM((rows, count), BF16),
            dma((n_p, splits)),
            dma((splits,)),
        ],
        22 * US,
        "self_forward",
    ))
    meet(
        results, mlp_gathers[0].kept, mlp_gathers[0].other, mlp_late, attn_gather.kept, attn_gather.other
    )
    hidden_one, self_kv, self_q, self_att, self_lse, attn_branch, after_self = results
    mlp_gathers[0].corner()
    mlp_gathers[0].core(1, 2)
    mlp_gathers.append(Gather(ring, jnp.stack(mlp_late)))
    mlp_gathers[1].sides()

    results = list(call(
        partial(cross_forward, n_p, splits),
        [("s", scal)]
        + vmem_of([after_self, text_feats, all_gain, bias_cross, all_cross_bias])
        + any_of(own_gather.pieces() + attn_gather.pieces()),
        [
            ("v", (D, rows), BF16),
            ("v", (D, text_count), BF16),
            ("a", (splits, text_count, 4 * WIN), BF16),
            ("v", (splits, rows, 2 * WIN), BF16),
            ("v", (splits, rows, 2 * WIN), BF16),
            ("v", (splits, 8, rows), F32),
            ("v", (rows, D), F32),
        ],
        [
            pltpu.VMEM((splits, text_count, 4 * WIN), BF16),
            shard_type,
            pltpu.VMEM((rows, text_count), F32),
            pltpu.VMEM((rows, text_count), F32),
            pltpu.VMEM((rows, text_count), BF16),
            dma((n_p, splits)),
            dma((splits,)),
        ],
        17 * US,
        "cross_forward",
    ))
    meet(results, mlp_gathers[0].kept, mlp_gathers[0].other, mlp_gathers[1].kept)
    hidden_two_t, text_t, cross_kv, cross_q, cross_att, cross_lse, after_cross = results
    mlp_gathers[0].core(3)
    mlp_gathers[1].corner()
    mlp_gathers[1].core(0, 1, 2)

    kept_half = [(m, (shape[0], half) + shape[2:], kind) for m, shape, kind in kept_out]
    kept_wide = [(m, shape[:3] + (2 * D,), kind) for m, shape, kind in kept_half]
    half_type = pltpu.VMEM((half, D, D), BF16)

    def back_scratch(keys):
        return [
            half_type,
            half_type,
            pltpu.VMEM((keys, rows), F32),
            pltpu.VMEM((3, keys, rows), BF16),
            pltpu.VMEM((3, keys, rows), BF16),
            pltpu.VMEM((keys, 4 * WIN), BF16),
            dma((n_p, half)),
            dma((n_p, half)),
        ]

    bias_type = [("v", (splits, 1, D), F32)]
    mlp_args = [after_cross, out_grad, mod, all_in_bias, all_out_bias]
    mlp_scratch = [
        pltpu.VMEM((half, D, 2 * D), BF16),
        pltpu.VMEM((half, D, 2 * D), BF16),
        dma((n_p, half)),
        dma((n_p, half)),
    ]
    results = call(
        partial(feed_forward, n_p, splits, 0, half),
        [("s", scal)] + vmem_of(mlp_args) + any_of(mlp_gathers[0].pieces()),
        kept_wide + bias_type + [("v", (rows, D), F32)] * 2,
        mlp_scratch,
        9 * US,
        "feed_forward_first",
    )
    results = list(results)
    meet(results, mlp_gathers[1].kept, mlp_gathers[1].other)
    mlp_gathers[1].core(3)
    sum_mlp = [GradSum(ring, results[:n_o])]
    in_bias_grad, mlp_state, mlp_back = results[n_o:]
    sum_mlp[0].core()
    results = call(
        partial(feed_forward, n_p, splits, half, splits),
        [("s", scal)]
        + vmem_of(mlp_args)
        + any_of(mlp_gathers[1].pieces())
        + vmem_of([mlp_state, mlp_back, in_bias_grad]),
        kept_wide
        + bias_type
        + [
            ("v", (rows, D), BF16),
            ("v", (rows, D), F32),
            ("v", (1, D), F32),
            ("v", (8, 3 * D), F32),
        ],
        [pltpu.VMEM((rows, D), F32), pltpu.VMEM((rows, D), F32)] + mlp_scratch,
        10 * US,
        "feed_forward_last",
    )
    results = list(results)
    meet(results, sum_mlp[0].moved)
    sum_mlp.append(GradSum(ring, results[:n_o]))
    in_bias_grad, layer_out, d_after_cross, out_bias_grad, sums_two = results[n_o:]
    sum_mlp[0].second()
    sum_mlp[1].core()
    cross_args = [
        d_after_cross,
        after_self,
        hidden_two_t,
        text_t,
        all_gain,
        mod,
        attn_branch,
        cross_kv,
        cross_q,
        cross_att,
        cross_lse,
    ]
    cross_state = [("v", (rows, D), F32), ("v", (text_count, D), F32)]
    results = call(
        partial(cross_backward, n_p, splits, 0, half),
        [("s", scal)] + vmem_of(cross_args) + any_of(own_gather.pieces() + attn_gather.pieces()),
        kept_half + bias_type + cross_state,
        back_scratch(text_count),
        14 * US,
        "cross_backward_first",
    )
    results = list(results)
    meet(results, sum_mlp[0].moved, sum_mlp[1].moved)
    sum_cross = [GradSum(ring, results[:n_o])]
    cross_bias_grad, cross_back, text_back = results[n_o:]
    sum_mlp[0].first()
    sum_mlp[1].second()
    sum_cross[0].core()
    results = call(
        partial(cross_backward, n_p, splits, half, splits),
        [("s", scal)]
        + vmem_of(cross_args)
        + any_of(own_gather.pieces() + attn_gather.pieces())
        + vmem_of([cross_back, text_back, cross_bias_grad]),
        kept_half
        + bias_type
        + [
            ("v", (rows, D), F32),
            ("v", (rows, D), BF16),
            ("v", (text_count, D), BF16),
            ("v", (8, D), F32),
            ("v", (8, D), F32),
        ],
        [pltpu.VMEM((rows, D), F32), pltpu.VMEM((text_count, D), F32)] + back_scratch(text_count),
        15 * US,
        "cross_backward_last",
    )
    results = list(results)
    meet(results, sum_mlp[0].moved, sum_mlp[1].moved, sum_cross[0].moved)
    sum_cross.append(GradSum(ring, results[:n_o]))
    cross_bias_grad, d_after_self, d_attn, text_out, cross_rows, gate_sums = results[n_o:]
    sum_mlp[1].first()
    sum_cross[0].second()
    sum_cross[1].core()
    text_got = lax.all_to_all(
        text_out.reshape(splits, text_count // splits, D), "head", 0, 0, tiled=True
    )
    self_args = [d_attn, hidden_one, self_kv, self_q, self_att, self_lse]
    results = call(
        partial(self_backward, n_p, splits, 0, half, False),
        [("s", scal)] + vmem_of(frame_blocks) + vmem_of(self_args) + any_of(own_gather.pieces() + attn_gather.pieces()),
        kept_half + bias_type + [("v", (count, D), F32)],
        back_scratch(count),
        17 * US,
        "self_backward_first",
    )
    results = list(results)
    meet(
        results,
        sum_mlp[0].moved,
        sum_mlp[1].moved,
        sum_cross[0].moved,
        sum_cross[1].moved,
    )
    sum_self = [GradSum(ring, results[:n_o])]
    self_bias_grad, self_back = results[n_o:]
    sum_mlp[0].shard(1)
    sum_mlp[1].shard(2)
    sum_cross[1].second()
    sum_self[0].core()
    small_args, small_outs, small_scratch, small_count = [], [], [], 0
    if ring.square:
        small_count = 32
        small_args = [jnp.asarray(bias_table(n_dp)), cross_bias_grad, in_bias_grad]
        small_args += [cross_rows, out_bias_grad, gate_sums, sums_two]
        small_outs = [("v", (small_count, D), F32)]
        small_scratch = [pltpu.VMEM((splits, small_count, D), F32)]
    results = call(
        partial(self_backward, n_p, splits, half, splits, ring.square),
        [("s", scal)]
        + vmem_of(frame_blocks)
        + vmem_of(self_args)
        + any_of(own_gather.pieces() + attn_gather.pieces())
        + vmem_of([self_back, self_bias_grad] + small_args),
        kept_half
        + bias_type
        + [("v", (rows, D), F32)]
        + [("v", (rows + small_count, D), BF16)] * (splits - 1)
        + [("v", (8, D), F32), ("v", (8, 2 * D), F32)]
        + small_outs,
        small_scratch + [pltpu.VMEM((count, D), F32)] + back_scratch(count),
        18 * US,
        "self_backward_last",
    )
    results = list(results)
    held = [in_bias_grad, out_bias_grad, cross_bias_grad, cross_rows, gate_sums, sums_two]
    held.append(text_got)
    meet(
        results,
        held,
        sum_mlp[0].arrived,
        sum_mlp[1].arrived,
        sum_cross[0].moved,
        sum_cross[1].moved,
        sum_self[0].moved,
    )
    sum_self.append(GradSum(ring, results[:n_o]))
    self_bias_grad, own_part = results[n_o : n_o + 2]
    parts = results[n_o + 2 : n_o + 1 + splits]
    self_rows, sums_one = results[n_o + 1 + splits : n_o + 3 + splits]
    sum_self[1].core()
    arrived = ring.z_back(parts)
    in_bias_grad, out_bias_grad, cross_bias_grad, cross_rows, gate_sums, sums_two, text_got = held
    early, late = arrived[:1], arrived[1:]
    meet(sum_self[1].moved, sum_cross[1].moved, early)
    far = join_second(*sum_self)
    near_cross = join_first(*sum_cross)
    meet(far, near_cross)
    join_take(*sum_self, far)
    join_take(*sum_cross, near_cross)
    near = join_first(*sum_self)
    meet(late, near)
    arrived = early + late
    join_take(*sum_self, near)
    last = join_shards([sum_cross, sum_self])
    if ring.square:
        small = results[-1] + sum(part[rows:].astype(F32) for part in arrived)
        mod_low = small[: 6 * clips].astype(BF16).astype(F32)
        sent = jnp.concatenate(
            [
                jnp.broadcast_to(mod_low[None], (n_dp,) + mod_low.shape),
                small[6 * clips : 6 * clips + n_dp, None],
            ],
            axis=1,
        )
        held = [lax.all_to_all(sent, "dp", 0, 0, tiled=True)]
    if ring.square:
        mod_all = held[0][:, : 6 * clips].reshape(n_dp * clips, -1).astype(BF16)
        bias_sum = jnp.sum(held[0][:, 6 * clips], axis=0)
        places = [0, 24, 2 * WIN, 4 * WIN, 48, 72, 3 * WIN, WIN, 5 * WIN]
    else:
        mod_all = mod_gradients(ring, [sums_one, gate_sums, sums_two], clips)
    step_part = lax.dot_general(
        mod_all, ada_weight, (((1,), (1,)), ((), ())), preferred_element_type=F32
    )
    (frames_grad,) = call(
        partial(finish, splits),
        [("s", scal)] + vmem_of([frames_in, mod, d_after_self, own_part]) + vmem_of(arrived),
        [("v", (rows, D), F32)],
        [],
        3 * US,
        "finish",
    )
    text_grad = jnp.sum(text_got.astype(F32), axis=0)

    grad_ada = lax.dot_general(
        silu_cols, mod_all, (((0,), (0,)), ((), ())), preferred_element_type=F32
    )
    dp_index = lax.axis_index("dp")
    bias_width = ada_bias.shape[0]
    grad_ada_bias = jnp.sum(
        lax.dynamic_slice_in_dim(mod_all, dp_index * bias_width, bias_width, 1).astype(F32), axis=0
    )
    step_got = lax.all_to_all(step_part.reshape(n_dp, clips, shard_rows), "dp", 0, 0, tiled=True)
    step_got = [step_got]
    meet(last, step_got)
    (step_got,) = step_got
    total_cross, total_self = (
        pair[0].own(0) + sum(part[:, i * D : (i + 1) * D].astype(F32) for part in last)
        for i, pair in enumerate((sum_cross, sum_self))
    )
    step_value = step_embed.astype(F32)
    _, silu_pull = jax.vjp(jax.nn.silu, step_value)
    step_grad = silu_pull(step_got.transpose(1, 0, 2).reshape(clips, D))[0]

    def spread(value):
        v = value.reshape(n_dp, 1, D // n_dp)
        return jnp.broadcast_to(v, (n_dp, splits, D // n_dp))

    def heads_out(value):
        n = value.shape[1] // (3 * n_dp)
        return value.reshape(splits, 3, n_dp, n).transpose(2, 0, 1, 3).reshape(n_dp, splits, 3 * n)

    sq, _, sv, _ = from_layout(self_bias_grad[:, 0])
    cq, _, cv, _ = from_layout(cross_bias_grad[:, 0])
    entries = [
        heads_out(sq),
        heads_out(sv),
        spread(self_rows[0]),
        spread(cross_rows[1]),
        heads_out(cq),
        heads_out(cv),
        spread(cross_rows[0]),
        heads_out(in_bias_grad[:, 0]),
        spread(out_bias_grad[0]),
    ]
    if not ring.square:
        packed = jnp.concatenate(entries, axis=2)
        places = [sum(e.shape[2] for e in entries[:i]) for i in range(len(entries))]
        bias_sum = jnp.sum(
            lax.all_to_all(packed.reshape(n_dp * splits, -1), both, 0, 0, tiled=True), axis=0
        )
    bias_out = [bias_sum[p : p + e.shape[2]] for p, e in zip(places, entries)]

    total_mlp = sum_mlp[0].own(0) + sum(
        part.astype(F32) for part in sum_mlp[0].arrived + sum_mlp[1].arrived
    )
    gq, gk, gv, go = from_layout(total_self)
    hq, hk, hv, ho = from_layout(total_cross)
    return (
        layer_out,
        frames_grad,
        step_grad,
        text_grad,
        grad_ada,
        grad_ada_bias,
        jnp.stack([gq, gk, gv], axis=1),
        jnp.stack([bias_out[0], bias_out[1]]).reshape(qv_bias.shape),
        go.T,
        bias_out[2],
        bias_out[3],
        hq,
        bias_out[4].reshape(cross_q_bias.shape),
        jnp.stack([hk, hv], axis=1),
        bias_out[5].reshape(cross_v_bias.shape),
        ho.T,
        bias_out[6],
        total_mlp[:, :D],
        bias_out[7].reshape(mlp_in_bias.shape),
        total_mlp[:, D:].T,
        bias_out[8],
    )


def solution(mesh):
    rows_all, by_dp = P(("dp", "head"), None), P("dp", None)
    head_dp, dp_head = P("head", "dp"), P("dp", "head")
    dp_three, vector = P("dp", None, "head"), P("dp")
    params = (
        by_dp,
        vector,
        dp_three,
        P(None, "head", "dp"),
        head_dp,
        vector,
        vector,
        dp_head,
        head_dp,
        dp_three,
        head_dp,
        head_dp,
        vector,
        dp_head,
        head_dp,
        head_dp,
        vector,
    )
    return jax.shard_map(
        on_device,
        mesh=mesh,
        in_specs=(rows_all, by_dp, by_dp, by_dp, by_dp, rows_all) + params,
        out_specs=(rows_all, rows_all, by_dp, rows_all) + params,
        check_vma=False,
    )
```

```python
from functools import partial

import jax
import jax.numpy as jnp
import numpy as np
from jax import lax
from jax.experimental import pallas as pl
from jax.experimental.pallas import tpu as pltpu
from jax.sharding import PartitionSpec as P

D = 768
HD = 64
TXT = 256
WIN = 128
EPS = 1e-06
NEG = -1e30
F32 = jnp.float32
BF16 = jnp.bfloat16
HIGH = lax.Precision.HIGHEST
S_Z, S_END, S_TOK, S_OFF = 0, 1, 3, 8
S_LEN = 16
US = 1.15e9


def nn(a, b):
    return lax.dot_general(a, b, (((1,), (0,)), ((), ())), preferred_element_type=F32)


def nt(a, b):
    return lax.dot_general(a, b, (((1,), (1,)), ((), ())), preferred_element_type=F32)


def tn(a, b):
    return lax.dot_general(a, b, (((0,), (0,)), ((), ())), preferred_element_type=F32)


def normalize(v):
    centered = v - jnp.mean(v, axis=-1, keepdims=True)
    inverse = lax.rsqrt(jnp.mean(centered * centered, axis=-1, keepdims=True) + EPS)
    return centered * inverse, inverse


def normalize_back(u, normed, inverse):
    return inverse * (
        u
        - jnp.mean(u, axis=-1, keepdims=True)
        - normed * jnp.mean(u * normed, axis=-1, keepdims=True)
    )


def clip_of(position, scal):
    return (position >= scal[S_END]).astype(jnp.int32) + (position >= scal[S_END + 1]).astype(
        jnp.int32
    )


def frame_position(index, block, rows, splits, scal):
    return lax.rem(scal[S_Z] - block + splits, splits) * rows + index


def per_row(mod_ref, part, clip):
    cols = slice(part * D, (part + 1) * D)
    first, second, third = (mod_ref[c : c + 1, cols] for c in range(3))
    return jnp.where(clip == 0, first, jnp.where(clip == 1, second, third))


def clip_sums(clip_row, value):
    which = lax.broadcasted_iota(jnp.int32, (8, clip_row.shape[1]), 0)
    choose = (which == clip_row).astype(F32)
    return lax.dot_general(
        choose, value, (((1,), (0,)), ((), ())), precision=HIGH, preferred_element_type=F32
    )


def lanes(rows, low):
    lane = lax.broadcasted_iota(jnp.int32, (rows, WIN), 1)
    return lane < HD if low else lane >= HD


def keep(value, low):
    return jnp.where(lanes(value.shape[0], low), value, jnp.zeros_like(value))


def swap(value):
    return pltpu.roll(value, HD, 1)


def load_start(groups, buffer, sems, scal, low=0, col=0):
    width = buffer.shape[2]

    def place(j, rows):
        return pl.ds(pl.multiple_of(scal[S_OFF + j], 32), rows)

    for z in range(buffer.shape[0]):
        for pieces, start in groups:
            at = low + z - start
            if 0 <= at < pieces[0].shape[0]:
                for j, piece in enumerate(pieces):
                    pltpu.make_async_copy(
                        piece.at[at, :, col : col + width],
                        buffer.at[z, place(j, piece.shape[1]), :],
                        sems.at[j, z],
                    ).start()

    def wait(z):
        for j, piece in enumerate(groups[0][0]):
            here = buffer.at[z, place(j, piece.shape[1]), :]
            pltpu.make_async_copy(here, here, sems.at[j, z]).wait()

    return wait


def own_and_others(pieces):
    half = len(pieces) // 2
    return [(pieces[:half], 0), (pieces[half:], 1)]


def store_copies(buffer, z, outs, sems, scal, col=0, first=0):
    copies = []
    j = 0
    for out in outs:
        for i in range(out.shape[0]):
            rows = out.shape[2]
            start = pl.multiple_of(scal[S_OFF + j], 32)
            copies.append(
                pltpu.make_async_copy(
                    buffer.at[z, pl.ds(start, rows), col : col + out.shape[3]],
                    out.at[i, z],
                    sems.at[first + j, z],
                )
            )
            j += 1
    return copies


def attend(queries, kv, mask, scores, probs, count):
    rows = queries.shape[0]
    step = 256
    outs = []
    lane = lax.broadcasted_iota(jnp.int32, (rows, WIN), 1)
    totals = jnp.zeros((rows, WIN), F32)
    for h in range(3):
        if h < 2:
            query = keep(queries[:, :WIN], h == 0)
            kcol, vcol = 0, 1
        else:
            query = queries[:, WIN:]
            kcol, vcol = 2, 3
        top = None
        for lo in range(0, count, step):
            part = nt(query, kv(lo, lo + step, kcol)) + mask[:, lo : lo + step]
            scores[:, lo : lo + step] = part
            top = part if top is None else jnp.maximum(top, part)
        peak = jnp.max(top, axis=1, keepdims=True)
        wide = jnp.zeros((rows, step), F32)
        for lo in range(0, count, step):
            part = jnp.exp(scores[:, lo : lo + step] - peak)
            wide = wide + part
            probs[:, lo : lo + step] = part.astype(BF16)
        total = jnp.sum(wide, axis=1, keepdims=True)
        outs.append(nn(probs[:, 0:count], kv(0, count, vcol)) * (1.0 / total))
        totals = jnp.where(lane == h, peak + jnp.log(total), totals)
    pair = jnp.where(lane < HD, outs[0], outs[1])
    attended = jnp.concatenate([keep(swap(outs[2]), False), pair], axis=1)
    return attended.astype(BF16), totals.T[0:8, :]


def attend_back(queries, kv, attended, out_grad, mask, totals, probs, dscore, count, put):
    rows = queries.shape[0]
    step = 256
    wide = out_grad.astype(F32)
    row = lax.broadcasted_iota(jnp.int32, (8, 2 * WIN), 0)
    part = lax.broadcasted_iota(jnp.int32, (8, 2 * WIN), 1) // HD
    choose = ((part == row + 2) & (row < 2)) | ((part == 1) & (row == 2))
    deltas = lax.dot_general(
        choose.astype(F32),
        wide * attended.astype(F32),
        (((1,), (1,)), ((), ())),
        precision=HIGH,
        preferred_element_type=F32,
    )
    second = keep(swap(wide[:, :WIN]), True).astype(BF16)
    query_parts = []
    heads = []
    key_t = [kv(0, count, col).astype(F32).T.astype(BF16) for col in (0, 2)]
    for h in range(3):
        if h < 2:
            query = keep(queries[:, :WIN], h == 0)
            given = keep(out_grad[:, WIN:], h == 0)
            kcol, vcol = 0, 1
        else:
            query, given = queries[:, WIN:], second
            kcol, vcol = 2, 3
        heads.append((query, given))
        total, delta = totals[h], deltas[h : h + 1, :]
        for lo in range(0, count, step):
            hi = lo + step
            weights = jnp.exp(nt(kv(lo, hi, kcol), query) + mask[lo:hi, :] - total)
            probs[h, lo:hi, :] = weights.astype(BF16)
            weight_grad = nt(kv(lo, hi, vcol), given)
            dscore[h, lo:hi, :] = (weights * (weight_grad - delta)).astype(BF16)
        query_parts.append(nn(key_t[h // 2], dscore[h, 0:count, :]))
    for lo in range(0, count, step):
        hi = lo + step
        put(
            lo,
            hi,
            nn(dscore[0, lo:hi, :], heads[0][0]) + nn(dscore[1, lo:hi, :], heads[1][0]),
            nn(probs[0, lo:hi, :], heads[0][1]) + nn(probs[1, lo:hi, :], heads[1][1]),
            nn(dscore[2, lo:hi, :], heads[2][0]),
            nn(probs[2, lo:hi, :], heads[2][1]),
        )
    both = jnp.concatenate(
        [
            query_parts[0][:HD],
            query_parts[1][HD:],
            query_parts[2][HD:],
            jnp.zeros((HD, rows), F32),
        ],
        axis=0,
    )
    both = (both * 0.125).T
    return both[:, :WIN], both[:, WIN:]


def self_mask(scal, mask, rows, splits, forward=False):
    clip = own_clip if forward else own_clip_row
    query = clip(scal, rows, splits)
    for block in range(splits):
        span = slice(block * rows, (block + 1) * rows)
        key = (own_clip_row if forward else own_clip)(scal, rows, splits, block)
        value = jnp.where(key == query, 0.0, NEG)
        if forward:
            mask[:, span] = value
        else:
            mask[span, :] = value


def cross_mask(scal, mask, rows, splits, clips, forward=False):
    query = (own_clip if forward else own_clip_row)(scal, rows, splits)
    shape = (1, TXT) if forward else (TXT, 1)
    slot = lax.broadcasted_iota(jnp.int32, shape, 1 if forward else 0)
    for c in range(clips):
        span = slice(c * TXT, (c + 1) * TXT)
        value = jnp.where((query == c) & (slot < scal[S_TOK + c]), 0.0, NEG)
        if forward:
            mask[:, span] = value
        else:
            mask[span, :] = value


def own_clip(scal, rows, splits, block=0):
    return clip_of(
        frame_position(lax.broadcasted_iota(jnp.int32, (rows, 1), 0), block, rows, splits, scal),
        scal,
    )


def own_clip_row(scal, rows, splits, block=0):
    return clip_of(
        frame_position(lax.broadcasted_iota(jnp.int32, (1, rows), 1), block, rows, splits, scal),
        scal,
    )


def shard_index(scal, z, splits):
    return lax.rem(scal[S_Z] - z + splits, splits)


def self_forward(n_p, splits, *refs):
    n_w = 2 * n_p
    scal = refs[0]
    frames = refs[1 : 1 + splits]
    mod, bias, out_bias = refs[1 + splits : 4 + splits]
    pieces = refs[4 + splits : 4 + splits + n_w]
    hidden_t, kv_out, q_out, att_out, lse, branch_out, after = refs[
        4 + splits + n_w : 11 + splits + n_w
    ]
    hidden, kv_buf, weights, mask, scores, probs, sems, kv_sems = refs[11 + splits + n_w :]
    rows = frames[0].shape[0]
    count = rows * splits
    load_wait = load_start(own_and_others(pieces), weights, sems, scal)
    self_mask(scal, mask, rows, splits, True)
    for block in range(splits):
        clip = own_clip(scal, rows, splits, block)
        normed, _ = normalize(frames[block][...].astype(F32))
        value = normed * (1.0 + per_row(mod, 1, clip)) + per_row(mod, 0, clip)
        hidden[block * rows : (block + 1) * rows, :] = value.astype(BF16)
        hidden_t[:, block * rows : (block + 1) * rows] = value.T.astype(BF16)
    branch_out[...] = jnp.broadcast_to(out_bias[...], branch_out.shape)

    def one(z, carry):
        load_wait(z)
        bias_row = bias[shard_index(scal, z, splits)]
        for block in range(splits):
            span = slice(block * rows, (block + 1) * rows)
            part = nn(hidden[span, :], weights[z, :, WIN : 5 * WIN]) + bias_row[:, WIN : 5 * WIN]
            kv_buf[z, span, :] = part.astype(BF16)
            if block == 0:
                third = keep(swap(part[:, 2 * WIN : 3 * WIN].astype(BF16).astype(F32)), False)
        pair = nn(hidden[0:rows, :], weights[z, :, 0:WIN]) + bias_row[:, 0:WIN]
        queries = (
            jnp.concatenate([pair.astype(BF16).astype(F32), third], axis=1) * 0.125
        ).astype(BF16)
        q_out[z] = queries
        pltpu.make_async_copy(kv_buf.at[z], kv_out.at[z], kv_sems.at[z]).start()

        def kv(lo, hi, col):
            return kv_buf[z, lo:hi, col * WIN : (col + 1) * WIN]

        attended, totals = attend(queries, kv, mask, scores, probs, count)
        att_out[z] = attended
        lse[z] = totals
        branch_out[...] += nt(attended, weights[z, :, 4 * WIN :])
        return carry

    lax.fori_loop(0, splits, one, 0)
    clip = own_clip(scal, rows, splits)
    after[...] = frames[0][...].astype(F32) + per_row(mod, 2, clip) * branch_out[...]
    for z in range(splits):
        pltpu.make_async_copy(kv_buf.at[z], kv_out.at[z], kv_sems.at[z]).wait()


def cross_forward(n_p, splits, *refs):
    n_w = 2 * n_p
    scal, after_self, text, gain, bias, out_bias = refs[:6]
    pieces = refs[6 : 6 + n_w]
    hidden_t, text_t, kv_out, q_out, att_out, lse, after = refs[6 + n_w : 13 + n_w]
    kv_buf, weights, mask, scores, probs, sems, kv_sems = refs[13 + n_w :]
    rows = after_self.shape[0]
    count = text.shape[0]
    load_wait = load_start(own_and_others(pieces), weights, sems, scal, 0, D)
    cross_mask(scal, mask, rows, splits, count // TXT, True)
    normed, _ = normalize(after_self[...])
    wide = normed * gain[...]
    hidden = wide.astype(BF16)
    hidden_t[...] = wide.T.astype(BF16)
    for lo in range(0, count, 256):
        text_t[:, lo : lo + 256] = text[lo : lo + 256, :].astype(F32).T.astype(BF16)
    after[...] = after_self[...] + out_bias[...]

    def one(z, carry):
        load_wait(z)
        bias_row = bias[shard_index(scal, z, splits)]
        for lo in range(0, count, 256):
            part = nn(text[lo : lo + 256, :], weights[z, :, WIN : 5 * WIN])
            kv_buf[z, lo : lo + 256, :] = (part + bias_row[:, WIN : 5 * WIN]).astype(BF16)
        pair = nn(hidden, weights[z, :, 0:WIN]) + bias_row[:, 0:WIN]
        third = nn(hidden, weights[z, :, 3 * WIN : 4 * WIN]) + bias_row[:, 3 * WIN : 4 * WIN]
        third = keep(swap(third.astype(BF16).astype(F32)), False)
        queries = (
            jnp.concatenate([pair.astype(BF16).astype(F32), third], axis=1) * 0.125
        ).astype(BF16)
        q_out[z] = queries
        pltpu.make_async_copy(kv_buf.at[z], kv_out.at[z], kv_sems.at[z]).start()

        def kv(lo, hi, col):
            return kv_buf[z, lo:hi, col * WIN : (col + 1) * WIN]

        attended, totals = attend(queries, kv, mask, scores, probs, count)
        att_out[z] = attended
        lse[z] = totals
        after[...] += nt(attended, weights[z, :, 4 * WIN :])
        return carry

    lax.fori_loop(0, splits, one, 0)
    for z in range(splits):
        pltpu.make_async_copy(kv_buf.at[z], kv_out.at[z], kv_sems.at[z]).wait()


def feed_forward(n_p, splits, low, high, *refs):
    scal, after_cross, upstream, mod, in_bias, out_bias = refs[:6]
    pieces = refs[6 : 6 + n_p]
    rest = refs[6 + n_p :]
    n_o = 2 if n_p > 1 else 1
    first, last = low == 0, high == splits
    if not first:
        mlp_in, back_in, bias_in = rest[:3]
        rest = rest[3:]
    grads = rest[:n_o]
    in_bias_grad = rest[n_o]
    rest = rest[n_o + 1 :]
    if last:
        layer_out, d_after, out_bias_grad, sums, mlp, back = rest[:6]
        rest = rest[6:]
    else:
        mlp, back = rest[:2]
        rest = rest[2:]
    weights, gbuf, load_sems, store_sems = rest
    rows = after_cross.shape[0]
    load_wait = load_start([(pieces, 0)], weights, load_sems, scal)
    clip = own_clip(scal, rows, splits)
    normed, inverse = normalize(after_cross[...])
    scale = 1.0 + per_row(mod, 4, clip)
    wide = normed * scale + per_row(mod, 3, clip)
    hidden = wide.astype(BF16)
    hidden_t = wide.T.astype(BF16)
    gate = per_row(mod, 5, clip)
    given = upstream[...].astype(F32)
    low_wide = given * gate
    lowered = low_wide.astype(BF16)
    low_t = low_wide.T.astype(BF16)
    if first:
        mlp[...] = jnp.broadcast_to(out_bias[...], mlp.shape)
        back[...] = jnp.zeros_like(back)
        in_bias_grad[...] = jnp.zeros_like(in_bias_grad)
    else:
        mlp[...] = mlp_in[...]
        back[...] = back_in[...]
        in_bias_grad[...] = bias_in[...]

    def one(i, carry):
        load_wait(i)
        place = shard_index(scal, i + low, splits)
        pre = nn(hidden, weights[i, :, 0:D]) + in_bias[place]
        inner = 0.7978845608028654 * (pre + 0.044715 * (pre * pre * pre))
        curve = jnp.tanh(inner)
        half = 0.5 * (1.0 + curve)
        active = (pre * half).astype(BF16)
        slope = half + 0.5 * pre * (1.0 - curve * curve) * 0.7978845608028654 * (
            1.0 + 3.0 * 0.044715 * pre * pre
        )
        pre_grad = (slope * nn(lowered, weights[i, :, D:])).astype(BF16)
        in_bias_grad[place] = jnp.sum(pre_grad.astype(F32), axis=0, keepdims=True)
        mlp[...] += nt(active, weights[i, :, D:])
        back[...] += nt(pre_grad, weights[i, :, 0:D])
        gbuf[i, :, 0:D] = nn(hidden_t, pre_grad).astype(BF16)
        gbuf[i, :, D:] = nn(low_t, active).astype(BF16)
        for copy in store_copies(gbuf, i, grads, store_sems, scal):
            copy.start()
        return carry

    lax.fori_loop(0, high - low, one, 0)
    if last:
        out_bias_grad[...] = jnp.sum(lowered.astype(F32), axis=0, keepdims=True)
        branch = mlp[...]
        layer_out[...] = (after_cross[...] + gate * branch).astype(BF16)
        hidden_grad = back[...]
        d_after[...] = given + normalize_back(hidden_grad * scale, normed, inverse)
        clip_row = own_clip_row(scal, rows, splits)
        sums[:, 0:D] = clip_sums(clip_row, hidden_grad)
        sums[:, D : 2 * D] = clip_sums(clip_row, hidden_grad * normed)
        sums[:, 2 * D :] = clip_sums(clip_row, given * branch)
    for i in range(high - low):
        for copy in store_copies(gbuf, i, grads, store_sems, scal):
            copy.wait()


def cross_backward(n_p, splits, low, high, *refs):
    n_w = 2 * n_p
    scal, d_cross, after_self, hidden_t, text_t, gain, mod, branch, kv_in, q_in, att_in, lse = refs[
        :12
    ]
    pieces = refs[12 : 12 + n_w]
    rest = refs[12 + n_w :]
    first, last = low == 0, high == splits
    if not first:
        back_in, text_in, bias_in = rest[:3]
        rest = rest[3:]
    n_o = 2 if n_p > 1 else 1
    grads = rest[:n_o]
    bias_grad = rest[n_o]
    rest = rest[n_o + 1 :]
    if last:
        d_after, d_attn, text_out, row_grads, sums, back, text_back = rest[:7]
        rest = rest[7:]
    else:
        back, text_back = rest[:2]
        rest = rest[2:]
    weights, gbuf, mask, probs, dscore, key_grad, load_sems, store_sems = rest
    rows = after_self.shape[0]
    count = text_t.shape[1]
    load_wait = load_start(own_and_others(pieces), weights, load_sems, scal, low, D)
    cross_mask(scal, mask, rows, splits, count // TXT)
    given = d_cross[...].astype(BF16)
    given_wide = given.astype(F32)
    given_t = given_wide.T.astype(BF16)
    if first:
        back[...] = jnp.zeros_like(back)
        text_back[...] = jnp.zeros_like(text_back)
        bias_grad[...] = jnp.zeros_like(bias_grad)
    else:
        back[...] = back_in[...]
        text_back[...] = text_in[...]
        bias_grad[...] = bias_in[...]

    def one(i, carry):
        load_wait(i)
        z = i + low
        place = shard_index(scal, z, splits)

        def kv(lo, hi, col):
            return kv_in[z, lo:hi, col * WIN : (col + 1) * WIN]

        def put(lo, hi, k01, v01, k2, v2):
            key_grad[lo:hi, 0:WIN] = k01.astype(BF16)
            key_grad[lo:hi, WIN : 2 * WIN] = v01.astype(BF16)
            key_grad[lo:hi, 2 * WIN : 3 * WIN] = k2.astype(BF16)
            key_grad[lo:hi, 3 * WIN : 4 * WIN] = v2.astype(BF16)

        head_grad = nn(given, weights[i, :, 4 * WIN :]).astype(BF16)
        totals = [lse[z, h : h + 1, :] for h in range(3)]
        pair, third = attend_back(
            q_in[z], kv, att_in[z], head_grad, mask, totals, probs, dscore, count, put
        )
        pair, third = pair.astype(BF16), third.astype(BF16)
        part = nn(text_t[...], key_grad[...])
        out_part = nn(given_t, att_in[z])
        gbuf[i, :, 0:WIN] = nn(hidden_t[...], pair).astype(BF16)
        gbuf[i, :, WIN : 3 * WIN] = part[:, 0 : 2 * WIN].astype(BF16)
        gbuf[i, :, 3 * WIN : 4 * WIN] = (
            part[:, 2 * WIN : 3 * WIN] + nn(hidden_t[...], third)
        ).astype(BF16)
        gbuf[i, :, 4 * WIN : 5 * WIN] = (part[:, 3 * WIN :] + out_part[:, 0:WIN]).astype(BF16)
        gbuf[i, :, 5 * WIN :] = out_part[:, WIN:].astype(BF16)
        for copy in store_copies(gbuf, i, grads, store_sems, scal):
            copy.start()
        back[...] += nt(pair, weights[i, :, 0:WIN]) + nt(third, weights[i, :, 3 * WIN : 4 * WIN])
        for lo in range(0, count, 256):
            text_back[lo : lo + 256, :] += nt(
                key_grad[lo : lo + 256, :], weights[i, :, WIN : 5 * WIN]
            )
        key_sums = jnp.sum(key_grad[...].astype(F32), axis=0, keepdims=True)
        bias_grad[place, :, 0:WIN] = jnp.sum(pair.astype(F32), axis=0, keepdims=True)
        bias_grad[place, :, WIN : 3 * WIN] = key_sums[:, 0 : 2 * WIN]
        bias_grad[place, :, 3 * WIN : 4 * WIN] = key_sums[:, 2 * WIN : 3 * WIN] + jnp.sum(
            third.astype(F32), axis=0, keepdims=True
        )
        bias_grad[place, :, 4 * WIN : 5 * WIN] = key_sums[:, 3 * WIN :]
        bias_grad[place, :, 5 * WIN :] = jnp.zeros((1, WIN), F32)
        return carry

    lax.fori_loop(0, high - low, one, 0)

    def finish_stores():
        for i in range(high - low):
            for copy in store_copies(gbuf, i, grads, store_sems, scal):
                copy.wait()

    if not last:
        finish_stores()
        return
    row_grads[...] = jnp.zeros_like(row_grads)
    row_grads[0:1, :] = jnp.sum(given_wide, axis=0, keepdims=True)
    normed, inverse = normalize(after_self[...])
    hidden_grad = back[...]
    row_grads[1:2, :] = jnp.sum(hidden_grad * normed, axis=0, keepdims=True)
    total = d_cross[...] + normalize_back(hidden_grad * gain[...], normed, inverse)
    d_after[...] = total
    clip = own_clip(scal, rows, splits)
    d_attn[...] = (total * per_row(mod, 2, clip)).astype(BF16)
    sums[...] = clip_sums(own_clip_row(scal, rows, splits), total * branch[...])
    text_out[...] = text_back[...].astype(BF16)
    finish_stores()


def pack_small(table, own, cross, inner, given_sum, cross_rows, out_row, first, gate, second, out):
    n_dp = table.shape[1] // WIN
    splits, clips = out.shape[0], 3
    lane = lax.broadcasted_iota(jnp.int32, (D, n_dp * WIN), 0)

    def moved(value, which):
        choose = (lane == table[which : which + 1, :]).astype(F32).astype(BF16)
        high = value.astype(BF16).astype(F32)
        middle = (value - high).astype(BF16).astype(F32)
        parts = jnp.concatenate([high, middle, value - high - middle], axis=0).astype(BF16)
        found = nn(parts, choose)
        count = value.shape[0]
        return found[:count] + found[count : 2 * count] + found[2 * count :]

    def by_shard(ref):
        return jnp.concatenate([ref[z] for z in range(splits)], axis=0)

    both = moved(jnp.concatenate([by_shard(own), by_shard(cross)], axis=0), 0)
    heads = both[:splits] + pltpu.roll(both[splits:], 48, 1)
    hidden = moved(by_shard(inner), 1)
    rows = moved(
        jnp.concatenate(
            [given_sum, cross_rows[0:2, :], out_row[...]] + [jnp.zeros((4, D), F32)], axis=0
        ),
        2,
    )
    out[...] = jnp.zeros_like(out)
    for z in range(splits):
        for c in range(clips):
            for j in range(6):
                source, col = ((first, j), (gate, 0), (second, j - 3))[(j > 1) + (j > 2)]
                out[z, c * 6 + j : c * 6 + j + 1, :] = source[c : c + 1, col * D : (col + 1) * D]
        for d in range(n_dp):
            span = slice(d * WIN, (d + 1) * WIN)
            parts = [heads[z : z + 1, span], hidden[z : z + 1, span]]
            parts += [rows[r : r + 1, span] for r in range(4)]
            spot = clips * 6 + d
            out[z, spot : spot + 1, :] = jnp.concatenate(parts, axis=1)


def self_backward(n_p, splits, low, high, small, *refs):
    n_w = 2 * n_p
    scal = refs[0]
    frames = refs[1 : 1 + splits]
    given_ref, hidden_t, kv_in, q_in, att_in, lse = refs[1 + splits : 7 + splits]
    pieces = refs[7 + splits : 7 + splits + n_w]
    rest = refs[7 + splits + n_w :]
    first, last = low == 0, high == splits
    if not first:
        back_in, bias_in = rest[:2]
        rest = rest[2:]
    if small:
        table, cross_bias, inner_bias, cross_rows, out_row, gate, second = rest[:7]
        rest = rest[7:]
    n_o = 2 if n_p > 1 else 1
    grads = rest[:n_o]
    bias_grad = rest[n_o]
    rest = rest[n_o + 1 :]
    if last:
        own = rest[0]
        parts = rest[1:splits]
        row_grads, sums = rest[splits : splits + 2]
        rest = rest[splits + 2 :]
        if small:
            own_small, small_rows, back = rest[0], rest[1], rest[2]
            rest = rest[3:]
        else:
            back = rest[0]
            rest = rest[1:]
    else:
        back = rest[0]
        rest = rest[1:]
    weights, gbuf, mask, probs, dscore, key_grad, load_sems, store_sems = rest
    rows = frames[0].shape[0]
    count = rows * splits
    load_wait = load_start(own_and_others(pieces), weights, load_sems, scal, low)
    self_mask(scal, mask, rows, splits)
    given = given_ref[...]
    given_wide = given.astype(F32)
    given_t = given_wide.T.astype(BF16)
    if first:
        back[...] = jnp.zeros_like(back)
        bias_grad[...] = jnp.zeros_like(bias_grad)
    else:
        back[...] = back_in[...]
        bias_grad[...] = bias_in[...]

    def one(i, carry):
        load_wait(i)
        z = i + low
        place = shard_index(scal, z, splits)

        def kv(lo, hi, col):
            return kv_in[z, lo:hi, col * WIN : (col + 1) * WIN]

        def put(lo, hi, k01, v01, k2, v2):
            key_grad[lo:hi, 0:WIN] = k01.astype(BF16)
            key_grad[lo:hi, WIN : 2 * WIN] = v01.astype(BF16)
            key_grad[lo:hi, 2 * WIN : 3 * WIN] = k2.astype(BF16)
            key_grad[lo:hi, 3 * WIN : 4 * WIN] = v2.astype(BF16)

        head_grad = nn(given, weights[i, :, 4 * WIN :]).astype(BF16)
        totals = [lse[z, h : h + 1, :] for h in range(3)]
        pair, third = attend_back(
            q_in[z], kv, att_in[z], head_grad, mask, totals, probs, dscore, count, put
        )
        pair = pair.astype(BF16)
        key_grad[0:rows, 2 * WIN : 3 * WIN] = (
            key_grad[0:rows, 2 * WIN : 3 * WIN].astype(F32) + third
        ).astype(BF16)
        part = nn(hidden_t[...], key_grad[...])
        out_part = nn(given_t, att_in[z])
        gbuf[i, :, 0:WIN] = nn(hidden_t[:, 0:rows], pair).astype(BF16)
        gbuf[i, :, WIN : 4 * WIN] = part[:, 0 : 3 * WIN].astype(BF16)
        gbuf[i, :, 4 * WIN : 5 * WIN] = (part[:, 3 * WIN :] + out_part[:, 0:WIN]).astype(BF16)
        gbuf[i, :, 5 * WIN :] = out_part[:, WIN:].astype(BF16)
        for copy in store_copies(gbuf, i, grads, store_sems, scal):
            copy.start()
        for lo in range(0, count, 256):
            back[lo : lo + 256, :] += nt(
                key_grad[lo : lo + 256, :], weights[i, :, WIN : 5 * WIN]
            )
        back[0:rows, :] += nt(pair, weights[i, :, 0:WIN])
        key_sums = jnp.sum(key_grad[...].astype(F32), axis=0, keepdims=True)
        bias_grad[place, :, 0:WIN] = jnp.sum(pair.astype(F32), axis=0, keepdims=True)
        bias_grad[place, :, WIN : 5 * WIN] = key_sums
        bias_grad[place, :, 5 * WIN :] = jnp.zeros((1, WIN), F32)
        return carry

    lax.fori_loop(0, high - low, one, 0)

    def finish_stores():
        for i in range(high - low):
            for copy in store_copies(gbuf, i, grads, store_sems, scal):
                copy.wait()

    if not last:
        finish_stores()
        return
    given_sum = jnp.sum(given_wide, axis=0, keepdims=True)
    row_grads[...] = jnp.zeros_like(row_grads)
    row_grads[0:1, :] = given_sum
    shift = jnp.zeros((8, D), F32)
    scale = jnp.zeros((8, D), F32)
    for block in range(splits):
        value = back[block * rows : (block + 1) * rows, :]
        if block == 0:
            own[...] = value
        else:
            parts[block - 1][0:rows, :] = value.astype(BF16)
        normed, _ = normalize(frames[block][...].astype(F32))
        clip_row = own_clip_row(scal, rows, splits, block)
        shift = shift + clip_sums(clip_row, value)
        scale = scale + clip_sums(clip_row, value * normed)
    sums[:, 0:D] = shift
    sums[:, D:] = scale
    if small:
        pack_small(
            table,
            bias_grad,
            cross_bias,
            inner_bias,
            given_sum,
            cross_rows,
            out_row,
            sums,
            gate,
            second,
            small_rows,
        )
        for k in range(splits):
            value = small_rows[shard_index(scal, k, splits)]
            if k == 0:
                own_small[...] = value
            else:
                parts[k - 1][rows:, :] = value.astype(BF16)
    finish_stores()


def finish(splits, *refs):
    scal, frames, mod, d_after, own = refs[:5]
    parts = refs[5 : 4 + splits]
    out = refs[4 + splits]
    rows = frames.shape[0]
    value = own[...]
    for part in parts:
        value = value + part[0 : own.shape[0], :].astype(F32)
    normed, inverse = normalize(frames[...].astype(F32))
    scale = 1.0 + per_row(mod, 1, own_clip(scal, rows, splits))
    out[...] = d_after[...] + normalize_back(value * scale, normed, inverse)


def bias_table(n_dp):
    table = np.full((8, n_dp * WIN), -1, np.int32)
    for d in range(n_dp):
        for i in range(48):
            part, h, r = i // 24, i % 24 // 8, i % 8
            spot = d * 8 + r
            start = (h * HD if h < 2 else 3 * WIN) if part == 0 else (2 + h / 2) * WIN
            table[0, d * WIN + i] = (start if part == 0 or h < 2 else 4 * WIN) + spot
        for i in range(96):
            table[1, d * WIN + i] = i // 32 * 256 + d * 32 + i % 32
            table[2, d * WIN + i] = d * 96 + i
    return table


MEMORY = {"v": pltpu.VMEM, "s": pltpu.SMEM, "a": pl.ANY}


def call(body, inputs, outs, scratch, flops, name):
    moved = sum(a.size * a.dtype.itemsize for _, a in inputs)
    moved += sum(_size(s, t) for _, s, t in outs)
    return pl.pallas_call(
        body,
        out_shape=tuple(jax.ShapeDtypeStruct(s, t) for _, s, t in outs),
        in_specs=[pl.BlockSpec(memory_space=MEMORY[m]) for m, _ in inputs],
        out_specs=tuple(pl.BlockSpec(memory_space=MEMORY[m]) for m, _, _ in outs),
        scratch_shapes=scratch,
        compiler_params=pltpu.CompilerParams(vmem_limit_bytes=58 * 1024 * 1024),
        cost_estimate=pl.CostEstimate(flops=int(flops), bytes_accessed=int(moved), transcendentals=0),
        name=name,
    )(*[a for _, a in inputs])


def _size(shape, kind):
    total = jnp.dtype(kind).itemsize
    for s in shape:
        total *= s
    return total


class Ring:
    def __init__(self):
        self.n_dp = lax.axis_size("dp")
        self.splits = lax.axis_size("head")
        self.square = self.n_dp == 8
        if self.square:
            self.core = [(i, i ^ 1) for i in range(8)]
            self.first = [(i, i ^ (4 if i & 1 else 2)) for i in range(8)]
            self.second = [(i, i ^ (2 if i & 1 else 4)) for i in range(8)]

    def offsets(self):
        if not self.square:
            return [jnp.int32(0)]
        me = lax.axis_index("dp")
        rows = D // 8

        def kept(d):
            odd = d & 1
            return [d, d ^ (2 + 2 * odd), d ^ (4 - 2 * odd), d ^ 6]

        return [place * rows for place in kept(me) + kept(me ^ 1)]

    def z_pieces(self, value, far=None):
        n = self.splits
        return [value] + [
            lax.ppermute(value, "head", [(s, (s + k) % n) for s in range(n)])
            for k in (range(1, n) if far is None else far)
        ]

    def z_back(self, parts):
        n = self.splits
        return [
            lax.ppermute(parts[k - 1], "head", [(s, (s - k) % n) for s in range(n)])
            for k in range(1, n)
        ]

    def across(self, value, how):
        return lax.ppermute(value, "dp", how)

    def z_move(self, value, k):
        n = self.splits
        return lax.ppermute(value, "head", [(s, (s - k) % n) for s in range(n)])


class GradSum:
    def __init__(self, ring, grads):
        self.ring, self.grads = ring, list(grads)
        self.moved = []
        self.arrived = []
        if not ring.square:
            self.whole = lax.psum_scatter(grads[0][0], "dp", scatter_dimension=1, tiled=True)

    def across(self, value, how):
        if self.ring.square:
            self.moved.append(self.ring.across(value.astype(BF16), how))

    def block(self, i):
        value = self.grads[0][i].astype(F32) + self.moved[0][i].astype(F32)
        if len(self.moved) > 1:
            value = value + self.moved[1][i].astype(F32)
        return value

    def core(self):
        if self.ring.square:
            self.across(self.grads[1], self.ring.core)

    def second(self):
        if self.ring.square:
            self.across(self.block(slice(2, 4)), self.ring.second)

    def first(self):
        if self.ring.square:
            self.across(self.block(1), self.ring.first)

    def own(self, i):
        if not self.ring.square:
            return self.whole[i].astype(F32)
        value = self.grads[0][0, i].astype(F32) + self.moved[2][i].astype(F32)
        return value + self.moved[0][0, i].astype(F32) + self.moved[1][0, i].astype(F32)

    def shard(self, start):
        count = self.grads[0].shape[1]
        for i in range(count):
            k = i if start == 1 else start + i
            if k > 0:
                self.arrived.append(self.ring.z_move(self.own(i).astype(BF16), k))


def join_second(low, high):
    if not low.ring.square:
        return []
    part = slice(2, 4)
    both = jnp.concatenate([low.block(part), high.block(part)], axis=1)
    return [low.ring.across(both.astype(BF16), low.ring.second)]


def join_first(low, high):
    if not low.ring.square:
        return []
    both = jnp.concatenate([low.block(1), high.block(1)], axis=0)
    return [low.ring.across(both.astype(BF16), low.ring.first)]


def join_take(low, high, moved):
    count = low.grads[0].shape[1]
    for value in moved:
        low.moved.append(value[..., :count, :, :])
        high.moved.append(value[..., count:, :, :])


def join_shards(pairs):
    ring = pairs[0][0].ring
    half = ring.splits // 2
    return [
        ring.z_move(
            jnp.concatenate([pair[k // half].own(k % half) for pair in pairs], axis=1).astype(BF16),
            k,
        )
        for k in range(1, ring.splits)
    ]


class Gather:
    def __init__(self, ring, mine):
        self.ring = ring
        if ring.square:
            self.kept, self.other = [mine], []
        else:
            self.kept, self.other = [lax.all_gather(mine, "dp", axis=1, tiled=True)], []

    def sides(self):
        if self.ring.square:
            self.kept.append(self.ring.across(self.kept[0], self.ring.first))
            self.kept.append(self.ring.across(self.kept[0], self.ring.second))

    def corner(self):
        if self.ring.square:
            self.kept.append(self.ring.across(self.kept[1], self.ring.second))

    def core(self, *which):
        if self.ring.square:
            for i in which:
                self.other.append(self.ring.across(self.kept[i], self.ring.core))

    def pieces(self):
        return self.kept + self.other


def meet(*groups):
    flat = [v for group in groups for v in group]
    flat = list(lax.optimization_barrier(tuple(flat)))
    for group in groups:
        for i in range(len(group)):
            group[i] = flat.pop(0)


def to_layout(q, k, v, o):
    return jnp.concatenate(
        [
            q[:, :WIN],
            k[:, :WIN],
            v[:, :WIN],
            q[:, WIN:],
            k[:, WIN:],
            v[:, WIN:],
            o[:, WIN:],
            o[:, :WIN],
        ],
        axis=1,
    )


def from_layout(value):
    def pick(pair, third):
        return jnp.concatenate(
            [value[:, pair : pair + WIN], value[:, third : third + HD]], axis=1
        )

    return pick(0, 3 * WIN), pick(WIN, 3 * WIN + HD), pick(2 * WIN, 4 * WIN), pick(
        5 * WIN, 4 * WIN + HD
    )


def mod_gradients(ring, sums, clips):
    part = jnp.concatenate(sums, axis=1)[:clips]
    got = lax.all_to_all(
        jnp.broadcast_to(part[None], (ring.splits,) + part.shape), "head", 0, 0, tiled=True
    )
    low = jnp.sum(got, axis=0).astype(BF16)
    return lax.all_to_all(
        jnp.broadcast_to(low[None], (ring.n_dp,) + low.shape), "dp", 0, 0, tiled=True
    ).reshape(ring.n_dp * clips, -1)


def on_device(
    frames_in,
    step_embed,
    text_feats,
    clip_frames,
    text_tokens,
    out_grad,
    ada_weight,
    ada_bias,
    qkv_weight,
    qv_bias,
    attn_out_weight,
    attn_out_bias,
    cross_gain,
    cross_q_weight,
    cross_q_bias,
    cross_kv_weight,
    cross_v_bias,
    cross_out_weight,
    cross_out_bias,
    mlp_in_weight,
    mlp_in_bias,
    mlp_out_weight,
    mlp_out_bias,
):
    both = ("dp", "head")
    ring = Ring()
    n_dp, splits = ring.n_dp, ring.splits
    z_index = lax.axis_index("head")
    rows = frames_in.shape[0]
    count = rows * splits
    text_count = text_feats.shape[0]
    clips = clip_frames.shape[1]
    width = D // splits
    shard_rows = D // n_dp
    ends = jnp.cumsum(clip_frames[0])
    offs = ring.offsets()
    n_p = len(offs)
    scal = jnp.stack(
        [z_index, ends[0], ends[1], text_tokens[0, 0], text_tokens[0, 1], text_tokens[0, 2]]
        + [jnp.int32(0)] * 2
        + [o.astype(jnp.int32) for o in offs]
        + [jnp.int32(0)] * (S_LEN - S_OFF - n_p)
    ).astype(jnp.int32)

    shard_self = to_layout(
        qkv_weight[:, 0], qkv_weight[:, 1], qkv_weight[:, 2], attn_out_weight.T
    )
    shard_cross = to_layout(
        cross_q_weight, cross_kv_weight[:, 0], cross_kv_weight[:, 1], cross_out_weight.T
    )

    biases = [
        ada_bias,
        qv_bias.reshape(-1),
        attn_out_bias,
        cross_gain,
        cross_q_bias.reshape(-1),
        cross_v_bias.reshape(-1),
        cross_out_bias,
        mlp_in_bias.reshape(-1),
        mlp_out_bias,
    ]
    flat = jnp.concatenate(biases)
    cols = step_embed.reshape(clips, n_dp, shard_rows).transpose(1, 0, 2).reshape(n_dp, -1)
    sent = jnp.concatenate(
        [
            jnp.broadcast_to(flat[None, None], (n_dp, splits, flat.shape[0])),
            jnp.broadcast_to(cols[:, None], (n_dp, splits, cols.shape[1])),
        ],
        axis=2,
    ).reshape(n_dp * splits, -1)
    got = lax.all_to_all(sent, both, 0, 0, tiled=True)
    attn_shard = jnp.concatenate([shard_self, shard_cross], axis=1)
    attn_shards = ring.z_pieces(attn_shard)[1:]
    own_gather = Gather(ring, attn_shard[None])
    own_gather.sides()
    own_gather.corner()
    own_gather.core(0, 1, 2, 3)
    mlp_shard = jnp.concatenate([mlp_in_weight, mlp_out_weight.T], axis=1)
    held = [got]
    meet(held, attn_shards, own_gather.kept)
    got = held[0].reshape(n_dp, splits, -1)
    step_cols = got[:, 0, flat.shape[0] :].reshape(n_dp * clips, shard_rows).astype(F32)
    silu_cols = jax.nn.silu(step_cols).astype(BF16)
    spots = []
    place = 0
    for b in biases:
        spots.append(got[:, :, place : place + b.shape[0]].astype(F32))
        place += b.shape[0]

    def over_dp(value):
        return value[:, 0].reshape(1, -1)

    def by_head(value, lead=1):
        n = value.shape[2] // (lead * 3)
        v = value.reshape(n_dp, splits, lead, 3, n).transpose(1, 2, 3, 0, 4)
        return v.reshape(splits, lead, 3 * n_dp * n)

    all_ada_bias = over_dp(spots[0])
    qv = by_head(spots[1], 2)
    nothing = jnp.zeros((splits, width), F32)
    bias_self = to_layout(qv[:, 0], nothing, qv[:, 1], nothing)[:, None]
    all_attn_bias = over_dp(spots[2])
    all_gain = over_dp(spots[3])
    bias_cross = to_layout(
        by_head(spots[4])[:, 0], nothing, by_head(spots[5])[:, 0], nothing
    )[:, None]
    all_cross_bias = over_dp(spots[6])
    all_in_bias = by_head(spots[7])
    all_out_bias = over_dp(spots[8])

    mod_part = jnp.dot(silu_cols, ada_weight, preferred_element_type=F32)
    mod_got = lax.all_to_all(mod_part.reshape(n_dp, clips, -1), "dp", 0, 0, tiled=True)

    half = splits // 2
    attn_gather = Gather(ring, jnp.stack(attn_shards))
    attn_gather.sides()
    frame_blocks = ring.z_pieces(frames_in)
    held = [mlp_shard]
    meet(held, attn_gather.kept)
    mlp_shard = held[0]
    mod = jnp.sum(mod_got, axis=0) + all_ada_bias
    attn_gather.corner()
    attn_gather.core(0, 1, 2, 3)
    mlp_shards = ring.z_pieces(mlp_shard, range(1, half))
    mlp_gathers = [Gather(ring, jnp.stack(mlp_shards))]
    mlp_gathers[0].sides()
    mlp_gathers[0].core(0)
    mlp_late = ring.z_pieces(mlp_shard, range(half, splits))[1:]

    def dma(n):
        return pltpu.SemaphoreType.DMA(n)

    def any_of(arrays):
        return [("a", a) for a in arrays]

    def vmem_of(arrays):
        return [("v", a) for a in arrays]

    piece_rows = D // n_p
    kept_out = [("a", (max(n_p // 2, 1), splits, piece_rows, D), BF16)] * (2 if n_p > 1 else 1)
    n_o = len(kept_out)
    shard_type = pltpu.VMEM((splits, D, D), BF16)

    results = list(call(
        partial(self_forward, n_p, splits),
        [("s", scal)]
        + vmem_of(frame_blocks)
        + vmem_of([mod, bias_self, all_attn_bias])
        + any_of(own_gather.pieces() + attn_gather.pieces()),
        [
            ("v", (D, count), BF16),
            ("a", (splits, count, 4 * WIN), BF16),
            ("v", (splits, rows, 2 * WIN), BF16),
            ("v", (splits, rows, 2 * WIN), BF16),
            ("v", (splits, 8, rows), F32),
            ("v", (rows, D), F32),
            ("v", (rows, D), F32),
        ],
        [
            pltpu.VMEM((count, D), BF16),
            pltpu.VMEM((splits, count, 4 * WIN), BF16),
            shard_type,
            pltpu.VMEM((rows, count), F32),
            pltpu.VMEM((rows, count), F32),
            pltpu.VMEM((rows, count), BF16),
            dma((n_p, splits)),
            dma((splits,)),
        ],
        22 * US,
        "self_forward",
    ))
    meet(
        results, mlp_gathers[0].kept, mlp_gathers[0].other, mlp_late, attn_gather.kept, attn_gather.other
    )
    hidden_one, self_kv, self_q, self_att, self_lse, attn_branch, after_self = results
    mlp_gathers[0].corner()
    mlp_gathers[0].core(1, 2)
    mlp_gathers.append(Gather(ring, jnp.stack(mlp_late)))
    mlp_gathers[1].sides()

    results = list(call(
        partial(cross_forward, n_p, splits),
        [("s", scal)]
        + vmem_of([after_self, text_feats, all_gain, bias_cross, all_cross_bias])
        + any_of(own_gather.pieces() + attn_gather.pieces()),
        [
            ("v", (D, rows), BF16),
            ("v", (D, text_count), BF16),
            ("a", (splits, text_count, 4 * WIN), BF16),
            ("v", (splits, rows, 2 * WIN), BF16),
            ("v", (splits, rows, 2 * WIN), BF16),
            ("v", (splits, 8, rows), F32),
            ("v", (rows, D), F32),
        ],
        [
            pltpu.VMEM((splits, text_count, 4 * WIN), BF16),
            shard_type,
            pltpu.VMEM((rows, text_count), F32),
            pltpu.VMEM((rows, text_count), F32),
            pltpu.VMEM((rows, text_count), BF16),
            dma((n_p, splits)),
            dma((splits,)),
        ],
        17 * US,
        "cross_forward",
    ))
    meet(results, mlp_gathers[0].kept, mlp_gathers[0].other, mlp_gathers[1].kept)
    hidden_two_t, text_t, cross_kv, cross_q, cross_att, cross_lse, after_cross = results
    mlp_gathers[0].core(3)
    mlp_gathers[1].corner()
    mlp_gathers[1].core(0, 1, 2)

    kept_half = [(m, (shape[0], half) + shape[2:], kind) for m, shape, kind in kept_out]
    kept_wide = [(m, shape[:3] + (2 * D,), kind) for m, shape, kind in kept_half]
    half_type = pltpu.VMEM((half, D, D), BF16)

    def back_scratch(keys):
        return [
            half_type,
            half_type,
            pltpu.VMEM((keys, rows), F32),
            pltpu.VMEM((3, keys, rows), BF16),
            pltpu.VMEM((3, keys, rows), BF16),
            pltpu.VMEM((keys, 4 * WIN), BF16),
            dma((n_p, half)),
            dma((n_p, half)),
        ]

    bias_type = [("v", (splits, 1, D), F32)]
    mlp_args = [after_cross, out_grad, mod, all_in_bias, all_out_bias]
    mlp_scratch = [
        pltpu.VMEM((half, D, 2 * D), BF16),
        pltpu.VMEM((half, D, 2 * D), BF16),
        dma((n_p, half)),
        dma((n_p, half)),
    ]
    results = call(
        partial(feed_forward, n_p, splits, 0, half),
        [("s", scal)] + vmem_of(mlp_args) + any_of(mlp_gathers[0].pieces()),
        kept_wide + bias_type + [("v", (rows, D), F32)] * 2,
        mlp_scratch,
        9 * US,
        "feed_forward_first",
    )
    results = list(results)
    meet(results, mlp_gathers[1].kept, mlp_gathers[1].other)
    mlp_gathers[1].core(3)
    sum_mlp = [GradSum(ring, results[:n_o])]
    in_bias_grad, mlp_state, mlp_back = results[n_o:]
    sum_mlp[0].core()
    results = call(
        partial(feed_forward, n_p, splits, half, splits),
        [("s", scal)]
        + vmem_of(mlp_args)
        + any_of(mlp_gathers[1].pieces())
        + vmem_of([mlp_state, mlp_back, in_bias_grad]),
        kept_wide
        + bias_type
        + [
            ("v", (rows, D), BF16),
            ("v", (rows, D), F32),
            ("v", (1, D), F32),
            ("v", (8, 3 * D), F32),
        ],
        [pltpu.VMEM((rows, D), F32), pltpu.VMEM((rows, D), F32)] + mlp_scratch,
        10 * US,
        "feed_forward_last",
    )
    results = list(results)
    meet(results, sum_mlp[0].moved)
    sum_mlp.append(GradSum(ring, results[:n_o]))
    in_bias_grad, layer_out, d_after_cross, out_bias_grad, sums_two = results[n_o:]
    sum_mlp[0].second()
    sum_mlp[1].core()
    cross_args = [
        d_after_cross,
        after_self,
        hidden_two_t,
        text_t,
        all_gain,
        mod,
        attn_branch,
        cross_kv,
        cross_q,
        cross_att,
        cross_lse,
    ]
    cross_state = [("v", (rows, D), F32), ("v", (text_count, D), F32)]
    results = call(
        partial(cross_backward, n_p, splits, 0, half),
        [("s", scal)] + vmem_of(cross_args) + any_of(own_gather.pieces() + attn_gather.pieces()),
        kept_half + bias_type + cross_state,
        back_scratch(text_count),
        14 * US,
        "cross_backward_first",
    )
    results = list(results)
    meet(results, sum_mlp[0].moved, sum_mlp[1].moved)
    sum_cross = [GradSum(ring, results[:n_o])]
    cross_bias_grad, cross_back, text_back = results[n_o:]
    sum_mlp[0].first()
    sum_mlp[1].second()
    sum_cross[0].core()
    results = call(
        partial(cross_backward, n_p, splits, half, splits),
        [("s", scal)]
        + vmem_of(cross_args)
        + any_of(own_gather.pieces() + attn_gather.pieces())
        + vmem_of([cross_back, text_back, cross_bias_grad]),
        kept_half
        + bias_type
        + [
            ("v", (rows, D), F32),
            ("v", (rows, D), BF16),
            ("v", (text_count, D), BF16),
            ("v", (8, D), F32),
            ("v", (8, D), F32),
        ],
        [pltpu.VMEM((rows, D), F32), pltpu.VMEM((text_count, D), F32)] + back_scratch(text_count),
        15 * US,
        "cross_backward_last",
    )
    results = list(results)
    meet(results, sum_mlp[0].moved, sum_mlp[1].moved, sum_cross[0].moved)
    sum_cross.append(GradSum(ring, results[:n_o]))
    cross_bias_grad, d_after_self, d_attn, text_out, cross_rows, gate_sums = results[n_o:]
    sum_mlp[1].first()
    sum_cross[0].second()
    sum_cross[1].core()
    text_got = lax.all_to_all(
        text_out.reshape(splits, text_count // splits, D), "head", 0, 0, tiled=True
    )
    self_args = [d_attn, hidden_one, self_kv, self_q, self_att, self_lse]
    results = call(
        partial(self_backward, n_p, splits, 0, half, False),
        [("s", scal)] + vmem_of(frame_blocks) + vmem_of(self_args) + any_of(own_gather.pieces() + attn_gather.pieces()),
        kept_half + bias_type + [("v", (count, D), F32)],
        back_scratch(count),
        17 * US,
        "self_backward_first",
    )
    results = list(results)
    meet(
        results,
        sum_mlp[0].moved,
        sum_mlp[1].moved,
        sum_cross[0].moved,
        sum_cross[1].moved,
    )
    sum_self = [GradSum(ring, results[:n_o])]
    self_bias_grad, self_back = results[n_o:]
    sum_mlp[0].shard(1)
    sum_mlp[1].shard(2)
    sum_cross[1].second()
    sum_self[0].core()
    small_args, small_outs, small_scratch, small_count = [], [], [], 0
    if ring.square:
        small_count = 32
        small_args = [jnp.asarray(bias_table(n_dp)), cross_bias_grad, in_bias_grad]
        small_args += [cross_rows, out_bias_grad, gate_sums, sums_two]
        small_outs = [("v", (small_count, D), F32)]
        small_scratch = [pltpu.VMEM((splits, small_count, D), F32)]
    results = call(
        partial(self_backward, n_p, splits, half, splits, ring.square),
        [("s", scal)]
        + vmem_of(frame_blocks)
        + vmem_of(self_args)
        + any_of(own_gather.pieces() + attn_gather.pieces())
        + vmem_of([self_back, self_bias_grad] + small_args),
        kept_half
        + bias_type
        + [("v", (rows, D), F32)]
        + [("v", (rows + small_count, D), BF16)] * (splits - 1)
        + [("v", (8, D), F32), ("v", (8, 2 * D), F32)]
        + small_outs,
        small_scratch + [pltpu.VMEM((count, D), F32)] + back_scratch(count),
        18 * US,
        "self_backward_last",
    )
    results = list(results)
    held = [in_bias_grad, out_bias_grad, cross_bias_grad, cross_rows, gate_sums, sums_two]
    held.append(text_got)
    meet(
        results,
        held,
        sum_mlp[0].arrived,
        sum_mlp[1].arrived,
        sum_cross[0].moved,
        sum_cross[1].moved,
        sum_self[0].moved,
    )
    sum_self.append(GradSum(ring, results[:n_o]))
    self_bias_grad, own_part = results[n_o : n_o + 2]
    parts = results[n_o + 2 : n_o + 1 + splits]
    self_rows, sums_one = results[n_o + 1 + splits : n_o + 3 + splits]
    sum_self[1].core()
    arrived = ring.z_back(parts)
    in_bias_grad, out_bias_grad, cross_bias_grad, cross_rows, gate_sums, sums_two, text_got = held
    early, late = arrived[:1], arrived[1:]
    meet(sum_self[1].moved, sum_cross[1].moved, early)
    far = join_second(*sum_self)
    near_cross = join_first(*sum_cross)
    meet(far, near_cross)
    join_take(*sum_self, far)
    join_take(*sum_cross, near_cross)
    near = join_first(*sum_self)
    meet(late, near)
    arrived = early + late
    join_take(*sum_self, near)
    last = join_shards([sum_cross, sum_self])
    if ring.square:
        small = results[-1] + sum(part[rows:].astype(F32) for part in arrived)
        mod_low = small[: 6 * clips].astype(BF16).astype(F32)
        sent = jnp.concatenate(
            [
                jnp.broadcast_to(mod_low[None], (n_dp,) + mod_low.shape),
                small[6 * clips : 6 * clips + n_dp, None],
            ],
            axis=1,
        )
        held = [lax.all_to_all(sent, "dp", 0, 0, tiled=True)]
    if ring.square:
        mod_all = held[0][:, : 6 * clips].reshape(n_dp * clips, -1).astype(BF16)
        bias_sum = jnp.sum(held[0][:, 6 * clips], axis=0)
        places = [0, 24, 2 * WIN, 4 * WIN, 48, 72, 3 * WIN, WIN, 5 * WIN]
    else:
        mod_all = mod_gradients(ring, [sums_one, gate_sums, sums_two], clips)
    step_part = lax.dot_general(
        mod_all, ada_weight, (((1,), (1,)), ((), ())), preferred_element_type=F32
    )
    (frames_grad,) = call(
        partial(finish, splits),
        [("s", scal)] + vmem_of([frames_in, mod, d_after_self, own_part]) + vmem_of(arrived),
        [("v", (rows, D), F32)],
        [],
        3 * US,
        "finish",
    )
    text_grad = jnp.sum(text_got.astype(F32), axis=0)

    grad_ada = lax.dot_general(
        silu_cols, mod_all, (((0,), (0,)), ((), ())), preferred_element_type=F32
    )
    dp_index = lax.axis_index("dp")
    bias_width = ada_bias.shape[0]
    grad_ada_bias = jnp.sum(
        lax.dynamic_slice_in_dim(mod_all, dp_index * bias_width, bias_width, 1).astype(F32), axis=0
    )
    step_got = lax.all_to_all(step_part.reshape(n_dp, clips, shard_rows), "dp", 0, 0, tiled=True)
    step_got = [step_got]
    meet(last, step_got)
    (step_got,) = step_got
    total_cross, total_self = (
        pair[0].own(0) + sum(part[:, i * D : (i + 1) * D].astype(F32) for part in last)
        for i, pair in enumerate((sum_cross, sum_self))
    )
    step_value = step_embed.astype(F32)
    _, silu_pull = jax.vjp(jax.nn.silu, step_value)
    step_grad = silu_pull(step_got.transpose(1, 0, 2).reshape(clips, D))[0]

    def spread(value):
        v = value.reshape(n_dp, 1, D // n_dp)
        return jnp.broadcast_to(v, (n_dp, splits, D // n_dp))

    def heads_out(value):
        n = value.shape[1] // (3 * n_dp)
        return value.reshape(splits, 3, n_dp, n).transpose(2, 0, 1, 3).reshape(n_dp, splits, 3 * n)

    sq, _, sv, _ = from_layout(self_bias_grad[:, 0])
    cq, _, cv, _ = from_layout(cross_bias_grad[:, 0])
    entries = [
        heads_out(sq),
        heads_out(sv),
        spread(self_rows[0]),
        spread(cross_rows[1]),
        heads_out(cq),
        heads_out(cv),
        spread(cross_rows[0]),
        heads_out(in_bias_grad[:, 0]),
        spread(out_bias_grad[0]),
    ]
    if not ring.square:
        packed = jnp.concatenate(entries, axis=2)
        places = [sum(e.shape[2] for e in entries[:i]) for i in range(len(entries))]
        bias_sum = jnp.sum(
            lax.all_to_all(packed.reshape(n_dp * splits, -1), both, 0, 0, tiled=True), axis=0
        )
    bias_out = [bias_sum[p : p + e.shape[2]] for p, e in zip(places, entries)]

    total_mlp = sum_mlp[0].own(0) + sum(
        part.astype(F32) for part in sum_mlp[0].arrived + sum_mlp[1].arrived
    )
    gq, gk, gv, go = from_layout(total_self)
    hq, hk, hv, ho = from_layout(total_cross)
    return (
        layer_out,
        frames_grad,
        step_grad,
        text_grad,
        grad_ada,
        grad_ada_bias,
        jnp.stack([gq, gk, gv], axis=1),
        jnp.stack([bias_out[0], bias_out[1]]).reshape(qv_bias.shape),
        go.T,
        bias_out[2],
        bias_out[3],
        hq,
        bias_out[4].reshape(cross_q_bias.shape),
        jnp.stack([hk, hv], axis=1),
        bias_out[5].reshape(cross_v_bias.shape),
        ho.T,
        bias_out[6],
        total_mlp[:, :D],
        bias_out[7].reshape(mlp_in_bias.shape),
        total_mlp[:, D:].T,
        bias_out[8],
    )


def solution(mesh):
    rows_all, by_dp = P(("dp", "head"), None), P("dp", None)
    head_dp, dp_head = P("head", "dp"), P("dp", "head")
    dp_three, vector = P("dp", None, "head"), P("dp")
    params = (
        by_dp,
        vector,
        dp_three,
        P(None, "head", "dp"),
        head_dp,
        vector,
        vector,
        dp_head,
        head_dp,
        dp_three,
        head_dp,
        head_dp,
        vector,
        dp_head,
        head_dp,
        head_dp,
        vector,
    )
    return jax.shard_map(
        on_device,
        mesh=mesh,
        in_specs=(rows_all, by_dp, by_dp, by_dp, by_dp, rows_all) + params,
        out_specs=(rows_all, rows_all, by_dp, rows_all) + params,
        check_vma=False,
    )
```
